32 devices in a mesh: dp: 8 (over y, x, core), tensor: 4 (over z).
Axes of the slice: x: 2, y: 2, z: 4, core: 2. Of those that a mesh axis runs over, the one named last changes fastest.
Arguments:
- hidden_in: bfloat16 [8192, 1536], P(('dp', 'tensor')), may hold values from -6 to 6
- out_grad: bfloat16 [8192, 1536], P(('dp', 'tensor')), may hold values from -6 to 6
- norm_gain: bfloat16 [2, 1536], P(None, 'dp'), may hold values from 0.5 to 1.5
- proj_z: bfloat16 [2, 1536, 3072], P(None, 'dp', 'tensor'), may hold values from -0.15625 to 0.15625
- proj_x: bfloat16 [2, 1536, 3072], P(None, 'dp', 'tensor'), may hold values from -0.15625 to 0.15625
- proj_bc: bfloat16 [2, 1536, 256], P(None, 'dp'), may hold values from -0.15625 to 0.15625
- proj_dt: bfloat16 [2, 1536, 48], P(None, 'dp', 'tensor'), may hold values from -0.15625 to 0.15625
- conv_value: bfloat16 [2, 4, 3072], P(None, None, 'tensor'), may hold values from -3 to 3
- conv_value_bias: bfloat16 [2, 3072], P(None, 'tensor'), may hold values from -3 to 3
- conv_state: bfloat16 [2, 4, 256], P(None, None, 'dp'), may hold values from -3 to 3
- conv_state_bias: bfloat16 [2, 256], P(None, 'dp'), may hold values from -3 to 3
- step_bias: bfloat16 [2, 48], P(None, 'tensor'), may hold values from -7 to -2
- log_decay: bfloat16 [2, 48], P(None, 'tensor'), may hold values from 0 to 2.6875
- skip_gain: bfloat16 [2, 48], P(None, 'tensor'), may hold values from 0.5 to 1.5
- gate_gain: bfloat16 [2, 3072], P(None, 'tensor'), may hold values from 0.5 to 1.5
- proj_out: bfloat16 [2, 3072, 1536], P(None, 'tensor', 'dp'), may hold values from -0.109375 to 0.109375
Outputs:
- hidden_out: float32 [8192, 1536], P(('dp', 'tensor'))
- hidden_grad: float32 [8192, 1536], P(('dp', 'tensor'))
- grad_norm_gain: float32 [2, 1536], P(None, 'dp')
- grad_proj_z: float32 [2, 1536, 3072], P(None, 'dp', 'tensor')
- grad_proj_x: float32 [2, 1536, 3072], P(None, 'dp', 'tensor')
- grad_proj_bc: float32 [2, 1536, 256], P(None, 'dp')
- grad_proj_dt: float32 [2, 1536, 48], P(None, 'dp', 'tensor')
- grad_conv_value: float32 [2, 4, 3072], P(None, None, 'tensor')
- grad_conv_value_bias: float32 [2, 3072], P(None, 'tensor')
- grad_conv_state: float32 [2, 4, 256], P(None, None, 'dp')
- grad_conv_state_bias: float32 [2, 256], P(None, 'dp')
- grad_step_bias: float32 [2, 48], P(None, 'tensor')
- grad_log_decay: float32 [2, 48], P(None, 'tensor')
- grad_skip_gain: float32 [2, 48], P(None, 'tensor')
- grad_gate_gain: float32 [2, 3072], P(None, 'tensor')
- grad_proj_out: float32 [2, 3072, 1536], P(None, 'tensor', 'dp')
The draws below stay inside these ranges and needn't reach their ends.
All inputs are finite; a program needn't handle non-finite values.
Results may differ from the reference program's by a relative error of at most 0.018.
Values may be sent and summed in bfloat16 or wider, within the bound.
A program may use at most 256 MiB of HBM per device.

```python
import jax
import jax.numpy as jnp
from jax import lax

D = 1536
HEADS = 48
STATE = 128
CONV = 4
GROUP = 256
LAYERS = 2
SEQ = 1024
INNER = 3072
TOKENS = 8192
N_DP = 8


def block_levels(rng, dims, pieces, low, high):
    def one(position, blocks):
        draws = jax.random.uniform(jax.random.fold_in(jax.random.fold_in(rng, 6), position), (blocks,), jnp.float32, low / len(pieces), high / len(pieces))
        return jnp.repeat(jnp.exp(draws), dims[position] // blocks).reshape((-1,) + (1,) * (len(dims) - position - 1))

    level = one(*pieces[0])
    for cut in pieces[1:]:
        level = level * one(*cut)
    return level


def bell_draw(own_key, dims, scale, reach, split=(), dtype=jnp.bfloat16):
    values = jax.random.normal(own_key, dims, jnp.float32) * scale
    if len(split) > 0:
        values = block_levels(own_key, dims, split, -0.22, 0.18) * values
    return jnp.clip(values, min=-reach, max=reach).astype(dtype)


def setup_inputs(seed: int = 0) -> dict:
    seeds = jax.random.split(jax.random.key(seed), 17)
    return {
        "hidden_in": bell_draw(seeds[0], (TOKENS, D), 1.0, 6.0, ((0, 32),)),
        "out_grad": bell_draw(seeds[1], (TOKENS, D), 1.0, 6.0, ((0, 32),)),
        "norm_gain": jnp.clip(1.0 + 0.1 * jax.random.normal(seeds[2], (LAYERS, D), jnp.float32), 0.5, 1.5).astype(jnp.bfloat16),
        "proj_z": bell_draw(seeds[3], (LAYERS, D, INNER), D ** -0.5, 0.15625, ((1, 8), (2, 4))),
        "proj_x": bell_draw(seeds[4], (LAYERS, D, INNER), D ** -0.5, 0.15625, ((1, 8), (2, 4))),
        "proj_bc": bell_draw(seeds[5], (LAYERS, D, 2 * STATE), D ** -0.5, 0.15625, ((1, 8),)),
        "proj_dt": bell_draw(seeds[6], (LAYERS, D, HEADS), D ** -0.5, 0.15625, ((1, 8), (2, 4))),
        "conv_value": bell_draw(seeds[7], (LAYERS, CONV, INNER), CONV ** -0.5, 3.0, ((2, 4),)),
        "conv_value_bias": bell_draw(seeds[8], (LAYERS, INNER), 0.5, 3.0, ((1, 4),)),
        "conv_state": bell_draw(seeds[9], (LAYERS, CONV, 2 * STATE), CONV ** -0.5, 3.0, ((2, 8),)),
        "conv_state_bias": bell_draw(seeds[10], (LAYERS, 2 * STATE), 0.5, 3.0, ((1, 8),)),
        "step_bias": jnp.clip(-7.0 + 5.0 * jax.random.uniform(seeds[11], (LAYERS, HEADS), jnp.float32) ** block_levels(seeds[11], (LAYERS, HEADS), ((1, 4),), -0.2, 0.2), -7.0, -2.0).astype(jnp.bfloat16),
        "log_decay": jnp.clip(2.6875 * jax.random.uniform(seeds[12], (LAYERS, HEADS), jnp.float32) ** block_levels(seeds[12], (LAYERS, HEADS), ((1, 4),), -0.2, 0.2), 0.0, 2.6875).astype(jnp.bfloat16),
        "skip_gain": jnp.clip(0.5 + 1.0 * jax.random.uniform(seeds[13], (LAYERS, HEADS), jnp.float32) ** block_levels(seeds[13], (LAYERS, HEADS), ((1, 4),), -0.2, 0.2), 0.5, 1.5).astype(jnp.bfloat16),
        "gate_gain": jnp.clip(1.0 + 0.1 * jax.random.normal(seeds[14], (LAYERS, INNER), jnp.float32), 0.5, 1.5).astype(jnp.bfloat16),
        "proj_out": bell_draw(seeds[15], (LAYERS, INNER, D), INNER ** -0.5, 0.109375, ((1, 4), (2, 8))),
    }


EPSILON = 1e-05
HIGHEST = lax.Precision.HIGHEST

@jax.custom_vjp
def low(v):
    return lax.optimization_barrier(v.astype(jnp.bfloat16)).astype(jnp.float32)

@jax.custom_vjp
def low_back(v):
    return v

def low_keep(v):
    return (low(v), None)

def low_pass(kept, grad):
    return (grad,)

def back_keep(v):
    return (v, None)

def back_low(kept, grad):
    return (low(grad),)
low.defvjp(low_keep, low_pass)
low_back.defvjp(back_keep, back_low)

def conv_silu(series, weight, offset):
    tap_count = weight.shape[0]
    length = series.shape[0]
    padded = jnp.pad(series, ((tap_count - 1, 0), (0, 0)))
    summed = jnp.zeros_like(series) + offset[None, :]
    for tap_index in range(tap_count):
        summed = summed + weight[tap_index][None, :] * padded[tap_index:tap_index + length]
    return jax.nn.silu(summed)

def ssd_scan(inputs, step_sizes, log_rates, b_values, c_values, skip_gain, block_size):
    length, head_count, head_width = inputs.shape
    state_size = b_values.shape[1]
    blocks = length // block_size
    decay_rates = (step_sizes * (-jnp.exp(log_rates))[None, :]).reshape(blocks, block_size, head_count)
    cumuls = jnp.cumsum(decay_rates, axis=1)
    weighted = (inputs * step_sizes[:, :, None]).reshape(blocks, block_size, head_count, head_width)
    b_blocks = b_values.reshape(blocks, block_size, state_size)
    c_blocks = c_values.reshape(blocks, block_size, state_size)
    scores = jnp.einsum('cqn,csn->cqs', c_blocks, b_blocks, precision=HIGHEST)
    causal = (jnp.arange(block_size)[:, None] >= jnp.arange(block_size)[None, :])[None, :, :, None]
    gap_sums = jnp.where(causal, cumuls[:, :, None, :] - cumuls[:, None, :, :], 0.0)
    decays = jnp.where(causal, jnp.exp(gap_sums), 0.0)
    inside = jnp.einsum('cqs,cqsh,cshp->cqhp', scores, decays, weighted, precision=HIGHEST)
    tail_decay = jnp.exp(cumuls[:, -1:, :] - cumuls)
    end_states = jnp.einsum('csh,cshp,csn->chpn', tail_decay, weighted, b_blocks, precision=HIGHEST)
    block_drops = jnp.exp(cumuls[:, -1, :])

    def carry_step(carried, paired):
        one_drop, fresh_state = paired
        return (carried * one_drop[:, None, None] + fresh_state, carried)
    _, entering = lax.scan(carry_step, jnp.zeros_like(end_states[0]), (block_drops, end_states))
    outside = jnp.einsum('cqn,chpn->cqhp', c_blocks, entering, precision=HIGHEST) * jnp.exp(cumuls)[:, :, :, None]
    return (inside + outside).reshape(length, head_count, head_width) + skip_gain[None, :, None] * inputs

def state_inputs(projected, conv_weight, conv_offset):
    conved = conv_silu(projected, conv_weight, conv_offset)
    half_width = conved.shape[1] // 2
    return (conved[:, :half_width], conved[:, half_width:])

def mixer(gate_in, value_in, step_in, b_values, c_values, conv_weight, conv_offset, step_offset, log_rates, skip_gain):
    length = value_in.shape[0]
    head_count = step_in.shape[1]
    conved = conv_silu(value_in, conv_weight, conv_offset)
    step_sizes = jax.nn.softplus(step_in + step_offset[None, :])
    mixed = ssd_scan(conved.reshape(length, head_count, -1), step_sizes, log_rates, b_values, c_values, skip_gain, GROUP)
    return mixed.reshape(length, -1) * jax.nn.silu(gate_in)

def mamba_layer(residual, params):
    gain_pre, weight_z, weight_x, weight_bc, weight_dt, conv_weight, conv_offset, conv_shared, conv_shared_offset, step_offset, log_rates, skip_gain, gain_gate, weight_out = params
    scale = lax.rsqrt(lax.optimization_barrier(jnp.mean(residual * residual, axis=1, keepdims=True)) + EPSILON)
    normed = low(residual * scale * gain_pre[None, :])
    gate_in = low_back(jnp.dot(normed, weight_z, precision=HIGHEST, preferred_element_type=jnp.float32))
    value_in = low_back(jnp.dot(normed, weight_x, precision=HIGHEST, preferred_element_type=jnp.float32))
    state_in = low_back(jnp.dot(normed, weight_bc, precision=HIGHEST, preferred_element_type=jnp.float32))
    step_in = low_back(jnp.dot(normed, weight_dt, precision=HIGHEST, preferred_element_type=jnp.float32))
    b_values, c_values = state_inputs(state_in, conv_shared, conv_shared_offset)
    gated = mixer(gate_in, value_in, step_in, b_values, c_values, conv_weight, conv_offset, step_offset, log_rates, skip_gain)
    inner_scale = lax.rsqrt(lax.optimization_barrier(jnp.mean(gated * gated, axis=1, keepdims=True)) + EPSILON)
    mixed = low(gated * inner_scale * gain_gate[None, :])
    branch = low_back(jnp.dot(mixed, weight_out, precision=HIGHEST, preferred_element_type=jnp.float32))
    return residual + branch

def reference(hidden_in, out_grad, norm_gain, proj_z, proj_x, proj_bc, proj_dt, conv_value, conv_value_bias, conv_state, conv_state_bias, step_bias, log_decay, skip_gain, gate_gain, proj_out):
    params = tuple((array.astype(jnp.float32) for array in (norm_gain, proj_z, proj_x, proj_bc, proj_dt, conv_value, conv_value_bias, conv_state, conv_state_bias, step_bias, log_decay, skip_gain, gate_gain, proj_out)))
    sequences = hidden_in.astype(jnp.float32).reshape(N_DP, SEQ, D)
    cotangents = out_grad.astype(jnp.float32).reshape(N_DP, SEQ, D)

    def forward(residual, weights):
        for layer_index in range(LAYERS):
            residual = mamba_layer(residual, tuple((member[layer_index] for member in weights)))
        return residual

    def one_sequence(totals, paired):
        sequence, cotangent = paired
        result, backward = jax.vjp(forward, sequence, params)
        grad_sequence, grad_params = backward(cotangent)
        return (jax.tree.map(jnp.add, totals, grad_params), (result, grad_sequence))
    totals, (results, grad_sequences) = lax.scan(one_sequence, jax.tree.map(jnp.zeros_like, params), (sequences, cotangents))
    return (results.reshape(TOKENS, D), grad_sequences.reshape(TOKENS, D), totals[0], totals[1], totals[2], totals[3], totals[4], totals[5], totals[6], totals[7], totals[8], totals[9], totals[10], totals[11], totals[12], totals[13])
```

```python
import functools

import jax
import jax.numpy as jnp
from jax import lax
from jax.sharding import PartitionSpec as P
import jax.experimental.pallas as pl
import jax.experimental.pallas.tpu as pltpu

GROUP = 256
EPSILON = 1e-05
BF = jnp.bfloat16
F32 = jnp.float32
WIDTH = 64
MIB = 1024 * 1024


def nn(a, b):
    return lax.dot_general(a, b, (((1,), (0,)), ((), ())), preferred_element_type=F32)


def nt(a, b):
    return lax.dot_general(a, b, (((1,), (1,)), ((), ())), preferred_element_type=F32)


def parts3(v):
    one = v.astype(BF)
    rest = v - one.astype(F32)
    two = rest.astype(BF)
    three = (rest - two.astype(F32)).astype(BF)
    return one, two, three


def sum_rows(select, v):
    one, two, three = parts3(v)
    return nn(select, one) + nn(select, two) + nn(select, three)


def sum_lanes(v, select):
    one = v.astype(BF)
    two = (v - one.astype(F32)).astype(BF)
    return nn(one, select) + nn(two, select)


def silu_parts(v):
    sig = 1.0 / (1.0 + jnp.exp(-v))
    return sig, v * sig


def softplus(v):
    return jnp.maximum(v, 0.0) + jnp.log1p(jnp.exp(-jnp.abs(v)))


def pair_spread(column_values, pair, lane_low):
    low = column_values[:, 2 * pair : 2 * pair + 1]
    high = column_values[:, 2 * pair + 1 : 2 * pair + 2]
    return jnp.where(lane_low, low, high)


def spread(column_values, pairs, lane_low):
    return jnp.concatenate([pair_spread(column_values, p, lane_low) for p in range(pairs)], axis=1)


def conv_pre(padded, taps, bias, length):
    count = 4
    total = bias
    for k in range(count):
        total = total + taps[k : k + 1, :] * padded[pl.ds(8 - (count - 1) + k, length), :]
    return total


def fwd_kernel(
    rows_ref, wz_ref, wx_ref, wbc_ref, wdt_ref, wot_ref,
    cv_ref, cvb_ref, cs_ref, csb_ref, sb_ref, rate_ref, skip_ref, gg_ref,
    gate_ref, val_ref, st_ref, dt_ref, y_ref, ent_ref, mixed_ref, part_ref, ssq_ref,
    state, vpad, spad,
):
    step = pl.program_id(0)
    length = rows_ref.shape[0]
    inner = wz_ref.shape[1]
    pairs = inner // 128

    @pl.when(step == 0)
    def _():
        state[...] = jnp.zeros_like(state)
        vpad[0:8, :] = jnp.zeros((8, inner), F32)
        spad[0:8, :] = jnp.zeros((8, spad.shape[1]), F32)

    @pl.when(step > 0)
    def _():
        vpad[0:8, :] = vpad[length : length + 8, :]
        spad[0:8, :] = spad[length : length + 8, :]

    rows = rows_ref[...]
    gate_ref[...] = nn(rows, wz_ref[...])
    val = nn(rows, wx_ref[...])
    val_ref[...] = val
    vpad[8 : length + 8, :] = val
    st = nn(rows, wbc_ref[...])
    st_ref[...] = st
    spad[8 : length + 8, :] = st
    dt_in = nn(rows, wdt_ref[...])
    dt_ref[...] = dt_in

    _, v = silu_parts(conv_pre(vpad, cv_ref, cvb_ref[...], length))
    _, bc = silu_parts(conv_pre(spad, cs_ref, csb_ref[...], length))
    half = bc.shape[1] // 2
    bb = bc[:, :half].astype(BF)
    cb = bc[:, half:].astype(BF)
    dt = softplus(dt_in + sb_ref[...])
    q_index = lax.broadcasted_iota(jnp.int32, (length, length), 0)
    s_index = lax.broadcasted_iota(jnp.int32, (length, length), 1)
    causal = q_index >= s_index
    tril = jnp.where(causal, 1.0, 0.0).astype(BF)
    a = sum_rows(tril, dt * rate_ref[...])
    a_rows = a.T
    lane_low = lax.broadcasted_iota(jnp.int32, (length, 128), 1) < WIDTH
    dt_x = spread(dt, pairs, lane_low)
    a_x = spread(a, pairs, lane_low)
    x = v * dt_x
    xb = x.astype(BF)
    scores = jnp.where(causal, nt(cb, bb), 0.0)
    inside = []
    zero = jnp.zeros((length, 128), BF)
    for p in range(pairs):
        xp = xb[:, 128 * p : 128 * (p + 1)]
        total = None
        for j in range(2):
            h = 2 * p + j
            decay = jnp.exp(jnp.minimum(a[:, h : h + 1] - a_rows[h : h + 1, :], 0.0))
            m = (scores * decay).astype(BF)
            term = nn(m, jnp.where(lane_low, xp, zero) if j == 0 else jnp.where(lane_low, zero, xp))
            total = term if total is None else total + term
        inside.append(total)
    entering = state[...]
    ent_ref[0] = entering
    outside = jnp.exp(a_x) * nn(cb, entering.astype(BF))
    a_last = a_x[length - 1 : length, :]
    xw = (x * jnp.exp(a_last - a_x)).astype(BF)
    state[...] = jnp.exp(a_last) * entering + nn(bc[:, :half].T.astype(BF), xw)
    y = jnp.concatenate(inside, axis=1) + outside + skip_ref[...] * v
    y_ref[...] = y
    _, sgate = silu_parts(gate_ref[...])
    gated = y * sgate
    square = (gated * gated).astype(BF)
    ssq_ref[...] = nt(jnp.ones((8, inner), BF), square)
    mixed = (gated * gg_ref[...]).astype(BF)
    mixed_ref[...] = mixed
    part_ref[...] = nt(mixed, wot_ref[...]).astype(BF)


def whole(shape):
    return pl.BlockSpec(shape, lambda i: (0,) * len(shape), pipeline_mode=pl.Buffered(1))


def forward_mix(rows, weights, params):
    tokens, width = rows.shape
    inner = weights[0].shape[1]
    bc_width = weights[2].shape[1]
    dt_width = weights[3].shape[1]
    half = bc_width // 2
    q = GROUP
    blocks = tokens // q
    tok = lambda n: pl.BlockSpec((q, n), lambda i: (i, 0))
    outs = [
        ((tokens, inner), F32, tok(inner)),
        ((tokens, inner), F32, tok(inner)),
        ((tokens, bc_width), F32, tok(bc_width)),
        ((tokens, dt_width), F32, tok(dt_width)),
        ((tokens, inner), F32, tok(inner)),
        ((blocks, half, inner), F32, pl.BlockSpec((1, half, inner), lambda i: (i, 0, 0))),
        ((tokens, inner), BF, tok(inner)),
        ((tokens, width), BF, tok(width)),
        ((8, tokens), F32, pl.BlockSpec((8, q), lambda i: (0, i))),
    ]
    return pl.pallas_call(
        fwd_kernel,
        grid=(blocks,),
        in_specs=[tok(width)] + [whole(w.shape) for w in (*weights, *params)],
        out_specs=[o[2] for o in outs],
        out_shape=[jax.ShapeDtypeStruct(o[0], o[1]) for o in outs],
        scratch_shapes=[
            pltpu.VMEM((half, inner), F32),
            pltpu.VMEM((q + 8, inner), F32),
            pltpu.VMEM((q + 8, bc_width), F32),
        ],
        compiler_params=pltpu.CompilerParams(
            dimension_semantics=("arbitrary",), vmem_limit_bytes=56 * MIB
        ),
        name="mix_forward",
    )(rows, *weights, *params)


def bwd_kernel(
    gb_ref, e_ref, gate_ref, val_ref, valp_ref, st_ref, stp_ref, dt_ref, y_ref, ent_ref,
    wz_ref, wx_ref, wbc_ref, wdt_ref, wot_ref,
    cv_ref, cvb_ref, cs_ref, csb_ref, sb_ref, rate_ref, skip_ref, gg_ref, pick_ref,
    dgate_ref, dval_ref, dst_ref, ddt_ref, dpart_ref, gvec_ref, gst_ref, gdt_ref,
    dstate, vpad, spad, dvpad, dspad,
):
    step = pl.program_id(0)
    blocks = pl.num_programs(0)
    length = gb_ref.shape[0]
    inner = wz_ref.shape[1]
    bc_width = wbc_ref.shape[1]
    half = bc_width // 2
    pairs = inner // 128

    @pl.when(step == 0)
    def _():
        dstate[...] = jnp.zeros_like(dstate)
        dvpad[length : length + 8, :] = jnp.zeros((8, inner), F32)
        dspad[length : length + 8, :] = jnp.zeros((8, bc_width), F32)
        gvec_ref[...] = jnp.zeros_like(gvec_ref)
        gst_ref[...] = jnp.zeros_like(gst_ref)
        gdt_ref[...] = jnp.zeros_like(gdt_ref)

    @pl.when(step > 0)
    def _():
        dvpad[length : length + 8, :] = dvpad[0:8, :]
        dspad[length : length + 8, :] = dspad[0:8, :]

    first = step == blocks - 1
    vpad[0:8, :] = jnp.where(first, 0.0, valp_ref[...])
    spad[0:8, :] = jnp.where(first, 0.0, stp_ref[...])
    vpad[8 : length + 8, :] = val_ref[...]
    spad[8 : length + 8, :] = st_ref[...]

    pre_v = conv_pre(vpad, cv_ref, cvb_ref[...], length)
    sig_v, v = silu_parts(pre_v)
    pre_s = conv_pre(spad, cs_ref, csb_ref[...], length)
    sig_s, bc = silu_parts(pre_s)
    bb = bc[:, :half].astype(BF)
    cb = bc[:, half:].astype(BF)
    z = dt_ref[...] + sb_ref[...]
    dt = softplus(z)
    rate = rate_ref[...]
    s_index = lax.broadcasted_iota(jnp.int32, (length, length), 0)
    q_index = lax.broadcasted_iota(jnp.int32, (length, length), 1)
    upper = q_index >= s_index
    a = sum_rows(jnp.where(s_index >= q_index, 1.0, 0.0).astype(BF), dt * rate)
    a_rows = a.T
    lane_low = lax.broadcasted_iota(jnp.int32, (length, 128), 1) < WIDTH
    dt_x = spread(dt, pairs, lane_low)
    a_x = spread(a, pairs, lane_low)
    x = v * dt_x
    xb = x.astype(BF)
    skip = skip_ref[...]

    y = y_ref[...]
    gate = gate_ref[...]
    sig_g, sgate = silu_parts(gate)
    gated = y * sgate
    dm = nn(gb_ref[...], wot_ref[...])
    e = e_ref[...].T[:, 0:1]
    dgated = dm * gg_ref[...] - e * gated
    dgate = (dgated * y * (sig_g * (1.0 + gate * (1.0 - sig_g)))).astype(BF)
    dgate_ref[...] = dgate
    dy = dgated * sgate
    dyb = dy.astype(BF)
    dyf = dyb.astype(F32)

    scores = jnp.where(upper, nt(bb, cb), 0.0)
    zero = jnp.zeros((length, 128), BF)
    dscores = jnp.zeros((length, length), F32)
    dx_list = []
    for p in range(pairs):
        xp = xb[:, 128 * p : 128 * (p + 1)]
        dp = dyb[:, 128 * p : 128 * (p + 1)]
        total = None
        for j in range(2):
            h = 2 * p + j
            decay = jnp.exp(jnp.minimum(a_rows[h : h + 1, :] - a[:, h : h + 1], 0.0))
            m = (scores * decay).astype(BF)
            dh = jnp.where(lane_low, dp, zero) if j == 0 else jnp.where(lane_low, zero, dp)
            term = nn(m, dh)
            total = term if total is None else total + term
            dscores = dscores + nt(xp, dh) * decay
        dx_list.append(total)
    dx_in = jnp.concatenate(dx_list, axis=1)
    dscores = jnp.where(upper, dscores, 0.0)
    db = nn(dscores.astype(BF), cb)
    dc = nn(dscores.T.astype(BF), bb)

    entering = ent_ref[0]
    dleaving = dstate[...]
    dleaving_b = dleaving.astype(BF)
    ea = jnp.exp(a_x)
    a_last = a_x[length - 1 : length, :]
    ea_last = jnp.exp(a_last)
    w = jnp.exp(a_last - a_x)
    dxw = nn(bb, dleaving_b) * w
    db = db + nt((x * w).astype(BF), dleaving_b)
    eady = (ea * dyf).astype(BF)
    dc = dc + nt(eady, entering.astype(BF))
    dstate[...] = ea_last * dleaving + nn(bc[:, half:].T.astype(BF), eady)
    dx = dx_in + dxw
    u = x * dxw
    last_add = jnp.sum(u, axis=0, keepdims=True) + ea_last * jnp.sum(
        entering * dleaving, axis=0, keepdims=True
    )
    da_x = dyf * (y - skip * v) - xb.astype(F32) * dx_in - u
    row_index = lax.broadcasted_iota(jnp.int32, (length, inner), 0)
    da_x = da_x + jnp.where(row_index == length - 1, last_add, 0.0)
    pick = pick_ref[...]
    da = sum_lanes(da_x, pick)
    dr = sum_rows(jnp.where(upper, 1.0, 0.0).astype(BF), da)
    ddt = sum_lanes(dx * v, pick) + dr * rate
    dz = ddt * (1.0 / (1.0 + jnp.exp(-z)))
    ddtb = dz.astype(BF)
    ddt_ref[...] = ddtb
    gdt_ref[0:1, :] += jnp.sum(dz, axis=0, keepdims=True)
    gdt_ref[1:2, :] += jnp.sum(dr * dt * rate, axis=0, keepdims=True)

    dpre_v = (skip * dy + dt_x * dx) * (sig_v * (1.0 + pre_v * (1.0 - sig_v)))
    dvpad[0:length, :] = dpre_v
    dval = jnp.zeros((length, inner), F32)
    for k in range(4):
        dval = dval + cv_ref[k : k + 1, :] * dvpad[pl.ds(3 - k, length), :]
        gvec_ref[k : k + 1, :] += jnp.sum(
            dpre_v * vpad[pl.ds(5 + k, length), :], axis=0, keepdims=True
        )
    gvec_ref[4:5, :] += jnp.sum(dpre_v, axis=0, keepdims=True)
    gvec_ref[5:6, :] += jnp.sum(gated * dm, axis=0, keepdims=True)
    gvec_ref[6:7, :] += jnp.sum(dy * v, axis=0, keepdims=True)
    dvalb = dval.astype(BF)
    dval_ref[...] = dvalb

    dbc = jnp.concatenate([db, dc], axis=1)
    dpre_s = dbc * (sig_s * (1.0 + pre_s * (1.0 - sig_s)))
    dspad[0:length, :] = dpre_s
    dst = jnp.zeros((length, bc_width), F32)
    for k in range(4):
        dst = dst + cs_ref[k : k + 1, :] * dspad[pl.ds(3 - k, length), :]
        gst_ref[k : k + 1, :] += jnp.sum(
            dpre_s * spad[pl.ds(5 + k, length), :], axis=0, keepdims=True
        )
    gst_ref[4:5, :] += jnp.sum(dpre_s, axis=0, keepdims=True)
    dstb = dst.astype(BF)
    dst_ref[...] = dstb
    dpart = nt(dgate, wz_ref[...]) + nt(dvalb, wx_ref[...])
    dpart = dpart + nt(dstb, wbc_ref[...]) + nt(ddtb, wdt_ref[...])
    dpart_ref[...] = dpart.astype(BF)


def backward_mix(gb, e_rows, kept, weights, params, pick):
    gate, val, st, dt, y, ent = kept
    tokens, width = gb.shape
    inner = weights[0].shape[1]
    bc_width = weights[2].shape[1]
    dt_width = weights[3].shape[1]
    half = bc_width // 2
    q = GROUP
    blocks = tokens // q
    back = lambda i: blocks - 1 - i
    tok = lambda n: pl.BlockSpec((q, n), lambda i: (back(i), 0))
    halo = lambda n: pl.BlockSpec(
        (8, n), lambda i: (jnp.maximum(back(i) * (q // 8) - 1, 0), 0)
    )
    fixed = lambda r, c: pl.BlockSpec((r, c), lambda i: (0, 0))
    outs = [
        ((tokens, inner), BF, tok(inner)),
        ((tokens, inner), BF, tok(inner)),
        ((tokens, bc_width), BF, tok(bc_width)),
        ((tokens, dt_width), BF, tok(dt_width)),
        ((tokens, width), BF, tok(width)),
        ((8, inner), F32, fixed(8, inner)),
        ((8, bc_width), F32, fixed(8, bc_width)),
        ((8, dt_width), F32, fixed(8, dt_width)),
    ]
    return pl.pallas_call(
        bwd_kernel,
        grid=(blocks,),
        in_specs=[
            tok(width),
            pl.BlockSpec((8, q), lambda i: (0, back(i))),
            tok(inner), tok(inner), halo(inner), tok(bc_width), halo(bc_width), tok(dt_width),
            tok(inner),
            pl.BlockSpec((1, half, inner), lambda i: (back(i), 0, 0)),
        ]
        + [whole(w.shape) for w in (*weights, *params, pick)],
        out_specs=[o[2] for o in outs],
        out_shape=[jax.ShapeDtypeStruct(o[0], o[1]) for o in outs],
        scratch_shapes=[
            pltpu.VMEM((half, inner), F32),
            pltpu.VMEM((q + 8, inner), F32),
            pltpu.VMEM((q + 8, bc_width), F32),
            pltpu.VMEM((q + 8, inner), F32),
            pltpu.VMEM((q + 8, bc_width), F32),
        ],
        compiler_params=pltpu.CompilerParams(
            dimension_semantics=("arbitrary",), vmem_limit_bytes=60 * MIB
        ),
        name="mix_backward",
    )(gb, e_rows, gate, val, val, st, st, dt, y, ent, *weights, *params, pick)


def pad_to(v, rows, columns):
    return jnp.pad(v, ((0, rows - v.shape[0]), (0, columns - v.shape[1])))


def shards(
    hidden_in,
    out_grad,
    norm_gain,
    proj_z,
    proj_x,
    proj_bc,
    proj_dt,
    conv_value,
    conv_value_bias,
    conv_state,
    conv_state_bias,
    step_bias,
    log_decay,
    skip_gain,
    gate_gain,
    proj_out,
):
    tensor_count = lax.axis_size("tensor")
    dp_count = lax.axis_size("dp")
    layers, shard_rows, inner = proj_z.shape
    rows_own, width = hidden_in.shape
    heads = step_bias.shape[1]
    bc_width = proj_bc.shape[2]
    inner_all = inner * tensor_count

    def gather_dp(v, axis=0):
        return lax.all_gather(v, "dp", axis=axis, tiled=True)

    def rows_of(v):
        return v.astype(F32).reshape(-1, v.shape[-1])

    small = jnp.concatenate(
        [
            conv_state.reshape(layers, -1),
            conv_state_bias,
        ],
        axis=1,
    )
    small = jnp.pad(small, ((0, 0), (0, shard_rows - small.shape[1])))
    step_block = jnp.concatenate(
        [
            proj_dt,
            norm_gain[:, :, None],
            small[:, :, None],
            jnp.zeros((layers, shard_rows, 128 - heads - 2), BF),
        ],
        axis=2,
    )
    weights, params, gains = [], [], []
    lane = jnp.arange(128)[None, :]
    for l in range(layers):
        wide = gather_dp(step_block[l])
        gains.append(wide[:, heads].astype(F32)[None, :])
        per = bc_width // dp_count
        smalls = wide[:, heads + 1].reshape(dp_count, shard_rows)[:, : 5 * per]
        smalls = smalls.astype(F32).reshape(dp_count, 5, per)
        smalls = jnp.transpose(smalls, (1, 0, 2)).reshape(5, bc_width)
        wdt = jnp.where(lane < heads, wide, jnp.zeros_like(wide))
        weights.append(
            (
                gather_dp(proj_z[l]),
                gather_dp(proj_x[l]),
                gather_dp(proj_bc[l]),
                wdt,
                gather_dp(proj_out[l].T),
            )
        )
        params.append(
            (
                pad_to(rows_of(conv_value[l]), 8, inner),
                rows_of(conv_value_bias[l]),
                pad_to(smalls[:4], 8, bc_width),
                smalls[4:5],
                pad_to(rows_of(step_bias[l]), 1, 128),
                pad_to(-jnp.exp(rows_of(log_decay[l])), 1, 128),
                jnp.repeat(rows_of(skip_gain[l]), WIDTH, axis=1),
                rows_of(gate_gain[l]),
            )
        )
    pick = (jnp.arange(inner)[:, None] // WIDTH == jnp.arange(128)[None, :]).astype(BF)

    residual = hidden_in.astype(F32)
    kept = []
    for l in range(layers):
        r1 = lax.rsqrt(jnp.mean(residual * residual, axis=1, keepdims=True) + EPSILON)
        normed = (residual * r1 * gains[l]).astype(BF)
        rows = lax.all_gather(normed, "tensor", axis=0, tiled=True)
        gate, val, st, dt, y, ent, mixed, part, ssq = forward_mix(rows, weights[l], params[l])
        total = lax.psum_scatter(part, "tensor", scatter_dimension=0, tiled=True).astype(F32)
        ssq_own = lax.psum_scatter(ssq[0], "tensor", scatter_dimension=0, tiled=True)
        r2 = lax.rsqrt(ssq_own / inner_all + EPSILON)[:, None]
        branch = total * r2
        kept.append((residual, r1, rows, (gate, val, st, dt, y, ent), mixed, r2, branch))
        residual = residual + branch
    gradient = out_grad.astype(F32)
    scattered = [None] * layers
    summed = [None] * layers
    for l in reversed(range(layers)):
        residual_in, r1, rows, saved, mixed, r2, branch = kept[l]
        gb = gradient.astype(BF)
        e = r2[:, 0] ** 2 * jnp.sum(gb.astype(F32) * branch, axis=1) / inner_all
        scaled = (r2 * gradient).astype(BF)
        grad_rows = lax.all_gather(scaled, "tensor", axis=0, tiled=True)
        e_rows = jnp.broadcast_to(
            lax.all_gather(e, "tensor", axis=0, tiled=True)[None, :], (8, rows.shape[0])
        )
        dgate, dval, dst, ddt, dpart, gvec, gst, gdt = backward_mix(
            grad_rows, e_rows, saved, weights[l], params[l], pick
        )
        dnormed = lax.psum_scatter(dpart, "tensor", scatter_dimension=0, tiled=True).astype(F32)
        back = lambda left, right: jnp.einsum(
            "td,tj->dj", left, right, preferred_element_type=F32
        )
        gain = gains[l]
        dn = dnormed * gain
        grad_gain = jnp.sum(residual_in * r1 * dnormed, axis=0)
        cross = jnp.sum(dn * residual_in, axis=1, keepdims=True)
        gradient = gradient + r1 * dn - r1**3 * residual_in * cross / width
        scatter = lambda v: lax.psum_scatter(
            v.astype(BF), "dp", scatter_dimension=0, tiled=True
        ).astype(F32)
        scattered[l] = (
            scatter(back(rows, dgate)),
            scatter(back(rows, dval)),
            scatter(back(rows, dst)),
            scatter(back(rows, ddt)),
            scatter(back(grad_rows, mixed)),
        )
        summed[l] = (gvec, gdt, gst, grad_gain)
    stack = lambda i: jnp.stack([scattered[l][i] for l in range(layers)])
    gvec = jnp.stack([s[0] for s in summed])
    gdt = jnp.stack([s[1] for s in summed])
    gst = jnp.stack([s[2] for s in summed])
    ggain = jnp.stack([s[3] for s in summed])
    gvec, gdt = lax.psum((gvec, gdt), "dp")
    gst, ggain, gbc = lax.psum((gst, ggain, stack(2).astype(BF)), "tensor")
    gst, ggain = lax.psum((gst, ggain), "dp")
    own = lambda v, axis: lax.dynamic_slice_in_dim(
        v, lax.axis_index("dp") * (v.shape[axis] // dp_count), v.shape[axis] // dp_count, axis
    )
    gst = own(gst, 2)
    return (
        residual,
        gradient,
        own(ggain, 1),
        stack(0),
        stack(1),
        gbc.astype(F32),
        stack(3)[:, :, :heads],
        gvec[:, 0:4],
        gvec[:, 4],
        gst[:, 0:4],
        gst[:, 4],
        gdt[:, 0, :heads],
        gdt[:, 1, :heads],
        jnp.sum(gvec[:, 6].reshape(layers, heads, WIDTH), axis=2),
        gvec[:, 5],
        jnp.transpose(stack(4), (0, 2, 1)),
    )


def solution(mesh):
    placed = (
        P(("dp", "tensor"), None),
        P(("dp", "tensor"), None),
        P(None, "dp"),
        P(None, "dp", "tensor"),
        P(None, "dp", "tensor"),
        P(None, "dp", None),
        P(None, "dp", "tensor"),
        P(None, None, "tensor"),
        P(None, "tensor"),
        P(None, None, "dp"),
        P(None, "dp"),
        P(None, "tensor"),
        P(None, "tensor"),
        P(None, "tensor"),
        P(None, "tensor"),
        P(None, "tensor", "dp"),
    )
    return jax.shard_map(
        shards,
        mesh=mesh,
        in_specs=placed,
        out_specs=(
            P(("dp", "tensor"), None),
            P(("dp", "tensor"), None),
            P(None, "dp"),
            P(None, "dp", "tensor"),
            P(None, "dp", "tensor"),
            P(None, "dp", None),
            P(None, "dp", "tensor"),
            P(None, None, "tensor"),
            P(None, "tensor"),
            P(None, None, "dp"),
            P(None, "dp"),
            P(None, "tensor"),
            P(None, "tensor"),
            P(None, "tensor"),
            P(None, "tensor"),
            P(None, "tensor", "dp"),
        ),
        check_vma=False,
    )
```

```python
import functools
import types

import jax
import jax.numpy as jnp
from jax import lax
from jax.sharding import PartitionSpec as P
import jax.experimental.pallas as pl
import jax.experimental.pallas.tpu as pltpu

GROUP = 256
EPSILON = 1e-05
BF = jnp.bfloat16
F32 = jnp.float32
WIDTH = 64
MIB = 1024 * 1024
WCHUNK = 384


def nn(a, b):
    return lax.dot_general(a, b, (((1,), (0,)), ((), ())), preferred_element_type=F32)


def nt(a, b):
    return lax.dot_general(a, b, (((1,), (1,)), ((), ())), preferred_element_type=F32)


def parts3(v):
    one = v.astype(BF)
    rest = v - one.astype(F32)
    two = rest.astype(BF)
    three = (rest - two.astype(F32)).astype(BF)
    return one, two, three


def sum_rows(select, v):
    one, two, three = parts3(v)
    return nn(select, one) + nn(select, two) + nn(select, three)


def sum_lanes(v, select):
    one = v.astype(BF)
    two = (v - one.astype(F32)).astype(BF)
    return nn(one, select) + nn(two, select)


def silu_parts(v):
    sig = 1.0 / (1.0 + jnp.exp(-v))
    return sig, v * sig


def softplus(v):
    return jnp.maximum(v, 0.0) + jnp.log1p(jnp.exp(-jnp.abs(v)))


def pair_spread(column_values, pair, lane_low):
    low = column_values[:, 2 * pair : 2 * pair + 1]
    high = column_values[:, 2 * pair + 1 : 2 * pair + 2]
    return jnp.where(lane_low, low, high)


def spread(column_values, pairs, lane_low):
    return jnp.concatenate([pair_spread(column_values, p, lane_low) for p in range(pairs)], axis=1)


def conv_pre(padded, taps, bias, length):
    count = 4
    total = bias
    for k in range(count):
        total = total + taps[k : k + 1, :] * padded[pl.ds(8 - (count - 1) + k, length), :]
    return total


def blocks_of(w_ref, inner, bc_width):
    sizes = (bc_width, 128, inner, inner, inner)
    starts = [sum(sizes[:i]) for i in range(5)]
    return [w_ref.at[:, pl.ds(s, z)] for s, z in zip(starts, sizes)]


def fwd_kernel(
    first, rows_ref, w_ref,
    cv_ref, cvb_ref, cs_ref, csb_ref, sb_ref, rate_ref, skip_ref, gg_ref, gain_ref,
    gate_ref, val_ref, st_ref, dt_ref, y_ref, ent_ref, part_ref, ssq_ref,
    *rest,
):
    normed_ref = rest[0] if first else None
    state, vpad, spad = rest[-3:]
    step = pl.program_id(0)
    length = rows_ref.shape[0]
    inner = gg_ref.shape[1]
    pairs = inner // 128
    wbc_ref, wdt_ref, wz_ref, wx_ref, wot_ref = blocks_of(w_ref, inner, cs_ref.shape[1])

    @pl.when(step == 0)
    def _():
        state[...] = jnp.zeros_like(state)
        vpad[0:8, :] = jnp.zeros((8, inner), F32)
        spad[0:8, :] = jnp.zeros((8, spad.shape[1]), F32)

    @pl.when(step > 0)
    def _():
        vpad[0:8, :] = vpad[length : length + 8, :]
        spad[0:8, :] = spad[length : length + 8, :]

    rows = rows_ref[...]
    if first:
        rows = rows.astype(F32)
        r1 = lax.rsqrt(jnp.mean(rows * rows, axis=1, keepdims=True) + EPSILON)
        rows = (rows * r1 * gain_ref[...]).astype(BF)
        normed_ref[...] = rows
    gate_ref[...] = nn(rows, wz_ref[...])
    val = nn(rows, wx_ref[...])
    val_ref[...] = val
    vpad[8 : length + 8, :] = val
    st = nn(rows, wbc_ref[...])
    st_ref[...] = st
    spad[8 : length + 8, :] = st
    dt_in = nn(rows, wdt_ref[...])
    dt_ref[...] = dt_in

    _, v = silu_parts(conv_pre(vpad, cv_ref, cvb_ref[...], length))
    _, bc = silu_parts(conv_pre(spad, cs_ref, csb_ref[...], length))
    half = bc.shape[1] // 2
    bb = bc[:, :half].astype(BF)
    cb = bc[:, half:].astype(BF)
    dt = softplus(dt_in + sb_ref[...])
    q_index = lax.broadcasted_iota(jnp.int32, (length, length), 0)
    s_index = lax.broadcasted_iota(jnp.int32, (length, length), 1)
    causal = q_index >= s_index
    tril = jnp.where(causal, 1.0, 0.0).astype(BF)
    a = sum_rows(tril, dt * rate_ref[...])
    a_rows = a.T
    lane_low = lax.broadcasted_iota(jnp.int32, (length, 128), 1) < WIDTH
    dt_x = spread(dt, pairs, lane_low)
    a_x = spread(a, pairs, lane_low)
    x = v * dt_x
    xb = x.astype(BF)
    scores = jnp.where(causal, nt(cb, bb), 0.0)
    inside = []
    zero = jnp.zeros((length, 128), BF)
    for p in range(pairs):
        xp = xb[:, 128 * p : 128 * (p + 1)]
        total = None
        for j in range(2):
            h = 2 * p + j
            decay = jnp.exp(jnp.minimum(a[:, h : h + 1] - a_rows[h : h + 1, :], 0.0))
            m = (scores * decay).astype(BF)
            term = nn(m, jnp.where(lane_low, xp, zero) if j == 0 else jnp.where(lane_low, zero, xp))
            total = term if total is None else total + term
        inside.append(total)
    entering = state[...]
    ent_ref[0] = entering
    outside = jnp.exp(a_x) * nn(cb, entering.astype(BF))
    a_last = a_x[length - 1 : length, :]
    xw = (x * jnp.exp(a_last - a_x)).astype(BF)
    state[...] = jnp.exp(a_last) * entering + nn(bc[:, :half].T.astype(BF), xw)
    y = jnp.concatenate(inside, axis=1) + outside + skip_ref[...] * v
    y_ref[...] = y
    _, sgate = silu_parts(gate_ref[...])
    gated = y * sgate
    square = (gated * gated).astype(BF)
    ssq_ref[...] = nt(jnp.ones((8, inner), BF), square)
    mixed = (gated * gg_ref[...]).astype(BF)
    part_ref[...] = nt(mixed, wot_ref[...]).astype(BF)


def whole(shape):
    return pl.BlockSpec(shape, lambda i: (0,) * len(shape), pipeline_mode=pl.Buffered(1))


def forward_mix(rows, packed, params, first):
    tokens, width = rows.shape
    inner = params[0].shape[1]
    bc_width = params[2].shape[1]
    dt_width = 128
    half = bc_width // 2
    q = GROUP
    blocks = tokens // q
    tok = lambda n: pl.BlockSpec((q, n), lambda i: (i, 0))
    outs = [
        ((tokens, inner), F32, tok(inner)),
        ((tokens, inner), F32, tok(inner)),
        ((tokens, bc_width), F32, tok(bc_width)),
        ((tokens, dt_width), F32, tok(dt_width)),
        ((tokens, inner), F32, tok(inner)),
        ((blocks, half, inner), F32, pl.BlockSpec((1, half, inner), lambda i: (i, 0, 0))),
        ((tokens, width), BF, tok(width)),
        ((8, tokens), F32, pl.BlockSpec((8, q), lambda i: (0, i))),
    ]
    if first:
        outs.append(((tokens, width), BF, tok(width)))
    return pl.pallas_call(
        functools.partial(fwd_kernel, first),
        grid=(blocks,),
        in_specs=[tok(width)] + [whole(w.shape) for w in (packed, *params)],
        out_specs=[o[2] for o in outs],
        out_shape=[jax.ShapeDtypeStruct(o[0], o[1]) for o in outs],
        scratch_shapes=[
            pltpu.VMEM((half, inner), F32),
            pltpu.VMEM((q + 8, inner), F32),
            pltpu.VMEM((q + 8, bc_width), F32),
        ],
        compiler_params=pltpu.CompilerParams(
            dimension_semantics=("arbitrary",), vmem_limit_bytes=56 * MIB
        ),
        name="mix_forward",
    )(rows, packed, *params)


def bwd_kernel(
    gb_ref, e_ref, gate_ref, val_ref, valp_ref, st_ref, stp_ref, dt_ref, y_ref, ent_ref,
    w_ref,
    cv_ref, cvb_ref, cs_ref, csb_ref, sb_ref, rate_ref, skip_ref, gg_ref, pick_ref,
    dcat_ref, dpart_ref, gvec_ref, gst_ref, gdt_ref,
    dstate, vpad, spad, dvpad, dspad,
):
    step = pl.program_id(0)
    blocks = pl.num_programs(0)
    length = gb_ref.shape[0]
    inner = gg_ref.shape[1]
    bc_width = cs_ref.shape[1]
    wbc_ref, wdt_ref, wz_ref, wx_ref, wot_ref = blocks_of(w_ref, inner, bc_width)
    dst_ref, ddt_ref, dgate_ref, dval_ref, mixed_ref = blocks_of(dcat_ref, inner, bc_width)
    half = bc_width // 2
    pairs = inner // 128

    @pl.when(step == 0)
    def _():
        dstate[...] = jnp.zeros_like(dstate)
        dvpad[length : length + 8, :] = jnp.zeros((8, inner), F32)
        dspad[length : length + 8, :] = jnp.zeros((8, bc_width), F32)
        gvec_ref[...] = jnp.zeros_like(gvec_ref)
        gst_ref[...] = jnp.zeros_like(gst_ref)
        gdt_ref[...] = jnp.zeros_like(gdt_ref)

    @pl.when(step > 0)
    def _():
        dvpad[length : length + 8, :] = dvpad[0:8, :]
        dspad[length : length + 8, :] = dspad[0:8, :]

    first = step == blocks - 1
    vpad[0:8, :] = jnp.where(first, 0.0, valp_ref[...])
    spad[0:8, :] = jnp.where(first, 0.0, stp_ref[...])
    vpad[8 : length + 8, :] = val_ref[...]
    spad[8 : length + 8, :] = st_ref[...]

    pre_v = conv_pre(vpad, cv_ref, cvb_ref[...], length)
    sig_v, v = silu_parts(pre_v)
    pre_s = conv_pre(spad, cs_ref, csb_ref[...], length)
    sig_s, bc = silu_parts(pre_s)
    bb = bc[:, :half].astype(BF)
    cb = bc[:, half:].astype(BF)
    z = dt_ref[...] + sb_ref[...]
    dt = softplus(z)
    rate = rate_ref[...]
    s_index = lax.broadcasted_iota(jnp.int32, (length, length), 0)
    q_index = lax.broadcasted_iota(jnp.int32, (length, length), 1)
    upper = q_index >= s_index
    a = sum_rows(jnp.where(s_index >= q_index, 1.0, 0.0).astype(BF), dt * rate)
    a_rows = a.T
    lane_low = lax.broadcasted_iota(jnp.int32, (length, 128), 1) < WIDTH
    dt_x = spread(dt, pairs, lane_low)
    a_x = spread(a, pairs, lane_low)
    x = v * dt_x
    xb = x.astype(BF)
    skip = skip_ref[...]

    y = y_ref[...]
    gate = gate_ref[...]
    sig_g, sgate = silu_parts(gate)
    gated = y * sgate
    dm = nn(gb_ref[...], wot_ref[...])
    e = e_ref[...].T[:, 0:1]
    dgated = dm * gg_ref[...] - e * gated
    mixed_ref[...] = (gated * gg_ref[...]).astype(BF)
    dgate = (dgated * y * (sig_g * (1.0 + gate * (1.0 - sig_g)))).astype(BF)
    dgate_ref[...] = dgate
    dy = dgated * sgate
    dyb = dy.astype(BF)
    dyf = dyb.astype(F32)

    scores = jnp.where(upper, nt(bb, cb), 0.0)
    zero = jnp.zeros((length, 128), BF)
    dscores = jnp.zeros((length, length), F32)
    dx_list = []
    for p in range(pairs):
        xp = xb[:, 128 * p : 128 * (p + 1)]
        dp = dyb[:, 128 * p : 128 * (p + 1)]
        total = None
        for j in range(2):
            h = 2 * p + j
            decay = jnp.exp(jnp.minimum(a_rows[h : h + 1, :] - a[:, h : h + 1], 0.0))
            m = (scores * decay).astype(BF)
            dh = jnp.where(lane_low, dp, zero) if j == 0 else jnp.where(lane_low, zero, dp)
            term = nn(m, dh)
            total = term if total is None else total + term
            dscores = dscores + nt(xp, dh) * decay
        dx_list.append(total)
    dx_in = jnp.concatenate(dx_list, axis=1)
    dscores = jnp.where(upper, dscores, 0.0)
    db = nn(dscores.astype(BF), cb)
    dc = nn(dscores.T.astype(BF), bb)

    entering = ent_ref[0]
    dleaving = dstate[...]
    dleaving_b = dleaving.astype(BF)
    ea = jnp.exp(a_x)
    a_last = a_x[length - 1 : length, :]
    ea_last = jnp.exp(a_last)
    w = jnp.exp(a_last - a_x)
    dxw = nn(bb, dleaving_b) * w
    db = db + nt((x * w).astype(BF), dleaving_b)
    eady = (ea * dyf).astype(BF)
    dc = dc + nt(eady, entering.astype(BF))
    dstate[...] = ea_last * dleaving + nn(bc[:, half:].T.astype(BF), eady)
    dx = dx_in + dxw
    u = x * dxw
    last_add = jnp.sum(u, axis=0, keepdims=True) + ea_last * jnp.sum(
        entering * dleaving, axis=0, keepdims=True
    )
    da_x = dyf * (y - skip * v) - xb.astype(F32) * dx_in - u
    row_index = lax.broadcasted_iota(jnp.int32, (length, inner), 0)
    da_x = da_x + jnp.where(row_index == length - 1, last_add, 0.0)
    pick = pick_ref[...]
    da = sum_lanes(da_x, pick)
    dr = sum_rows(jnp.where(upper, 1.0, 0.0).astype(BF), da)
    ddt = sum_lanes(dx * v, pick) + dr * rate
    dz = ddt * (1.0 / (1.0 + jnp.exp(-z)))
    ddtb = dz.astype(BF)
    ddt_ref[...] = ddtb
    gdt_ref[0:1, :] += jnp.sum(dz, axis=0, keepdims=True)
    gdt_ref[1:2, :] += jnp.sum(dr * dt * rate, axis=0, keepdims=True)

    dpre_v = (skip * dy + dt_x * dx) * (sig_v * (1.0 + pre_v * (1.0 - sig_v)))
    dvpad[0:length, :] = dpre_v
    dval = jnp.zeros((length, inner), F32)
    for k in range(4):
        dval = dval + cv_ref[k : k + 1, :] * dvpad[pl.ds(3 - k, length), :]
        gvec_ref[k : k + 1, :] += jnp.sum(
            dpre_v * vpad[pl.ds(5 + k, length), :], axis=0, keepdims=True
        )
    gvec_ref[4:5, :] += jnp.sum(dpre_v, axis=0, keepdims=True)
    gvec_ref[5:6, :] += jnp.sum(gated * dm, axis=0, keepdims=True)
    gvec_ref[6:7, :] += jnp.sum(dy * v, axis=0, keepdims=True)
    dvalb = dval.astype(BF)
    dval_ref[...] = dvalb

    dbc = jnp.concatenate([db, dc], axis=1)
    dpre_s = dbc * (sig_s * (1.0 + pre_s * (1.0 - sig_s)))
    dspad[0:length, :] = dpre_s
    dst = jnp.zeros((length, bc_width), F32)
    for k in range(4):
        dst = dst + cs_ref[k : k + 1, :] * dspad[pl.ds(3 - k, length), :]
        gst_ref[k : k + 1, :] += jnp.sum(
            dpre_s * spad[pl.ds(5 + k, length), :], axis=0, keepdims=True
        )
    gst_ref[4:5, :] += jnp.sum(dpre_s, axis=0, keepdims=True)
    dstb = dst.astype(BF)
    dst_ref[...] = dstb
    dpart = nt(dgate, wz_ref[...]) + nt(dvalb, wx_ref[...])
    dpart = dpart + nt(dstb, wbc_ref[...]) + nt(ddtb, wdt_ref[...])
    dpart_ref[...] = dpart.astype(BF)


def backward_mix(gb, e_rows, kept, packed, params, pick):
    gate, val, st, dt, y, ent = kept
    tokens, width = gb.shape
    inner = params[0].shape[1]
    bc_width = params[2].shape[1]
    dt_width = 128
    packed_width = packed.shape[1]
    half = bc_width // 2
    q = GROUP
    blocks = tokens // q
    back = lambda i: blocks - 1 - i
    tok = lambda n: pl.BlockSpec((q, n), lambda i: (back(i), 0))
    halo = lambda n: pl.BlockSpec(
        (8, n), lambda i: (jnp.maximum(back(i) * (q // 8) - 1, 0), 0)
    )
    fixed = lambda r, c: pl.BlockSpec((r, c), lambda i: (0, 0))
    outs = [
        ((tokens, packed_width), BF, tok(packed_width)),
        ((tokens, width), BF, tok(width)),
        ((8, inner), F32, fixed(8, inner)),
        ((8, bc_width), F32, fixed(8, bc_width)),
        ((8, dt_width), F32, fixed(8, dt_width)),
    ]
    return pl.pallas_call(
        bwd_kernel,
        grid=(blocks,),
        in_specs=[
            tok(width),
            pl.BlockSpec((8, q), lambda i: (0, back(i))),
            tok(inner), tok(inner), halo(inner), tok(bc_width), halo(bc_width), tok(dt_width),
            tok(inner),
            pl.BlockSpec((1, half, inner), lambda i: (back(i), 0, 0)),
        ]
        + [whole(w.shape) for w in (packed, *params, pick)],
        out_specs=[o[2] for o in outs],
        out_shape=[jax.ShapeDtypeStruct(o[0], o[1]) for o in outs],
        scratch_shapes=[
            pltpu.VMEM((half, inner), F32),
            pltpu.VMEM((q + 8, inner), F32),
            pltpu.VMEM((q + 8, bc_width), F32),
            pltpu.VMEM((q + 8, inner), F32),
            pltpu.VMEM((q + 8, bc_width), F32),
        ],
        compiler_params=pltpu.CompilerParams(
            dimension_semantics=("arbitrary",), vmem_limit_bytes=60 * MIB
        ),
        name="mix_backward",
    )(gb, e_rows, gate, val, val, st, st, dt, y, ent, packed, *params, pick)


class Step:
    def __init__(self, **given):
        self.rows = 0
        self.width = 0
        self.line = 4
        self.chunks = 8
        self.partial = False
        self.gather = False
        self.late = False
        self.scale = False
        self.inner = False
        self.weights = 0
        self.grads = 0
        self.bits = 0
        self.middle = None
        self.__dict__.update(given)


def remote(src, dst, send, recv, device):
    return pltpu.make_async_remote_copy(
        src_ref=src, dst_ref=dst, send_sem=send, recv_sem=recv,
        device_id=device, device_id_type=pl.DeviceIdType.MESH,
    )


def when(condition):
    return pl.when(condition)


def comm_kernel(o, names, *refs):
    r = types.SimpleNamespace(**dict(zip(names, refs)))
    r.gbuf = [v for k, v in zip(names, refs) if k.startswith("gbuf")]
    n, count, rows = o.line, o.chunks, o.rows
    size = rows // count
    t = lax.axis_index("tensor")
    me = lax.axis_index("dp")
    own_bits = [(me // (1 << b)) % 2 for b in range(o.bits)]
    partner = [me + (1 - 2 * own_bits[b]) * (1 << b) for b in range(o.bits)]

    barrier = pltpu.get_barrier_semaphore()
    for k in range(1, n):
        pl.semaphore_signal(
            barrier, inc=1, device_id={"tensor": lax.rem(t + k, n)},
            device_id_type=pl.DeviceIdType.MESH,
        )
    over_dp = o.weights or o.grads
    if over_dp:
        for b in range(o.bits):
            pl.semaphore_signal(
                barrier, inc=1, device_id={"dp": partner[b]}, device_id_type=pl.DeviceIdType.MESH
            )
    pl.semaphore_wait(barrier, n - 1 + (o.bits if over_dp else 0))

    def at(s, c):
        return pl.ds(pl.multiple_of(s * rows + c * size, size), size)

    def piece(c):
        return pl.ds(pl.multiple_of(c * size, size), size)

    def hop(side, s, c, src):
        buf = r.rbuf if side == 0 else r.lbuf
        return remote(
            src, buf.at[s, piece(c)], r.rs_send.at[side, s], r.rs_recv.at[side, s, c],
            {"tensor": t + 1 if side == 0 else t - 1},
        )

    def reduce_items(side, c):
        buf = r.rbuf if side == 0 else r.lbuf
        edge = t == 0 if side == 0 else t == n - 1
        order = range(n - 1, 0, -1) if side == 0 else range(0, n - 1)
        for s in order:
            further = s > t if side == 0 else s < t

            @when(further & edge)
            def _():
                hop(side, s, c, r.part.at[at(s, c)]).start()

            @when(further & jnp.logical_not(edge))
            def _():
                hop(side, s, c, buf.at[s, piece(c)]).wait_recv()
                total = buf[s, piece(c), :].astype(F32) + r.part[at(s, c), :].astype(F32)
                buf[s, piece(c), :] = total.astype(BF)
                hop(side, s, c, buf.at[s, piece(c)]).start()

    def own_total(c):
        acc = r.acc
        acc[...] = r.part[at(t, c), :].astype(F32)

        @when(t > 0)
        def _():
            hop(0, t, c, r.rbuf.at[t, piece(c)]).wait_recv()
            acc[...] += r.rbuf[t, piece(c), :].astype(F32)

        @when(t < n - 1)
        def _():
            hop(1, t, c, r.lbuf.at[t, piece(c)]).wait_recv()
            acc[...] += r.lbuf[t, piece(c), :].astype(F32)

    def pass_on(side, s, c):
        spot = r.full.at[at(s, c)]
        return remote(
            spot, spot, r.ag_send.at[side, s], r.ag_recv.at[side, s, c],
            {"tensor": t + 1 if side == 0 else t - 1},
        )

    def forward_items(side, tau):
        order = range(n - 2, -1, -1) if side == 0 else range(1, n)
        for s in order:
            away = t - s if side == 0 else s - t
            late = max(s, n - 1 - s) if o.late else 0
            c = tau - late - away

            @when((away > 0) & (c >= 0) & (c < count))
            def _():
                pass_on(side, s, c).wait_recv()

                @when(t < n - 1 if side == 0 else t > 0)
                def _():
                    pass_on(side, s, c).start()

    def spot_of(k, ref):
        return ref.at[:, pl.ds(pl.multiple_of(k * rows, rows), rows)]

    def square_copy(k):
        dest = lax.rem(t + k, n)
        return remote(
            spot_of(dest, r.ssq), r.sqbuf.at[k - 1], r.sq_send.at[k - 1],
            r.sq_recv.at[k - 1], {"tensor": dest},
        )

    def inner_copy(k):
        return remote(
            spot_of(t, r.inner), spot_of(t, r.inner), r.in_send.at[k - 1],
            r.in_recv.at[k - 1], {"tensor": lax.rem(t + k, n)},
        )

    def inner_arrival(k):
        source = lax.rem(t + n - k, n)
        return remote(
            spot_of(source, r.inner), spot_of(source, r.inner), r.in_send.at[k - 1],
            r.in_recv.at[k - 1], {"tensor": source},
        )

    def bit_order(parity):
        high = list(range(o.bits - 1, 0, -1))
        if parity == 1:
            high = high[1:] + high[:1]
        return high + [0]

    def cols(j):
        return pl.ds(pl.multiple_of(j * WCHUNK, WCHUNK), WCHUNK)

    def spots(known):
        return tuple(slice(None) if b in known else own_bits[b] for b in range(o.bits - 1, -1, -1))

    def weight_copy(parity, stage, j):
        order = bit_order(parity)
        spot = r.wfull.at[(*spots(order[:stage]), slice(None), cols(j))]
        src = r.wown.at[:, cols(j)] if stage == 0 else spot
        return remote(
            src, spot, r.wg_send.at[stage, j], r.wg_recv.at[stage, j],
            {"dp": partner[order[stage]]},
        )

    def own_weights():
        return pltpu.make_async_copy(r.wown, r.wfull.at[spots([])], r.wl_sem)

    def each_parity(j, fn):
        for parity in range(2):
            @when((j >= 0) & (j < max(o.weights, o.grads)) & (lax.rem(j, 2) == parity))
            def _():
                fn(parity, j)

    def weight_items(tau):
        for stage in range(o.bits + 1):
            def run(parity, j):
                if stage > 0:
                    weight_copy(parity, stage - 1, j).wait_recv()
                if stage < o.bits:
                    weight_copy(parity, stage, j).start()
            each_parity(tau - stage, run)

    def grad_order(parity):
        high = list(range(1, o.bits))
        if parity == 1:
            high = high[1:] + high[:1]
        return [0] + high

    def grad_spot(parity, stage, mine):
        order = grad_order(parity)
        done, bit = order[:stage], order[stage]
        spot = []
        for b in range(o.bits - 1, -1, -1):
            if b in done:
                spot.append(own_bits[b])
            elif b == bit:
                spot.append(own_bits[b] if mine else 1 - own_bits[b])
            else:
                spot.append(slice(None))
        return tuple(spot)

    def grad_copy(parity, stage, j):
        order = grad_order(parity)
        return remote(
            r.grad.at[(j, *grad_spot(parity, stage, False))], r.gbuf[stage].at[j],
            r.gr_send.at[stage, j], r.gr_recv.at[stage, j],
            {"dp": partner[order[stage]]},
        )

    def product(j):
        left = lax.div(j, jnp.int32(5)) if o.bits else 0

        def one(i, _):
            spot = tuple((i // (1 << b)) % 2 for b in range(o.bits - 1, -1, -1))
            depth = r.grad.shape[-2]
            lhs = r.left[left, pl.ds(pl.multiple_of(i * depth, depth), depth), :]
            r.grad[(j, *spot)] = nn(lhs, r.right[:, cols(j)]).astype(BF)
            return 0

        lax.fori_loop(0, 1 << o.bits, one, 0)

    def grad_items(tau):
        def first(parity, j):
            product(j)
            grad_copy(parity, 0, j).start()

        each_parity(tau, first)
        for stage in range(1, o.bits + 1):
            def run(parity, j):
                grad_copy(parity, stage - 1, j).wait_recv()
                spot = grad_spot(parity, stage - 1, True)
                free = [i for i, v in enumerate(spot) if isinstance(v, slice)]
                buf = r.gbuf[stage - 1]
                for combo in range(1 << len(free)):
                    pick = [(combo >> i) % 2 for i in range(len(free))]
                    full = list(spot)
                    for i, v in zip(free, pick):
                        full[i] = v
                    total = r.grad[(j, *full)].astype(F32) + buf[(j, *pick)].astype(F32)
                    if stage < o.bits:
                        r.grad[(j, *full)] = total.astype(BF)
                    else:
                        r.gout[:, cols(j)] = total
                if stage < o.bits:
                    grad_copy(parity, stage, j).start()
            each_parity(tau - stage, run)

    if o.scale:
        for k in range(1, n):
            square_copy(k).start()
    if o.weights:
        own_weights().start()
    if o.grads:
        def turn(i, _):
            strip = pl.ds(pl.multiple_of(i * 128, 128), 128)
            r.left[0, strip, :] = r.lrows[:, strip].T
            r.left[1, strip, :] = r.lgrad[:, strip].T
            return 0
        lax.fori_loop(0, o.width // 128, turn, 0)
    if o.scale:
        total = spot_of(t, r.ssq)[...]
        for k in range(1, n):
            square_copy(k).wait_recv()
            total = total + r.sqbuf[k - 1]
        scale = lax.rsqrt(total / (o.scale * 1.0) + EPSILON)
        r.r2[...] = jnp.broadcast_to(scale.T[:, 0:1], (rows, 128))
    if o.gather and not o.late:
        r.full[pl.ds(pl.multiple_of(t * rows, rows), rows), :] = o.payload(r)
    if o.middle is not None:
        o.middle(r, None, None)

    ends = [count + (n - 1)]
    if o.late:
        ends.append(count + 2 * (n - 1))
    if over_dp:
        ends.append(max(o.weights, o.grads) + o.bits)

    def iteration(tau, _):
        if o.partial:
            for side in range(2):
                c = tau - (t if side == 0 else n - 1 - t)

                @when((c >= 0) & (c < count))
                def _():
                    reduce_items(side, c)

            c_own = tau - jnp.maximum(t, n - 1 - t)

            @when((c_own >= 0) & (c_own < count))
            def _():
                own_total(c_own)
                out = o.middle(r, piece(c_own), r.acc[...])
                if o.late:
                    r.full[at(t, c_own), :] = out
        if o.gather:
            c_out = tau - jnp.maximum(t, n - 1 - t) if o.late else tau

            @when((c_out >= 0) & (c_out < count))
            def _():
                @when(t < n - 1)
                def _():
                    pass_on(0, t, c_out).start()

                @when(t > 0)
                def _():
                    pass_on(1, t, c_out).start()

            for side in range(2):
                forward_items(side, tau)
        if o.weights:
            @when(tau == 1)
            def _():
                own_weights().wait()
            weight_items(tau)
        if o.grads:
            grad_items(tau)
        return 0

    lax.fori_loop(0, max(ends), iteration, 0)

    if o.inner:
        spot_of(t, r.inner)[...] = r.icol[...].T[0:8, :]
        for k in range(1, n):
            inner_copy(k).start()
        for k in range(1, n):
            inner_arrival(k).wait_recv()
        for k in range(1, n):
            inner_copy(k).wait_send()
    if o.scale:
        for k in range(1, n):
            square_copy(k).wait_send()
    for s in range(n):
        for side in range(2):
            inside = t < n - 1 if side == 0 else t > 0
            if o.partial:
                @when((s > t if side == 0 else s < t) & inside)
                def _():
                    buf = (r.rbuf if side == 0 else r.lbuf).at[s]
                    remote(
                        buf, buf, r.rs_send.at[side, s], r.rs_recv.at[side, s, 0],
                        {"tensor": t + 1 if side == 0 else t - 1},
                    ).wait_send()
            if o.gather:
                @when((s <= t if side == 0 else s >= t) & inside)
                def _():
                    spot = r.full.at[pl.ds(s * rows, rows)]
                    remote(
                        spot, spot, r.ag_send.at[side, s], r.ag_recv.at[side, s, 0],
                        {"tensor": t + 1 if side == 0 else t - 1},
                    ).wait_send()
    for j in range(o.weights):
        for stage in range(o.bits):
            weight_copy(j % 2, stage, jnp.int32(j)).wait_send()
    for j in range(o.grads):
        for stage in range(o.bits):
            grad_copy(j % 2, stage, jnp.int32(j)).wait_send()


def comm_call(o, name, collective, inputs, outputs, **scratch):
    n, count, rows, width = o.line, o.chunks, o.rows, o.width
    dma = pltpu.SemaphoreType.DMA
    if o.partial:
        scratch.update(
            rbuf=pltpu.VMEM((n, rows, width), BF),
            lbuf=pltpu.VMEM((n, rows, width), BF),
            acc=pltpu.VMEM((rows // count, width), F32),
            rs_send=dma((2, n)),
            rs_recv=dma((2, n, count)),
        )
    if o.gather:
        scratch.update(ag_send=dma((2, n)), ag_recv=dma((2, n, count)))
    if o.scale:
        scratch.update(
            sqbuf=pltpu.VMEM((n - 1, 8, rows), F32), sq_send=dma((n - 1,)), sq_recv=dma((n - 1,))
        )
    if o.inner:
        scratch.update(
            icol=pltpu.VMEM((rows, 128), F32), in_send=dma((n - 1,)), in_recv=dma((n - 1,))
        )
    if o.weights:
        scratch.update(
            wl_sem=dma(()),
            wg_send=dma((o.bits, o.weights)),
            wg_recv=dma((o.bits, o.weights)),
        )
    if o.grads:
        depth = o.width >> o.bits
        scratch.update(
            grad=pltpu.VMEM((o.grads, *(2,) * o.bits, depth, WCHUNK), BF),
            left=pltpu.VMEM((2, width, n * rows), BF),
            gr_send=dma((o.bits, o.grads)),
            gr_recv=dma((o.bits, o.grads)),
        )
        for stage in range(o.bits):
            scratch["gbuf%d" % stage] = pltpu.VMEM(
                (o.grads, *(2,) * (o.bits - 1 - stage), depth, WCHUNK), BF
            )
    names = [*inputs, *outputs, *scratch]
    out = pl.pallas_call(
        functools.partial(comm_kernel, o, names),
        in_specs=[pl.BlockSpec(memory_space=i[1]) for i in inputs.values()],
        out_specs=[pl.BlockSpec(memory_space=i[2]) for i in outputs.values()],
        out_shape=[jax.ShapeDtypeStruct(i[0], i[1]) for i in outputs.values()],
        scratch_shapes=list(scratch.values()),
        compiler_params=pltpu.CompilerParams(
            collective_id=collective, has_side_effects=True, vmem_limit_bytes=62 * MIB
        ),
        name=name,
    )(*[i[0] for i in inputs.values()])
    return dict(zip(outputs, out))


def plain_payload(r):
    return r.own[...]


def scaled_payload(r):
    return (r.r2[:, 0:1] * r.grad_in[...].astype(F32)).astype(BF)


def forward_middle(r, at, total):
    if at is None:
        return None
    branch = total * r.r2[at, 0:1]
    residual = r.res[at, :].astype(F32) + branch
    r.branch[at, :] = branch
    r.res_out[at, :] = residual
    r1 = lax.rsqrt(jnp.mean(residual * residual, axis=1, keepdims=True) + EPSILON)
    return (residual * r1 * r.gain[...]).astype(BF)


def last_middle(inner_all, r, at, total):
    if at is None:
        return None
    r2 = r.r2[at, 0:1]
    branch = total * r2
    r.res_out[at, :] = r.res[at, :].astype(F32) + branch
    dot = jnp.sum(r.grad_in[at, :].astype(F32) * branch, axis=1, keepdims=True)
    r.icol[at, :] = jnp.broadcast_to(r2 * r2 * dot / inner_all, (dot.shape[0], 128))
    return None


def backward_middle(inner_all, r, at, total):
    if at is None:
        r.ggain[...] = jnp.zeros_like(r.ggain)
        return None
    res = r.res[at, :].astype(F32)
    width = res.shape[1]
    r1 = lax.rsqrt(jnp.mean(res * res, axis=1, keepdims=True) + EPSILON)
    hat = res * r1
    r.ggain[0:1, :] += jnp.sum(hat * total, axis=0, keepdims=True)
    dn = total * r.gain[...]
    cross = jnp.sum(dn * hat, axis=1, keepdims=True) / width
    grad = r.grad_in[at, :].astype(F32) + r1 * (dn - hat * cross)
    r.grad_out[at, :] = grad
    if inner_all is None:
        return None
    r2 = r.r2[at, 0:1]
    dot = jnp.sum(grad.astype(BF).astype(F32) * r.branch[at, :], axis=1, keepdims=True)
    r.icol[at, :] = jnp.broadcast_to(r2 * r2 * dot / inner_all, (dot.shape[0], 128))
    return (r2 * grad).astype(BF)


def pad_to(v, rows, columns):
    return jnp.pad(v, ((0, rows - v.shape[0]), (0, columns - v.shape[1])))


def rows_of(v):
    return v.astype(F32).reshape(-1, v.shape[-1])


def shards(
    hidden_in,
    out_grad,
    norm_gain,
    proj_z,
    proj_x,
    proj_bc,
    proj_dt,
    conv_value,
    conv_value_bias,
    conv_state,
    conv_state_bias,
    step_bias,
    log_decay,
    skip_gain,
    gate_gain,
    proj_out,
):
    tensor_count = lax.axis_size("tensor")
    dp_count = lax.axis_size("dp")
    bits = dp_count.bit_length() - 1
    layers, shard_rows, inner = proj_z.shape
    rows_own, width = hidden_in.shape
    tokens = rows_own * tensor_count
    heads = step_bias.shape[1]
    bc_width = proj_bc.shape[2]
    inner_all = inner * tensor_count
    packed_width = bc_width + 128 + 3 * inner
    column_chunks = packed_width // WCHUNK
    vmem, far = pltpu.VMEM, pl.ANY

    small = jnp.concatenate([conv_state.reshape(layers, -1), conv_state_bias], axis=1)
    small = jnp.pad(small, ((0, 0), (0, shard_rows - small.shape[1])))
    extra = jnp.stack([norm_gain, small], axis=1).reshape(2 * layers, shard_rows).T
    packs = []
    for l in range(layers):
        packs.append(
            jnp.concatenate(
                [
                    proj_bc[l],
                    proj_dt[l],
                    extra,
                    jnp.zeros((shard_rows, 128 - heads - 2 * layers), BF),
                    proj_z[l],
                    proj_x[l],
                    proj_out[l].T,
                ],
                axis=1,
            )
        )
    full_shape = ((2,) * bits) + (shard_rows, packed_width)
    common = dict(rows=rows_own, width=width, line=tensor_count, bits=bits)

    def weight_io(l):
        return dict(wown=(packs[l], far)), dict(wfull=(full_shape, BF, far))

    whole_rows, own_rows = ((tokens, width), BF, vmem), ((rows_own, width), F32, vmem)
    win, wout = weight_io(0)
    got = comm_call(
        Step(gather=True, payload=plain_payload, weights=column_chunks, **common),
        "gather_first", 1,
        dict(own=(hidden_in, vmem), **win),
        dict(full=whole_rows, **wout),
    )
    x_rows = got["full"]
    packed = [got["wfull"].reshape(width, packed_width)]
    start = bc_width + heads
    extra_all = packed[0][:, start : start + 2 * layers].astype(F32)
    gains, params = [], []
    per = bc_width // dp_count
    for l in range(layers):
        gains.append(extra_all[:, 2 * l][None, :])
        smalls = extra_all[:, 2 * l + 1].reshape(dp_count, shard_rows)[:, : 5 * per]
        smalls = jnp.transpose(smalls.reshape(dp_count, 5, per), (1, 0, 2)).reshape(5, bc_width)
        params.append(
            (
                pad_to(rows_of(conv_value[l]), 8, inner),
                rows_of(conv_value_bias[l]),
                pad_to(smalls[:4], 8, bc_width),
                smalls[4:5],
                pad_to(rows_of(step_bias[l]), 1, 128),
                pad_to(-jnp.exp(rows_of(log_decay[l])), 1, 128),
                jnp.repeat(rows_of(skip_gain[l]), WIDTH, axis=1),
                rows_of(gate_gain[l]),
            )
        )
    pick = (jnp.arange(inner)[:, None] // WIDTH == jnp.arange(128)[None, :]).astype(BF)

    out = forward_mix(x_rows, packed[0], params[0] + (gains[0],), True)
    saved, rows = [out[:6]], [out[8]]
    residuals, branches, r2s = [hidden_in], [], []
    for l in range(layers - 1):
        win, wout = weight_io(l + 1)
        got = comm_call(
            Step(
                partial=True, gather=True, late=True, scale=inner_all, middle=forward_middle,
                weights=column_chunks, **common,
            ),
            "between_forward", 2 + l,
            dict(part=(out[6], vmem), ssq=(out[7], vmem), res=(residuals[l], vmem),
                 gain=(gains[l + 1], vmem), **win),
            dict(full=whole_rows, branch=own_rows, res_out=own_rows,
                 r2=((rows_own, 128), F32, vmem), **wout),
        )
        rows.append(got["full"])
        branches.append(got["branch"])
        residuals.append(got["res_out"])
        r2s.append(got["r2"])
        packed.append(got["wfull"].reshape(width, packed_width))
        out = forward_mix(rows[-1], packed[-1], params[l + 1] + (gains[l + 1],), False)
        saved.append(out[:6])
    got = comm_call(
        Step(
            partial=True, gather=True, scale=inner_all, inner=True, payload=scaled_payload,
            middle=functools.partial(last_middle, inner_all), **common,
        ),
        "turn_around", 16,
        dict(part=(out[6], vmem), ssq=(out[7], vmem), res=(residuals[-1], vmem),
             grad_in=(out_grad, vmem)),
        dict(full=whole_rows, res_out=own_rows, inner=((8, tokens), F32, vmem)),
        r2=pltpu.VMEM((rows_own, 128), F32),
    )
    hidden_out = got["res_out"]
    gradient = out_grad
    scattered, summed = [None] * layers, [None] * layers
    for l in reversed(range(layers)):
        grad_rows = got["full"]
        dcat, dpart, gvec, gst, gdt = backward_mix(
            grad_rows, got["inner"], saved[l], packed[l], params[l], pick
        )
        more = l > 0
        inputs = dict(
            part=(dpart, vmem), res=(residuals[l], vmem), gain=(gains[l], vmem),
            grad_in=(gradient, vmem), lrows=(rows[l], vmem), lgrad=(grad_rows, vmem),
            right=(dcat, vmem),
        )
        outputs = dict(
            grad_out=own_rows, ggain=((8, width), F32, vmem),
            gout=((shard_rows, packed_width), F32, vmem),
        )
        if more:
            inputs.update(r2=(r2s[l - 1], vmem), branch=(branches[l - 1], vmem))
            outputs.update(full=whole_rows, inner=((8, tokens), F32, vmem))
        got = comm_call(
            Step(
                partial=True, gather=more, late=more, inner=more, grads=column_chunks,
                middle=functools.partial(backward_middle, inner_all if more else None), **common,
            ),
            "between_backward" if more else "last_backward", 17 + l, inputs, outputs,
        )
        gradient = got["grad_out"]
        scattered[l] = got["gout"]
        summed[l] = (gvec, gdt, gst, got["ggain"][0])
    gout = jnp.stack(scattered)
    gvec, gdt, gst, ggain = (jnp.stack([s[i] for s in summed]) for i in range(4))
    gvec, gdt = lax.psum((gvec, gdt), "dp")
    gst, ggain = lax.psum((gst, ggain), ("dp", "tensor"))
    gbc = lax.psum(gout[:, :, :bc_width].astype(BF), "tensor").astype(F32)
    own = lambda v, axis: lax.dynamic_slice_in_dim(
        v, lax.axis_index("dp") * (v.shape[axis] // dp_count), v.shape[axis] // dp_count, axis
    )
    gst = own(gst, 2)
    first = bc_width + 128
    return (
        hidden_out,
        gradient,
        own(ggain, 1),
        gout[:, :, first : first + inner],
        gout[:, :, first + inner : first + 2 * inner],
        gbc,
        gout[:, :, bc_width : bc_width + heads],
        gvec[:, 0:4],
        gvec[:, 4],
        gst[:, 0:4],
        gst[:, 4],
        gdt[:, 0, :heads],
        gdt[:, 1, :heads],
        jnp.sum(gvec[:, 6].reshape(layers, heads, WIDTH), axis=2),
        gvec[:, 5],
        jnp.transpose(gout[:, :, first + 2 * inner :], (0, 2, 1)),
    )


def solution(mesh):
    placed = (
        P(("dp", "tensor"), None),
        P(("dp", "tensor"), None),
        P(None, "dp"),
        P(None, "dp", "tensor"),
        P(None, "dp", "tensor"),
        P(None, "dp", None),
        P(None, "dp", "tensor"),
        P(None, None, "tensor"),
        P(None, "tensor"),
        P(None, None, "dp"),
        P(None, "dp"),
        P(None, "tensor"),
        P(None, "tensor"),
        P(None, "tensor"),
        P(None, "tensor"),
        P(None, "tensor", "dp"),
    )
    return jax.shard_map(
        shards,
        mesh=mesh,
        in_specs=placed,
        out_specs=(
            P(("dp", "tensor"), None),
            P(("dp", "tensor"), None),
            P(None, "dp"),
            P(None, "dp", "tensor"),
            P(None, "dp", "tensor"),
            P(None, "dp", None),
            P(None, "dp", "tensor"),
            P(None, None, "tensor"),
            P(None, "tensor"),
            P(None, None, "dp"),
            P(None, "dp"),
            P(None, "tensor"),
            P(None, "tensor"),
            P(None, "tensor"),
            P(None, "tensor"),
            P(None, "tensor", "dp"),
        ),
        check_vma=False,
    )
```

```python
import functools
import types

import jax
import jax.numpy as jnp
from jax import lax
from jax.sharding import PartitionSpec as P
import jax.experimental.pallas as pl
import jax.experimental.pallas.tpu as pltpu

GROUP = 256
EPSILON = 1e-05
BF = jnp.bfloat16
F32 = jnp.float32
WIDTH = 64
MIB = 1024 * 1024
WCHUNK = 384


def nn(a, b):
    return lax.dot_general(a, b, (((1,), (0,)), ((), ())), preferred_element_type=F32)


def nt(a, b):
    return lax.dot_general(a, b, (((1,), (1,)), ((), ())), preferred_element_type=F32)


def parts3(v):
    one = v.astype(BF)
    rest = v - one.astype(F32)
    two = rest.astype(BF)
    three = (rest - two.astype(F32)).astype(BF)
    return one, two, three


def sum_rows(select, v):
    one, two, three = parts3(v)
    return nn(select, one) + nn(select, two) + nn(select, three)


def sum_lanes(v, select):
    one = v.astype(BF)
    two = (v - one.astype(F32)).astype(BF)
    return nn(one, select) + nn(two, select)


def silu_parts(v):
    sig = 1.0 / (1.0 + jnp.exp(-v))
    return sig, v * sig


def softplus(v):
    return jnp.maximum(v, 0.0) + jnp.log1p(jnp.exp(-jnp.abs(v)))


def pair_spread(column_values, pair, lane_low):
    low = column_values[:, 2 * pair : 2 * pair + 1]
    high = column_values[:, 2 * pair + 1 : 2 * pair + 2]
    return jnp.where(lane_low, low, high)


def spread(column_values, pairs, lane_low):
    return jnp.concatenate([pair_spread(column_values, p, lane_low) for p in range(pairs)], axis=1)


def conv_pre(padded, taps, bias, length):
    count = 4
    total = bias
    for k in range(count):
        total = total + taps[k : k + 1, :] * padded[pl.ds(8 - (count - 1) + k, length), :]
    return total


def blocks_of(w_ref, inner, bc_width):
    sizes = (bc_width, 128, inner, inner, inner)
    starts = [sum(sizes[:i]) for i in range(5)]
    return [w_ref.at[:, pl.ds(s, z)] for s, z in zip(starts, sizes)]


def small_refs(vec_ref, cst_ref, tiny_ref):
    vec, cst, tiny = vec_ref.at[0], cst_ref.at[0], tiny_ref.at[0]
    return (
        vec.at[0:4], vec.at[4:5], vec.at[5:6], vec.at[6:7],
        cst.at[0:4], cst.at[4:5], tiny.at[0:1], tiny.at[1:2],
    )


def fwd_kernel(
    first, rows_ref, w_ref, vec_ref, cst_ref, tiny_ref, gain_ref,
    gate_ref, val_ref, st_ref, dt_ref, y_ref, ent_ref, part_ref, ssq_ref,
    *rest,
):
    normed_ref = rest[0] if first else None
    state, vpad, spad = rest[-3:]
    step = pl.program_id(0)
    length = rows_ref.shape[0]
    cv_ref, cvb_ref, skip_ref, gg_ref, cs_ref, csb_ref, sb_ref, rate_ref = small_refs(
        vec_ref, cst_ref, tiny_ref
    )
    inner = gg_ref.shape[1]
    pairs = inner // 128
    wbc_ref, wdt_ref, wz_ref, wx_ref, wot_ref = blocks_of(w_ref, inner, cs_ref.shape[1])

    @pl.when(step == 0)
    def _():
        state[...] = jnp.zeros_like(state)
        vpad[0:8, :] = jnp.zeros((8, inner), F32)
        spad[0:8, :] = jnp.zeros((8, spad.shape[1]), F32)

    @pl.when(step > 0)
    def _():
        vpad[0:8, :] = vpad[length : length + 8, :]
        spad[0:8, :] = spad[length : length + 8, :]

    rows = rows_ref[...]
    if first:
        rows = rows.astype(F32)
        r1 = lax.rsqrt(jnp.mean(rows * rows, axis=1, keepdims=True) + EPSILON)
        rows = (rows * r1 * gain_ref[0]).astype(BF)
        normed_ref[...] = rows
    gate_ref[...] = nn(rows, wz_ref[...])
    val = nn(rows, wx_ref[...])
    val_ref[...] = val
    vpad[8 : length + 8, :] = val
    st = nn(rows, wbc_ref[...])
    st_ref[...] = st
    spad[8 : length + 8, :] = st
    dt_in = nn(rows, wdt_ref[...])
    dt_ref[...] = dt_in

    _, v = silu_parts(conv_pre(vpad, cv_ref, cvb_ref[...], length))
    _, bc = silu_parts(conv_pre(spad, cs_ref, csb_ref[...], length))
    half = bc.shape[1] // 2
    bb = bc[:, :half].astype(BF)
    cb = bc[:, half:].astype(BF)
    dt = softplus(dt_in + sb_ref[...])
    q_index = lax.broadcasted_iota(jnp.int32, (length, length), 0)
    s_index = lax.broadcasted_iota(jnp.int32, (length, length), 1)
    causal = q_index >= s_index
    tril = jnp.where(causal, 1.0, 0.0).astype(BF)
    a = sum_rows(tril, dt * rate_ref[...])
    a_rows = a.T
    lane_low = lax.broadcasted_iota(jnp.int32, (length, 128), 1) < WIDTH
    dt_x = spread(dt, pairs, lane_low)
    a_x = spread(a, pairs, lane_low)
    x = v * dt_x
    xb = x.astype(BF)
    scores = jnp.where(causal, nt(cb, bb), 0.0)
    inside = []
    zero = jnp.zeros((length, 128), BF)
    for p in range(pairs):
        xp = xb[:, 128 * p : 128 * (p + 1)]
        total = None
        for j in range(2):
            h = 2 * p + j
            decay = jnp.exp(jnp.minimum(a[:, h : h + 1] - a_rows[h : h + 1, :], 0.0))
            m = (scores * decay).astype(BF)
            term = nn(m, jnp.where(lane_low, xp, zero) if j == 0 else jnp.where(lane_low, zero, xp))
            total = term if total is None else total + term
        inside.append(total)
    entering = state[...]
    ent_ref[0] = entering
    outside = jnp.exp(a_x) * nn(cb, entering.astype(BF))
    a_last = a_x[length - 1 : length, :]
    xw = (x * jnp.exp(a_last - a_x)).astype(BF)
    state[...] = jnp.exp(a_last) * entering + nn(bc[:, :half].T.astype(BF), xw)
    y = jnp.concatenate(inside, axis=1) + outside + skip_ref[...] * v
    y_ref[...] = y
    _, sgate = silu_parts(gate_ref[...])
    gated = y * sgate
    square = (gated * gated).astype(BF)
    ssq_ref[...] = nt(jnp.ones((8, inner), BF), square)
    mixed = (gated * gg_ref[...]).astype(BF)
    part_ref[...] = nt(mixed, wot_ref[...]).astype(BF)


def whole(shape):
    return pl.BlockSpec(shape, lambda i: (0,) * len(shape), pipeline_mode=pl.Buffered(1))


def layer_specs(params, l):
    return [
        pl.BlockSpec((1,) + p.shape[1:], lambda i: (l, 0, 0), pipeline_mode=pl.Buffered(1))
        for p in params
    ]


def forward_mix(rows, packed, params, l):
    first = l == 0
    tokens, width = rows.shape
    inner = params[0].shape[2]
    bc_width = params[1].shape[2]
    dt_width = 128
    half = bc_width // 2
    q = GROUP
    blocks = tokens // q
    tok = lambda n: pl.BlockSpec((q, n), lambda i: (i, 0))
    outs = [
        ((tokens, inner), F32, tok(inner)),
        ((tokens, inner), F32, tok(inner)),
        ((tokens, bc_width), F32, tok(bc_width)),
        ((tokens, dt_width), F32, tok(dt_width)),
        ((tokens, inner), F32, tok(inner)),
        ((blocks, half, inner), F32, pl.BlockSpec((1, half, inner), lambda i: (i, 0, 0))),
        ((tokens, width), BF, tok(width)),
        ((8, tokens), F32, pl.BlockSpec((8, q), lambda i: (0, i))),
    ]
    if first:
        outs.append(((tokens, width), BF, tok(width)))
    return pl.pallas_call(
        functools.partial(fwd_kernel, first),
        grid=(blocks,),
        in_specs=[tok(width), whole(packed.shape)] + layer_specs(params, l),
        out_specs=[o[2] for o in outs],
        out_shape=[jax.ShapeDtypeStruct(o[0], o[1]) for o in outs],
        scratch_shapes=[
            pltpu.VMEM((half, inner), F32),
            pltpu.VMEM((q + 8, inner), F32),
            pltpu.VMEM((q + 8, bc_width), F32),
        ],
        compiler_params=pltpu.CompilerParams(
            dimension_semantics=("arbitrary",), vmem_limit_bytes=56 * MIB
        ),
        name="mix_forward",
    )(rows, packed, *params)


def bwd_kernel(
    gb_ref, e_ref, gate_ref, val_ref, valp_ref, st_ref, stp_ref, dt_ref, y_ref, ent_ref,
    w_ref, vec_ref, cst_ref, tiny_ref, pick_ref,
    dcat_ref, dpart_ref, gvec_ref, gst_ref, gdt_ref,
    dstate, vpad, spad, dvpad, dspad,
):
    step = pl.program_id(0)
    blocks = pl.num_programs(0)
    length = gb_ref.shape[0]
    cv_ref, cvb_ref, skip_ref, gg_ref, cs_ref, csb_ref, sb_ref, rate_ref = small_refs(
        vec_ref, cst_ref, tiny_ref
    )
    inner = gg_ref.shape[1]
    bc_width = cs_ref.shape[1]
    wbc_ref, wdt_ref, wz_ref, wx_ref, wot_ref = blocks_of(w_ref, inner, bc_width)
    dst_ref, ddt_ref, dgate_ref, dval_ref, mixed_ref = blocks_of(dcat_ref, inner, bc_width)
    half = bc_width // 2
    pairs = inner // 128

    @pl.when(step == 0)
    def _():
        dstate[...] = jnp.zeros_like(dstate)
        dvpad[length : length + 8, :] = jnp.zeros((8, inner), F32)
        dspad[length : length + 8, :] = jnp.zeros((8, bc_width), F32)
        gvec_ref[...] = jnp.zeros_like(gvec_ref)
        gst_ref[...] = jnp.zeros_like(gst_ref)
        gdt_ref[...] = jnp.zeros_like(gdt_ref)

    @pl.when(step > 0)
    def _():
        dvpad[length : length + 8, :] = dvpad[0:8, :]
        dspad[length : length + 8, :] = dspad[0:8, :]

    first = step == blocks - 1
    vpad[0:8, :] = jnp.where(first, 0.0, valp_ref[...])
    spad[0:8, :] = jnp.where(first, 0.0, stp_ref[...])
    vpad[8 : length + 8, :] = val_ref[...]
    spad[8 : length + 8, :] = st_ref[...]

    pre_v = conv_pre(vpad, cv_ref, cvb_ref[...], length)
    sig_v, v = silu_parts(pre_v)
    pre_s = conv_pre(spad, cs_ref, csb_ref[...], length)
    sig_s, bc = silu_parts(pre_s)
    bb = bc[:, :half].astype(BF)
    cb = bc[:, half:].astype(BF)
    z = dt_ref[...] + sb_ref[...]
    dt = softplus(z)
    rate = rate_ref[...]
    s_index = lax.broadcasted_iota(jnp.int32, (length, length), 0)
    q_index = lax.broadcasted_iota(jnp.int32, (length, length), 1)
    upper = q_index >= s_index
    a = sum_rows(jnp.where(s_index >= q_index, 1.0, 0.0).astype(BF), dt * rate)
    a_rows = a.T
    lane_low = lax.broadcasted_iota(jnp.int32, (length, 128), 1) < WIDTH
    dt_x = spread(dt, pairs, lane_low)
    a_x = spread(a, pairs, lane_low)
    x = v * dt_x
    xb = x.astype(BF)
    skip = skip_ref[...]

    y = y_ref[...]
    gate = gate_ref[...]
    sig_g, sgate = silu_parts(gate)
    gated = y * sgate
    per_token = e_ref[...].T
    e, r2 = per_token[:, 0:1], per_token[:, 1:2]
    dm = nn(gb_ref[...], wot_ref[...]) * r2
    dgated = dm * gg_ref[...] - e * gated
    mixed_ref[...] = (gated * r2 * gg_ref[...]).astype(BF)
    dgate = (dgated * y * (sig_g * (1.0 + gate * (1.0 - sig_g)))).astype(BF)
    dgate_ref[...] = dgate
    dy = dgated * sgate
    dyb = dy.astype(BF)
    dyf = dyb.astype(F32)

    scores = jnp.where(upper, nt(bb, cb), 0.0)
    zero = jnp.zeros((length, 128), BF)
    dscores = jnp.zeros((length, length), F32)
    dx_list = []
    for p in range(pairs):
        xp = xb[:, 128 * p : 128 * (p + 1)]
        dp = dyb[:, 128 * p : 128 * (p + 1)]
        total = None
        for j in range(2):
            h = 2 * p + j
            decay = jnp.exp(jnp.minimum(a_rows[h : h + 1, :] - a[:, h : h + 1], 0.0))
            m = (scores * decay).astype(BF)
            dh = jnp.where(lane_low, dp, zero) if j == 0 else jnp.where(lane_low, zero, dp)
            term = nn(m, dh)
            total = term if total is None else total + term
            dscores = dscores + nt(xp, dh) * decay
        dx_list.append(total)
    dx_in = jnp.concatenate(dx_list, axis=1)
    dscores = jnp.where(upper, dscores, 0.0)
    db = nn(dscores.astype(BF), cb)
    dc = nn(dscores.T.astype(BF), bb)

    entering = ent_ref[0]
    dleaving = dstate[...]
    dleaving_b = dleaving.astype(BF)
    ea = jnp.exp(a_x)
    a_last = a_x[length - 1 : length, :]
    ea_last = jnp.exp(a_last)
    w = jnp.exp(a_last - a_x)
    dxw = nn(bb, dleaving_b) * w
    db = db + nt((x * w).astype(BF), dleaving_b)
    eady = (ea * dyf).astype(BF)
    dc = dc + nt(eady, entering.astype(BF))
    dstate[...] = ea_last * dleaving + nn(bc[:, half:].T.astype(BF), eady)
    dx = dx_in + dxw
    u = x * dxw
    last_add = jnp.sum(u, axis=0, keepdims=True) + ea_last * jnp.sum(
        entering * dleaving, axis=0, keepdims=True
    )
    da_x = dyf * (y - skip * v) - xb.astype(F32) * dx_in - u
    row_index = lax.broadcasted_iota(jnp.int32, (length, inner), 0)
    da_x = da_x + jnp.where(row_index == length - 1, last_add, 0.0)
    pick = pick_ref[...]
    da = sum_lanes(da_x, pick)
    dr = sum_rows(jnp.where(upper, 1.0, 0.0).astype(BF), da)
    ddt = sum_lanes(dx * v, pick) + dr * rate
    dz = ddt * (1.0 / (1.0 + jnp.exp(-z)))
    ddtb = dz.astype(BF)
    ddt_ref[...] = ddtb
    gdt_ref[0:1, :] += jnp.sum(dz, axis=0, keepdims=True)
    gdt_ref[1:2, :] += jnp.sum(dr * dt * rate, axis=0, keepdims=True)

    dpre_v = (skip * dy + dt_x * dx) * (sig_v * (1.0 + pre_v * (1.0 - sig_v)))
    dvpad[0:length, :] = dpre_v
    dval = jnp.zeros((length, inner), F32)
    for k in range(4):
        dval = dval + cv_ref[k : k + 1, :] * dvpad[pl.ds(3 - k, length), :]
        gvec_ref[k : k + 1, :] += jnp.sum(
            dpre_v * vpad[pl.ds(5 + k, length), :], axis=0, keepdims=True
        )
    gvec_ref[4:5, :] += jnp.sum(dpre_v, axis=0, keepdims=True)
    gvec_ref[5:6, :] += jnp.sum(gated * dm, axis=0, keepdims=True)
    gvec_ref[6:7, :] += jnp.sum(dy * v, axis=0, keepdims=True)
    dvalb = dval.astype(BF)
    dval_ref[...] = dvalb

    dbc = jnp.concatenate([db, dc], axis=1)
    dpre_s = dbc * (sig_s * (1.0 + pre_s * (1.0 - sig_s)))
    dspad[0:length, :] = dpre_s
    dst = jnp.zeros((length, bc_width), F32)
    for k in range(4):
        dst = dst + cs_ref[k : k + 1, :] * dspad[pl.ds(3 - k, length), :]
        gst_ref[k : k + 1, :] += jnp.sum(
            dpre_s * spad[pl.ds(5 + k, length), :], axis=0, keepdims=True
        )
    gst_ref[4:5, :] += jnp.sum(dpre_s, axis=0, keepdims=True)
    dstb = dst.astype(BF)
    dst_ref[...] = dstb
    dpart = nt(dgate, wz_ref[...]) + nt(dvalb, wx_ref[...])
    dpart = dpart + nt(dstb, wbc_ref[...]) + nt(ddtb, wdt_ref[...])
    dpart_ref[...] = dpart.astype(BF)


def backward_mix(gb, e_rows, kept, packed, params, pick, l):
    gate, val, st, dt, y, ent = kept
    tokens, width = gb.shape
    inner = params[0].shape[2]
    bc_width = params[1].shape[2]
    dt_width = 128
    packed_width = packed.shape[1]
    half = bc_width // 2
    q = GROUP
    blocks = tokens // q
    back = lambda i: blocks - 1 - i
    tok = lambda n: pl.BlockSpec((q, n), lambda i: (back(i), 0))
    halo = lambda n: pl.BlockSpec(
        (8, n), lambda i: (jnp.maximum(back(i) * (q // 8) - 1, 0), 0)
    )
    fixed = lambda r, c: pl.BlockSpec((r, c), lambda i: (0, 0))
    outs = [
        ((tokens, packed_width), BF, tok(packed_width)),
        ((tokens, width), BF, tok(width)),
        ((8, inner), F32, fixed(8, inner)),
        ((8, bc_width), F32, fixed(8, bc_width)),
        ((8, dt_width), F32, fixed(8, dt_width)),
    ]
    return pl.pallas_call(
        bwd_kernel,
        grid=(blocks,),
        in_specs=[
            tok(width),
            pl.BlockSpec((8, q), lambda i: (0, back(i))),
            tok(inner), tok(inner), halo(inner), tok(bc_width), halo(bc_width), tok(dt_width),
            tok(inner),
            pl.BlockSpec((1, half, inner), lambda i: (back(i), 0, 0)),
        ]
        + [whole(packed.shape)] + layer_specs(params, l) + [whole(pick.shape)],
        out_specs=[o[2] for o in outs],
        out_shape=[jax.ShapeDtypeStruct(o[0], o[1]) for o in outs],
        scratch_shapes=[
            pltpu.VMEM((half, inner), F32),
            pltpu.VMEM((q + 8, inner), F32),
            pltpu.VMEM((q + 8, bc_width), F32),
            pltpu.VMEM((q + 8, inner), F32),
            pltpu.VMEM((q + 8, bc_width), F32),
        ],
        compiler_params=pltpu.CompilerParams(
            dimension_semantics=("arbitrary",), vmem_limit_bytes=60 * MIB
        ),
        name="mix_backward",
    )(gb, e_rows, gate, val, val, st, st, dt, y, ent, packed, *params, pick)


class Step:
    def __init__(self, **given):
        self.rows = 0
        self.width = 0
        self.line = 4
        self.chunks = 8
        self.hop = 1
        self.slack = 0
        self.partial = False
        self.gather = False
        self.late = False
        self.scale = False
        self.inner = False
        self.weights = 0
        self.grads = 0
        self.states = 0
        self.sums = False
        self.bits = 0
        self.middle = None
        self.__dict__.update(given)


def remote(src, dst, send, recv, device):
    return pltpu.make_async_remote_copy(
        src_ref=src, dst_ref=dst, send_sem=send, recv_sem=recv,
        device_id=device, device_id_type=pl.DeviceIdType.MESH,
    )


def when(condition):
    return pl.when(condition)


def comm_kernel(o, names, *refs):
    r = types.SimpleNamespace(**dict(zip(names, refs)))
    r.gbuf = [v for k, v in zip(names, refs) if k.startswith("gbuf")]
    n, count, rows = o.line, o.chunks, o.rows
    size = rows // count
    t = lax.axis_index("tensor")
    me = lax.axis_index("dp")
    own_bits = [(me // (1 << b)) % 2 for b in range(o.bits)]
    partner = [me + (1 - 2 * own_bits[b]) * (1 << b) for b in range(o.bits)]

    barrier = pltpu.get_barrier_semaphore()
    for k in range(1, n):
        pl.semaphore_signal(
            barrier, inc=1, device_id={"tensor": lax.rem(t + k, n)},
            device_id_type=pl.DeviceIdType.MESH,
        )
    over_dp = o.weights or o.grads
    r.early = [v for k, v in zip(names, refs) if k.startswith("esum")]
    r.lined = [v for k, v in zip(names, refs) if k.startswith("lsum")]
    r.gains = [v for k, v in zip(names, refs) if k.startswith("gsum")]
    if over_dp:
        for b in range(o.bits):
            pl.semaphore_signal(
                barrier, inc=1, device_id={"dp": partner[b]}, device_id_type=pl.DeviceIdType.MESH
            )
    pl.semaphore_wait(barrier, n - 1 + (o.bits if over_dp else 0))

    def at(s, c):
        return pl.ds(pl.multiple_of(s * rows + c * size, size), size)

    def piece(c):
        return pl.ds(pl.multiple_of(c * size, size), size)

    def hop(side, s, c, src):
        buf = r.rbuf if side == 0 else r.lbuf
        return remote(
            src, buf.at[s, piece(c)], r.rs_send.at[side, s], r.rs_recv.at[side, s, c],
            {"tensor": t + 1 if side == 0 else t - 1},
        )

    def reduce_items(side, c):
        buf = r.rbuf if side == 0 else r.lbuf
        edge = t == 0 if side == 0 else t == n - 1
        order = range(n - 1, 0, -1) if side == 0 else range(0, n - 1)
        for s in order:
            further = s > t if side == 0 else s < t

            @when(further & edge)
            def _():
                hop(side, s, c, r.part.at[at(s, c)]).start()

            @when(further & jnp.logical_not(edge))
            def _():
                hop(side, s, c, buf.at[s, piece(c)]).wait_recv()
                total = buf[s, piece(c), :].astype(F32) + r.part[at(s, c), :].astype(F32)
                buf[s, piece(c), :] = total.astype(BF)
                hop(side, s, c, buf.at[s, piece(c)]).start()

    def own_total(c):
        acc = r.acc
        acc[...] = r.part[at(t, c), :].astype(F32)

        @when(t > 0)
        def _():
            hop(0, t, c, r.rbuf.at[t, piece(c)]).wait_recv()
            acc[...] += r.rbuf[t, piece(c), :].astype(F32)

        @when(t < n - 1)
        def _():
            hop(1, t, c, r.lbuf.at[t, piece(c)]).wait_recv()
            acc[...] += r.lbuf[t, piece(c), :].astype(F32)

    def pass_on(side, s, c):
        spot = r.full.at[at(s, c)]
        return remote(
            spot, spot, r.ag_send.at[side, s], r.ag_recv.at[side, s, c],
            {"tensor": t + 1 if side == 0 else t - 1},
        )

    def forward_items(side, tau):
        order = range(n - 2, -1, -1) if side == 0 else range(1, n)
        for s in order:
            away = t - s if side == 0 else s - t
            late = o.hop * max(s, n - 1 - s) + o.slack if o.late else 0
            c = tau - late - o.hop * away

            @when((away > 0) & (c >= 0) & (c < count))
            def _():
                pass_on(side, s, c).wait_recv()

                @when(t < n - 1 if side == 0 else t > 0)
                def _():
                    pass_on(side, s, c).start()

    def spot_of(k, ref):
        return ref.at[:, pl.ds(pl.multiple_of(k * rows, rows), rows)]

    def square_copy(k):
        dest = lax.rem(t + k, n)
        return remote(
            spot_of(dest, r.ssq), r.sqbuf.at[k - 1], r.sq_send.at[k - 1],
            r.sq_recv.at[k - 1], {"tensor": dest},
        )

    def inner_copy(k):
        return remote(
            spot_of(t, r.inner), spot_of(t, r.inner), r.in_send.at[k - 1],
            r.in_recv.at[k - 1], {"tensor": lax.rem(t + k, n)},
        )

    def inner_arrival(k):
        source = lax.rem(t + n - k, n)
        return remote(
            spot_of(source, r.inner), spot_of(source, r.inner), r.in_send.at[k - 1],
            r.in_recv.at[k - 1], {"tensor": source},
        )

    def bit_order(parity):
        high = list(range(o.bits - 1, 0, -1))
        if parity == 1:
            high = high[1:] + high[:1]
        return high + [0]

    def cols(j):
        return pl.ds(pl.multiple_of(j * WCHUNK, WCHUNK), WCHUNK)

    def spots(known):
        return tuple(slice(None) if b in known else own_bits[b] for b in range(o.bits - 1, -1, -1))

    def weight_copy(parity, stage, j):
        order = bit_order(parity)
        depth = r.wown.shape[0] // o.weights
        strip = pl.ds(pl.multiple_of(j * depth, depth), depth)
        spot = r.wfull.at[(*spots(order[:stage]), strip)]
        src = r.wown.at[strip] if stage == 0 else spot
        return remote(
            src, spot, r.wg_send.at[stage, j], r.wg_recv.at[stage, j],
            {"dp": partner[order[stage]]},
        )

    def own_weights():
        return pltpu.make_async_copy(r.wown, r.wfull.at[spots([])], r.wl_sem)

    def each_parity(pair, fn):
        for parity in range(2):
            j = 2 * pair + parity

            @when((j >= 0) & (j < max(o.weights, o.grads)))
            def _():
                fn(parity, j)

    def weight_items(tau):
        for stage in range(o.bits + 1):
            def run(parity, j):
                if stage > 0:
                    weight_copy(parity, stage - 1, j).wait_recv()
                if stage < o.bits:
                    weight_copy(parity, stage, j).start()
            each_parity(tau - stage, run)

    def grad_order(parity):
        high = list(range(1, o.bits))
        if parity == 1:
            high = high[1:] + high[:1]
        return [0] + high

    def grad_spot(parity, stage, mine):
        order = grad_order(parity)
        done, bit = order[:stage], order[stage]
        spot = []
        for b in range(o.bits - 1, -1, -1):
            if b in done:
                spot.append(own_bits[b])
            elif b == bit:
                spot.append(own_bits[b] if mine else 1 - own_bits[b])
            else:
                spot.append(slice(None))
        return tuple(spot)

    def grad_copy(parity, stage, j):
        order = grad_order(parity)
        return remote(
            r.grad.at[(j, *grad_spot(parity, stage, False))], r.gbuf[stage].at[j],
            r.gr_send.at[stage, j], r.gr_recv.at[stage, j],
            {"dp": partner[order[stage]]},
        )

    def product(j):
        left = lax.div(j, jnp.int32(5)) if o.bits else 0

        def one(i, _):
            spot = tuple((i // (1 << b)) % 2 for b in range(o.bits - 1, -1, -1))
            depth = r.grad.shape[-2]
            lhs = r.left[left, pl.ds(pl.multiple_of(i * depth, depth), depth), :]
            r.grad[(j, *spot)] = nn(lhs, r.right[:, cols(j)]).astype(BF)
            return 0

        lax.fori_loop(0, 1 << o.bits, one, 0)

    def grad_items(tau):
        def first(parity, j):
            product(j)
            grad_copy(parity, 0, j).start()

        each_parity(tau, first)
        for stage in range(1, o.bits + 1):
            def run(parity, j):
                grad_copy(parity, stage - 1, j).wait_recv()
                spot = grad_spot(parity, stage - 1, True)
                free = [i for i, v in enumerate(spot) if isinstance(v, slice)]
                buf = r.gbuf[stage - 1]
                for combo in range(1 << len(free)):
                    pick = [(combo >> i) % 2 for i in range(len(free))]
                    full = list(spot)
                    for i, v in zip(free, pick):
                        full[i] = v
                    total = r.grad[(j, *full)].astype(F32) + buf[(j, *pick)].astype(F32)
                    if stage < o.bits:
                        r.grad[(j, *full)] = total.astype(BF)
                    else:
                        r.gout[:, cols(j)] = total
                if stage < o.bits:
                    grad_copy(parity, stage, j).start()
            each_parity(tau - stage, run)

    def share(buf, send, recv, k):
        return remote(buf.at[t], buf.at[t], send.at[k - 1], recv.at[k - 1],
                      {"tensor": lax.rem(t + k, n)})

    def shared(buf, send, recv):
        for k in range(1, n):
            source = lax.rem(t + n - k, n)
            remote(buf.at[source], buf.at[source], send.at[k - 1], recv.at[k - 1],
                   {"tensor": source}).wait_recv()

    def line_total(buf):
        total = buf[0]
        for k in range(1, n):
            total = total + buf[k]
        return total

    def double(acc, buf, send, recv, b):
        return remote(acc.at[b], buf.at[b], send.at[b], recv.at[b], {"dp": partner[b]})

    def doubled(acc, buf, send, recv, b):
        double(acc, buf, send, recv, b).wait_recv()
        acc[b + 1] = acc[b] + buf[b]

    def lanes(index, ref):
        return slice(index * ref.shape[1], (index + 1) * ref.shape[1])

    line_groups, dp_groups = [], []
    if o.sums:
        line_groups = [(r.lbank, r.lb_send, r.lb_recv)]
        dp_groups = [(r.dbank, r.dbuf, r.db_send, r.db_recv)]
        if r.gains:
            line_groups.append((r.gbank, r.gb_send, r.gb_recv))
            dp_groups.append((r.hbank, r.hbuf, r.hb_send, r.hb_recv))

    def sum_items(tau):
        @when(tau == 2)
        def _():
            for g in line_groups:
                shared(*g)
            off = 0
            for v in r.early:
                r.dbank[0, :, off : off + v.shape[1]] = v[...]
                off += v.shape[1]
            r.dbank[0, :, off:] = line_total(r.lbank)
            if r.gains:
                r.hbank[0] = line_total(r.gbank)
            for g in dp_groups:
                double(*g, 0).start()

        for b in range(o.bits):
            @when(tau == 4 + b)
            def _():
                for g in dp_groups:
                    doubled(*g, b)
                    if b < o.bits - 1:
                        double(*g, b + 1).start()

    def state_items(tau):
        at_first = o.bits + 1
        quarter = r.gout.shape[0] // n

        @when(tau == at_first)
        def _():
            for s in range(n):
                r.qsend[s] = r.gout[s * quarter : (s + 1) * quarter, 0 : o.states].astype(BF)
            for k in range(1, n):
                state_out(k).start()

        @when(tau == at_first + 2)
        def _():
            total = r.qsend[t].astype(F32)
            for k in range(1, n):
                state_out(k).wait_recv()
                total = total + r.qbuf[k - 1].astype(F32)
            r.qall[t] = total.astype(BF)
            for k in range(1, n):
                share(r.qall, r.qa_send, r.qa_recv, k).start()

    def state_out(k):
        dest = lax.rem(t + k, n)
        return remote(r.qsend.at[dest], r.qbuf.at[k - 1], r.qs_send.at[k - 1],
                      r.qs_recv.at[k - 1], {"tensor": dest})

    if o.sums:
        off = 0
        for v in r.lined:
            r.lbank[t, :, off : off + v.shape[1]] = v[...]
            off += v.shape[1]
        for i, v in enumerate(r.gains):
            r.gbank[t, :, lanes(i, v)] = v[0:1, :]
        for g in line_groups:
            for k in range(1, n):
                share(*g, k).start()
    if o.scale:
        for k in range(1, n):
            square_copy(k).start()
    if o.weights:
        own_weights().start()
    if o.grads:
        def turn(i, _):
            strip = pl.ds(pl.multiple_of(i * 128, 128), 128)
            r.left[0, strip, :] = r.lrows[:, strip].T
            r.left[1, strip, :] = r.lgrad[:, strip].T
            return 0
        lax.fori_loop(0, o.width // 128, turn, 0)
    if o.scale:
        total = spot_of(t, r.ssq)[...]
        for k in range(1, n):
            square_copy(k).wait_recv()
            total = total + r.sqbuf[k - 1]
        scale = lax.rsqrt(total / (o.scale * 1.0) + EPSILON)
        r.r2[...] = jnp.broadcast_to(scale.T[:, 0:1], (rows, 128))
    if o.gather and not o.late:
        r.full[pl.ds(pl.multiple_of(t * rows, rows), rows), :] = o.payload(r)
    if o.middle is not None:
        o.middle(r, None, None)

    ends = [count + o.hop * (n - 1) + o.slack]
    if o.late:
        ends.append(ends[0] + o.hop * (n - 1))
    if over_dp:
        ends.append((max(o.weights, o.grads) + 1) // 2 + o.bits)
    if o.grads:
        ends.append(o.bits + 4)
    if o.sums:
        ends.append(4 + o.bits)

    def iteration(tau, _):
        if o.partial:
            for side in range(2):
                c = tau - o.hop * (t if side == 0 else n - 1 - t)

                @when((c >= 0) & (c < count))
                def _():
                    reduce_items(side, c)

            c_own = tau - o.hop * jnp.maximum(t, n - 1 - t) - o.slack

            @when((c_own >= 0) & (c_own < count))
            def _():
                own_total(c_own)
                out = o.middle(r, piece(c_own), r.acc[...])
                if o.late:
                    r.full[at(t, c_own), :] = out
        if o.gather:
            c_out = tau - o.hop * jnp.maximum(t, n - 1 - t) - o.slack if o.late else tau

            @when((c_out >= 0) & (c_out < count))
            def _():
                @when(t < n - 1)
                def _():
                    pass_on(0, t, c_out).start()

                @when(t > 0)
                def _():
                    pass_on(1, t, c_out).start()

            for side in range(2):
                forward_items(side, tau)
        if o.weights:
            @when(tau == 1)
            def _():
                own_weights().wait()
            weight_items(tau)
        if o.grads:
            grad_items(tau)
            state_items(tau)
        if o.sums:
            sum_items(tau)
        return 0

    lax.fori_loop(0, max(ends), iteration, 0)

    if o.sums:
        r.jbank[t] = r.ggain[0:1, :]
        for k in range(1, n):
            share(r.jbank, r.jb_send, r.jb_recv, k).start()
    if o.inner:
        spot_of(t, r.inner)[...] = r.icol[...].T[0:8, :]
        for k in range(1, n):
            inner_copy(k).start()
        for k in range(1, n):
            inner_arrival(k).wait_recv()
        for k in range(1, n):
            inner_copy(k).wait_send()
    if o.sums:
        last = (r.kbank, r.kbuf, r.kb_send, r.kb_recv)
        shared(r.jbank, r.jb_send, r.jb_recv)
        r.kbank[0] = line_total(r.jbank)
        for b in range(o.bits):
            double(*last, b).start()
            doubled(*last, b)
        r.sums[...] = r.dbank[o.bits]
        r.gain_sums[0:1, :] = r.kbank[o.bits]
        for i, v in enumerate(r.gains):
            r.gain_sums[i + 1 : i + 2, :] = r.hbank[o.bits, :, lanes(i, v)]
        for g in line_groups + [(r.jbank, r.jb_send, r.jb_recv)]:
            for k in range(1, n):
                share(*g, k).wait_send()
        for g in dp_groups + [last]:
            for b in range(o.bits):
                double(*g, b).wait_send()
    if o.grads:
        shared(r.qall, r.qa_send, r.qa_recv)
        quarter = r.gout.shape[0] // n
        for s in range(n):
            r.gout[s * quarter : (s + 1) * quarter, 0 : o.states] = r.qall[s].astype(F32)
        for k in range(1, n):
            state_out(k).wait_send()
            share(r.qall, r.qa_send, r.qa_recv, k).wait_send()
    if o.scale:
        for k in range(1, n):
            square_copy(k).wait_send()
    for s in range(n):
        for side in range(2):
            inside = t < n - 1 if side == 0 else t > 0
            if o.partial:
                @when((s > t if side == 0 else s < t) & inside)
                def _():
                    buf = (r.rbuf if side == 0 else r.lbuf).at[s]
                    remote(
                        buf, buf, r.rs_send.at[side, s], r.rs_recv.at[side, s, 0],
                        {"tensor": t + 1 if side == 0 else t - 1},
                    ).wait_send()
            if o.gather:
                @when((s <= t if side == 0 else s >= t) & inside)
                def _():
                    spot = r.full.at[pl.ds(s * rows, rows)]
                    remote(
                        spot, spot, r.ag_send.at[side, s], r.ag_recv.at[side, s, 0],
                        {"tensor": t + 1 if side == 0 else t - 1},
                    ).wait_send()
    for j in range(o.weights):
        for stage in range(o.bits):
            weight_copy(j % 2, stage, jnp.int32(j)).wait_send()
    for j in range(o.grads):
        for stage in range(o.bits):
            grad_copy(j % 2, stage, jnp.int32(j)).wait_send()


def comm_call(o, name, collective, inputs, outputs, **scratch):
    n, count, rows, width = o.line, o.chunks, o.rows, o.width
    dma = pltpu.SemaphoreType.DMA
    if o.partial:
        scratch.update(
            rbuf=pltpu.VMEM((n, rows, width), BF),
            lbuf=pltpu.VMEM((n, rows, width), BF),
            acc=pltpu.VMEM((rows // count, width), F32),
            rs_send=dma((2, n)),
            rs_recv=dma((2, n, count)),
        )
    if o.gather:
        scratch.update(ag_send=dma((2, n)), ag_recv=dma((2, n, count)))
    if o.scale:
        scratch.update(
            sqbuf=pltpu.VMEM((n - 1, 8, rows), F32), sq_send=dma((n - 1,)), sq_recv=dma((n - 1,))
        )
    if o.inner:
        scratch.update(
            icol=pltpu.VMEM((rows, 128), F32), in_send=dma((n - 1,)), in_recv=dma((n - 1,))
        )
    if o.weights:
        scratch.update(
            wl_sem=dma(()),
            wg_send=dma((o.bits, o.weights)),
            wg_recv=dma((o.bits, o.weights)),
        )
    if o.grads:
        depth = o.width >> o.bits
        scratch.update(
            grad=pltpu.VMEM((o.grads, *(2,) * o.bits, depth, WCHUNK), BF),
            left=pltpu.VMEM((2, width, n * rows), BF),
            gr_send=dma((o.bits, o.grads)),
            gr_recv=dma((o.bits, o.grads)),
        )
        for stage in range(o.bits):
            scratch["gbuf%d" % stage] = pltpu.VMEM(
                (o.grads, *(2,) * (o.bits - 1 - stage), depth, WCHUNK), BF
            )
        part = (n, (width >> o.bits) // n, o.states)
        scratch.update(
            qsend=pltpu.VMEM(part, BF), qall=pltpu.VMEM(part, BF),
            qbuf=pltpu.VMEM((n - 1,) + part[1:], BF),
            qs_send=dma((n - 1,)), qs_recv=dma((n - 1,)),
            qa_send=dma((n - 1,)), qa_recv=dma((n - 1,)),
        )
    if o.sums:
        def lanes_of(start):
            return sum(v[0].shape[1] for k, v in inputs.items() if k.startswith(start))

        lined, early, gains = lanes_of("lsum"), lanes_of("esum"), lanes_of("gsum")
        for name_of, tall, line_width, dp_width in (
            ("lb db", 8, lined, lined + early), ("gb hb", 1, gains, gains), ("jb kb", 1, width, width)
        ):
            if line_width:
                one, two = name_of.split()
                scratch[one + "ank"] = pltpu.VMEM((n, tall, line_width), F32)
                scratch[two + "ank"] = pltpu.VMEM((o.bits + 1, tall, dp_width), F32)
                scratch[two + "uf"] = pltpu.VMEM((o.bits, tall, dp_width), F32)
                for key, size in ((one, n - 1), (two, o.bits)):
                    scratch[key + "_send"] = dma((size,))
                    scratch[key + "_recv"] = dma((size,))
    names = [*inputs, *outputs, *scratch]
    out = pl.pallas_call(
        functools.partial(comm_kernel, o, names),
        in_specs=[pl.BlockSpec(memory_space=i[1]) for i in inputs.values()],
        out_specs=[pl.BlockSpec(memory_space=i[2]) for i in outputs.values()],
        out_shape=[jax.ShapeDtypeStruct(i[0], i[1]) for i in outputs.values()],
        scratch_shapes=list(scratch.values()),
        compiler_params=pltpu.CompilerParams(
            collective_id=collective, has_side_effects=True, vmem_limit_bytes=62 * MIB
        ),
        name=name,
    )(*[i[0] for i in inputs.values()])
    return dict(zip(outputs, out))


def plain_payload(r):
    return r.own[...]


def token_columns(first, second):
    lane = lax.broadcasted_iota(jnp.int32, (first.shape[0], 128), 1)
    return jnp.where(lane == 0, first, second)


def forward_middle(r, at, total):
    if at is None:
        return None
    branch = total * r.r2[at, 0:1]
    residual = r.res[at, :].astype(F32) + branch
    r.branch[at, :] = branch
    r.res_out[at, :] = residual
    r1 = lax.rsqrt(jnp.mean(residual * residual, axis=1, keepdims=True) + EPSILON)
    return (residual * r1 * r.gain[...]).astype(BF)


def last_middle(inner_all, r, at, total):
    if at is None:
        return None
    r2 = r.r2[at, 0:1]
    branch = total * r2
    r.res_out[at, :] = r.res[at, :].astype(F32) + branch
    dot = jnp.sum(r.grad_in[at, :].astype(F32) * branch, axis=1, keepdims=True)
    r.icol[at, :] = token_columns(r2 * r2 * dot / inner_all, r2)
    return None


def backward_middle(inner_all, r, at, total):
    if at is None:
        r.ggain[...] = jnp.zeros_like(r.ggain)
        return None
    res = r.res[at, :].astype(F32)
    width = res.shape[1]
    r1 = lax.rsqrt(jnp.mean(res * res, axis=1, keepdims=True) + EPSILON)
    hat = res * r1
    r.ggain[0:1, :] += jnp.sum(hat * total, axis=0, keepdims=True)
    dn = total * r.gain[...]
    cross = jnp.sum(dn * hat, axis=1, keepdims=True) / width
    grad = r.grad_in[at, :].astype(F32) + r1 * (dn - hat * cross)
    r.grad_out[at, :] = grad
    if inner_all is None:
        return None
    r2 = r.r2[at, 0:1]
    dot = jnp.sum(grad.astype(BF).astype(F32) * r.branch[at, :], axis=1, keepdims=True)
    r.icol[at, :] = token_columns(r2 * r2 * dot / inner_all, r2)
    return grad.astype(BF)


def pad_to(v, rows, columns):
    return jnp.pad(v, ((0, rows - v.shape[0]), (0, columns - v.shape[1])))


def rows_of(v):
    return v.astype(F32).reshape(-1, v.shape[-1])


def shards(
    hidden_in,
    out_grad,
    norm_gain,
    proj_z,
    proj_x,
    proj_bc,
    proj_dt,
    conv_value,
    conv_value_bias,
    conv_state,
    conv_state_bias,
    step_bias,
    log_decay,
    skip_gain,
    gate_gain,
    proj_out,
):
    tensor_count = lax.axis_size("tensor")
    dp_count = lax.axis_size("dp")
    bits = dp_count.bit_length() - 1
    layers, shard_rows, inner = proj_z.shape
    rows_own, width = hidden_in.shape
    tokens = rows_own * tensor_count
    heads = step_bias.shape[1]
    bc_width = proj_bc.shape[2]
    inner_all = inner * tensor_count
    packed_width = bc_width + 128 + 3 * inner
    column_chunks, row_chunks = packed_width // WCHUNK, shard_rows // 16
    vmem, far = pltpu.VMEM, pl.ANY

    small = jnp.concatenate([conv_state.reshape(layers, -1), conv_state_bias], axis=1)
    small = jnp.pad(small, ((0, 0), (0, shard_rows - small.shape[1])))
    extra = jnp.stack([norm_gain, small], axis=1).reshape(2 * layers, shard_rows).T
    packs = []
    for l in range(layers):
        packs.append(
            jnp.concatenate(
                [
                    proj_bc[l],
                    proj_dt[l],
                    extra,
                    jnp.zeros((shard_rows, 128 - heads - 2 * layers), BF),
                    proj_z[l],
                    proj_x[l],
                    proj_out[l].T,
                ],
                axis=1,
            )
        )
    full_shape = ((2,) * bits) + (shard_rows, packed_width)
    common = dict(rows=rows_own, width=width, line=tensor_count, bits=bits)

    def weight_io(l):
        return dict(wown=(packs[l], vmem)), dict(wfull=(full_shape, BF, far))

    vec = jnp.concatenate(
        [
            conv_value,
            conv_value_bias[:, None],
            jnp.repeat(skip_gain, WIDTH, axis=1)[:, None],
            gate_gain[:, None],
        ],
        axis=1,
    ).astype(F32)
    tiny = jnp.stack([step_bias.astype(F32), -jnp.exp(log_decay.astype(F32))], axis=1)
    tiny = jnp.pad(tiny, ((0, 0), (0, 0), (0, 128 - heads)))
    pick = (jnp.arange(inner)[:, None] // WIDTH == jnp.arange(128)[None, :]).astype(BF)

    whole_rows, own_rows = ((tokens, width), BF, vmem), ((rows_own, width), F32, vmem)
    win, wout = weight_io(0)
    got = comm_call(
        Step(gather=True, payload=plain_payload, weights=row_chunks, **common),
        "gather_first", 1,
        dict(own=(hidden_in, vmem), **win),
        dict(full=whole_rows, **wout),
    )
    x_rows = got["full"]
    out_grad, x_rows = lax.optimization_barrier((out_grad, x_rows))
    grad_rows = lax.all_gather(out_grad, "tensor", axis=0, tiled=True)
    packed = [got["wfull"].reshape(width, packed_width)]
    start = bc_width + heads
    extra_all = packed[0][:, start : start + 2 * layers].astype(F32)
    gain_rows = extra_all[:, 0 : 2 * layers : 2].T[:, None, :]
    per = bc_width // dp_count
    smalls = extra_all[:, 1 : 2 * layers : 2].reshape(dp_count, shard_rows, layers)
    smalls = smalls[:, : 5 * per].reshape(dp_count, 5, per, layers)
    cst = jnp.transpose(smalls, (3, 1, 0, 2)).reshape(layers, 5, bc_width)
    params = (vec, cst, tiny)

    out = forward_mix(x_rows, packed[0], params + (gain_rows,), 0)
    saved, rows = [out[:6]], [out[8]]
    residuals, branches, r2s = [hidden_in], [], []
    for l in range(layers - 1):
        win, wout = weight_io(l + 1)
        got = comm_call(
            Step(
                partial=True, gather=True, late=True, scale=inner_all, middle=forward_middle,
                weights=row_chunks, **common,
            ),
            "between_forward", 2 + l,
            dict(part=(out[6], vmem), ssq=(out[7], vmem), res=(residuals[l], vmem),
                 gain=(gain_rows[l + 1], vmem), **win),
            dict(full=whole_rows, branch=own_rows, res_out=own_rows,
                 r2=((rows_own, 128), F32, vmem), **wout),
        )
        rows.append(got["full"])
        branches.append(got["branch"])
        residuals.append(got["res_out"])
        r2s.append(got["r2"])
        packed.append(got["wfull"].reshape(width, packed_width))
        out = forward_mix(rows[-1], packed[-1], params + (gain_rows,), l + 1)
        saved.append(out[:6])
    got = comm_call(
        Step(
            partial=True, scale=inner_all, inner=True,
            middle=functools.partial(last_middle, inner_all), **common,
        ),
        "turn_around", 16,
        dict(part=(out[6], vmem), ssq=(out[7], vmem), res=(residuals[-1], vmem),
             grad_in=(out_grad, vmem)),
        dict(res_out=own_rows, inner=((8, tokens), F32, vmem)),
        r2=pltpu.VMEM((rows_own, 128), F32),
    )
    hidden_out = got["res_out"]
    gradient = out_grad
    scattered, summed, gain_grads = [None] * layers, [None] * layers, [None] * layers
    for l in reversed(range(layers)):
        dcat, dpart, *small_grads = backward_mix(
            grad_rows, got["inner"], saved[l], packed[l], params, pick, l
        )
        summed[l] = small_grads
        more = l > 0
        inputs = dict(
            part=(dpart, vmem), res=(residuals[l], vmem), gain=(gain_rows[l], vmem),
            grad_in=(gradient, vmem), lrows=(rows[l], vmem), lgrad=(grad_rows, vmem),
            right=(dcat, vmem),
        )
        outputs = dict(
            grad_out=own_rows, ggain=((8, width), F32, vmem),
            gout=((shard_rows, packed_width), F32, vmem),
        )
        if more:
            inputs.update(r2=(r2s[l - 1], vmem), branch=(branches[l - 1], vmem))
            outputs.update(full=whole_rows, inner=((8, tokens), F32, vmem))
        else:
            for i in range(layers):
                gvec, gst, gdt = summed[i]
                inputs["esum%d" % i], inputs["esum_%d" % i] = (gvec, vmem), (gdt, vmem)
                inputs["lsum%d" % i] = (gst, vmem)
            for i in range(1, layers):
                inputs["gsum%d" % i] = (gain_grads[i], vmem)
            early = sum(v.shape[1] for i in range(layers) for v in summed[i])
            outputs.update(
                sums=((8, early), F32, vmem), gain_sums=((8, width), F32, vmem)
            )
        got = comm_call(
            Step(
                partial=True, gather=more, late=more, inner=more, grads=column_chunks,
                states=bc_width, sums=not more,
                middle=functools.partial(backward_middle, inner_all if more else None), **common,
            ),
            "between_backward" if more else "last_backward", 17 + l, inputs, outputs,
        )
        gradient = got["grad_out"]
        scattered[l], gain_grads[l] = got["gout"], got["ggain"]
        if more:
            grad_rows = got["full"]
    gout = jnp.stack(scattered)
    sums, ggain = got["sums"], got["gain_sums"][:layers]
    each = inner + 128
    gvec = jnp.stack([sums[:, i * each : i * each + inner] for i in range(layers)])
    gdt = jnp.stack([sums[:, i * each + inner : (i + 1) * each] for i in range(layers)])
    gst = jnp.stack(
        [sums[:, layers * each + i * bc_width :][:, :bc_width] for i in range(layers)]
    )
    own = lambda v, axis: lax.dynamic_slice_in_dim(
        v, lax.axis_index("dp") * (v.shape[axis] // dp_count), v.shape[axis] // dp_count, axis
    )
    gst = own(gst, 2)
    first = bc_width + 128
    return (
        hidden_out,
        gradient,
        own(ggain, 1),
        gout[:, :, first : first + inner],
        gout[:, :, first + inner : first + 2 * inner],
        gout[:, :, :bc_width],
        gout[:, :, bc_width : bc_width + heads],
        gvec[:, 0:4],
        gvec[:, 4],
        gst[:, 0:4],
        gst[:, 4],
        gdt[:, 0, :heads],
        gdt[:, 1, :heads],
        jnp.sum(gvec[:, 6].reshape(layers, heads, WIDTH), axis=2),
        gvec[:, 5],
        jnp.transpose(gout[:, :, first + 2 * inner :], (0, 2, 1)),
    )


def solution(mesh):
    placed = (
        P(("dp", "tensor"), None),
        P(("dp", "tensor"), None),
        P(None, "dp"),
        P(None, "dp", "tensor"),
        P(None, "dp", "tensor"),
        P(None, "dp", None),
        P(None, "dp", "tensor"),
        P(None, None, "tensor"),
        P(None, "tensor"),
        P(None, None, "dp"),
        P(None, "dp"),
        P(None, "tensor"),
        P(None, "tensor"),
        P(None, "tensor"),
        P(None, "tensor"),
        P(None, "tensor", "dp"),
    )
    return jax.shard_map(
        shards,
        mesh=mesh,
        in_specs=placed,
        out_specs=(
            P(("dp", "tensor"), None),
            P(("dp", "tensor"), None),
            P(None, "dp"),
            P(None, "dp", "tensor"),
            P(None, "dp", "tensor"),
            P(None, "dp", None),
            P(None, "dp", "tensor"),
            P(None, None, "tensor"),
            P(None, "tensor"),
            P(None, None, "dp"),
            P(None, "dp"),
            P(None, "tensor"),
            P(None, "tensor"),
            P(None, "tensor"),
            P(None, "tensor"),
            P(None, "tensor", "dp"),
        ),
        check_vma=False,
    )
```

```python
import functools
import types

import jax
import jax.numpy as jnp
from jax import lax
from jax.sharding import PartitionSpec as P
import jax.experimental.pallas as pl
import jax.experimental.pallas.tpu as pltpu

GROUP = 256
EPSILON = 1e-05
BF = jnp.bfloat16
F32 = jnp.float32
WIDTH = 64
MIB = 1024 * 1024
WCHUNK = 384


def nn(a, b):
    return lax.dot_general(a, b, (((1,), (0,)), ((), ())), preferred_element_type=F32)


def tn(a, b):
    return lax.dot_general(a, b, (((0,), (0,)), ((), ())), preferred_element_type=F32)


def nt(a, b):
    return lax.dot_general(a, b, (((1,), (1,)), ((), ())), preferred_element_type=F32)


def parts3(v):
    one = v.astype(BF)
    rest = v - one.astype(F32)
    two = rest.astype(BF)
    three = (rest - two.astype(F32)).astype(BF)
    return one, two, three


def sum_rows(select, v):
    one, two, three = parts3(v)
    return nn(select, one) + nn(select, two) + nn(select, three)


def sum_lanes(v, select):
    one = v.astype(BF)
    two = (v - one.astype(F32)).astype(BF)
    return nn(one, select) + nn(two, select)


def silu_parts(v):
    sig = 1.0 / (1.0 + jnp.exp(-v))
    return sig, v * sig


def softplus(v):
    return jnp.maximum(v, 0.0) + jnp.log1p(jnp.exp(-jnp.abs(v)))


def pair_spread(column_values, pair, lane_low):
    low = column_values[:, 2 * pair : 2 * pair + 1]
    high = column_values[:, 2 * pair + 1 : 2 * pair + 2]
    return jnp.where(lane_low, low, high)


def spread(column_values, pairs, lane_low):
    return jnp.concatenate([pair_spread(column_values, p, lane_low) for p in range(pairs)], axis=1)


def conv_pre(padded, taps, bias, length):
    count = 4
    total = bias
    for k in range(count):
        total = total + taps[k : k + 1, :] * padded[pl.ds(8 - (count - 1) + k, length), :]
    return total


def blocks_of(w_ref, inner, bc_width):
    sizes = (bc_width, 128, inner, inner, inner)
    starts = [sum(sizes[:i]) for i in range(5)]
    return [w_ref.at[:, pl.ds(s, z)] for s, z in zip(starts, sizes)]


def small_refs(vec_ref, cst_ref, tiny_ref):
    vec, cst, tiny = vec_ref.at[0], cst_ref.at[0], tiny_ref.at[0]
    return (
        vec.at[0:4], vec.at[4:5], vec.at[5:6], vec.at[6:7],
        cst.at[0:4], cst.at[4:5], tiny.at[0:1], tiny.at[1:2],
    )


def fwd_kernel(
    first, last, rows_ref, w_ref, vec_ref, cst_ref, tiny_ref, gain_ref, *rest,
):
    if last:
        gb_ref, *rest = rest
    gate_ref, val_ref, st_ref, dt_ref, y_ref, ent_ref, part_ref, ssq_ref, *rest = rest
    if first:
        normed_ref, *rest = rest
    if last:
        dm_ref, *rest = rest
    state, vpad, spad = rest[-3:]
    step = pl.program_id(0)
    length = rows_ref.shape[0]
    cv_ref, cvb_ref, skip_ref, gg_ref, cs_ref, csb_ref, sb_ref, rate_ref = small_refs(
        vec_ref, cst_ref, tiny_ref
    )
    inner = gg_ref.shape[1]
    pairs = inner // 128
    wbc_ref, wdt_ref, wz_ref, wx_ref, wot_ref = blocks_of(w_ref, inner, cs_ref.shape[1])

    @pl.when(step == 0)
    def _():
        state[...] = jnp.zeros_like(state)
        vpad[0:8, :] = jnp.zeros((8, inner), F32)
        spad[0:8, :] = jnp.zeros((8, spad.shape[1]), F32)

    @pl.when(step > 0)
    def _():
        vpad[0:8, :] = vpad[length : length + 8, :]
        spad[0:8, :] = spad[length : length + 8, :]

    rows = rows_ref[...]
    if first:
        rows = rows.astype(F32)
        r1 = lax.rsqrt(jnp.mean(rows * rows, axis=1, keepdims=True) + EPSILON)
        rows = (rows * r1 * gain_ref[0]).astype(BF)
        normed_ref[...] = rows
    gate_ref[...] = nn(rows, wz_ref[...])
    val = nn(rows, wx_ref[...])
    val_ref[...] = val
    vpad[8 : length + 8, :] = val
    st = nn(rows, wbc_ref[...])
    st_ref[...] = st
    spad[8 : length + 8, :] = st
    dt_in = nn(rows, wdt_ref[...])
    dt_ref[...] = dt_in

    _, v = silu_parts(conv_pre(vpad, cv_ref, cvb_ref[...], length))
    _, bc = silu_parts(conv_pre(spad, cs_ref, csb_ref[...], length))
    half = bc.shape[1] // 2
    bb = bc[:, :half].astype(BF)
    cb = bc[:, half:].astype(BF)
    dt = softplus(dt_in + sb_ref[...])
    q_index = lax.broadcasted_iota(jnp.int32, (length, length), 0)
    s_index = lax.broadcasted_iota(jnp.int32, (length, length), 1)
    causal = q_index >= s_index
    tril = jnp.where(causal, 1.0, 0.0).astype(BF)
    a = sum_rows(tril, dt * rate_ref[...])
    a_rows = a.T
    lane_low = lax.broadcasted_iota(jnp.int32, (length, 128), 1) < WIDTH
    dt_x = spread(dt, pairs, lane_low)
    a_x = spread(a, pairs, lane_low)
    x = v * dt_x
    xb = x.astype(BF)
    scores = jnp.where(causal, nt(cb, bb), 0.0)
    inside = []
    zero = jnp.zeros((length, 128), BF)
    for p in range(pairs):
        xp = xb[:, 128 * p : 128 * (p + 1)]
        total = None
        for j in range(2):
            h = 2 * p + j
            decay = jnp.exp(jnp.minimum(a[:, h : h + 1] - a_rows[h : h + 1, :], 0.0))
            m = (scores * decay).astype(BF)
            term = nn(m, jnp.where(lane_low, xp, zero) if j == 0 else jnp.where(lane_low, zero, xp))
            total = term if total is None else total + term
        inside.append(total)
    entering = state[...]
    ent_ref[0] = entering
    outside = jnp.exp(a_x) * nn(cb, entering.astype(BF))
    a_last = a_x[length - 1 : length, :]
    xw = (x * jnp.exp(a_last - a_x)).astype(BF)
    state[...] = jnp.exp(a_last) * entering + nn(bc[:, :half].T.astype(BF), xw)
    y = jnp.concatenate(inside, axis=1) + outside + skip_ref[...] * v
    y_ref[...] = y
    _, sgate = silu_parts(gate_ref[...])
    gated = y * sgate
    square = (gated * gated).astype(BF)
    ssq_ref[...] = nt(jnp.ones((8, inner), BF), square)
    mixed = (gated * gg_ref[...]).astype(BF)
    part_ref[...] = nt(mixed, wot_ref[...]).astype(BF)
    if last:
        dm = nn(gb_ref[...], wot_ref[...])
        dm_ref[...] = dm
        dots = nt(jnp.ones((8, inner), BF), (dm * gg_ref[...] * gated).astype(BF))
        row = lax.broadcasted_iota(jnp.int32, dots.shape, 0)
        ssq_ref[...] = jnp.where(row == 0, ssq_ref[...], dots)


def whole(shape):
    return pl.BlockSpec(shape, lambda i: (0,) * len(shape), pipeline_mode=pl.Buffered(1))


def layer_specs(params, l):
    return [
        pl.BlockSpec((1,) + p.shape[1:], lambda i: (l, 0, 0), pipeline_mode=pl.Buffered(1))
        for p in params
    ]


def forward_mix(rows, packed, params, l, gb=None):
    first, last = l == 0, gb is not None
    tokens, width = rows.shape
    inner = params[0].shape[2]
    bc_width = params[1].shape[2]
    dt_width = 128
    half = bc_width // 2
    q = GROUP
    blocks = tokens // q
    tok = lambda n: pl.BlockSpec((q, n), lambda i: (i, 0))
    outs = [
        ((tokens, inner), F32, tok(inner)),
        ((tokens, inner), F32, tok(inner)),
        ((tokens, bc_width), F32, tok(bc_width)),
        ((tokens, dt_width), F32, tok(dt_width)),
        ((tokens, inner), F32, tok(inner)),
        ((blocks, half, inner), F32, pl.BlockSpec((1, half, inner), lambda i: (i, 0, 0))),
        ((tokens, width), BF, tok(width)),
        ((8, tokens), F32, pl.BlockSpec((8, q), lambda i: (0, i))),
    ]
    if first:
        outs.append(((tokens, width), BF, tok(width)))
    if last:
        outs.append(((tokens, inner), F32, tok(inner)))
    return pl.pallas_call(
        functools.partial(fwd_kernel, first, last),
        grid=(blocks,),
        in_specs=[tok(width), whole(packed.shape)]
        + layer_specs(params, l)
        + ([tok(width)] if last else []),
        out_specs=[o[2] for o in outs],
        out_shape=[jax.ShapeDtypeStruct(o[0], o[1]) for o in outs],
        scratch_shapes=[
            pltpu.VMEM((half, inner), F32),
            pltpu.VMEM((q + 8, inner), F32),
            pltpu.VMEM((q + 8, bc_width), F32),
        ],
        compiler_params=pltpu.CompilerParams(
            dimension_semantics=("arbitrary",), vmem_limit_bytes=56 * MIB
        ),
        name="mix_forward",
    )(rows, packed, *params, *([gb] if last else []))


def bwd_kernel(
    ready, gb_ref, e_ref, gate_ref, val_ref, valp_ref, st_ref, stp_ref, dt_ref, y_ref, ent_ref,
    w_ref, vec_ref, cst_ref, tiny_ref, pick_ref,
    dcat_ref, dpart_ref, gvec_ref, gst_ref, gdt_ref,
    dstate, vpad, spad, dvpad, dspad,
):
    step = pl.program_id(0)
    blocks = pl.num_programs(0)
    length = gb_ref.shape[0]
    cv_ref, cvb_ref, skip_ref, gg_ref, cs_ref, csb_ref, sb_ref, rate_ref = small_refs(
        vec_ref, cst_ref, tiny_ref
    )
    inner = gg_ref.shape[1]
    bc_width = cs_ref.shape[1]
    wbc_ref, wdt_ref, wz_ref, wx_ref, wot_ref = blocks_of(w_ref, inner, bc_width)
    dst_ref, ddt_ref, dgate_ref, dval_ref, mixed_ref = blocks_of(dcat_ref, inner, bc_width)
    half = bc_width // 2
    pairs = inner // 128

    @pl.when(step == 0)
    def _():
        dstate[...] = jnp.zeros_like(dstate)
        dvpad[length : length + 8, :] = jnp.zeros((8, inner), F32)
        dspad[length : length + 8, :] = jnp.zeros((8, bc_width), F32)
        gvec_ref[...] = jnp.zeros_like(gvec_ref)
        gst_ref[...] = jnp.zeros_like(gst_ref)
        gdt_ref[...] = jnp.zeros_like(gdt_ref)

    @pl.when(step > 0)
    def _():
        dvpad[length : length + 8, :] = dvpad[0:8, :]
        dspad[length : length + 8, :] = dspad[0:8, :]

    first = step == blocks - 1
    vpad[0:8, :] = jnp.where(first, 0.0, valp_ref[...])
    spad[0:8, :] = jnp.where(first, 0.0, stp_ref[...])
    vpad[8 : length + 8, :] = val_ref[...]
    spad[8 : length + 8, :] = st_ref[...]

    pre_v = conv_pre(vpad, cv_ref, cvb_ref[...], length)
    sig_v, v = silu_parts(pre_v)
    pre_s = conv_pre(spad, cs_ref, csb_ref[...], length)
    sig_s, bc = silu_parts(pre_s)
    bb = bc[:, :half].astype(BF)
    cb = bc[:, half:].astype(BF)
    z = dt_ref[...] + sb_ref[...]
    dt = softplus(z)
    rate = rate_ref[...]
    s_index = lax.broadcasted_iota(jnp.int32, (length, length), 0)
    q_index = lax.broadcasted_iota(jnp.int32, (length, length), 1)
    upper = q_index >= s_index
    a = sum_rows(jnp.where(s_index >= q_index, 1.0, 0.0).astype(BF), dt * rate)
    a_rows = a.T
    lane_low = lax.broadcasted_iota(jnp.int32, (length, 128), 1) < WIDTH
    dt_x = spread(dt, pairs, lane_low)
    a_x = spread(a, pairs, lane_low)
    x = v * dt_x
    xb = x.astype(BF)
    skip = skip_ref[...]

    y = y_ref[...]
    gate = gate_ref[...]
    sig_g, sgate = silu_parts(gate)
    gated = y * sgate
    per_token = e_ref[...].T
    e, r2 = per_token[:, 0:1], per_token[:, 1:2]
    dm = (gb_ref[...] if ready else nn(gb_ref[...], wot_ref[...])) * r2
    dgated = dm * gg_ref[...] - e * gated
    mixed_ref[...] = (gated * r2 * gg_ref[...]).astype(BF)
    dgate = (dgated * y * (sig_g * (1.0 + gate * (1.0 - sig_g)))).astype(BF)
    dgate_ref[...] = dgate
    dy = dgated * sgate
    dyb = dy.astype(BF)
    dyf = dyb.astype(F32)

    scores = jnp.where(upper, nt(bb, cb), 0.0)
    zero = jnp.zeros((length, 128), BF)
    dscores = jnp.zeros((length, length), F32)
    dx_list = []
    for p in range(pairs):
        xp = xb[:, 128 * p : 128 * (p + 1)]
        dp = dyb[:, 128 * p : 128 * (p + 1)]
        total = None
        for j in range(2):
            h = 2 * p + j
            decay = jnp.exp(jnp.minimum(a_rows[h : h + 1, :] - a[:, h : h + 1], 0.0))
            m = (scores * decay).astype(BF)
            dh = jnp.where(lane_low, dp, zero) if j == 0 else jnp.where(lane_low, zero, dp)
            term = nn(m, dh)
            total = term if total is None else total + term
            dscores = dscores + nt(xp, dh) * decay
        dx_list.append(total)
    dx_in = jnp.concatenate(dx_list, axis=1)
    dscores = jnp.where(upper, dscores, 0.0)
    db = nn(dscores.astype(BF), cb)
    dc = nn(dscores.T.astype(BF), bb)

    entering = ent_ref[0]
    dleaving = dstate[...]
    dleaving_b = dleaving.astype(BF)
    ea = jnp.exp(a_x)
    a_last = a_x[length - 1 : length, :]
    ea_last = jnp.exp(a_last)
    w = jnp.exp(a_last - a_x)
    dxw = nn(bb, dleaving_b) * w
    db = db + nt((x * w).astype(BF), dleaving_b)
    eady = (ea * dyf).astype(BF)
    dc = dc + nt(eady, entering.astype(BF))
    dstate[...] = ea_last * dleaving + nn(bc[:, half:].T.astype(BF), eady)
    dx = dx_in + dxw
    u = x * dxw
    last_add = jnp.sum(u, axis=0, keepdims=True) + ea_last * jnp.sum(
        entering * dleaving, axis=0, keepdims=True
    )
    da_x = dyf * (y - skip * v) - xb.astype(F32) * dx_in - u
    row_index = lax.broadcasted_iota(jnp.int32, (length, inner), 0)
    da_x = da_x + jnp.where(row_index == length - 1, last_add, 0.0)
    pick = pick_ref[...]
    da = sum_lanes(da_x, pick)
    dr = sum_rows(jnp.where(upper, 1.0, 0.0).astype(BF), da)
    ddt = sum_lanes(dx * v, pick) + dr * rate
    dz = ddt * (1.0 / (1.0 + jnp.exp(-z)))
    ddtb = dz.astype(BF)
    ddt_ref[...] = ddtb
    gdt_ref[0:1, :] += jnp.sum(dz, axis=0, keepdims=True)
    gdt_ref[1:2, :] += jnp.sum(dr * dt * rate, axis=0, keepdims=True)

    dpre_v = (skip * dy + dt_x * dx) * (sig_v * (1.0 + pre_v * (1.0 - sig_v)))
    dvpad[0:length, :] = dpre_v
    dval = jnp.zeros((length, inner), F32)
    for k in range(4):
        dval = dval + cv_ref[k : k + 1, :] * dvpad[pl.ds(3 - k, length), :]
        gvec_ref[k : k + 1, :] += jnp.sum(
            dpre_v * vpad[pl.ds(5 + k, length), :], axis=0, keepdims=True
        )
    gvec_ref[4:5, :] += jnp.sum(dpre_v, axis=0, keepdims=True)
    gvec_ref[5:6, :] += jnp.sum(gated * dm, axis=0, keepdims=True)
    gvec_ref[6:7, :] += jnp.sum(dy * v, axis=0, keepdims=True)
    dvalb = dval.astype(BF)
    dval_ref[...] = dvalb

    dbc = jnp.concatenate([db, dc], axis=1)
    dpre_s = dbc * (sig_s * (1.0 + pre_s * (1.0 - sig_s)))
    dspad[0:length, :] = dpre_s
    dst = jnp.zeros((length, bc_width), F32)
    for k in range(4):
        dst = dst + cs_ref[k : k + 1, :] * dspad[pl.ds(3 - k, length), :]
        gst_ref[k : k + 1, :] += jnp.sum(
            dpre_s * spad[pl.ds(5 + k, length), :], axis=0, keepdims=True
        )
    gst_ref[4:5, :] += jnp.sum(dpre_s, axis=0, keepdims=True)
    dstb = dst.astype(BF)
    dst_ref[...] = dstb
    dpart = nt(dgate, wz_ref[...]) + nt(dvalb, wx_ref[...])
    dpart = dpart + nt(dstb, wbc_ref[...]) + nt(ddtb, wdt_ref[...])
    dpart_ref[...] = dpart.astype(BF)


def backward_mix(gb, ready, e_rows, kept, packed, params, pick, l):
    gate, val, st, dt, y, ent = kept
    tokens, width = gb.shape[0], packed.shape[0]
    inner = params[0].shape[2]
    bc_width = params[1].shape[2]
    dt_width = 128
    packed_width = packed.shape[1]
    half = bc_width // 2
    q = GROUP
    blocks = tokens // q
    back = lambda i: blocks - 1 - i
    tok = lambda n: pl.BlockSpec((q, n), lambda i: (back(i), 0))
    halo = lambda n: pl.BlockSpec(
        (8, n), lambda i: (jnp.maximum(back(i) * (q // 8) - 1, 0), 0)
    )
    fixed = lambda r, c: pl.BlockSpec((r, c), lambda i: (0, 0))
    outs = [
        ((tokens, packed_width), BF, tok(packed_width)),
        ((tokens, width), BF, tok(width)),
        ((8, inner), F32, fixed(8, inner)),
        ((8, bc_width), F32, fixed(8, bc_width)),
        ((8, dt_width), F32, fixed(8, dt_width)),
    ]
    return pl.pallas_call(
        functools.partial(bwd_kernel, ready),
        grid=(blocks,),
        in_specs=[
            tok(gb.shape[1]),
            pl.BlockSpec((8, q), lambda i: (0, back(i))),
            tok(inner), tok(inner), halo(inner), tok(bc_width), halo(bc_width), tok(dt_width),
            tok(inner),
            pl.BlockSpec((1, half, inner), lambda i: (back(i), 0, 0)),
        ]
        + [whole(packed.shape)] + layer_specs(params, l) + [whole(pick.shape)],
        out_specs=[o[2] for o in outs],
        out_shape=[jax.ShapeDtypeStruct(o[0], o[1]) for o in outs],
        scratch_shapes=[
            pltpu.VMEM((half, inner), F32),
            pltpu.VMEM((q + 8, inner), F32),
            pltpu.VMEM((q + 8, bc_width), F32),
            pltpu.VMEM((q + 8, inner), F32),
            pltpu.VMEM((q + 8, bc_width), F32),
        ],
        compiler_params=pltpu.CompilerParams(
            dimension_semantics=("arbitrary",), vmem_limit_bytes=60 * MIB
        ),
        name="mix_backward",
    )(gb, e_rows, gate, val, val, st, st, dt, y, ent, packed, *params, pick)


class Step:
    def __init__(self, **given):
        self.rows = 0
        self.width = 0
        self.line = 4
        self.chunks = 8
        self.hop = 1
        self.pass_hop = 1
        self.slack = 0
        self.partial = False
        self.gather = False
        self.late = False
        self.scale = False
        self.inner = False
        self.weights = 0
        self.grads = 0
        self.tail = 2
        self.lag = 1
        self.states = 0
        self.sums = False
        self.bits = 0
        self.middle = None
        self.__dict__.update(given)


def remote(src, dst, send, recv, device):
    return pltpu.make_async_remote_copy(
        src_ref=src, dst_ref=dst, send_sem=send, recv_sem=recv,
        device_id=device, device_id_type=pl.DeviceIdType.MESH,
    )


def when(condition):
    return pl.when(condition)


def comm_kernel(o, names, *refs):
    r = types.SimpleNamespace(**dict(zip(names, refs)))
    r.gbuf = [v for k, v in zip(names, refs) if k.startswith("gbuf")]
    n, count, rows = o.line, o.chunks, o.rows
    size = rows // count
    t = lax.axis_index("tensor")
    me = lax.axis_index("dp")
    own_bits = [(me // (1 << b)) % 2 for b in range(o.bits)]
    partner = [me + (1 - 2 * own_bits[b]) * (1 << b) for b in range(o.bits)]

    barrier = pltpu.get_barrier_semaphore()
    for k in range(1, n):
        pl.semaphore_signal(
            barrier, inc=1, device_id={"tensor": lax.rem(t + k, n)},
            device_id_type=pl.DeviceIdType.MESH,
        )
    over_dp = o.weights or o.grads
    r.early = [v for k, v in zip(names, refs) if k.startswith("esum")]
    r.lined = [v for k, v in zip(names, refs) if k.startswith("lsum")]
    r.gains = [v for k, v in zip(names, refs) if k.startswith("gsum")]
    if over_dp:
        for b in range(o.bits):
            pl.semaphore_signal(
                barrier, inc=1, device_id={"dp": partner[b]}, device_id_type=pl.DeviceIdType.MESH
            )
    pl.semaphore_wait(barrier, n - 1 + (o.bits if over_dp else 0))

    def at(s, c):
        return pl.ds(pl.multiple_of(s * rows + c * size, size), size)

    def piece(c):
        return pl.ds(pl.multiple_of(c * size, size), size)

    def hop(side, s, c, src):
        buf = r.rbuf if side == 0 else r.lbuf
        return remote(
            src, buf.at[s, piece(c)], r.rs_send.at[side, s], r.rs_recv.at[side, s, c],
            {"tensor": t + 1 if side == 0 else t - 1},
        )

    def reduce_items(side, c):
        buf = r.rbuf if side == 0 else r.lbuf
        edge = t == 0 if side == 0 else t == n - 1
        order = range(n - 1, 0, -1) if side == 0 else range(0, n - 1)
        for s in order:
            further = s > t if side == 0 else s < t

            @when(further & edge)
            def _():
                hop(side, s, c, r.part.at[at(s, c)]).start()

            @when(further & jnp.logical_not(edge))
            def _():
                hop(side, s, c, buf.at[s, piece(c)]).wait_recv()
                total = buf[s, piece(c), :].astype(F32) + r.part[at(s, c), :].astype(F32)
                buf[s, piece(c), :] = total.astype(BF)
                hop(side, s, c, buf.at[s, piece(c)]).start()

    def own_total(c):
        acc = r.acc
        acc[...] = r.part[at(t, c), :].astype(F32)

        @when(t > 0)
        def _():
            hop(0, t, c, r.rbuf.at[t, piece(c)]).wait_recv()
            acc[...] += r.rbuf[t, piece(c), :].astype(F32)

        @when(t < n - 1)
        def _():
            hop(1, t, c, r.lbuf.at[t, piece(c)]).wait_recv()
            acc[...] += r.lbuf[t, piece(c), :].astype(F32)

    def pass_on(side, s, c):
        spot = r.full.at[at(s, c)]
        return remote(
            spot, spot, r.ag_send.at[side, s], r.ag_recv.at[side, s, c],
            {"tensor": t + 1 if side == 0 else t - 1},
        )

    def forward_items(side, tau):
        order = range(n - 2, -1, -1) if side == 0 else range(1, n)
        for s in order:
            away = t - s if side == 0 else s - t
            late = o.hop * max(s, n - 1 - s) + o.slack if o.late else 0
            c = tau - late - o.pass_hop * away

            @when((away > 0) & (c >= 0) & (c < count))
            def _():
                pass_on(side, s, c).wait_recv()

                @when(t < n - 1 if side == 0 else t > 0)
                def _():
                    pass_on(side, s, c).start()

    def spot_of(k, ref):
        return ref.at[:, pl.ds(pl.multiple_of(k * rows, rows), rows)]

    def square_copy(k):
        dest = lax.rem(t + k, n)
        return remote(
            spot_of(dest, r.ssq), r.sqbuf.at[k - 1], r.sq_send.at[k - 1],
            r.sq_recv.at[k - 1], {"tensor": dest},
        )

    def inner_copy(k):
        return remote(
            spot_of(t, r.inner), spot_of(t, r.inner), r.in_send.at[k - 1],
            r.in_recv.at[k - 1], {"tensor": lax.rem(t + k, n)},
        )

    def inner_arrival(k):
        source = lax.rem(t + n - k, n)
        return remote(
            spot_of(source, r.inner), spot_of(source, r.inner), r.in_send.at[k - 1],
            r.in_recv.at[k - 1], {"tensor": source},
        )

    def bit_order(parity):
        high = list(range(o.bits - 1, 0, -1))
        if parity == 1:
            high = high[1:] + high[:1]
        return high + [0]

    def cols(j):
        return pl.ds(pl.multiple_of(j * WCHUNK, WCHUNK), WCHUNK)

    def spots(known):
        return tuple(slice(None) if b in known else own_bits[b] for b in range(o.bits - 1, -1, -1))

    def weight_copy(parity, stage, j):
        order = bit_order(parity)
        depth = r.wown.shape[0] // o.weights
        strip = pl.ds(pl.multiple_of(j * depth, depth), depth)
        spot = r.wfull.at[(*spots(order[:stage]), strip)]
        src = r.wown.at[strip] if stage == 0 else spot
        return remote(
            src, spot, r.wg_send.at[stage, j], r.wg_recv.at[stage, j],
            {"dp": partner[order[stage]]},
        )

    def own_weights():
        return pltpu.make_async_copy(r.wown, r.wfull.at[spots([])], r.wl_sem)

    def each_parity(pair, fn):
        for parity in range(2):
            j = 2 * pair + parity

            @when((j >= 0) & (j < o.weights))
            def _():
                fn(parity, j)

    def weight_items(tau):
        for stage in range(o.bits + 1):
            def run(parity, j):
                if stage > 0:
                    weight_copy(parity, stage - 1, j).wait_recv()
                if stage < o.bits:
                    weight_copy(parity, stage, j).start()
            each_parity(tau - stage, run)

    def grad_order(parity):
        high = list(range(1, o.bits))
        if parity == 1:
            high = high[1:] + high[:1]
        return [0] + high

    def grad_spot(parity, stage, mine):
        order = grad_order(parity)
        done, bit = order[:stage], order[stage]
        spot = []
        for b in range(o.bits - 1, -1, -1):
            if b in done:
                spot.append(own_bits[b])
            elif b == bit:
                spot.append(own_bits[b] if mine else 1 - own_bits[b])
            else:
                spot.append(slice(None))
        return tuple(spot)

    def grad_copy(parity, stage, j):
        order = grad_order(parity)
        return remote(
            r.grad.at[(j, *grad_spot(parity, stage, False))], r.gbuf[stage].at[j],
            r.gr_send.at[stage, j], r.gr_recv.at[stage, j],
            {"dp": partner[order[stage]]},
        )

    def product(j):
        slab = o.width // 2
        inner_shape = (2,) * (o.bits - 1) + (slab >> (o.bits - 1), WCHUNK)

        def slabs(left):
            for i in range(2):
                out = tn(left[:, pl.ds(i * slab, slab)], r.right[:, cols(j)])
                r.grad[j, i] = out.astype(BF).reshape(inner_shape)

        @when(j < o.grads - o.tail)
        def _():
            slabs(r.lrows)

        @when(j >= o.grads - o.tail)
        def _():
            slabs(r.lgrad)

    def each_chunk(j, fn):
        for parity in range(2):
            @when((j >= 0) & (j < o.grads) & (lax.rem(j, 2) == parity))
            def _():
                fn(parity, j)

    def grad_items(tau):
        @when(tau < o.grads)
        def _():
            product(tau)

        def first(parity, j):
            grad_copy(parity, 0, j).start()

        each_chunk(tau, first)
        for stage in range(1, o.bits + 1):
            def run(parity, j):
                grad_copy(parity, stage - 1, j).wait_recv()
                spot = grad_spot(parity, stage - 1, True)
                free = [i for i, v in enumerate(spot) if isinstance(v, slice)]
                buf = r.gbuf[stage - 1]
                for combo in range(1 << len(free)):
                    pick = [(combo >> i) % 2 for i in range(len(free))]
                    full = list(spot)
                    for i, v in zip(free, pick):
                        full[i] = v
                    total = r.grad[(j, *full)].astype(F32) + buf[(j, *pick)].astype(F32)
                    if stage < o.bits:
                        r.grad[(j, *full)] = total.astype(BF)
                    else:
                        r.gout[:, cols(j)] = total
                if stage < o.bits:
                    grad_copy(parity, stage, j).start()
            each_chunk(tau - grad_lag(stage), run)

    def grad_lag(stage):
        return o.lag * (2 * stage - 1) if stage else 0

    def share(buf, send, recv, k):
        return remote(buf.at[t], buf.at[t], send.at[k - 1], recv.at[k - 1],
                      {"tensor": lax.rem(t + k, n)})

    def shared(buf, send, recv):
        for k in range(1, n):
            source = lax.rem(t + n - k, n)
            remote(buf.at[source], buf.at[source], send.at[k - 1], recv.at[k - 1],
                   {"tensor": source}).wait_recv()

    def line_total(buf):
        total = buf[0]
        for k in range(1, n):
            total = total + buf[k]
        return total

    def double(acc, buf, send, recv, b):
        return remote(acc.at[b], buf.at[b], send.at[b], recv.at[b], {"dp": partner[b]})

    def doubled(acc, buf, send, recv, b):
        double(acc, buf, send, recv, b).wait_recv()
        acc[b + 1] = acc[b] + buf[b]

    def lanes(index, ref):
        return slice(index * ref.shape[1], (index + 1) * ref.shape[1])

    line_groups, dp_groups = [], []
    if o.sums:
        line_groups = [(r.lbank, r.lb_send, r.lb_recv)]
        dp_groups = [(r.dbank, r.dbuf, r.db_send, r.db_recv)]
        if r.gains:
            line_groups.append((r.gbank, r.gb_send, r.gb_recv))
            dp_groups.append((r.hbank, r.hbuf, r.hb_send, r.hb_recv))

    def sum_items(tau):
        @when(tau == 2)
        def _():
            for g in line_groups:
                shared(*g)
            off = 0
            for v in r.early:
                r.dbank[0, :, off : off + v.shape[1]] = v[...]
                off += v.shape[1]
            r.dbank[0, :, off:] = line_total(r.lbank)
            if r.gains:
                r.hbank[0] = line_total(r.gbank)
            for g in dp_groups:
                double(*g, 0).start()

        for b in range(o.bits):
            @when(tau == 4 + b)
            def _():
                for g in dp_groups:
                    doubled(*g, b)
                    if b < o.bits - 1:
                        double(*g, b + 1).start()

    def state_items(tau):
        at_first = grad_lag(o.bits) + 1
        quarter = r.gout.shape[0] // n

        @when(tau == at_first)
        def _():
            for s in range(n):
                r.qsend[s] = r.gout[s * quarter : (s + 1) * quarter, 0 : o.states].astype(BF)
            for k in range(1, n):
                state_out(k).start()

        @when(tau == at_first + 2)
        def _():
            total = r.qsend[t].astype(F32)
            for k in range(1, n):
                state_out(k).wait_recv()
                total = total + r.qbuf[k - 1].astype(F32)
            r.qall[t] = total.astype(BF)
            for k in range(1, n):
                share(r.qall, r.qa_send, r.qa_recv, k).start()

    def state_out(k):
        dest = lax.rem(t + k, n)
        return remote(r.qsend.at[dest], r.qbuf.at[k - 1], r.qs_send.at[k - 1],
                      r.qs_recv.at[k - 1], {"tensor": dest})

    if o.sums:
        off = 0
        for v in r.lined:
            r.lbank[t, :, off : off + v.shape[1]] = v[...]
            off += v.shape[1]
        for i, v in enumerate(r.gains):
            r.gbank[t, :, lanes(i, v)] = v[0:1, :]
        for g in line_groups:
            for k in range(1, n):
                share(*g, k).start()
    if o.scale:
        for k in range(1, n):
            square_copy(k).start()
    if o.weights:
        own_weights().start()
    if o.scale:
        total = spot_of(t, r.ssq)[...]
        for k in range(1, n):
            square_copy(k).wait_recv()
            total = total + r.sqbuf[k - 1]
        scale = lax.rsqrt(total / (o.scale * 1.0) + EPSILON)
        r.r2[...] = jnp.broadcast_to(scale.T[:, 0:1], (rows, 128))
    if o.gather and not o.late:
        r.full[pl.ds(pl.multiple_of(t * rows, rows), rows), :] = o.payload(r)
    if o.middle is not None:
        o.middle(r, None, None)

    ends = [count + o.hop * (n - 1) + o.slack]
    if o.late:
        ends.append(ends[0] + o.pass_hop * (n - 1))
    elif o.gather:
        ends.append(count + o.pass_hop * (n - 1))
    if o.weights:
        ends.append((o.weights + 1) // 2 + o.bits)
    if o.grads:
        ends.append(o.grads + grad_lag(o.bits))
        ends.append(grad_lag(o.bits) + 4)
    if o.sums:
        ends.append(4 + o.bits)

    def iteration(tau, _):
        if o.partial:
            for side in range(2):
                c = tau - o.hop * (t if side == 0 else n - 1 - t)

                @when((c >= 0) & (c < count))
                def _():
                    reduce_items(side, c)

            c_own = tau - o.hop * jnp.maximum(t, n - 1 - t) - o.slack

            @when((c_own >= 0) & (c_own < count))
            def _():
                own_total(c_own)
                out = o.middle(r, piece(c_own), r.acc[...])
                if o.late:
                    r.full[at(t, c_own), :] = out
        if o.gather:
            c_out = tau - o.hop * jnp.maximum(t, n - 1 - t) - o.slack if o.late else tau

            @when((c_out >= 0) & (c_out < count))
            def _():
                @when(t < n - 1)
                def _():
                    pass_on(0, t, c_out).start()

                @when(t > 0)
                def _():
                    pass_on(1, t, c_out).start()

            for side in range(2):
                forward_items(side, tau)
        if o.weights:
            @when(tau == 1)
            def _():
                own_weights().wait()
            weight_items(tau)
        if o.grads:
            grad_items(tau)
            state_items(tau)
        if o.sums:
            sum_items(tau)
        return 0

    lax.fori_loop(0, max(ends), iteration, 0)

    if o.sums:
        r.jbank[t] = r.ggain[0:1, :]
        for k in range(1, n):
            share(r.jbank, r.jb_send, r.jb_recv, k).start()
    if o.inner:
        spot_of(t, r.inner)[...] = r.icol[...].T[0:8, :]
        for k in range(1, n):
            inner_copy(k).start()
        for k in range(1, n):
            inner_arrival(k).wait_recv()
        for k in range(1, n):
            inner_copy(k).wait_send()
    if o.sums:
        last = (r.kbank, r.kbuf, r.kb_send, r.kb_recv)
        shared(r.jbank, r.jb_send, r.jb_recv)
        r.kbank[0] = line_total(r.jbank)
        for b in range(o.bits):
            double(*last, b).start()
            doubled(*last, b)
        r.sums[...] = r.dbank[o.bits]
        r.gain_sums[0:1, :] = r.kbank[o.bits]
        for i, v in enumerate(r.gains):
            r.gain_sums[i + 1 : i + 2, :] = r.hbank[o.bits, :, lanes(i, v)]
        for g in line_groups + [(r.jbank, r.jb_send, r.jb_recv)]:
            for k in range(1, n):
                share(*g, k).wait_send()
        for g in dp_groups + [last]:
            for b in range(o.bits):
                double(*g, b).wait_send()
    if o.grads:
        shared(r.qall, r.qa_send, r.qa_recv)
        quarter = r.gout.shape[0] // n
        for s in range(n):
            r.gout[s * quarter : (s + 1) * quarter, 0 : o.states] = r.qall[s].astype(F32)
        for k in range(1, n):
            state_out(k).wait_send()
            share(r.qall, r.qa_send, r.qa_recv, k).wait_send()
    if o.scale:
        for k in range(1, n):
            square_copy(k).wait_send()
    for s in range(n):
        for side in range(2):
            inside = t < n - 1 if side == 0 else t > 0
            if o.partial:
                @when((s > t if side == 0 else s < t) & inside)
                def _():
                    buf = (r.rbuf if side == 0 else r.lbuf).at[s]
                    remote(
                        buf, buf, r.rs_send.at[side, s], r.rs_recv.at[side, s, 0],
                        {"tensor": t + 1 if side == 0 else t - 1},
                    ).wait_send()
            if o.gather:
                @when((s <= t if side == 0 else s >= t) & inside)
                def _():
                    spot = r.full.at[pl.ds(s * rows, rows)]
                    remote(
                        spot, spot, r.ag_send.at[side, s], r.ag_recv.at[side, s, 0],
                        {"tensor": t + 1 if side == 0 else t - 1},
                    ).wait_send()
    for j in range(o.weights):
        for stage in range(o.bits):
            weight_copy(j % 2, stage, jnp.int32(j)).wait_send()
    for j in range(o.grads):
        for stage in range(o.bits):
            grad_copy(j % 2, stage, jnp.int32(j)).wait_send()


def comm_call(o, name, collective, inputs, outputs, **scratch):
    n, count, rows, width = o.line, o.chunks, o.rows, o.width
    dma = pltpu.SemaphoreType.DMA
    if o.partial:
        scratch.update(
            rbuf=pltpu.VMEM((n, rows, width), BF),
            lbuf=pltpu.VMEM((n, rows, width), BF),
            acc=pltpu.VMEM((rows // count, width), F32),
            rs_send=dma((2, n)),
            rs_recv=dma((2, n, count)),
        )
    if o.gather:
        scratch.update(ag_send=dma((2, n)), ag_recv=dma((2, n, count)))
    if o.scale:
        scratch.update(
            sqbuf=pltpu.VMEM((n - 1, 8, rows), F32), sq_send=dma((n - 1,)), sq_recv=dma((n - 1,))
        )
    if o.inner:
        scratch.update(
            icol=pltpu.VMEM((rows, 128), F32), in_send=dma((n - 1,)), in_recv=dma((n - 1,))
        )
    if o.weights:
        scratch.update(
            wl_sem=dma(()),
            wg_send=dma((o.bits, o.weights)),
            wg_recv=dma((o.bits, o.weights)),
        )
    if o.grads:
        depth = o.width >> o.bits
        scratch.update(
            grad=pltpu.VMEM((o.grads, *(2,) * o.bits, depth, WCHUNK), BF),
            gr_send=dma((o.bits, o.grads)),
            gr_recv=dma((o.bits, o.grads)),
        )
        for stage in range(o.bits):
            scratch["gbuf%d" % stage] = pltpu.VMEM(
                (o.grads, *(2,) * (o.bits - 1 - stage), depth, WCHUNK), BF
            )
        part = (n, (width >> o.bits) // n, o.states)
        scratch.update(
            qsend=pltpu.VMEM(part, BF), qall=pltpu.VMEM(part, BF),
            qbuf=pltpu.VMEM((n - 1,) + part[1:], BF),
            qs_send=dma((n - 1,)), qs_recv=dma((n - 1,)),
            qa_send=dma((n - 1,)), qa_recv=dma((n - 1,)),
        )
    if o.sums:
        def lanes_of(start):
            return sum(v[0].shape[1] for k, v in inputs.items() if k.startswith(start))

        lined, early, gains = lanes_of("lsum"), lanes_of("esum"), lanes_of("gsum")
        for name_of, tall, line_width, dp_width in (
            ("lb db", 8, lined, lined + early), ("gb hb", 1, gains, gains), ("jb kb", 1, width, width)
        ):
            if line_width:
                one, two = name_of.split()
                scratch[one + "ank"] = pltpu.VMEM((n, tall, line_width), F32)
                scratch[two + "ank"] = pltpu.VMEM((o.bits + 1, tall, dp_width), F32)
                scratch[two + "uf"] = pltpu.VMEM((o.bits, tall, dp_width), F32)
                for key, size in ((one, n - 1), (two, o.bits)):
                    scratch[key + "_send"] = dma((size,))
                    scratch[key + "_recv"] = dma((size,))
    names = [*inputs, *outputs, *scratch]
    out = pl.pallas_call(
        functools.partial(comm_kernel, o, names),
        in_specs=[pl.BlockSpec(memory_space=i[1]) for i in inputs.values()],
        out_specs=[pl.BlockSpec(memory_space=i[2]) for i in outputs.values()],
        out_shape=[jax.ShapeDtypeStruct(i[0], i[1]) for i in outputs.values()],
        scratch_shapes=list(scratch.values()),
        compiler_params=pltpu.CompilerParams(
            collective_id=collective, has_side_effects=True, vmem_limit_bytes=62 * MIB
        ),
        name=name,
    )(*[i[0] for i in inputs.values()])
    return dict(zip(outputs, out))


def meet_kernel(n, inner_all, own_ref, out_ref, bank, send, recv):
    t = lax.axis_index("tensor")
    barrier = pltpu.get_barrier_semaphore()
    for k in range(1, n):
        pl.semaphore_signal(
            barrier, inc=1, device_id={"tensor": lax.rem(t + k, n)},
            device_id_type=pl.DeviceIdType.MESH,
        )
    pl.semaphore_wait(barrier, n - 1)
    copies = [
        remote(own_ref, bank.at[t], send.at[k - 1], recv.at[k - 1], {"tensor": lax.rem(t + k, n)})
        for k in range(1, n)
    ]
    for copy in copies:
        copy.start()
    bank[t] = own_ref[...]
    for k in range(1, n):
        source = lax.rem(t + n - k, n)
        remote(
            own_ref, bank.at[source], send.at[k - 1], recv.at[k - 1], {"tensor": source}
        ).wait_recv()
    total = bank[0]
    for s in range(1, n):
        total = total + bank[s]
    scale = lax.rsqrt(total[0:1, :] / inner_all + EPSILON)
    row = lax.broadcasted_iota(jnp.int32, total.shape, 0)
    e = scale * scale * scale * (total[1:2, :] / inner_all)
    out_ref[...] = jnp.where(row == 0, e, scale)
    for copy in copies:
        copy.wait_send()


def meet(own, n, inner_all, collective):
    vmem = pl.BlockSpec(memory_space=pltpu.VMEM)
    dma = pltpu.SemaphoreType.DMA
    return pl.pallas_call(
        functools.partial(meet_kernel, n, inner_all),
        in_specs=[vmem],
        out_specs=vmem,
        out_shape=jax.ShapeDtypeStruct(own.shape, F32),
        scratch_shapes=[pltpu.VMEM((n,) + own.shape, F32), dma((n - 1,)), dma((n - 1,))],
        compiler_params=pltpu.CompilerParams(collective_id=collective, has_side_effects=True),
        name="turn_around",
    )(own)


def plain_payload(r):
    return r.own[...]


def token_columns(first, second):
    lane = lax.broadcasted_iota(jnp.int32, (first.shape[0], 128), 1)
    return jnp.where(lane == 0, first, second)


def forward_middle(r, at, total):
    if at is None:
        return None
    branch = total * r.r2[at, 0:1]
    residual = r.res[at, :].astype(F32) + branch
    r.branch[at, :] = branch
    r.res_out[at, :] = residual
    r1 = lax.rsqrt(jnp.mean(residual * residual, axis=1, keepdims=True) + EPSILON)
    return (residual * r1 * r.gain[...]).astype(BF)


def backward_middle(inner_all, r, at, total):
    if at is None:
        r.ggain[...] = jnp.zeros_like(r.ggain)
        return None
    res = r.res[at, :].astype(F32)
    width = res.shape[1]
    r1 = lax.rsqrt(jnp.mean(res * res, axis=1, keepdims=True) + EPSILON)
    hat = res * r1
    r.ggain[0:1, :] += jnp.sum(hat * total, axis=0, keepdims=True)
    dn = total * r.gain[...]
    cross = jnp.sum(dn * hat, axis=1, keepdims=True) / width
    grad = r.grad_in[at, :].astype(F32) + r1 * (dn - hat * cross)
    r.grad_out[at, :] = grad
    if inner_all is None:
        return None
    r2 = r.r2[at, 0:1]
    dot = jnp.sum(grad.astype(BF).astype(F32) * r.branch[at, :], axis=1, keepdims=True)
    r.icol[at, :] = token_columns(r2 * r2 * dot / inner_all, r2)
    return grad.astype(BF)


def pad_to(v, rows, columns):
    return jnp.pad(v, ((0, rows - v.shape[0]), (0, columns - v.shape[1])))


def rows_of(v):
    return v.astype(F32).reshape(-1, v.shape[-1])


def shards(
    hidden_in,
    out_grad,
    norm_gain,
    proj_z,
    proj_x,
    proj_bc,
    proj_dt,
    conv_value,
    conv_value_bias,
    conv_state,
    conv_state_bias,
    step_bias,
    log_decay,
    skip_gain,
    gate_gain,
    proj_out,
):
    tensor_count = lax.axis_size("tensor")
    dp_count = lax.axis_size("dp")
    bits = dp_count.bit_length() - 1
    layers, shard_rows, inner = proj_z.shape
    rows_own, width = hidden_in.shape
    tokens = rows_own * tensor_count
    heads = step_bias.shape[1]
    bc_width = proj_bc.shape[2]
    inner_all = inner * tensor_count
    packed_width = bc_width + 128 + 3 * inner
    column_chunks, row_chunks = packed_width // WCHUNK, shard_rows // 16
    vmem, far = pltpu.VMEM, pl.ANY

    small = jnp.concatenate([conv_state.reshape(layers, -1), conv_state_bias], axis=1)
    small = jnp.pad(small, ((0, 0), (0, shard_rows - small.shape[1])))
    extra = jnp.stack([norm_gain, small], axis=1).reshape(2 * layers, shard_rows).T
    packs = []
    for l in range(layers):
        packs.append(
            jnp.concatenate(
                [
                    proj_bc[l],
                    proj_dt[l],
                    extra,
                    jnp.zeros((shard_rows, 128 - heads - 2 * layers), BF),
                    proj_z[l],
                    proj_x[l],
                    proj_out[l].T,
                ],
                axis=1,
            )
        )
    full_shape = ((2,) * bits) + (shard_rows, packed_width)
    common = dict(rows=rows_own, width=width, line=tensor_count, bits=bits)

    def weight_io(l):
        return dict(wown=(packs[l], vmem)), dict(wfull=(full_shape, BF, far))

    vec = jnp.concatenate(
        [
            conv_value,
            conv_value_bias[:, None],
            jnp.repeat(skip_gain, WIDTH, axis=1)[:, None],
            gate_gain[:, None],
        ],
        axis=1,
    ).astype(F32)
    tiny = jnp.stack([step_bias.astype(F32), -jnp.exp(log_decay.astype(F32))], axis=1)
    tiny = jnp.pad(tiny, ((0, 0), (0, 0), (0, 128 - heads)))
    pick = (jnp.arange(inner)[:, None] // WIDTH == jnp.arange(128)[None, :]).astype(BF)

    whole_rows, own_rows = ((tokens, width), BF, vmem), ((rows_own, width), F32, vmem)
    win, wout = weight_io(0)
    got = comm_call(
        Step(gather=True, payload=plain_payload, weights=row_chunks, **common),
        "gather_first", 1,
        dict(own=(hidden_in, vmem), **win),
        dict(full=whole_rows, **wout),
    )
    x_rows = got["full"]
    out_grad, x_rows = lax.optimization_barrier((out_grad, x_rows))
    grad_rows = lax.all_gather(out_grad, "tensor", axis=0, tiled=True)
    packed = [got["wfull"].reshape(width, packed_width)]
    start = bc_width + heads
    extra_all = packed[0][:, start : start + 2 * layers].astype(F32)
    gain_rows = extra_all[:, 0 : 2 * layers : 2].T[:, None, :]
    per = bc_width // dp_count
    smalls = extra_all[:, 1 : 2 * layers : 2].reshape(dp_count, shard_rows, layers)
    smalls = smalls[:, : 5 * per].reshape(dp_count, 5, per, layers)
    cst = jnp.transpose(smalls, (3, 1, 0, 2)).reshape(layers, 5, bc_width)
    params = (vec, cst, tiny)

    out = forward_mix(x_rows, packed[0], params + (gain_rows,), 0)
    saved, rows = [out[:6]], [out[8]]
    residuals, branches, r2s = [hidden_in], [], []
    for l in range(layers - 1):
        win, wout = weight_io(l + 1)
        got = comm_call(
            Step(
                partial=True, gather=True, late=True, scale=inner_all, middle=forward_middle,
                weights=row_chunks, **common,
            ),
            "between_forward", 2 + l,
            dict(part=(out[6], vmem), ssq=(out[7], vmem), res=(residuals[l], vmem),
                 gain=(gain_rows[l + 1], vmem), **win),
            dict(full=whole_rows, branch=own_rows, res_out=own_rows,
                 r2=((rows_own, 128), F32, vmem), **wout),
        )
        rows.append(got["full"])
        branches.append(got["branch"])
        residuals.append(got["res_out"])
        r2s.append(got["r2"])
        packed.append(got["wfull"].reshape(width, packed_width))
        gb = grad_rows if l + 1 == layers - 1 else None
        out = forward_mix(rows[-1], packed[-1], params + (gain_rows,), l + 1, gb)
        saved.append(out[:6])
    total = lax.psum_scatter(out[6], "tensor", scatter_dimension=0, tiled=True)
    token_rows = meet(out[7], tensor_count, inner_all, 16)
    r2_own = lax.dynamic_slice_in_dim(
        token_rows[1], lax.axis_index("tensor") * rows_own, rows_own, 0
    )
    hidden_out = residuals[-1].astype(F32) + r2_own[:, None] * total.astype(F32)
    product = out[8]
    gradient = out_grad
    scattered, summed, gain_grads = [None] * layers, [None] * layers, [None] * layers
    for l in reversed(range(layers)):
        last = l == layers - 1
        dcat, dpart, *small_grads = backward_mix(
            product if last else grad_rows, last, token_rows, saved[l], packed[l], params, pick, l
        )
        summed[l] = small_grads
        more = l > 0
        inputs = dict(
            part=(dpart, vmem), res=(residuals[l], vmem), gain=(gain_rows[l], vmem),
            grad_in=(gradient, vmem), lrows=(rows[l], vmem), lgrad=(grad_rows, vmem),
            right=(dcat, vmem),
        )
        outputs = dict(
            grad_out=own_rows, ggain=((8, width), F32, vmem),
            gout=((shard_rows, packed_width), F32, vmem),
        )
        if more:
            inputs.update(r2=(r2s[l - 1], vmem), branch=(branches[l - 1], vmem))
            outputs.update(full=whole_rows, inner=((8, tokens), F32, vmem))
        else:
            for i in range(layers):
                gvec, gst, gdt = summed[i]
                inputs["esum%d" % i], inputs["esum_%d" % i] = (gvec, vmem), (gdt, vmem)
                inputs["lsum%d" % i] = (gst, vmem)
            for i in range(1, layers):
                inputs["gsum%d" % i] = (gain_grads[i], vmem)
            early = sum(v.shape[1] for i in range(layers) for v in summed[i])
            outputs.update(
                sums=((8, early), F32, vmem), gain_sums=((8, width), F32, vmem)
            )
        got = comm_call(
            Step(
                partial=True, gather=more, late=more, inner=more, grads=column_chunks,
                states=bc_width, sums=not more,
                middle=functools.partial(backward_middle, inner_all if more else None), **common,
            ),
            "between_backward" if more else "last_backward", 17 + l, inputs, outputs,
        )
        gradient = got["grad_out"]
        scattered[l], gain_grads[l] = got["gout"], got["ggain"]
        if more:
            grad_rows, token_rows = got["full"], got["inner"]
    gout = jnp.stack(scattered)
    sums, ggain = got["sums"], got["gain_sums"][:layers]
    each = inner + 128
    gvec = jnp.stack([sums[:, i * each : i * each + inner] for i in range(layers)])
    gdt = jnp.stack([sums[:, i * each + inner : (i + 1) * each] for i in range(layers)])
    gst = jnp.stack(
        [sums[:, layers * each + i * bc_width :][:, :bc_width] for i in range(layers)]
    )
    own = lambda v, axis: lax.dynamic_slice_in_dim(
        v, lax.axis_index("dp") * (v.shape[axis] // dp_count), v.shape[axis] // dp_count, axis
    )
    gst = own(gst, 2)
    first = bc_width + 128
    return (
        hidden_out,
        gradient,
        own(ggain, 1),
        gout[:, :, first : first + inner],
        gout[:, :, first + inner : first + 2 * inner],
        gout[:, :, :bc_width],
        gout[:, :, bc_width : bc_width + heads],
        gvec[:, 0:4],
        gvec[:, 4],
        gst[:, 0:4],
        gst[:, 4],
        gdt[:, 0, :heads],
        gdt[:, 1, :heads],
        jnp.sum(gvec[:, 6].reshape(layers, heads, WIDTH), axis=2),
        gvec[:, 5],
        jnp.transpose(gout[:, :, first + 2 * inner :], (0, 2, 1)),
    )


def solution(mesh):
    placed = (
        P(("dp", "tensor"), None),
        P(("dp", "tensor"), None),
        P(None, "dp"),
        P(None, "dp", "tensor"),
        P(None, "dp", "tensor"),
        P(None, "dp", None),
        P(None, "dp", "tensor"),
        P(None, None, "tensor"),
        P(None, "tensor"),
        P(None, None, "dp"),
        P(None, "dp"),
        P(None, "tensor"),
        P(None, "tensor"),
        P(None, "tensor"),
        P(None, "tensor"),
        P(None, "tensor", "dp"),
    )
    return jax.shard_map(
        shards,
        mesh=mesh,
        in_specs=placed,
        out_specs=(
            P(("dp", "tensor"), None),
            P(("dp", "tensor"), None),
            P(None, "dp"),
            P(None, "dp", "tensor"),
            P(None, "dp", "tensor"),
            P(None, "dp", None),
            P(None, "dp", "tensor"),
            P(None, None, "tensor"),
            P(None, "tensor"),
            P(None, None, "dp"),
            P(None, "dp"),
            P(None, "tensor"),
            P(None, "tensor"),
            P(None, "tensor"),
            P(None, "tensor"),
            P(None, "tensor", "dp"),
        ),
        check_vma=False,
    )
```

```python
import functools
import types

import jax
import jax.numpy as jnp
from jax import lax
from jax.sharding import PartitionSpec as P
import jax.experimental.pallas as pl
import jax.experimental.pallas.tpu as pltpu

GROUP = 256
EPSILON = 1e-05
BF = jnp.bfloat16
F32 = jnp.float32
WIDTH = 64
MIB = 1024 * 1024
WCHUNK = 384


def nn(a, b):
    return lax.dot_general(a, b, (((1,), (0,)), ((), ())), preferred_element_type=F32)


def tn(a, b):
    return lax.dot_general(a, b, (((0,), (0,)), ((), ())), preferred_element_type=F32)


def nt(a, b):
    return lax.dot_general(a, b, (((1,), (1,)), ((), ())), preferred_element_type=F32)


def parts3(v):
    one = v.astype(BF)
    rest = v - one.astype(F32)
    two = rest.astype(BF)
    three = (rest - two.astype(F32)).astype(BF)
    return one, two, three


def sum_rows(select, v):
    one, two, three = parts3(v)
    return nn(select, one) + nn(select, two) + nn(select, three)


def sum_lanes(v, select):
    one = v.astype(BF)
    two = (v - one.astype(F32)).astype(BF)
    return nn(one, select) + nn(two, select)


def silu_parts(v):
    sig = 1.0 / (1.0 + jnp.exp(-v))
    return sig, v * sig


def softplus(v):
    return jnp.maximum(v, 0.0) + jnp.log1p(jnp.exp(-jnp.abs(v)))


def pair_spread(column_values, pair, lane_low):
    low = column_values[:, 2 * pair : 2 * pair + 1]
    high = column_values[:, 2 * pair + 1 : 2 * pair + 2]
    return jnp.where(lane_low, low, high)


def spread(column_values, pairs, lane_low):
    return jnp.concatenate([pair_spread(column_values, p, lane_low) for p in range(pairs)], axis=1)


def conv_pre(padded, taps, bias, length):
    count = 4
    total = bias
    for k in range(count):
        total = total + taps[k : k + 1, :] * padded[pl.ds(8 - (count - 1) + k, length), :]
    return total


def blocks_of(w_ref, inner, bc_width):
    sizes = (bc_width, 128, inner, inner, inner)
    starts = [sum(sizes[:i]) for i in range(5)]
    return [w_ref.at[:, pl.ds(s, z)] for s, z in zip(starts, sizes)]


def small_refs(vec_ref, cst_ref, tiny_ref):
    vec, cst, tiny = vec_ref.at[0], cst_ref.at[0], tiny_ref.at[0]
    return (
        vec.at[0:4], vec.at[4:5], vec.at[5:6], vec.at[6:7],
        cst.at[0:4], cst.at[4:5], tiny.at[0:1], tiny.at[1:2],
    )


def fwd_kernel(
    first, last, rows_ref, w_ref, vec_ref, cst_ref, tiny_ref, gain_ref, *rest,
):
    if last:
        gb_ref, *rest = rest
    gate_ref, val_ref, st_ref, dt_ref, y_ref, ent_ref, part_ref, ssq_ref, *rest = rest
    if first:
        normed_ref, *rest = rest
    if last:
        dm_ref, *rest = rest
    state, vpad, spad = rest[-3:]
    step = pl.program_id(0)
    length = rows_ref.shape[0]
    cv_ref, cvb_ref, skip_ref, gg_ref, cs_ref, csb_ref, sb_ref, rate_ref = small_refs(
        vec_ref, cst_ref, tiny_ref
    )
    inner = gg_ref.shape[1]
    pairs = inner // 128
    wbc_ref, wdt_ref, wz_ref, wx_ref, wot_ref = blocks_of(w_ref, inner, cs_ref.shape[1])

    @pl.when(step == 0)
    def _():
        state[...] = jnp.zeros_like(state)
        vpad[0:8, :] = jnp.zeros((8, inner), F32)
        spad[0:8, :] = jnp.zeros((8, spad.shape[1]), F32)

    @pl.when(step > 0)
    def _():
        vpad[0:8, :] = vpad[length : length + 8, :]
        spad[0:8, :] = spad[length : length + 8, :]

    rows = rows_ref[...]
    if first:
        rows = rows.astype(F32)
        r1 = lax.rsqrt(jnp.mean(rows * rows, axis=1, keepdims=True) + EPSILON)
        rows = (rows * r1 * gain_ref[0]).astype(BF)
        normed_ref[...] = rows
    gate_ref[...] = nn(rows, wz_ref[...])
    val = nn(rows, wx_ref[...])
    val_ref[...] = val
    vpad[8 : length + 8, :] = val
    st = nn(rows, wbc_ref[...])
    st_ref[...] = st
    spad[8 : length + 8, :] = st
    dt_in = nn(rows, wdt_ref[...])
    dt_ref[...] = dt_in

    _, v = silu_parts(conv_pre(vpad, cv_ref, cvb_ref[...], length))
    _, bc = silu_parts(conv_pre(spad, cs_ref, csb_ref[...], length))
    half = bc.shape[1] // 2
    bb = bc[:, :half].astype(BF)
    cb = bc[:, half:].astype(BF)
    dt = softplus(dt_in + sb_ref[...])
    q_index = lax.broadcasted_iota(jnp.int32, (length, length), 0)
    s_index = lax.broadcasted_iota(jnp.int32, (length, length), 1)
    causal = q_index >= s_index
    tril = jnp.where(causal, 1.0, 0.0).astype(BF)
    a = sum_rows(tril, dt * rate_ref[...])
    a_rows = a.T
    lane_low = lax.broadcasted_iota(jnp.int32, (length, 128), 1) < WIDTH
    dt_x = spread(dt, pairs, lane_low)
    a_x = spread(a, pairs, lane_low)
    x = v * dt_x
    xb = x.astype(BF)
    scores = jnp.where(causal, nt(cb, bb), 0.0)
    inside = []
    zero = jnp.zeros((length, 128), BF)
    for p in range(pairs):
        xp = xb[:, 128 * p : 128 * (p + 1)]
        total = None
        for j in range(2):
            h = 2 * p + j
            decay = jnp.exp(jnp.minimum(a[:, h : h + 1] - a_rows[h : h + 1, :], 0.0))
            m = (scores * decay).astype(BF)
            term = nn(m, jnp.where(lane_low, xp, zero) if j == 0 else jnp.where(lane_low, zero, xp))
            total = term if total is None else total + term
        inside.append(total)
    entering = state[...]
    ent_ref[0] = entering
    outside = jnp.exp(a_x) * nn(cb, entering.astype(BF))
    a_last = a_x[length - 1 : length, :]
    xw = (x * jnp.exp(a_last - a_x)).astype(BF)
    state[...] = jnp.exp(a_last) * entering + nn(bc[:, :half].T.astype(BF), xw)
    y = jnp.concatenate(inside, axis=1) + outside + skip_ref[...] * v
    y_ref[...] = y
    _, sgate = silu_parts(gate_ref[...])
    gated = y * sgate
    square = (gated * gated).astype(BF)
    ssq_ref[...] = nt(jnp.ones((8, inner), BF), square)
    mixed = (gated * gg_ref[...]).astype(BF)
    part_ref[...] = nt(mixed, wot_ref[...]).astype(BF)
    if last:
        dm = nn(gb_ref[...], wot_ref[...])
        dm_ref[...] = dm
        dots = nt(jnp.ones((8, inner), BF), (dm * gg_ref[...] * gated).astype(BF))
        row = lax.broadcasted_iota(jnp.int32, dots.shape, 0)
        ssq_ref[...] = jnp.where(row == 0, ssq_ref[...], dots)


def whole(shape):
    return pl.BlockSpec(shape, lambda i: (0,) * len(shape), pipeline_mode=pl.Buffered(1))


def layer_specs(params, l):
    return [
        pl.BlockSpec((1,) + p.shape[1:], lambda i: (l, 0, 0), pipeline_mode=pl.Buffered(1))
        for p in params
    ]


def forward_mix(rows, packed, params, l, gb=None):
    first, last = l == 0, gb is not None
    tokens, width = rows.shape
    inner = params[0].shape[2]
    bc_width = params[1].shape[2]
    dt_width = 128
    half = bc_width // 2
    q = GROUP
    blocks = tokens // q
    tok = lambda n: pl.BlockSpec((q, n), lambda i: (i, 0))
    outs = [
        ((tokens, inner), F32, tok(inner)),
        ((tokens, inner), F32, tok(inner)),
        ((tokens, bc_width), F32, tok(bc_width)),
        ((tokens, dt_width), F32, tok(dt_width)),
        ((tokens, inner), F32, tok(inner)),
        ((blocks, half, inner), F32, pl.BlockSpec((1, half, inner), lambda i: (i, 0, 0))),
        ((tokens, width), BF, tok(width)),
        ((8, tokens), F32, pl.BlockSpec((8, q), lambda i: (0, i))),
    ]
    if first:
        outs.append(((tokens, width), BF, tok(width)))
    if last:
        outs.append(((tokens, inner), F32, tok(inner)))
    return pl.pallas_call(
        functools.partial(fwd_kernel, first, last),
        grid=(blocks,),
        in_specs=[tok(width), whole(packed.shape)]
        + layer_specs(params, l)
        + ([tok(width)] if last else []),
        out_specs=[o[2] for o in outs],
        out_shape=[jax.ShapeDtypeStruct(o[0], o[1]) for o in outs],
        scratch_shapes=[
            pltpu.VMEM((half, inner), F32),
            pltpu.VMEM((q + 8, inner), F32),
            pltpu.VMEM((q + 8, bc_width), F32),
        ],
        compiler_params=pltpu.CompilerParams(
            dimension_semantics=("arbitrary",), vmem_limit_bytes=56 * MIB
        ),
        name="mix_forward",
    )(rows, packed, *params, *([gb] if last else []))


def bwd_kernel(
    ready, gb_ref, e_ref, rows_ref, gate_ref, val_ref, valp_ref, st_ref, stp_ref, dt_ref, y_ref,
    ent_ref, w_ref, vec_ref, cst_ref, tiny_ref, gain_ref, pick_ref,
    dcat_ref, dpart_ref, gvec_ref, gst_ref, gdt_ref, ggain_ref,
    dstate, vpad, spad, dvpad, dspad,
):
    step = pl.program_id(0)
    blocks = pl.num_programs(0)
    length = gb_ref.shape[0]
    cv_ref, cvb_ref, skip_ref, gg_ref, cs_ref, csb_ref, sb_ref, rate_ref = small_refs(
        vec_ref, cst_ref, tiny_ref
    )
    inner = gg_ref.shape[1]
    bc_width = cs_ref.shape[1]
    wbc_ref, wdt_ref, wz_ref, wx_ref, wot_ref = blocks_of(w_ref, inner, bc_width)
    dst_ref, ddt_ref, dgate_ref, dval_ref, mixed_ref = blocks_of(dcat_ref, inner, bc_width)
    half = bc_width // 2
    pairs = inner // 128

    @pl.when(step == 0)
    def _():
        dstate[...] = jnp.zeros_like(dstate)
        dvpad[length : length + 8, :] = jnp.zeros((8, inner), F32)
        dspad[length : length + 8, :] = jnp.zeros((8, bc_width), F32)
        gvec_ref[...] = jnp.zeros_like(gvec_ref)
        gst_ref[...] = jnp.zeros_like(gst_ref)
        gdt_ref[...] = jnp.zeros_like(gdt_ref)
        ggain_ref[...] = jnp.zeros_like(ggain_ref)

    @pl.when(step > 0)
    def _():
        dvpad[length : length + 8, :] = dvpad[0:8, :]
        dspad[length : length + 8, :] = dspad[0:8, :]

    first = step == blocks - 1
    vpad[0:8, :] = jnp.where(first, 0.0, valp_ref[...])
    spad[0:8, :] = jnp.where(first, 0.0, stp_ref[...])
    vpad[8 : length + 8, :] = val_ref[...]
    spad[8 : length + 8, :] = st_ref[...]

    pre_v = conv_pre(vpad, cv_ref, cvb_ref[...], length)
    sig_v, v = silu_parts(pre_v)
    pre_s = conv_pre(spad, cs_ref, csb_ref[...], length)
    sig_s, bc = silu_parts(pre_s)
    bb = bc[:, :half].astype(BF)
    cb = bc[:, half:].astype(BF)
    z = dt_ref[...] + sb_ref[...]
    dt = softplus(z)
    rate = rate_ref[...]
    s_index = lax.broadcasted_iota(jnp.int32, (length, length), 0)
    q_index = lax.broadcasted_iota(jnp.int32, (length, length), 1)
    upper = q_index >= s_index
    a = sum_rows(jnp.where(s_index >= q_index, 1.0, 0.0).astype(BF), dt * rate)
    a_rows = a.T
    lane_low = lax.broadcasted_iota(jnp.int32, (length, 128), 1) < WIDTH
    dt_x = spread(dt, pairs, lane_low)
    a_x = spread(a, pairs, lane_low)
    x = v * dt_x
    xb = x.astype(BF)
    skip = skip_ref[...]

    y = y_ref[...]
    gate = gate_ref[...]
    sig_g, sgate = silu_parts(gate)
    gated = y * sgate
    per_token = e_ref[...].T
    e, r2 = per_token[:, 0:1], per_token[:, 1:2]
    dm = (gb_ref[...] if ready else nn(gb_ref[...], wot_ref[...])) * r2
    dgated = dm * gg_ref[...] - e * gated
    mixed_ref[...] = (gated * r2 * gg_ref[...]).astype(BF)
    dgate = (dgated * y * (sig_g * (1.0 + gate * (1.0 - sig_g)))).astype(BF)
    dgate_ref[...] = dgate
    dy = dgated * sgate
    dyb = dy.astype(BF)
    dyf = dyb.astype(F32)

    scores = jnp.where(upper, nt(bb, cb), 0.0)
    zero = jnp.zeros((length, 128), BF)
    dscores = jnp.zeros((length, length), F32)
    dx_list = []
    for p in range(pairs):
        xp = xb[:, 128 * p : 128 * (p + 1)]
        dp = dyb[:, 128 * p : 128 * (p + 1)]
        total = None
        for j in range(2):
            h = 2 * p + j
            decay = jnp.exp(jnp.minimum(a_rows[h : h + 1, :] - a[:, h : h + 1], 0.0))
            m = (scores * decay).astype(BF)
            dh = jnp.where(lane_low, dp, zero) if j == 0 else jnp.where(lane_low, zero, dp)
            term = nn(m, dh)
            total = term if total is None else total + term
            dscores = dscores + nt(xp, dh) * decay
        dx_list.append(total)
    dx_in = jnp.concatenate(dx_list, axis=1)
    dscores = jnp.where(upper, dscores, 0.0)
    db = nn(dscores.astype(BF), cb)
    dc = nn(dscores.T.astype(BF), bb)

    entering = ent_ref[0]
    dleaving = dstate[...]
    dleaving_b = dleaving.astype(BF)
    ea = jnp.exp(a_x)
    a_last = a_x[length - 1 : length, :]
    ea_last = jnp.exp(a_last)
    w = jnp.exp(a_last - a_x)
    dxw = nn(bb, dleaving_b) * w
    db = db + nt((x * w).astype(BF), dleaving_b)
    eady = (ea * dyf).astype(BF)
    dc = dc + nt(eady, entering.astype(BF))
    dstate[...] = ea_last * dleaving + nn(bc[:, half:].T.astype(BF), eady)
    dx = dx_in + dxw
    u = x * dxw
    last_add = jnp.sum(u, axis=0, keepdims=True) + ea_last * jnp.sum(
        entering * dleaving, axis=0, keepdims=True
    )
    da_x = dyf * (y - skip * v) - xb.astype(F32) * dx_in - u
    row_index = lax.broadcasted_iota(jnp.int32, (length, inner), 0)
    da_x = da_x + jnp.where(row_index == length - 1, last_add, 0.0)
    pick = pick_ref[...]
    da = sum_lanes(da_x, pick)
    dr = sum_rows(jnp.where(upper, 1.0, 0.0).astype(BF), da)
    ddt = sum_lanes(dx * v, pick) + dr * rate
    dz = ddt * (1.0 / (1.0 + jnp.exp(-z)))
    ddtb = dz.astype(BF)
    ddt_ref[...] = ddtb
    gdt_ref[0:1, :] += jnp.sum(dz, axis=0, keepdims=True)
    gdt_ref[1:2, :] += jnp.sum(dr * dt * rate, axis=0, keepdims=True)

    dpre_v = (skip * dy + dt_x * dx) * (sig_v * (1.0 + pre_v * (1.0 - sig_v)))
    dvpad[0:length, :] = dpre_v
    dval = jnp.zeros((length, inner), F32)
    for k in range(4):
        dval = dval + cv_ref[k : k + 1, :] * dvpad[pl.ds(3 - k, length), :]
        gvec_ref[k : k + 1, :] += jnp.sum(
            dpre_v * vpad[pl.ds(5 + k, length), :], axis=0, keepdims=True
        )
    gvec_ref[4:5, :] += jnp.sum(dpre_v, axis=0, keepdims=True)
    gvec_ref[5:6, :] += jnp.sum(gated * dm, axis=0, keepdims=True)
    gvec_ref[6:7, :] += jnp.sum(dy * v, axis=0, keepdims=True)
    dvalb = dval.astype(BF)
    dval_ref[...] = dvalb

    dbc = jnp.concatenate([db, dc], axis=1)
    dpre_s = dbc * (sig_s * (1.0 + pre_s * (1.0 - sig_s)))
    dspad[0:length, :] = dpre_s
    dst = jnp.zeros((length, bc_width), F32)
    for k in range(4):
        dst = dst + cs_ref[k : k + 1, :] * dspad[pl.ds(3 - k, length), :]
        gst_ref[k : k + 1, :] += jnp.sum(
            dpre_s * spad[pl.ds(5 + k, length), :], axis=0, keepdims=True
        )
    gst_ref[4:5, :] += jnp.sum(dpre_s, axis=0, keepdims=True)
    dstb = dst.astype(BF)
    dst_ref[...] = dstb
    dpart = nt(dgate, wz_ref[...]) + nt(dvalb, wx_ref[...])
    dpart = dpart + nt(dstb, wbc_ref[...]) + nt(ddtb, wdt_ref[...])
    dpart_ref[...] = dpart.astype(BF)
    ggain_ref[0:1, :] += jnp.sum(rows_ref[...].astype(F32) * dpart, axis=0, keepdims=True)

    @pl.when(step == blocks - 1)
    def _():
        ggain_ref[0:1, :] = ggain_ref[0:1, :] / gain_ref[0]


def backward_mix(gb, ready, e_rows, rows, kept, packed, params, pick, l):
    gate, val, st, dt, y, ent = kept
    tokens, width = gb.shape[0], packed.shape[0]
    inner = params[0].shape[2]
    bc_width = params[1].shape[2]
    dt_width = 128
    packed_width = packed.shape[1]
    half = bc_width // 2
    q = GROUP
    blocks = tokens // q
    back = lambda i: blocks - 1 - i
    tok = lambda n: pl.BlockSpec((q, n), lambda i: (back(i), 0))
    halo = lambda n: pl.BlockSpec(
        (8, n), lambda i: (jnp.maximum(back(i) * (q // 8) - 1, 0), 0)
    )
    fixed = lambda r, c: pl.BlockSpec((r, c), lambda i: (0, 0))
    outs = [
        ((tokens, packed_width), BF, tok(packed_width)),
        ((tokens, width), BF, tok(width)),
        ((8, inner), F32, fixed(8, inner)),
        ((8, bc_width), F32, fixed(8, bc_width)),
        ((8, dt_width), F32, fixed(8, dt_width)),
        ((8, width), F32, fixed(8, width)),
    ]
    return pl.pallas_call(
        functools.partial(bwd_kernel, ready),
        grid=(blocks,),
        in_specs=[
            tok(gb.shape[1]),
            pl.BlockSpec((8, q), lambda i: (0, back(i))),
            tok(width),
            tok(inner), tok(inner), halo(inner), tok(bc_width), halo(bc_width), tok(dt_width),
            tok(inner),
            pl.BlockSpec((1, half, inner), lambda i: (back(i), 0, 0)),
        ]
        + [whole(packed.shape)] + layer_specs(params, l) + [whole(pick.shape)],
        out_specs=[o[2] for o in outs],
        out_shape=[jax.ShapeDtypeStruct(o[0], o[1]) for o in outs],
        scratch_shapes=[
            pltpu.VMEM((half, inner), F32),
            pltpu.VMEM((q + 8, inner), F32),
            pltpu.VMEM((q + 8, bc_width), F32),
            pltpu.VMEM((q + 8, inner), F32),
            pltpu.VMEM((q + 8, bc_width), F32),
        ],
        compiler_params=pltpu.CompilerParams(
            dimension_semantics=("arbitrary",), vmem_limit_bytes=60 * MIB
        ),
        name="mix_backward",
    )(gb, e_rows, rows, gate, val, val, st, st, dt, y, ent, packed, *params, pick)


class Step:
    def __init__(self, **given):
        self.rows = 0
        self.width = 0
        self.line = 4
        self.chunks = 8
        self.hop = 1
        self.pass_hop = 1
        self.slack = 0
        self.partial = False
        self.gather = False
        self.late = False
        self.scale = False
        self.inner = False
        self.layer = 0
        self.weights = 0
        self.grads = 0
        self.tail = 2
        self.lag = 1
        self.states = 0
        self.sums = False
        self.bits = 0
        self.middle = None
        self.lazy = ()
        self.__dict__.update(given)


def remote(src, dst, send, recv, device):
    return pltpu.make_async_remote_copy(
        src_ref=src, dst_ref=dst, send_sem=send, recv_sem=recv,
        device_id=device, device_id_type=pl.DeviceIdType.MESH,
    )


def when(condition):
    return pl.when(condition)


def pack_weights(r, l):
    start = 0
    for part in (r.p_bc.at[l], r.p_dt.at[l], r.p_z.at[l], r.p_x.at[l], r.p_out.at[l]):
        r.wown[:, start : start + part.shape[1]] = part[...]
        start += part.shape[1]


def comm_kernel(o, names, *refs):
    r = types.SimpleNamespace(**dict(zip(names, refs)))
    r.gbuf = [v for k, v in zip(names, refs) if k.startswith("gbuf")]
    n, count, rows = o.line, o.chunks, o.rows
    size = rows // count
    t = lax.axis_index("tensor")
    me = lax.axis_index("dp")
    own_bits = [(me // (1 << b)) % 2 for b in range(o.bits)]
    partner = [me + (1 - 2 * own_bits[b]) * (1 << b) for b in range(o.bits)]

    lazy = []
    for i, name in enumerate(o.lazy):
        near = getattr(r, name + "_v")
        lazy.append(pltpu.make_async_copy(getattr(r, name), near, r.lazy_sem.at[i]))
        setattr(r, name, near)
    for copy in lazy:
        copy.start()

    barrier = pltpu.get_barrier_semaphore()
    for k in range(1, n):
        pl.semaphore_signal(
            barrier, inc=1, device_id={"tensor": lax.rem(t + k, n)},
            device_id_type=pl.DeviceIdType.MESH,
        )
    over_dp = o.weights or o.grads
    r.early = [v for k, v in zip(names, refs) if k.startswith("esum")]
    r.lined = [v for k, v in zip(names, refs) if k.startswith("lsum")]
    r.gains = [v for k, v in zip(names, refs) if k.startswith("gsum")]
    if over_dp:
        for b in range(o.bits):
            pl.semaphore_signal(
                barrier, inc=1, device_id={"dp": partner[b]}, device_id_type=pl.DeviceIdType.MESH
            )
    pl.semaphore_wait(barrier, n - 1 + (o.bits if over_dp else 0))

    def at(s, c):
        return pl.ds(pl.multiple_of(s * rows + c * size, size), size)

    def piece(c):
        return pl.ds(pl.multiple_of(c * size, size), size)

    def hop(side, s, c, src):
        buf = r.rbuf if side == 0 else r.lbuf
        return remote(
            src, buf.at[s, piece(c)], r.rs_send.at[side, s], r.rs_recv.at[side, s, c],
            {"tensor": t + 1 if side == 0 else t - 1},
        )

    def reduce_items(side, c):
        buf = r.rbuf if side == 0 else r.lbuf
        edge = t == 0 if side == 0 else t == n - 1
        order = range(n - 1, 0, -1) if side == 0 else range(0, n - 1)
        for s in order:
            further = s > t if side == 0 else s < t

            @when(further & edge)
            def _():
                hop(side, s, c, r.part.at[at(s, c)]).start()

            @when(further & jnp.logical_not(edge))
            def _():
                hop(side, s, c, buf.at[s, piece(c)]).wait_recv()
                total = buf[s, piece(c), :].astype(F32) + r.part[at(s, c), :].astype(F32)
                buf[s, piece(c), :] = total.astype(BF)
                hop(side, s, c, buf.at[s, piece(c)]).start()

    def own_total(c):
        acc = r.acc
        acc[...] = r.part[at(t, c), :].astype(F32)

        @when(t > 0)
        def _():
            hop(0, t, c, r.rbuf.at[t, piece(c)]).wait_recv()
            acc[...] += r.rbuf[t, piece(c), :].astype(F32)

        @when(t < n - 1)
        def _():
            hop(1, t, c, r.lbuf.at[t, piece(c)]).wait_recv()
            acc[...] += r.lbuf[t, piece(c), :].astype(F32)

    def pass_on(side, s, c):
        spot = r.full.at[at(s, c)]
        return remote(
            spot, spot, r.ag_send.at[side, s], r.ag_recv.at[side, s, c],
            {"tensor": t + 1 if side == 0 else t - 1},
        )

    def forward_items(side, tau):
        order = range(n - 2, -1, -1) if side == 0 else range(1, n)
        for s in order:
            away = t - s if side == 0 else s - t
            late = o.hop * max(s, n - 1 - s) + o.slack if o.late else 0
            c = tau - late - o.pass_hop * away

            @when((away > 0) & (c >= 0) & (c < count))
            def _():
                pass_on(side, s, c).wait_recv()

                @when(t < n - 1 if side == 0 else t > 0)
                def _():
                    pass_on(side, s, c).start()

    def spot_of(k, ref):
        return ref.at[:, pl.ds(pl.multiple_of(k * rows, rows), rows)]

    def square_copy(k):
        dest = lax.rem(t + k, n)
        return remote(
            spot_of(dest, r.ssq), r.sqbuf.at[k - 1], r.sq_send.at[k - 1],
            r.sq_recv.at[k - 1], {"tensor": dest},
        )

    def inner_copy(k):
        return remote(
            spot_of(t, r.inner), spot_of(t, r.inner), r.in_send.at[k - 1],
            r.in_recv.at[k - 1], {"tensor": lax.rem(t + k, n)},
        )

    def inner_arrival(k):
        source = lax.rem(t + n - k, n)
        return remote(
            spot_of(source, r.inner), spot_of(source, r.inner), r.in_send.at[k - 1],
            r.in_recv.at[k - 1], {"tensor": source},
        )

    def bit_order(parity):
        high = list(range(o.bits - 1, 0, -1))
        if parity == 1:
            high = high[1:] + high[:1]
        return high + [0]

    def cols(j):
        return pl.ds(pl.multiple_of(j * WCHUNK, WCHUNK), WCHUNK)

    def spots(known):
        return tuple(slice(None) if b in known else own_bits[b] for b in range(o.bits - 1, -1, -1))

    def weight_copy(parity, stage, j):
        order = bit_order(parity)
        depth = r.wown.shape[0] // o.weights
        strip = pl.ds(pl.multiple_of(j * depth, depth), depth)
        spot = r.wfull.at[(*spots(order[:stage]), strip)]
        src = r.wown.at[strip] if stage == 0 else spot
        return remote(
            src, spot, r.wg_send.at[stage, j], r.wg_recv.at[stage, j],
            {"dp": partner[order[stage]]},
        )

    def own_weights():
        return pltpu.make_async_copy(r.wown, r.wfull.at[spots([])], r.wl_sem)

    def each_parity(pair, fn):
        for parity in range(2):
            j = 2 * pair + parity

            @when((j >= 0) & (j < o.weights))
            def _():
                fn(parity, j)

    def weight_items(tau):
        for stage in range(o.bits + 1):
            def run(parity, j):
                if stage > 0:
                    weight_copy(parity, stage - 1, j).wait_recv()
                if stage < o.bits:
                    weight_copy(parity, stage, j).start()
            each_parity(tau - stage, run)

    def grad_order(parity):
        high = list(range(1, o.bits))
        if parity == 1:
            high = high[1:] + high[:1]
        return [0] + high

    def grad_spot(parity, stage, mine):
        order = grad_order(parity)
        done, bit = order[:stage], order[stage]
        spot = []
        for b in range(o.bits - 1, -1, -1):
            if b in done:
                spot.append(own_bits[b])
            elif b == bit:
                spot.append(own_bits[b] if mine else 1 - own_bits[b])
            else:
                spot.append(slice(None))
        return tuple(spot)

    def grad_copy(parity, stage, j):
        order = grad_order(parity)
        return remote(
            r.grad.at[(j, *grad_spot(parity, stage, False))], r.gbuf[stage].at[j],
            r.gr_send.at[stage, j], r.gr_recv.at[stage, j],
            {"dp": partner[order[stage]]},
        )

    def product(j):
        slab = o.width // 2
        inner_shape = (2,) * (o.bits - 1) + (slab >> (o.bits - 1), WCHUNK)

        def slabs(left):
            for i in range(2):
                out = tn(left[:, pl.ds(i * slab, slab)], r.right[:, cols(j)])
                r.grad[j, i] = out.astype(BF).reshape(inner_shape)

        @when(j < o.grads - o.tail)
        def _():
            slabs(r.lrows)

        @when(j >= o.grads - o.tail)
        def _():
            slabs(r.lgrad)

    def each_chunk(j, fn):
        for parity in range(2):
            @when((j >= 0) & (j < o.grads) & (lax.rem(j, 2) == parity))
            def _():
                fn(parity, j)

    def grad_items(tau):
        @when((tau >= 0) & (tau < o.grads))
        def _():
            product(tau)

        def first(parity, j):
            grad_copy(parity, 0, j).start()

        each_chunk(tau, first)
        for stage in range(1, o.bits + 1):
            def run(parity, j):
                grad_copy(parity, stage - 1, j).wait_recv()
                spot = grad_spot(parity, stage - 1, True)
                free = [i for i, v in enumerate(spot) if isinstance(v, slice)]
                buf = r.gbuf[stage - 1]
                for combo in range(1 << len(free)):
                    pick = [(combo >> i) % 2 for i in range(len(free))]
                    full = list(spot)
                    for i, v in zip(free, pick):
                        full[i] = v
                    total = r.grad[(j, *full)].astype(F32) + buf[(j, *pick)].astype(F32)
                    if stage < o.bits:
                        r.grad[(j, *full)] = total.astype(BF)
                    else:
                        r.gout[:, cols(j)] = total
                if stage < o.bits:
                    grad_copy(parity, stage, j).start()
            each_chunk(tau - grad_lag(stage), run)

    def grad_lag(stage):
        return o.lag * (2 * stage - 1) if stage else 0

    def share(buf, send, recv, k):
        return remote(buf.at[t], buf.at[t], send.at[k - 1], recv.at[k - 1],
                      {"tensor": lax.rem(t + k, n)})

    def shared(buf, send, recv):
        for k in range(1, n):
            source = lax.rem(t + n - k, n)
            remote(buf.at[source], buf.at[source], send.at[k - 1], recv.at[k - 1],
                   {"tensor": source}).wait_recv()

    def line_total(buf):
        total = buf[0]
        for k in range(1, n):
            total = total + buf[k]
        return total

    def double(acc, buf, send, recv, b):
        return remote(acc.at[b], buf.at[b], send.at[b], recv.at[b], {"dp": partner[b]})

    def doubled(acc, buf, send, recv, b):
        double(acc, buf, send, recv, b).wait_recv()
        acc[b + 1] = acc[b] + buf[b]

    def lanes(index, ref):
        return slice(index * ref.shape[1], (index + 1) * ref.shape[1])

    line_groups, dp_groups = [], []
    if o.sums:
        line_groups = [(r.lbank, r.lb_send, r.lb_recv), (r.gbank, r.gb_send, r.gb_recv)]
        dp_groups = [
            (r.dbank, r.dbuf, r.db_send, r.db_recv), (r.hbank, r.hbuf, r.hb_send, r.hb_recv)
        ]

    def sum_items(tau):
        @when(tau == 2)
        def _():
            for g in line_groups:
                shared(*g)
            off = 0
            for v in r.early:
                r.dbank[0, :, off : off + v.shape[1]] = v[...]
                off += v.shape[1]
            r.dbank[0, :, off:] = line_total(r.lbank)
            r.hbank[0] = line_total(r.gbank)
            for g in dp_groups:
                double(*g, 0).start()

        for b in range(o.bits):
            @when(tau == 4 + b)
            def _():
                for g in dp_groups:
                    doubled(*g, b)
                    if b < o.bits - 1:
                        double(*g, b + 1).start()

    def state_items(tau):
        at_first = grad_lag(o.bits) + 1
        quarter = r.gout.shape[0] // n

        @when(tau == at_first)
        def _():
            for s in range(n):
                r.qsend[s] = r.gout[s * quarter : (s + 1) * quarter, 0 : o.states].astype(BF)
            for k in range(1, n):
                state_out(k).start()

        @when(tau == at_first + 2)
        def _():
            total = r.qsend[t].astype(F32)
            for k in range(1, n):
                state_out(k).wait_recv()
                total = total + r.qbuf[k - 1].astype(F32)
            r.qall[t] = total.astype(BF)
            for k in range(1, n):
                share(r.qall, r.qa_send, r.qa_recv, k).start()

    def state_out(k):
        dest = lax.rem(t + k, n)
        return remote(r.qsend.at[dest], r.qbuf.at[k - 1], r.qs_send.at[k - 1],
                      r.qs_recv.at[k - 1], {"tensor": dest})

    if o.sums:
        off = 0
        for v in r.lined:
            r.lbank[t, :, off : off + v.shape[1]] = v[...]
            off += v.shape[1]
        for i, v in enumerate(r.gains):
            r.gbank[t, :, lanes(i, v)] = v[0:1, :]
        for g in line_groups:
            for k in range(1, n):
                share(*g, k).start()
    if o.scale:
        for k in range(1, n):
            square_copy(k).start()
    if o.weights:
        pack_weights(r, o.layer)
        own_weights().start()
    if o.scale:
        total = spot_of(t, r.ssq)[...]
        for k in range(1, n):
            square_copy(k).wait_recv()
            total = total + r.sqbuf[k - 1]
        scale = lax.rsqrt(total / (o.scale * 1.0) + EPSILON)
        r.r2[...] = jnp.broadcast_to(scale.T[:, 0:1], (rows, 128))
    if o.gather and not o.late:
        r.full[pl.ds(pl.multiple_of(t * rows, rows), rows), :] = o.payload(r)
    if o.middle is not None:
        o.middle(r, None, None)

    ends = [count + o.hop * (n - 1) + o.slack]
    if o.late:
        ends.append(ends[0] + o.pass_hop * (n - 1))
    elif o.gather:
        ends.append(count + o.pass_hop * (n - 1))
    if o.weights:
        ends.append((o.weights + 1) // 2 + o.bits)
    if o.grads:
        ends.append(1 + o.grads + grad_lag(o.bits))
        ends.append(grad_lag(o.bits) + 5)
    if o.sums:
        ends.append(4 + o.bits)

    def iteration(tau, _):
        if lazy:
            @when(tau == 1)
            def _():
                for copy in lazy:
                    copy.wait()
        if o.partial:
            for side in range(2):
                c = tau - o.hop * (t if side == 0 else n - 1 - t)

                @when((c >= 0) & (c < count))
                def _():
                    reduce_items(side, c)

            c_own = tau - o.hop * jnp.maximum(t, n - 1 - t) - o.slack

            @when((c_own >= 0) & (c_own < count))
            def _():
                own_total(c_own)
                out = o.middle(r, piece(c_own), r.acc[...])
                if o.late:
                    r.full[at(t, c_own), :] = out
        if o.gather:
            c_out = tau - o.hop * jnp.maximum(t, n - 1 - t) - o.slack if o.late else tau

            @when((c_out >= 0) & (c_out < count))
            def _():
                @when(t < n - 1)
                def _():
                    pass_on(0, t, c_out).start()

                @when(t > 0)
                def _():
                    pass_on(1, t, c_out).start()

            for side in range(2):
                forward_items(side, tau)
        if o.weights:
            @when(tau == 1)
            def _():
                own_weights().wait()
            weight_items(tau)
        if o.grads:
            grad_items(tau - 1)
            state_items(tau - 1)
        if o.sums:
            sum_items(tau)
        return 0

    lax.fori_loop(0, max(ends), iteration, 0)

    if o.inner:
        spot_of(t, r.inner)[...] = r.icol[...].T[0:8, :]
        for k in range(1, n):
            inner_copy(k).start()
        for k in range(1, n):
            inner_arrival(k).wait_recv()
        for k in range(1, n):
            inner_copy(k).wait_send()
    if o.sums:
        r.sums[...] = r.dbank[o.bits]
        for i, v in enumerate(r.gains):
            r.gain_sums[i : i + 1, :] = r.hbank[o.bits, :, lanes(i, v)]
        for g in line_groups:
            for k in range(1, n):
                share(*g, k).wait_send()
        for g in dp_groups:
            for b in range(o.bits):
                double(*g, b).wait_send()
    if o.grads:
        shared(r.qall, r.qa_send, r.qa_recv)
        quarter = r.gout.shape[0] // n
        for s in range(n):
            r.gout[s * quarter : (s + 1) * quarter, 0 : o.states] = r.qall[s].astype(F32)
        for k in range(1, n):
            state_out(k).wait_send()
            share(r.qall, r.qa_send, r.qa_recv, k).wait_send()
    if o.scale:
        for k in range(1, n):
            square_copy(k).wait_send()
    for s in range(n):
        for side in range(2):
            inside = t < n - 1 if side == 0 else t > 0
            if o.partial:
                @when((s > t if side == 0 else s < t) & inside)
                def _():
                    buf = (r.rbuf if side == 0 else r.lbuf).at[s]
                    remote(
                        buf, buf, r.rs_send.at[side, s], r.rs_recv.at[side, s, 0],
                        {"tensor": t + 1 if side == 0 else t - 1},
                    ).wait_send()
            if o.gather:
                @when((s <= t if side == 0 else s >= t) & inside)
                def _():
                    spot = r.full.at[pl.ds(s * rows, rows)]
                    remote(
                        spot, spot, r.ag_send.at[side, s], r.ag_recv.at[side, s, 0],
                        {"tensor": t + 1 if side == 0 else t - 1},
                    ).wait_send()
    for j in range(o.weights):
        for stage in range(o.bits):
            weight_copy(j % 2, stage, jnp.int32(j)).wait_send()
    for j in range(o.grads):
        for stage in range(o.bits):
            grad_copy(j % 2, stage, jnp.int32(j)).wait_send()


def comm_call(o, name, collective, inputs, outputs, **scratch):
    n, count, rows, width = o.line, o.chunks, o.rows, o.width
    dma = pltpu.SemaphoreType.DMA
    if o.lazy:
        for key in o.lazy:
            value = inputs[key][0]
            inputs[key] = (value, pl.ANY)
            scratch[key + "_v"] = pltpu.VMEM(value.shape, value.dtype)
        scratch.update(lazy_sem=dma((len(o.lazy),)))
    if o.partial:
        scratch.update(
            rbuf=pltpu.VMEM((n, rows, width), BF),
            lbuf=pltpu.VMEM((n, rows, width), BF),
            acc=pltpu.VMEM((rows // count, width), F32),
            rs_send=dma((2, n)),
            rs_recv=dma((2, n, count)),
        )
    if o.gather:
        scratch.update(ag_send=dma((2, n)), ag_recv=dma((2, n, count)))
    if o.scale:
        scratch.update(
            sqbuf=pltpu.VMEM((n - 1, 8, rows), F32), sq_send=dma((n - 1,)), sq_recv=dma((n - 1,))
        )
    if o.inner:
        scratch.update(
            icol=pltpu.VMEM((rows, 128), F32), in_send=dma((n - 1,)), in_recv=dma((n - 1,))
        )
    if o.weights:
        rows_of_pack = inputs["p_bc"][0].shape[1]
        pack_width = sum(v[0].shape[2] for k, v in inputs.items() if k.startswith("p_"))
        scratch.update(
            wown=pltpu.VMEM((rows_of_pack, pack_width), BF),
            wl_sem=dma(()),
            wg_send=dma((o.bits, o.weights)),
            wg_recv=dma((o.bits, o.weights)),
        )
    if o.grads:
        depth = o.width >> o.bits
        scratch.update(
            grad=pltpu.VMEM((o.grads, *(2,) * o.bits, depth, WCHUNK), BF),
            gr_send=dma((o.bits, o.grads)),
            gr_recv=dma((o.bits, o.grads)),
        )
        for stage in range(o.bits):
            scratch["gbuf%d" % stage] = pltpu.VMEM(
                (o.grads, *(2,) * (o.bits - 1 - stage), depth, WCHUNK), BF
            )
        part = (n, (width >> o.bits) // n, o.states)
        scratch.update(
            qsend=pltpu.VMEM(part, BF), qall=pltpu.VMEM(part, BF),
            qbuf=pltpu.VMEM((n - 1,) + part[1:], BF),
            qs_send=dma((n - 1,)), qs_recv=dma((n - 1,)),
            qa_send=dma((n - 1,)), qa_recv=dma((n - 1,)),
        )
    if o.sums:
        def lanes_of(start):
            return sum(v[0].shape[1] for k, v in inputs.items() if k.startswith(start))

        lined, early, gains = lanes_of("lsum"), lanes_of("esum"), lanes_of("gsum")
        for one, two, tall, line_width, dp_width in (
            ("lb", "db", 8, lined, lined + early), ("gb", "hb", 1, gains, gains)
        ):
            scratch[one + "ank"] = pltpu.VMEM((n, tall, line_width), F32)
            scratch[two + "ank"] = pltpu.VMEM((o.bits + 1, tall, dp_width), F32)
            scratch[two + "uf"] = pltpu.VMEM((o.bits, tall, dp_width), F32)
            for key, size in ((one, n - 1), (two, o.bits)):
                scratch[key + "_send"] = dma((size,))
                scratch[key + "_recv"] = dma((size,))
    names = [*inputs, *outputs, *scratch]
    out = pl.pallas_call(
        functools.partial(comm_kernel, o, names),
        in_specs=[pl.BlockSpec(memory_space=i[1]) for i in inputs.values()],
        out_specs=[pl.BlockSpec(memory_space=i[2]) for i in outputs.values()],
        out_shape=[jax.ShapeDtypeStruct(i[0], i[1]) for i in outputs.values()],
        scratch_shapes=list(scratch.values()),
        compiler_params=pltpu.CompilerParams(
            collective_id=collective, has_side_effects=True, vmem_limit_bytes=62 * MIB
        ),
        name=name,
    )(*[i[0] for i in inputs.values()])
    return dict(zip(outputs, out))


def meet_kernel(n, inner_all, own_ref, out_ref, scale_ref, bank, send, recv):
    t = lax.axis_index("tensor")
    barrier = pltpu.get_barrier_semaphore()
    for k in range(1, n):
        pl.semaphore_signal(
            barrier, inc=1, device_id={"tensor": lax.rem(t + k, n)},
            device_id_type=pl.DeviceIdType.MESH,
        )
    pl.semaphore_wait(barrier, n - 1)
    copies = [
        remote(own_ref, bank.at[t], send.at[k - 1], recv.at[k - 1], {"tensor": lax.rem(t + k, n)})
        for k in range(1, n)
    ]
    for copy in copies:
        copy.start()
    bank[t] = own_ref[...]
    for k in range(1, n):
        source = lax.rem(t + n - k, n)
        remote(
            own_ref, bank.at[source], send.at[k - 1], recv.at[k - 1], {"tensor": source}
        ).wait_recv()
    total = bank[0]
    for s in range(1, n):
        total = total + bank[s]
    scale = lax.rsqrt(total[0:1, :] / inner_all + EPSILON)
    row = lax.broadcasted_iota(jnp.int32, total.shape, 0)
    e = scale * scale * scale * (total[1:2, :] / inner_all)
    out_ref[...] = jnp.where(row == 0, e, scale)
    rows = scale_ref.shape[0]
    mine = out_ref[:, pl.ds(pl.multiple_of(t * rows, rows), rows)].T
    scale_ref[...] = jnp.broadcast_to(mine[:, 1:2], scale_ref.shape)
    for copy in copies:
        copy.wait_send()


def meet(own, n, inner_all, collective):
    vmem = pl.BlockSpec(memory_space=pltpu.VMEM)
    dma = pltpu.SemaphoreType.DMA
    return pl.pallas_call(
        functools.partial(meet_kernel, n, inner_all),
        in_specs=[vmem],
        out_specs=[vmem, vmem],
        out_shape=[
            jax.ShapeDtypeStruct(own.shape, F32),
            jax.ShapeDtypeStruct((own.shape[1] // n, 128), F32),
        ],
        scratch_shapes=[pltpu.VMEM((n,) + own.shape, F32), dma((n - 1,)), dma((n - 1,))],
        compiler_params=pltpu.CompilerParams(collective_id=collective, has_side_effects=True),
        name="turn_around",
    )(own)


def plain_payload(r):
    return r.own[...]


def token_columns(first, second):
    lane = lax.broadcasted_iota(jnp.int32, (first.shape[0], 128), 1)
    return jnp.where(lane == 0, first, second)


def forward_middle(r, at, total):
    if at is None:
        return None
    branch = total * r.r2[at, 0:1]
    residual = r.res[at, :].astype(F32) + branch
    r.branch[at, :] = branch
    r.res_out[at, :] = residual
    r1 = lax.rsqrt(jnp.mean(residual * residual, axis=1, keepdims=True) + EPSILON)
    return (residual * r1 * r.gain[...]).astype(BF)


def backward_middle(inner_all, r, at, total):
    if at is None:
        return None
    res = r.res[at, :].astype(F32)
    width = res.shape[1]
    r1 = lax.rsqrt(jnp.mean(res * res, axis=1, keepdims=True) + EPSILON)
    hat = res * r1
    dn = total * r.gain[...]
    cross = jnp.sum(dn * hat, axis=1, keepdims=True) / width
    grad = r.grad_in[at, :].astype(F32) + r1 * (dn - hat * cross)
    r.grad_out[at, :] = grad
    if inner_all is None:
        return None
    r2 = r.r2[at, 0:1]
    dot = jnp.sum(grad.astype(BF).astype(F32) * r.branch[at, :], axis=1, keepdims=True)
    r.icol[at, :] = token_columns(r2 * r2 * dot / inner_all, r2)
    return grad.astype(BF)


def pad_to(v, rows, columns):
    return jnp.pad(v, ((0, rows - v.shape[0]), (0, columns - v.shape[1])))


def rows_of(v):
    return v.astype(F32).reshape(-1, v.shape[-1])


def shards(
    hidden_in,
    out_grad,
    norm_gain,
    proj_z,
    proj_x,
    proj_bc,
    proj_dt,
    conv_value,
    conv_value_bias,
    conv_state,
    conv_state_bias,
    step_bias,
    log_decay,
    skip_gain,
    gate_gain,
    proj_out,
):
    tensor_count = lax.axis_size("tensor")
    dp_count = lax.axis_size("dp")
    bits = dp_count.bit_length() - 1
    layers, shard_rows, inner = proj_z.shape
    rows_own, width = hidden_in.shape
    tokens = rows_own * tensor_count
    heads = step_bias.shape[1]
    bc_width = proj_bc.shape[2]
    inner_all = inner * tensor_count
    packed_width = bc_width + 128 + 3 * inner
    column_chunks, row_chunks = packed_width // WCHUNK, shard_rows // 16
    vmem, far = pltpu.VMEM, pl.ANY

    small = jnp.concatenate([conv_state.reshape(layers, -1), conv_state_bias], axis=1)
    small = jnp.pad(small, ((0, 0), (0, shard_rows - small.shape[1])))
    extra = jnp.stack([norm_gain, small], axis=1).reshape(2 * layers, shard_rows).T
    step_block = jnp.concatenate(
        [
            proj_dt,
            jnp.broadcast_to(extra[None], (layers,) + extra.shape),
            jnp.zeros((layers, shard_rows, 128 - heads - 2 * layers), BF),
        ],
        axis=2,
    )
    out_turned = jnp.transpose(proj_out, (0, 2, 1))
    full_shape = ((2,) * bits) + (shard_rows, packed_width)
    common = dict(rows=rows_own, width=width, line=tensor_count, bits=bits)

    weight_in = dict(
        p_bc=(proj_bc, vmem), p_dt=(step_block, vmem), p_z=(proj_z, vmem), p_x=(proj_x, vmem),
        p_out=(out_turned, vmem),
    )
    weight_out = dict(wfull=(full_shape, BF, far))

    vec = jnp.concatenate(
        [
            conv_value,
            conv_value_bias[:, None],
            jnp.repeat(skip_gain, WIDTH, axis=1)[:, None],
            gate_gain[:, None],
        ],
        axis=1,
    ).astype(F32)
    tiny = jnp.stack([step_bias.astype(F32), -jnp.exp(log_decay.astype(F32))], axis=1)
    tiny = jnp.pad(tiny, ((0, 0), (0, 0), (0, 128 - heads)))
    pick = (jnp.arange(inner)[:, None] // WIDTH == jnp.arange(128)[None, :]).astype(BF)

    whole_rows, own_rows = ((tokens, width), BF, vmem), ((rows_own, width), F32, vmem)
    got = comm_call(
        Step(gather=True, payload=plain_payload, weights=row_chunks, layer=0, **common),
        "gather_first", 1,
        dict(own=(hidden_in, vmem), **weight_in),
        dict(full=whole_rows, **weight_out),
    )
    x_rows = got["full"]
    out_grad, x_rows = lax.optimization_barrier((out_grad, x_rows))
    grad_rows = lax.all_gather(out_grad, "tensor", axis=0, tiled=True)
    packed = [got["wfull"].reshape(width, packed_width)]
    start = bc_width + heads
    extra_all = packed[0][:, start : start + 2 * layers].astype(F32)
    gain_rows = extra_all[:, 0 : 2 * layers : 2].T[:, None, :]
    per = bc_width // dp_count
    smalls = extra_all[:, 1 : 2 * layers : 2].reshape(dp_count, shard_rows, layers)
    smalls = smalls[:, : 5 * per].reshape(dp_count, 5, per, layers)
    cst = jnp.transpose(smalls, (3, 1, 0, 2)).reshape(layers, 5, bc_width)
    params = (vec, cst, tiny)

    out = forward_mix(x_rows, packed[0], params + (gain_rows,), 0)
    saved, rows = [out[:6]], [out[8]]
    residuals, branches, r2s = [hidden_in], [], []
    for l in range(layers - 1):
        got = comm_call(
            Step(
                partial=True, gather=True, late=True, scale=inner_all, middle=forward_middle,
                weights=row_chunks, layer=l + 1, **common,
            ),
            "between_forward", 2 + l,
            dict(part=(out[6], vmem), ssq=(out[7], vmem), res=(residuals[l], vmem),
                 gain=(gain_rows[l + 1], vmem), **weight_in),
            dict(full=whole_rows, branch=own_rows, res_out=own_rows,
                 r2=((rows_own, 128), F32, vmem), **weight_out),
        )
        rows.append(got["full"])
        branches.append(got["branch"])
        residuals.append(got["res_out"])
        r2s.append(got["r2"])
        packed.append(got["wfull"].reshape(width, packed_width))
        gb = grad_rows if l + 1 == layers - 1 else None
        out = forward_mix(rows[-1], packed[-1], params + (gain_rows,), l + 1, gb)
        saved.append(out[:6])
    total = lax.psum_scatter(out[6], "tensor", scatter_dimension=0, tiled=True)
    token_rows, r2_own = meet(out[7], tensor_count, inner_all, 16)
    hidden_out = residuals[-1].astype(F32) + r2_own[:, 0:1] * total.astype(F32)
    product = out[8]
    gradient = out_grad
    scattered, summed, gain_grads = [None] * layers, [None] * layers, [None] * layers
    for l in reversed(range(layers)):
        last = l == layers - 1
        dcat, dpart, *small_grads = backward_mix(
            product if last else grad_rows, last, token_rows, rows[l], saved[l], packed[l],
            params + (gain_rows,), pick, l,
        )
        *summed[l], gain_grads[l] = small_grads
        more = l > 0
        inputs = dict(
            part=(dpart, vmem), res=(residuals[l], vmem), gain=(gain_rows[l], vmem),
            grad_in=(gradient, vmem), lrows=(rows[l], vmem), lgrad=(grad_rows, vmem),
            right=(dcat, vmem),
        )
        outputs = dict(
            grad_out=own_rows,
            gout=((shard_rows, packed_width), F32, vmem),
        )
        if more:
            inputs.update(r2=(r2s[l - 1], vmem), branch=(branches[l - 1], vmem))
            outputs.update(full=whole_rows, inner=((8, tokens), F32, vmem))
        else:
            for i in range(layers):
                gvec, gst, gdt = summed[i]
                inputs["esum%d" % i], inputs["esum_%d" % i] = (gvec, vmem), (gdt, vmem)
                inputs["lsum%d" % i] = (gst, vmem)
            for i in range(layers):
                inputs["gsum%d" % i] = (gain_grads[i], vmem)
            early = sum(v.shape[1] for i in range(layers) for v in summed[i])
            outputs.update(
                sums=((8, early), F32, vmem), gain_sums=((8, width), F32, vmem)
            )
        got = comm_call(
            Step(
                partial=True, gather=more, late=more, inner=more, grads=column_chunks,
                states=bc_width, sums=not more,
                lazy=("right", "lrows", "lgrad", "res", "grad_in") + (("branch",) if more else ()),
                middle=functools.partial(backward_middle, inner_all if more else None), **common,
            ),
            "between_backward" if more else "last_backward", 17 + l, inputs, outputs,
        )
        gradient = got["grad_out"]
        scattered[l] = got["gout"]
        if more:
            grad_rows, token_rows = got["full"], got["inner"]
    gout = jnp.stack(scattered)
    sums, ggain = got["sums"], got["gain_sums"][:layers]
    each = inner + 128
    gvec = jnp.stack([sums[:, i * each : i * each + inner] for i in range(layers)])
    gdt = jnp.stack([sums[:, i * each + inner : (i + 1) * each] for i in range(layers)])
    gst = jnp.stack(
        [sums[:, layers * each + i * bc_width :][:, :bc_width] for i in range(layers)]
    )
    own = lambda v, axis: lax.dynamic_slice_in_dim(
        v, lax.axis_index("dp") * (v.shape[axis] // dp_count), v.shape[axis] // dp_count, axis
    )
    gst = own(gst, 2)
    first = bc_width + 128
    return (
        hidden_out,
        gradient,
        own(ggain, 1),
        gout[:, :, first : first + inner],
        gout[:, :, first + inner : first + 2 * inner],
        gout[:, :, :bc_width],
        gout[:, :, bc_width : bc_width + heads],
        gvec[:, 0:4],
        gvec[:, 4],
        gst[:, 0:4],
        gst[:, 4],
        gdt[:, 0, :heads],
        gdt[:, 1, :heads],
        jnp.sum(gvec[:, 6].reshape(layers, heads, WIDTH), axis=2),
        gvec[:, 5],
        jnp.transpose(gout[:, :, first + 2 * inner :], (0, 2, 1)),
    )


def solution(mesh):
    placed = (
        P(("dp", "tensor"), None),
        P(("dp", "tensor"), None),
        P(None, "dp"),
        P(None, "dp", "tensor"),
        P(None, "dp", "tensor"),
        P(None, "dp", None),
        P(None, "dp", "tensor"),
        P(None, None, "tensor"),
        P(None, "tensor"),
        P(None, None, "dp"),
        P(None, "dp"),
        P(None, "tensor"),
        P(None, "tensor"),
        P(None, "tensor"),
        P(None, "tensor"),
        P(None, "tensor", "dp"),
    )
    return jax.shard_map(
        shards,
        mesh=mesh,
        in_specs=placed,
        out_specs=(
            P(("dp", "tensor"), None),
            P(("dp", "tensor"), None),
            P(None, "dp"),
            P(None, "dp", "tensor"),
            P(None, "dp", "tensor"),
            P(None, "dp", None),
            P(None, "dp", "tensor"),
            P(None, None, "tensor"),
            P(None, "tensor"),
            P(None, None, "dp"),
            P(None, "dp"),
            P(None, "tensor"),
            P(None, "tensor"),
            P(None, "tensor"),
            P(None, "tensor"),
            P(None, "tensor", "dp"),
        ),
        check_vma=False,
    )
```

```python
import functools
import types

import jax
import jax.numpy as jnp
from jax import lax
from jax.sharding import PartitionSpec as P
import jax.experimental.pallas as pl
import jax.experimental.pallas.tpu as pltpu

GROUP = 256
EPSILON = 1e-05
BF = jnp.bfloat16
F32 = jnp.float32
WIDTH = 64
MIB = 1024 * 1024
WCHUNK = 384


def nn(a, b):
    return lax.dot_general(a, b, (((1,), (0,)), ((), ())), preferred_element_type=F32)


def tn(a, b):
    return lax.dot_general(a, b, (((0,), (0,)), ((), ())), preferred_element_type=F32)


def nt(a, b):
    return lax.dot_general(a, b, (((1,), (1,)), ((), ())), preferred_element_type=F32)


def parts3(v):
    one = v.astype(BF)
    rest = v - one.astype(F32)
    two = rest.astype(BF)
    three = (rest - two.astype(F32)).astype(BF)
    return one, two, three


def sum_rows(select, v):
    one, two, three = parts3(v)
    return nn(select, one) + nn(select, two) + nn(select, three)


def sum_lanes(v, select):
    one = v.astype(BF)
    two = (v - one.astype(F32)).astype(BF)
    return nn(one, select) + nn(two, select)


def silu_parts(v):
    sig = 1.0 / (1.0 + jnp.exp(-v))
    return sig, v * sig


def softplus(v):
    return jnp.maximum(v, 0.0) + jnp.log1p(jnp.exp(-jnp.abs(v)))


def pair_spread(column_values, pair, lane_low):
    low = column_values[:, 2 * pair : 2 * pair + 1]
    high = column_values[:, 2 * pair + 1 : 2 * pair + 2]
    return jnp.where(lane_low, low, high)


def spread(column_values, pairs, lane_low):
    return jnp.concatenate([pair_spread(column_values, p, lane_low) for p in range(pairs)], axis=1)


def conv_pre(padded, taps, bias, length):
    count = 4
    total = bias
    for k in range(count):
        total = total + taps[k : k + 1, :] * padded[pl.ds(8 - (count - 1) + k, length), :]
    return total


def blocks_of(w_ref, inner, bc_width):
    sizes = (bc_width, 128, inner, inner, inner)
    starts = [sum(sizes[:i]) for i in range(5)]
    return [w_ref.at[:, pl.ds(s, z)] for s, z in zip(starts, sizes)]


def small_refs(vec_ref, cst_ref, tiny_ref):
    vec, cst, tiny = vec_ref.at[0], cst_ref.at[0], tiny_ref.at[0]
    return (
        vec.at[0:4], vec.at[4:5], vec.at[5:6], vec.at[6:7],
        cst.at[0:4], cst.at[4:5], tiny.at[0:1], tiny.at[1:2],
    )


def fwd_kernel(
    first, last, rows_ref, w_ref, vec_ref, cst_ref, tiny_ref, gain_ref, *rest,
):
    if last:
        gb_ref, *rest = rest
    gate_ref, val_ref, st_ref, dt_ref, y_ref, ent_ref, pre_ref, part_ref, ssq_ref, *rest = rest
    if first:
        normed_ref, *rest = rest
    if last:
        dm_ref, *rest = rest
    state, vpad, spad = rest[-3:]
    step = pl.program_id(0)
    length = rows_ref.shape[0]
    cv_ref, cvb_ref, skip_ref, gg_ref, cs_ref, csb_ref, sb_ref, rate_ref = small_refs(
        vec_ref, cst_ref, tiny_ref
    )
    inner = gg_ref.shape[1]
    pairs = inner // 128
    wbc_ref, wdt_ref, wz_ref, wx_ref, wot_ref = blocks_of(w_ref, inner, cs_ref.shape[1])

    @pl.when(step == 0)
    def _():
        state[...] = jnp.zeros_like(state)
        vpad[0:8, :] = jnp.zeros((8, inner), F32)
        spad[0:8, :] = jnp.zeros((8, spad.shape[1]), F32)

    @pl.when(step > 0)
    def _():
        vpad[0:8, :] = vpad[length : length + 8, :]
        spad[0:8, :] = spad[length : length + 8, :]

    rows = rows_ref[...]
    if first:
        rows = rows.astype(F32)
        r1 = lax.rsqrt(jnp.mean(rows * rows, axis=1, keepdims=True) + EPSILON)
        rows = (rows * r1 * gain_ref[0:1, :]).astype(BF)
        normed_ref[...] = rows
    gate_ref[...] = nn(rows, wz_ref[...])
    val = nn(rows, wx_ref[...])
    val_ref[...] = val
    vpad[8 : length + 8, :] = val
    st = nn(rows, wbc_ref[...])
    st_ref[...] = st
    spad[8 : length + 8, :] = st
    dt_in = nn(rows, wdt_ref[...])
    dt_ref[...] = dt_in

    pre = conv_pre(vpad, cv_ref, cvb_ref[...], length)
    pre_ref[...] = pre
    _, v = silu_parts(pre)
    _, bc = silu_parts(conv_pre(spad, cs_ref, csb_ref[...], length))
    half = bc.shape[1] // 2
    bb = bc[:, :half].astype(BF)
    cb = bc[:, half:].astype(BF)
    dt = softplus(dt_in + sb_ref[...])
    q_index = lax.broadcasted_iota(jnp.int32, (length, length), 0)
    s_index = lax.broadcasted_iota(jnp.int32, (length, length), 1)
    causal = q_index >= s_index
    tril = jnp.where(causal, 1.0, 0.0).astype(BF)
    a = sum_rows(tril, dt * rate_ref[...])
    a_rows = a.T
    lane_low = lax.broadcasted_iota(jnp.int32, (length, 128), 1) < WIDTH
    dt_x = spread(dt, pairs, lane_low)
    a_x = spread(a, pairs, lane_low)
    x = v * dt_x
    xb = x.astype(BF)
    scores = jnp.where(causal, nt(cb, bb), 0.0)
    inside = []
    zero = jnp.zeros((length, 128), BF)
    for p in range(pairs):
        xp = xb[:, 128 * p : 128 * (p + 1)]
        total = None
        for j in range(2):
            h = 2 * p + j
            decay = jnp.exp(jnp.minimum(a[:, h : h + 1] - a_rows[h : h + 1, :], 0.0))
            m = (scores * decay).astype(BF)
            term = nn(m, jnp.where(lane_low, xp, zero) if j == 0 else jnp.where(lane_low, zero, xp))
            total = term if total is None else total + term
        inside.append(total)
    entering = state[...]
    ent_ref[0] = entering
    outside = jnp.exp(a_x) * nn(cb, entering.astype(BF))
    a_last = a_x[length - 1 : length, :]
    xw = (x * jnp.exp(a_last - a_x)).astype(BF)
    state[...] = jnp.exp(a_last) * entering + nn(bc[:, :half].T.astype(BF), xw)
    y = jnp.concatenate(inside, axis=1) + outside + skip_ref[...] * v
    y_ref[...] = y
    _, sgate = silu_parts(gate_ref[...])
    gated = y * sgate
    square = (gated * gated).astype(BF)
    ssq_ref[...] = nt(jnp.ones((8, inner), BF), square)
    mixed = (gated * gg_ref[...]).astype(BF)
    part_ref[...] = nt(mixed, wot_ref[...]).astype(BF)
    if last:
        dm = nn(gb_ref[...], wot_ref[...])
        dm_ref[...] = dm
        dots = nt(jnp.ones((8, inner), BF), (dm * gg_ref[...] * gated).astype(BF))
        row = lax.broadcasted_iota(jnp.int32, dots.shape, 0)
        ssq_ref[...] = jnp.where(row == 0, ssq_ref[...], dots)


def whole(shape):
    return pl.BlockSpec(shape, lambda i: (0,) * len(shape), pipeline_mode=pl.Buffered(1))


def layer_specs(params, l):
    return [
        pl.BlockSpec((1,) + p.shape[1:], lambda i: (l, 0, 0), pipeline_mode=pl.Buffered(1))
        for p in params[:-1]
    ] + [whole(params[-1].shape)]


def forward_mix(rows, packed, params, l, gb=None):
    first, last = l == 0, gb is not None
    tokens, width = rows.shape
    inner = params[0].shape[2]
    bc_width = params[1].shape[2]
    dt_width = 128
    half = bc_width // 2
    q = GROUP
    blocks = tokens // q
    tok = lambda n: pl.BlockSpec((q, n), lambda i: (i, 0))
    outs = [
        ((tokens, inner), F32, tok(inner)),
        ((tokens, inner), F32, tok(inner)),
        ((tokens, bc_width), F32, tok(bc_width)),
        ((tokens, dt_width), F32, tok(dt_width)),
        ((tokens, inner), F32, tok(inner)),
        ((blocks, half, inner), F32, pl.BlockSpec((1, half, inner), lambda i: (i, 0, 0))),
        ((tokens, inner), F32, tok(inner)),
        ((tokens, width), BF, tok(width)),
        ((8, tokens), F32, pl.BlockSpec((8, q), lambda i: (0, i))),
    ]
    if first:
        outs.append(((tokens, width), BF, tok(width)))
    if last:
        outs.append(((tokens, inner), F32, tok(inner)))
    return pl.pallas_call(
        functools.partial(fwd_kernel, first, last),
        grid=(blocks,),
        in_specs=[tok(width), whole(packed.shape)]
        + layer_specs(params, l)
        + ([tok(width)] if last else []),
        out_specs=[o[2] for o in outs],
        out_shape=[jax.ShapeDtypeStruct(o[0], o[1]) for o in outs],
        scratch_shapes=[
            pltpu.VMEM((half, inner), F32),
            pltpu.VMEM((q + 8, inner), F32),
            pltpu.VMEM((q + 8, bc_width), F32),
        ],
        compiler_params=pltpu.CompilerParams(
            dimension_semantics=("arbitrary",), vmem_limit_bytes=56 * MIB
        ),
        name="mix_forward",
    )(rows, packed, *params, *([gb] if last else []))


def bwd_kernel(
    ready, layer, gb_ref, e_ref, rows_ref, gate_ref, val_ref, st_ref, stp_ref, dt_ref, y_ref,
    ent_ref, pre_ref, w_ref, vec_ref, cst_ref, tiny_ref, gain_ref, pick_ref, *rest,
):
    if not ready:
        res_ref, total_ref, scale_ref, *rest = rest
    dcat_ref, dpart_ref, gvec_ref, gst_ref, gdt_ref, ggain_ref, *rest = rest
    if not ready:
        hidden_ref, *rest = rest
        hidden_ref[...] = res_ref[...] + scale_ref[:, 0:1] * total_ref[...].astype(F32)
    dstate, spad, dvpad, dspad = rest
    step = pl.program_id(0)
    blocks = pl.num_programs(0)
    length = gb_ref.shape[0]
    cv_ref, cvb_ref, skip_ref, gg_ref, cs_ref, csb_ref, sb_ref, rate_ref = small_refs(
        vec_ref, cst_ref, tiny_ref
    )
    inner = gg_ref.shape[1]
    bc_width = cs_ref.shape[1]
    wbc_ref, wdt_ref, wz_ref, wx_ref, wot_ref = blocks_of(w_ref, inner, bc_width)
    dst_ref, ddt_ref, dgate_ref, dval_ref, mixed_ref = blocks_of(dcat_ref, inner, bc_width)
    half = bc_width // 2
    pairs = inner // 128

    @pl.when(step == 0)
    def _():
        dstate[...] = jnp.zeros_like(dstate)
        dvpad[length : length + 8, :] = jnp.zeros((8, inner), F32)
        dspad[length : length + 8, :] = jnp.zeros((8, bc_width), F32)
        gvec_ref[...] = jnp.zeros_like(gvec_ref)
        gst_ref[...] = jnp.zeros_like(gst_ref)
        gdt_ref[...] = jnp.zeros_like(gdt_ref)
        ggain_ref[...] = jnp.zeros_like(ggain_ref)

    @pl.when(step > 0)
    def _():
        dvpad[length : length + 8, :] = dvpad[0:8, :]
        dspad[length : length + 8, :] = dspad[0:8, :]

    first = step == blocks - 1
    spad[0:8, :] = jnp.where(first, 0.0, stp_ref[...])
    spad[8 : length + 8, :] = st_ref[...]

    pre_v = pre_ref[...]
    sig_v, v = silu_parts(pre_v)
    pre_s = conv_pre(spad, cs_ref, csb_ref[...], length)
    sig_s, bc = silu_parts(pre_s)
    bb = bc[:, :half].astype(BF)
    cb = bc[:, half:].astype(BF)
    z = dt_ref[...] + sb_ref[...]
    dt = softplus(z)
    rate = rate_ref[...]
    s_index = lax.broadcasted_iota(jnp.int32, (length, length), 0)
    q_index = lax.broadcasted_iota(jnp.int32, (length, length), 1)
    upper = q_index >= s_index
    a = sum_rows(jnp.where(s_index >= q_index, 1.0, 0.0).astype(BF), dt * rate)
    a_rows = a.T
    lane_low = lax.broadcasted_iota(jnp.int32, (length, 128), 1) < WIDTH
    dt_x = spread(dt, pairs, lane_low)
    a_x = spread(a, pairs, lane_low)
    x = v * dt_x
    xb = x.astype(BF)
    skip = skip_ref[...]

    y = y_ref[...]
    gate = gate_ref[...]
    sig_g, sgate = silu_parts(gate)
    gated = y * sgate
    per_token = e_ref[...].T
    e, r2 = per_token[:, 0:1], per_token[:, 1:2]
    dm = (gb_ref[...] if ready else nn(gb_ref[...], wot_ref[...])) * r2
    dgated = dm * gg_ref[...] - e * gated
    mixed_ref[...] = (gated * r2 * gg_ref[...]).astype(BF)
    dgate = (dgated * y * (sig_g * (1.0 + gate * (1.0 - sig_g)))).astype(BF)
    dgate_ref[...] = dgate
    dy = dgated * sgate
    dyb = dy.astype(BF)
    dyf = dyb.astype(F32)

    scores = jnp.where(upper, nt(bb, cb), 0.0)
    zero = jnp.zeros((length, 128), BF)
    dscores = jnp.zeros((length, length), F32)
    dx_list = []
    for p in range(pairs):
        xp = xb[:, 128 * p : 128 * (p + 1)]
        dp = dyb[:, 128 * p : 128 * (p + 1)]
        total = None
        for j in range(2):
            h = 2 * p + j
            decay = jnp.exp(jnp.minimum(a_rows[h : h + 1, :] - a[:, h : h + 1], 0.0))
            m = (scores * decay).astype(BF)
            dh = jnp.where(lane_low, dp, zero) if j == 0 else jnp.where(lane_low, zero, dp)
            term = nn(m, dh)
            total = term if total is None else total + term
            dscores = dscores + nt(xp, dh) * decay
        dx_list.append(total)
    dx_in = jnp.concatenate(dx_list, axis=1)
    dscores = jnp.where(upper, dscores, 0.0)
    db = nn(dscores.astype(BF), cb)
    dc = nn(dscores.T.astype(BF), bb)

    entering = ent_ref[0]
    dleaving = dstate[...]
    dleaving_b = dleaving.astype(BF)
    ea = jnp.exp(a_x)
    a_last = a_x[length - 1 : length, :]
    ea_last = jnp.exp(a_last)
    w = jnp.exp(a_last - a_x)
    dxw = nn(bb, dleaving_b) * w
    db = db + nt((x * w).astype(BF), dleaving_b)
    eady = (ea * dyf).astype(BF)
    dc = dc + nt(eady, entering.astype(BF))
    dstate[...] = ea_last * dleaving + nn(bc[:, half:].T.astype(BF), eady)
    dx = dx_in + dxw
    u = x * dxw
    last_add = jnp.sum(u, axis=0, keepdims=True) + ea_last * jnp.sum(
        entering * dleaving, axis=0, keepdims=True
    )
    da_x = dyf * (y - skip * v) - xb.astype(F32) * dx_in - u
    row_index = lax.broadcasted_iota(jnp.int32, (length, inner), 0)
    da_x = da_x + jnp.where(row_index == length - 1, last_add, 0.0)
    pick = pick_ref[...]
    da = sum_lanes(da_x, pick)
    dr = sum_rows(jnp.where(upper, 1.0, 0.0).astype(BF), da)
    ddt = sum_lanes(dx * v, pick) + dr * rate
    dz = ddt * (1.0 / (1.0 + jnp.exp(-z)))
    ddtb = dz.astype(BF)
    ddt_ref[...] = ddtb
    gdt_ref[0:1, :] += jnp.sum(dz, axis=0, keepdims=True)
    gdt_ref[1:2, :] += jnp.sum(dr * dt * rate, axis=0, keepdims=True)

    dpre_v = (skip * dy + dt_x * dx) * (sig_v * (1.0 + pre_v * (1.0 - sig_v)))
    dvpad[0:length, :] = dpre_v
    dval = jnp.zeros((length, inner), F32)
    val = val_ref[...]
    for k in range(4):
        later = dvpad[pl.ds(3 - k, length), :]
        dval = dval + cv_ref[k : k + 1, :] * later
        gvec_ref[k : k + 1, :] += jnp.sum(later * val, axis=0, keepdims=True)
    gvec_ref[4:5, :] += jnp.sum(dpre_v, axis=0, keepdims=True)
    gvec_ref[5:6, :] += jnp.sum(gated * dm, axis=0, keepdims=True)
    gvec_ref[6:7, :] += jnp.sum(dy * v, axis=0, keepdims=True)
    dvalb = dval.astype(BF)
    dval_ref[...] = dvalb

    dbc = jnp.concatenate([db, dc], axis=1)
    dpre_s = dbc * (sig_s * (1.0 + pre_s * (1.0 - sig_s)))
    dspad[0:length, :] = dpre_s
    dst = jnp.zeros((length, bc_width), F32)
    st = st_ref[...]
    for k in range(4):
        later = dspad[pl.ds(3 - k, length), :]
        dst = dst + cs_ref[k : k + 1, :] * later
        gst_ref[k : k + 1, :] += jnp.sum(later * st, axis=0, keepdims=True)
    gst_ref[4:5, :] += jnp.sum(dpre_s, axis=0, keepdims=True)
    dstb = dst.astype(BF)
    dst_ref[...] = dstb
    dpart = nt(dgate, wz_ref[...]) + nt(dvalb, wx_ref[...])
    dpart = dpart + nt(dstb, wbc_ref[...]) + nt(ddtb, wdt_ref[...])
    dpart_ref[...] = dpart.astype(BF)
    ggain_ref[0:1, :] += jnp.sum(rows_ref[...].astype(F32) * dpart, axis=0, keepdims=True)

    @pl.when(step == blocks - 1)
    def _():
        ggain_ref[0:1, :] = ggain_ref[0:1, :] / gain_ref[2 * layer : 2 * layer + 1, :]


def backward_mix(gb, ready, e_rows, rows, kept, packed, params, pick, l, last=()):
    gate, val, st, dt, y, ent, pre = kept
    tokens, width = gb.shape[0], packed.shape[0]
    inner = params[0].shape[2]
    bc_width = params[1].shape[2]
    dt_width = 128
    packed_width = packed.shape[1]
    half = bc_width // 2
    q = GROUP
    blocks = tokens // q
    back = lambda i: blocks - 1 - i
    tok = lambda n: pl.BlockSpec((q, n), lambda i: (back(i), 0))
    halo = lambda n: pl.BlockSpec(
        (8, n), lambda i: (jnp.maximum(back(i) * (q // 8) - 1, 0), 0)
    )
    fixed = lambda r, c: pl.BlockSpec((r, c), lambda i: (0, 0))
    outs = [
        ((tokens, packed_width), BF, tok(packed_width)),
        ((tokens, width), BF, tok(width)),
        ((8, inner), F32, fixed(8, inner)),
        ((8, bc_width), F32, fixed(8, bc_width)),
        ((8, dt_width), F32, fixed(8, dt_width)),
        ((8, width), F32, fixed(8, width)),
    ]
    few = [pl.BlockSpec((v.shape[0] // blocks, v.shape[1]), lambda i: (i, 0)) for v in last]
    if last:
        outs.append((last[0].shape, F32, few[0]))
    return pl.pallas_call(
        functools.partial(bwd_kernel, ready, l),
        grid=(blocks,),
        in_specs=[
            tok(gb.shape[1]),
            pl.BlockSpec((8, q), lambda i: (0, back(i))),
            tok(width),
            tok(inner), tok(inner), tok(bc_width), halo(bc_width), tok(dt_width),
            tok(inner),
            pl.BlockSpec((1, half, inner), lambda i: (back(i), 0, 0)),
            tok(inner),
        ]
        + [whole(packed.shape)] + layer_specs(params, l) + [whole(pick.shape)] + few,
        out_specs=[o[2] for o in outs],
        out_shape=[jax.ShapeDtypeStruct(o[0], o[1]) for o in outs],
        scratch_shapes=[
            pltpu.VMEM((half, inner), F32),
            pltpu.VMEM((q + 8, bc_width), F32),
            pltpu.VMEM((q + 8, inner), F32),
            pltpu.VMEM((q + 8, bc_width), F32),
        ],
        compiler_params=pltpu.CompilerParams(
            dimension_semantics=("arbitrary",), vmem_limit_bytes=60 * MIB
        ),
        name="mix_backward",
    )(gb, e_rows, rows, gate, val, st, st, dt, y, ent, pre, packed, *params, pick, *last)


class Step:
    def __init__(self, **given):
        self.rows = 0
        self.width = 0
        self.line = 4
        self.chunks = 8
        self.hop = 1
        self.pass_hop = 1
        self.slack = 0
        self.partial = False
        self.gather = False
        self.late = False
        self.scale = False
        self.inner = False
        self.layer = 0
        self.small = 0
        self.gain_row = 0
        self.weights = 0
        self.grads = 0
        self.tail = 2
        self.lag = 1
        self.states = 0
        self.sums = False
        self.bits = 0
        self.middle = None
        self.lazy = ()
        self.__dict__.update(given)


def remote(src, dst, send, recv, device):
    return pltpu.make_async_remote_copy(
        src_ref=src, dst_ref=dst, send_sem=send, recv_sem=recv,
        device_id=device, device_id_type=pl.DeviceIdType.MESH,
    )


def when(condition):
    return pl.when(condition)


def pack_weights(r, l):
    start = 0
    for part in (r.p_bc.at[l], r.p_dt.at[l], r.p_z.at[l], r.p_x.at[l], r.p_out.at[l]):
        r.wown[:, start : start + part.shape[1]] = part[...]
        start += part.shape[1]


def comm_kernel(o, names, *refs):
    r = types.SimpleNamespace(**dict(zip(names, refs)))
    r.gain_row = slice(o.gain_row, o.gain_row + 1)
    r.gbuf = [v for k, v in zip(names, refs) if k.startswith("gbuf")]
    n, count, rows = o.line, o.chunks, o.rows
    size = rows // count
    t = lax.axis_index("tensor")
    me = lax.axis_index("dp")
    own_bits = [(me // (1 << b)) % 2 for b in range(o.bits)]
    partner = [me + (1 - 2 * own_bits[b]) * (1 << b) for b in range(o.bits)]

    lazy = []
    for i, name in enumerate(o.lazy):
        near = getattr(r, name + "_v")
        lazy.append(pltpu.make_async_copy(getattr(r, name), near, r.lazy_sem.at[i]))
        setattr(r, name, near)
    for copy in lazy:
        copy.start()

    barrier = pltpu.get_barrier_semaphore()
    for k in range(1, n):
        pl.semaphore_signal(
            barrier, inc=1, device_id={"tensor": lax.rem(t + k, n)},
            device_id_type=pl.DeviceIdType.MESH,
        )
    over_dp = o.weights or o.grads
    r.early = [v for k, v in zip(names, refs) if k.startswith("esum")]
    r.lined = [v for k, v in zip(names, refs) if k.startswith("lsum")]
    r.gains = [v for k, v in zip(names, refs) if k.startswith("gsum")]
    if over_dp:
        for b in range(o.bits):
            pl.semaphore_signal(
                barrier, inc=1, device_id={"dp": partner[b]}, device_id_type=pl.DeviceIdType.MESH
            )
    pl.semaphore_wait(barrier, n - 1 + (o.bits if over_dp else 0))

    def at(s, c):
        return pl.ds(pl.multiple_of(s * rows + c * size, size), size)

    def piece(c):
        return pl.ds(pl.multiple_of(c * size, size), size)

    def hop(side, s, c, src):
        buf = r.rbuf if side == 0 else r.lbuf
        return remote(
            src, buf.at[s, piece(c)], r.rs_send.at[side, s], r.rs_recv.at[side, s, c],
            {"tensor": t + 1 if side == 0 else t - 1},
        )

    def reduce_items(side, c):
        buf = r.rbuf if side == 0 else r.lbuf
        edge = t == 0 if side == 0 else t == n - 1
        order = range(n - 1, 0, -1) if side == 0 else range(0, n - 1)
        for s in order:
            further = s > t if side == 0 else s < t

            @when(further & edge)
            def _():
                hop(side, s, c, r.part.at[at(s, c)]).start()

            @when(further & jnp.logical_not(edge))
            def _():
                hop(side, s, c, buf.at[s, piece(c)]).wait_recv()
                total = buf[s, piece(c), :].astype(F32) + r.part[at(s, c), :].astype(F32)
                buf[s, piece(c), :] = total.astype(BF)
                hop(side, s, c, buf.at[s, piece(c)]).start()

    def own_total(c):
        acc = r.acc
        acc[...] = r.part[at(t, c), :].astype(F32)

        @when(t > 0)
        def _():
            hop(0, t, c, r.rbuf.at[t, piece(c)]).wait_recv()
            acc[...] += r.rbuf[t, piece(c), :].astype(F32)

        @when(t < n - 1)
        def _():
            hop(1, t, c, r.lbuf.at[t, piece(c)]).wait_recv()
            acc[...] += r.lbuf[t, piece(c), :].astype(F32)

    def pass_on(side, s, c):
        spot = r.full.at[at(s, c)]
        return remote(
            spot, spot, r.ag_send.at[side, s], r.ag_recv.at[side, s, c],
            {"tensor": t + 1 if side == 0 else t - 1},
        )

    def forward_items(side, tau):
        order = range(n - 2, -1, -1) if side == 0 else range(1, n)
        for s in order:
            away = t - s if side == 0 else s - t
            late = o.hop * max(s, n - 1 - s) + o.slack if o.late else 0
            c = tau - late - o.pass_hop * away

            @when((away > 0) & (c >= 0) & (c < count))
            def _():
                pass_on(side, s, c).wait_recv()

                @when(t < n - 1 if side == 0 else t > 0)
                def _():
                    pass_on(side, s, c).start()

    def spot_of(k, ref):
        return ref.at[:, pl.ds(pl.multiple_of(k * rows, rows), rows)]

    def square_copy(k):
        dest = lax.rem(t + k, n)
        return remote(
            spot_of(dest, r.ssq), r.sqbuf.at[k - 1], r.sq_send.at[k - 1],
            r.sq_recv.at[k - 1], {"tensor": dest},
        )

    def inner_copy(k):
        return remote(
            spot_of(t, r.inner), spot_of(t, r.inner), r.in_send.at[k - 1],
            r.in_recv.at[k - 1], {"tensor": lax.rem(t + k, n)},
        )

    def inner_arrival(k):
        source = lax.rem(t + n - k, n)
        return remote(
            spot_of(source, r.inner), spot_of(source, r.inner), r.in_send.at[k - 1],
            r.in_recv.at[k - 1], {"tensor": source},
        )

    def bit_order(parity):
        high = list(range(o.bits - 1, 0, -1))
        if parity == 1:
            high = high[1:] + high[:1]
        return high + [0]

    def cols(j):
        return pl.ds(pl.multiple_of(j * WCHUNK, WCHUNK), WCHUNK)

    def spots(known):
        return tuple(slice(None) if b in known else own_bits[b] for b in range(o.bits - 1, -1, -1))

    def weight_copy(parity, stage, j):
        order = bit_order(parity)
        depth = r.wown.shape[0] // o.weights
        strip = pl.ds(pl.multiple_of(j * depth, depth), depth)
        spot = r.wfull.at[(*spots(order[:stage]), strip)]
        src = r.wown.at[strip] if stage == 0 else spot
        return remote(
            src, spot, r.wg_send.at[stage, j], r.wg_recv.at[stage, j],
            {"dp": partner[order[stage]]},
        )

    def small_columns():
        lanes_at = pl.ds(o.small // 128 * 128, 128)
        return pltpu.make_async_copy(
            r.wfull.at[(*spots(range(o.bits)), slice(None), lanes_at)], r.columns, r.small_sem
        )

    def small_items(tau):
        done = (o.weights + 1) // 2 + o.bits

        @when(tau == done)
        def _():
            small_columns().start()

        @when(tau == done + 1)
        def _():
            small_columns().wait()
            turned = r.columns[...].reshape(o.width, 128).astype(F32).T
            r.small[...] = turned[o.small % 128 : o.small % 128 + 8, :]

    def own_weights():
        return pltpu.make_async_copy(r.wown, r.wfull.at[spots([])], r.wl_sem)

    def each_parity(pair, fn):
        for parity in range(2):
            j = 2 * pair + parity

            @when((j >= 0) & (j < o.weights))
            def _():
                fn(parity, j)

    def weight_items(tau):
        for stage in range(o.bits + 1):
            def run(parity, j):
                if stage > 0:
                    weight_copy(parity, stage - 1, j).wait_recv()
                if stage < o.bits:
                    weight_copy(parity, stage, j).start()
            each_parity(tau - stage, run)

    def grad_order(parity):
        high = list(range(1, o.bits))
        if parity == 1:
            high = high[1:] + high[:1]
        return [0] + high

    def grad_spot(parity, stage, mine):
        order = grad_order(parity)
        done, bit = order[:stage], order[stage]
        spot = []
        for b in range(o.bits - 1, -1, -1):
            if b in done:
                spot.append(own_bits[b])
            elif b == bit:
                spot.append(own_bits[b] if mine else 1 - own_bits[b])
            else:
                spot.append(slice(None))
        return tuple(spot)

    def grad_copy(parity, stage, j):
        order = grad_order(parity)
        return remote(
            r.grad.at[(j, *grad_spot(parity, stage, False))], r.gbuf[stage].at[j],
            r.gr_send.at[stage, j], r.gr_recv.at[stage, j],
            {"dp": partner[order[stage]]},
        )

    def product(j, i):
        slab = o.width // 2
        inner_shape = (2,) * (o.bits - 1) + (slab >> (o.bits - 1), WCHUNK)

        def one(left):
            out = tn(left[:, pl.ds(i * slab, slab)], r.right[:, cols(j)])
            r.grad[j, i] = out.astype(BF).reshape(inner_shape)

        @when((j >= 0) & (j < o.grads - o.tail))
        def _():
            one(r.lrows)

        @when((j >= o.grads - o.tail) & (j < o.grads))
        def _():
            one(r.lgrad)

    def each_chunk(j, fn):
        for parity in range(2):
            @when((j >= 0) & (j < o.grads) & (lax.rem(j, 2) == parity))
            def _():
                fn(parity, j)

    def grad_items(tau):
        product(tau, 1)

        def first(parity, j):
            grad_copy(parity, 0, j).start()

        each_chunk(tau, first)
        for stage in range(1, o.bits + 1):
            def run(parity, j):
                grad_copy(parity, stage - 1, j).wait_recv()
                spot = grad_spot(parity, stage - 1, True)
                free = [i for i, v in enumerate(spot) if isinstance(v, slice)]
                buf = r.gbuf[stage - 1]
                for combo in range(1 << len(free)):
                    pick = [(combo >> i) % 2 for i in range(len(free))]
                    full = list(spot)
                    for i, v in zip(free, pick):
                        full[i] = v
                    total = r.grad[(j, *full)].astype(F32) + buf[(j, *pick)].astype(F32)
                    if stage < o.bits:
                        r.grad[(j, *full)] = total.astype(BF)
                    else:
                        r.gout[:, cols(j)] = total
                if stage < o.bits:
                    grad_copy(parity, stage, j).start()
            each_chunk(tau - grad_lag(stage), run)

    def grad_lag(stage):
        return o.lag * (2 * stage - 1) if stage else 0

    def share(buf, send, recv, k):
        return remote(buf.at[t], buf.at[t], send.at[k - 1], recv.at[k - 1],
                      {"tensor": lax.rem(t + k, n)})

    def shared(buf, send, recv):
        for k in range(1, n):
            source = lax.rem(t + n - k, n)
            remote(buf.at[source], buf.at[source], send.at[k - 1], recv.at[k - 1],
                   {"tensor": source}).wait_recv()

    def line_total(buf):
        total = buf[0]
        for k in range(1, n):
            total = total + buf[k]
        return total

    def double(acc, buf, send, recv, b):
        return remote(acc.at[b], buf.at[b], send.at[b], recv.at[b], {"dp": partner[b]})

    def doubled(acc, buf, send, recv, b):
        double(acc, buf, send, recv, b).wait_recv()
        acc[b + 1] = acc[b] + buf[b]

    def lanes(index, ref):
        return slice(index * ref.shape[1], (index + 1) * ref.shape[1])

    line_groups, dp_groups = [], []
    if o.sums:
        line_groups = [(r.lbank, r.lb_send, r.lb_recv), (r.gbank, r.gb_send, r.gb_recv)]
        dp_groups = [
            (r.dbank, r.dbuf, r.db_send, r.db_recv), (r.hbank, r.hbuf, r.hb_send, r.hb_recv)
        ]

    def sum_items(tau):
        @when(tau == 2)
        def _():
            for g in line_groups:
                shared(*g)
            off = 0
            for v in r.early:
                r.dbank[0, :, off : off + v.shape[1]] = v[...]
                off += v.shape[1]
            r.dbank[0, :, off:] = line_total(r.lbank)
            r.hbank[0] = line_total(r.gbank)
            for g in dp_groups:
                double(*g, 0).start()

        for b in range(o.bits):
            @when(tau == 4 + b)
            def _():
                for g in dp_groups:
                    doubled(*g, b)
                    if b < o.bits - 1:
                        double(*g, b + 1).start()

    def state_items(tau):
        at_first = grad_lag(o.bits) + 1
        quarter = r.gout.shape[0] // n

        @when(tau == at_first)
        def _():
            for s in range(n):
                r.qsend[s] = r.gout[s * quarter : (s + 1) * quarter, 0 : o.states].astype(BF)
            for k in range(1, n):
                state_out(k).start()

        @when(tau == at_first + 2)
        def _():
            total = r.qsend[t].astype(F32)
            for k in range(1, n):
                state_out(k).wait_recv()
                total = total + r.qbuf[k - 1].astype(F32)
            r.qall[t] = total.astype(BF)
            for k in range(1, n):
                share(r.qall, r.qa_send, r.qa_recv, k).start()

    def state_out(k):
        dest = lax.rem(t + k, n)
        return remote(r.qsend.at[dest], r.qbuf.at[k - 1], r.qs_send.at[k - 1],
                      r.qs_recv.at[k - 1], {"tensor": dest})

    if o.sums:
        off = 0
        for v in r.lined:
            r.lbank[t, :, off : off + v.shape[1]] = v[...]
            off += v.shape[1]
        for i, v in enumerate(r.gains):
            r.gbank[t, :, lanes(i, v)] = v[0:1, :]
        for g in line_groups:
            for k in range(1, n):
                share(*g, k).start()
    if o.scale:
        for k in range(1, n):
            square_copy(k).start()
    if o.weights:
        pack_weights(r, o.layer)
        own_weights().start()
    if o.scale:
        total = spot_of(t, r.ssq)[...]
        for k in range(1, n):
            square_copy(k).wait_recv()
            total = total + r.sqbuf[k - 1]
        scale = lax.rsqrt(total / (o.scale * 1.0) + EPSILON)
        r.r2[...] = jnp.broadcast_to(scale.T[:, 0:1], (rows, 128))
    if o.gather and not o.late:
        r.full[pl.ds(pl.multiple_of(t * rows, rows), rows), :] = o.payload(r)
    if o.middle is not None:
        o.middle(r, None, None)

    ends = [count + o.hop * (n - 1) + o.slack]
    if o.late:
        ends.append(ends[0] + o.pass_hop * (n - 1))
    elif o.gather:
        ends.append(count + o.pass_hop * (n - 1))
    if o.weights:
        ends.append((o.weights + 1) // 2 + o.bits + (2 if o.small else 0))
    if o.grads:
        ends.append(1 + o.grads + grad_lag(o.bits))
        ends.append(grad_lag(o.bits) + 5)
    if o.sums:
        ends.append(4 + o.bits)

    def iteration(tau, _):
        if lazy:
            @when(tau == 1)
            def _():
                for copy in lazy:
                    copy.wait()
        if o.grads:
            product(tau - 1, 0)
        if o.partial:
            for side in range(2):
                c = tau - o.hop * (t if side == 0 else n - 1 - t)

                @when((c >= 0) & (c < count))
                def _():
                    reduce_items(side, c)

            c_own = tau - o.hop * jnp.maximum(t, n - 1 - t) - o.slack

            @when((c_own >= 0) & (c_own < count))
            def _():
                own_total(c_own)
                out = o.middle(r, piece(c_own), r.acc[...])
                if o.late:
                    r.full[at(t, c_own), :] = out
        if o.gather:
            c_out = tau - o.hop * jnp.maximum(t, n - 1 - t) - o.slack if o.late else tau

            @when((c_out >= 0) & (c_out < count))
            def _():
                @when(t < n - 1)
                def _():
                    pass_on(0, t, c_out).start()

                @when(t > 0)
                def _():
                    pass_on(1, t, c_out).start()

            for side in range(2):
                forward_items(side, tau)
        if o.weights:
            @when(tau == 1)
            def _():
                own_weights().wait()
            weight_items(tau)
            if o.small:
                small_items(tau)
        if o.grads:
            grad_items(tau - 1)
            state_items(tau - 1)
        if o.sums:
            sum_items(tau)
        return 0

    lax.fori_loop(0, max(ends), iteration, 0)

    if o.inner:
        spot_of(t, r.inner)[...] = r.icol[...].T[0:8, :]
        for k in range(1, n):
            inner_copy(k).start()
        for k in range(1, n):
            inner_arrival(k).wait_recv()
        for k in range(1, n):
            inner_copy(k).wait_send()
    if o.sums:
        r.sums[...] = r.dbank[o.bits]
        for i, v in enumerate(r.gains):
            r.gain_sums[i : i + 1, :] = r.hbank[o.bits, :, lanes(i, v)]
        for g in line_groups:
            for k in range(1, n):
                share(*g, k).wait_send()
        for g in dp_groups:
            for b in range(o.bits):
                double(*g, b).wait_send()
    if o.grads:
        shared(r.qall, r.qa_send, r.qa_recv)
        quarter = r.gout.shape[0] // n
        for s in range(n):
            r.gout[s * quarter : (s + 1) * quarter, 0 : o.states] = r.qall[s].astype(F32)
        for k in range(1, n):
            state_out(k).wait_send()
            share(r.qall, r.qa_send, r.qa_recv, k).wait_send()
    if o.scale:
        for k in range(1, n):
            square_copy(k).wait_send()
    for s in range(n):
        for side in range(2):
            inside = t < n - 1 if side == 0 else t > 0
            if o.partial:
                @when((s > t if side == 0 else s < t) & inside)
                def _():
                    buf = (r.rbuf if side == 0 else r.lbuf).at[s]
                    remote(
                        buf, buf, r.rs_send.at[side, s], r.rs_recv.at[side, s, 0],
                        {"tensor": t + 1 if side == 0 else t - 1},
                    ).wait_send()
            if o.gather:
                @when((s <= t if side == 0 else s >= t) & inside)
                def _():
                    spot = r.full.at[pl.ds(s * rows, rows)]
                    remote(
                        spot, spot, r.ag_send.at[side, s], r.ag_recv.at[side, s, 0],
                        {"tensor": t + 1 if side == 0 else t - 1},
                    ).wait_send()
    for j in range(o.weights):
        for stage in range(o.bits):
            weight_copy(j % 2, stage, jnp.int32(j)).wait_send()
    for j in range(o.grads):
        for stage in range(o.bits):
            grad_copy(j % 2, stage, jnp.int32(j)).wait_send()


def comm_call(o, name, collective, inputs, outputs, **scratch):
    n, count, rows, width = o.line, o.chunks, o.rows, o.width
    dma = pltpu.SemaphoreType.DMA
    if o.lazy:
        for key in o.lazy:
            value = inputs[key][0]
            inputs[key] = (value, pl.ANY)
            scratch[key + "_v"] = pltpu.VMEM(value.shape, value.dtype)
        scratch.update(lazy_sem=dma((len(o.lazy),)))
    if o.partial:
        scratch.update(
            rbuf=pltpu.VMEM((n, rows, width), BF),
            lbuf=pltpu.VMEM((n, rows, width), BF),
            acc=pltpu.VMEM((rows // count, width), F32),
            rs_send=dma((2, n)),
            rs_recv=dma((2, n, count)),
        )
    if o.gather:
        scratch.update(ag_send=dma((2, n)), ag_recv=dma((2, n, count)))
    if o.scale:
        scratch.update(
            sqbuf=pltpu.VMEM((n - 1, 8, rows), F32), sq_send=dma((n - 1,)), sq_recv=dma((n - 1,))
        )
    if o.inner:
        scratch.update(
            icol=pltpu.VMEM((rows, 128), F32), in_send=dma((n - 1,)), in_recv=dma((n - 1,))
        )
    if o.weights:
        rows_of_pack = inputs["p_bc"][0].shape[1]
        pack_width = sum(v[0].shape[2] for k, v in inputs.items() if k.startswith("p_"))
        scratch.update(
            columns=pltpu.VMEM((*(2,) * o.bits, rows_of_pack, 128), BF),
            small_sem=dma(()),
            wown=pltpu.VMEM((rows_of_pack, pack_width), BF),
            wl_sem=dma(()),
            wg_send=dma((o.bits, o.weights)),
            wg_recv=dma((o.bits, o.weights)),
        )
    if o.grads:
        depth = o.width >> o.bits
        scratch.update(
            grad=pltpu.VMEM((o.grads, *(2,) * o.bits, depth, WCHUNK), BF),
            gr_send=dma((o.bits, o.grads)),
            gr_recv=dma((o.bits, o.grads)),
        )
        for stage in range(o.bits):
            scratch["gbuf%d" % stage] = pltpu.VMEM(
                (o.grads, *(2,) * (o.bits - 1 - stage), depth, WCHUNK), BF
            )
        part = (n, (width >> o.bits) // n, o.states)
        scratch.update(
            qsend=pltpu.VMEM(part, BF), qall=pltpu.VMEM(part, BF),
            qbuf=pltpu.VMEM((n - 1,) + part[1:], BF),
            qs_send=dma((n - 1,)), qs_recv=dma((n - 1,)),
            qa_send=dma((n - 1,)), qa_recv=dma((n - 1,)),
        )
    if o.sums:
        def lanes_of(start):
            return sum(v[0].shape[1] for k, v in inputs.items() if k.startswith(start))

        lined, early, gains = lanes_of("lsum"), lanes_of("esum"), lanes_of("gsum")
        for one, two, tall, line_width, dp_width in (
            ("lb", "db", 8, lined, lined + early), ("gb", "hb", 1, gains, gains)
        ):
            scratch[one + "ank"] = pltpu.VMEM((n, tall, line_width), F32)
            scratch[two + "ank"] = pltpu.VMEM((o.bits + 1, tall, dp_width), F32)
            scratch[two + "uf"] = pltpu.VMEM((o.bits, tall, dp_width), F32)
            for key, size in ((one, n - 1), (two, o.bits)):
                scratch[key + "_send"] = dma((size,))
                scratch[key + "_recv"] = dma((size,))
    names = [*inputs, *outputs, *scratch]
    out = pl.pallas_call(
        functools.partial(comm_kernel, o, names),
        in_specs=[pl.BlockSpec(memory_space=i[1]) for i in inputs.values()],
        out_specs=[pl.BlockSpec(memory_space=i[2]) for i in outputs.values()],
        out_shape=[jax.ShapeDtypeStruct(i[0], i[1]) for i in outputs.values()],
        scratch_shapes=list(scratch.values()),
        compiler_params=pltpu.CompilerParams(
            collective_id=collective, has_side_effects=True, vmem_limit_bytes=62 * MIB
        ),
        name=name,
    )(*[i[0] for i in inputs.values()])
    return dict(zip(outputs, out))


def meet_kernel(n, inner_all, own_ref, out_ref, scale_ref, bank, send, recv):
    t = lax.axis_index("tensor")
    barrier = pltpu.get_barrier_semaphore()
    for k in range(1, n):
        pl.semaphore_signal(
            barrier, inc=1, device_id={"tensor": lax.rem(t + k, n)},
            device_id_type=pl.DeviceIdType.MESH,
        )
    pl.semaphore_wait(barrier, n - 1)
    copies = [
        remote(own_ref, bank.at[t], send.at[k - 1], recv.at[k - 1], {"tensor": lax.rem(t + k, n)})
        for k in range(1, n)
    ]
    for copy in copies:
        copy.start()
    bank[t] = own_ref[...]
    for k in range(1, n):
        source = lax.rem(t + n - k, n)
        remote(
            own_ref, bank.at[source], send.at[k - 1], recv.at[k - 1], {"tensor": source}
        ).wait_recv()
    total = bank[0]
    for s in range(1, n):
        total = total + bank[s]
    scale = lax.rsqrt(total[0:1, :] / inner_all + EPSILON)
    row = lax.broadcasted_iota(jnp.int32, total.shape, 0)
    e = scale * scale * scale * (total[1:2, :] / inner_all)
    out_ref[...] = jnp.where(row == 0, e, scale)
    rows = scale_ref.shape[0]
    mine = out_ref[:, pl.ds(pl.multiple_of(t * rows, rows), rows)].T
    scale_ref[...] = jnp.broadcast_to(mine[:, 1:2], scale_ref.shape)
    for copy in copies:
        copy.wait_send()


def meet(own, n, inner_all, collective):
    vmem = pl.BlockSpec(memory_space=pltpu.VMEM)
    dma = pltpu.SemaphoreType.DMA
    return pl.pallas_call(
        functools.partial(meet_kernel, n, inner_all),
        in_specs=[vmem],
        out_specs=[vmem, vmem],
        out_shape=[
            jax.ShapeDtypeStruct(own.shape, F32),
            jax.ShapeDtypeStruct((own.shape[1] // n, 128), F32),
        ],
        scratch_shapes=[pltpu.VMEM((n,) + own.shape, F32), dma((n - 1,)), dma((n - 1,))],
        compiler_params=pltpu.CompilerParams(collective_id=collective, has_side_effects=True),
        name="turn_around",
    )(own)


def plain_payload(r):
    return r.own[...]


def token_columns(first, second):
    lane = lax.broadcasted_iota(jnp.int32, (first.shape[0], 128), 1)
    return jnp.where(lane == 0, first, second)


def forward_middle(r, at, total):
    if at is None:
        return None
    branch = total * r.r2[at, 0:1]
    residual = r.res[at, :].astype(F32) + branch
    r.branch[at, :] = branch
    r.res_out[at, :] = residual
    r1 = lax.rsqrt(jnp.mean(residual * residual, axis=1, keepdims=True) + EPSILON)
    return (residual * r1 * r.gain[r.gain_row, :]).astype(BF)


def backward_middle(inner_all, r, at, total):
    if at is None:
        return None
    res = r.res[at, :].astype(F32)
    width = res.shape[1]
    r1 = lax.rsqrt(jnp.mean(res * res, axis=1, keepdims=True) + EPSILON)
    hat = res * r1
    dn = total * r.gain[r.gain_row, :]
    cross = jnp.sum(dn * hat, axis=1, keepdims=True) / width
    grad = r.grad_in[at, :].astype(F32) + r1 * (dn - hat * cross)
    r.grad_out[at, :] = grad
    if inner_all is None:
        return None
    r2 = r.r2[at, 0:1]
    dot = jnp.sum(grad.astype(BF).astype(F32) * r.branch[at, :], axis=1, keepdims=True)
    r.icol[at, :] = token_columns(r2 * r2 * dot / inner_all, r2)
    return grad.astype(BF)


def assemble_kernel(layers, dp_count, heads, bc_width, inner, *refs):
    gouts, (sums, gains, pick), outs = refs[:layers], refs[layers : layers + 3], refs[layers + 3 :]
    norm, gz, gx, gbc, gdt, cv, cvb, cs, csb, sb, ld, sk, gg, po = outs
    me = lax.axis_index("dp")

    def own(v):
        share = v.shape[1] // dp_count
        return pltpu.roll(v, v.shape[1] - me * share, 1)[:, :share]

    norm[...] = own(gains[...])[0:layers]
    for l in range(layers):
        full = gouts[l]
        first = bc_width + 128
        gbc[l] = full[:, 0:bc_width]
        gdt[:, l, :] = full[:, bc_width:first].T[0:heads, :]
        gz[l] = full[:, first : first + inner]
        gx[l] = full[:, first + inner : first + 2 * inner]
        po[l] = full[:, first + 2 * inner :]
        base = l * (inner + 128)
        vec = sums[:, base : base + inner]
        step = sums[:, base + inner : base + inner + 128]
        start = layers * (inner + 128) + l * bc_width
        state = own(sums[:, start : start + bc_width])
        cv[l] = vec[0:4]
        cvb[l : l + 1] = vec[4:5]
        gg[l : l + 1] = vec[5:6]
        one, two, three = parts3(vec)
        head_sums = nn(one, pick[...]) + nn(two, pick[...]) + nn(three, pick[...])
        sk[l : l + 1] = head_sums[6:7, 0:heads]
        sb[l : l + 1] = step[0:1, 0:heads]
        ld[l : l + 1] = step[1:2, 0:heads]
        cs[l] = state[0:4]
        csb[l : l + 1] = state[4:5]


def assemble(gouts, sums, gains, pick, dp_count, heads, bc_width, inner):
    layers, (rows, _) = len(gouts), gouts[0].shape
    vmem = pl.BlockSpec(memory_space=pltpu.VMEM)
    share = bc_width // dp_count
    shapes = [
        (layers, gains.shape[1] // dp_count),
        (layers, rows, inner), (layers, rows, inner), (layers, rows, bc_width),
        (heads, layers, rows), (layers, 4, inner), (layers, inner), (layers, 4, share),
        (layers, share), (layers, heads), (layers, heads), (layers, heads), (layers, inner),
        (layers, rows, inner),
    ]
    inputs = [*gouts, sums, gains, pick]
    return pl.pallas_call(
        functools.partial(assemble_kernel, layers, dp_count, heads, bc_width, inner),
        in_specs=[vmem] * len(inputs),
        out_specs=[vmem] * len(shapes),
        out_shape=[jax.ShapeDtypeStruct(v, F32) for v in shapes],
        compiler_params=pltpu.CompilerParams(vmem_limit_bytes=62 * MIB),
        name="assemble",
    )(*inputs)


def shards(
    hidden_in,
    out_grad,
    norm_gain,
    proj_z,
    proj_x,
    proj_bc,
    proj_dt,
    conv_value,
    conv_value_bias,
    conv_state,
    conv_state_bias,
    step_bias,
    log_decay,
    skip_gain,
    gate_gain,
    proj_out,
):
    tensor_count = lax.axis_size("tensor")
    dp_count = lax.axis_size("dp")
    bits = dp_count.bit_length() - 1
    layers, shard_rows, inner = proj_z.shape
    rows_own, width = hidden_in.shape
    tokens = rows_own * tensor_count
    heads = step_bias.shape[1]
    bc_width = proj_bc.shape[2]
    inner_all = inner * tensor_count
    packed_width = bc_width + 128 + 3 * inner
    column_chunks, row_chunks = packed_width // WCHUNK, shard_rows // 16
    vmem, far = pltpu.VMEM, pl.ANY

    small = jnp.concatenate([conv_state.reshape(layers, -1), conv_state_bias], axis=1)
    small = jnp.pad(small, ((0, 0), (0, shard_rows - small.shape[1])))
    extra = jnp.stack([norm_gain, small], axis=1).reshape(2 * layers, shard_rows).T
    step_block = jnp.concatenate(
        [
            proj_dt,
            jnp.broadcast_to(extra[None], (layers,) + extra.shape),
            jnp.zeros((layers, shard_rows, 128 - heads - 2 * layers), BF),
        ],
        axis=2,
    )
    out_turned = jnp.transpose(proj_out, (0, 2, 1))
    full_shape = ((2,) * bits) + (shard_rows, packed_width)
    common = dict(rows=rows_own, width=width, line=tensor_count, bits=bits)

    weight_in = dict(
        p_bc=(proj_bc, vmem), p_dt=(step_block, vmem), p_z=(proj_z, vmem), p_x=(proj_x, vmem),
        p_out=(out_turned, vmem),
    )
    weight_out = dict(wfull=(full_shape, BF, far))

    vec = jnp.concatenate(
        [
            conv_value,
            conv_value_bias[:, None],
            jnp.repeat(skip_gain, WIDTH, axis=1)[:, None],
            gate_gain[:, None],
        ],
        axis=1,
    ).astype(F32)
    tiny = jnp.stack([step_bias.astype(F32), -jnp.exp(log_decay.astype(F32))], axis=1)
    tiny = jnp.pad(tiny, ((0, 0), (0, 0), (0, 128 - heads)))
    pick = (jnp.arange(inner)[:, None] // WIDTH == jnp.arange(128)[None, :]).astype(BF)

    whole_rows, own_rows = ((tokens, width), BF, vmem), ((rows_own, width), F32, vmem)
    got = comm_call(
        Step(gather=True, payload=plain_payload, weights=row_chunks,
             small=bc_width + heads, **common),
        "gather_first", 1,
        dict(own=(hidden_in, vmem), **weight_in),
        dict(full=whole_rows, small=((8, width), F32, vmem), **weight_out),
    )
    x_rows = got["full"]
    out_grad, x_rows = lax.optimization_barrier((out_grad, x_rows))
    grad_rows = lax.all_gather(out_grad, "tensor", axis=0, tiled=True)
    packed = [got["wfull"].reshape(width, packed_width)]
    small = got["small"]
    per = bc_width // dp_count
    smalls = small[1 : 2 * layers : 2].reshape(layers, dp_count, shard_rows)[:, :, : 5 * per]
    cst = jnp.transpose(smalls.reshape(layers, dp_count, 5, per), (0, 2, 1, 3))
    cst = cst.reshape(layers, 5, bc_width)
    params = (vec, cst, tiny, small)

    out = forward_mix(x_rows, packed[0], params, 0)
    saved, rows = [out[:7]], [out[9]]
    residuals, branches, r2s = [hidden_in], [], []
    for l in range(layers - 1):
        got = comm_call(
            Step(
                partial=True, gather=True, late=True, scale=inner_all, middle=forward_middle, chunks=16,
                weights=row_chunks, layer=l + 1, gain_row=2 * (l + 1), **common,
            ),
            "between_forward", 2 + l,
            dict(part=(out[7], vmem), ssq=(out[8], vmem), res=(residuals[l], vmem),
                 gain=(small, vmem), **weight_in),
            dict(full=whole_rows, branch=own_rows, res_out=own_rows,
                 r2=((rows_own, 128), F32, vmem), **weight_out),
        )
        rows.append(got["full"])
        branches.append(got["branch"])
        residuals.append(got["res_out"])
        r2s.append(got["r2"])
        packed.append(got["wfull"].reshape(width, packed_width))
        gb = grad_rows if l + 1 == layers - 1 else None
        out = forward_mix(rows[-1], packed[-1], params, l + 1, gb)
        saved.append(out[:7])
    total = lax.psum_scatter(out[7], "tensor", scatter_dimension=0, tiled=True)
    token_rows, r2_own = meet(out[8], tensor_count, inner_all, 16)
    product = out[9]
    gradient = out_grad
    scattered, summed, gain_grads = [None] * layers, [None] * layers, [None] * layers
    for l in reversed(range(layers)):
        last = l == layers - 1
        dcat, dpart, *small_grads = backward_mix(
            product if last else grad_rows, last, token_rows, rows[l], saved[l], packed[l],
            params, pick, l, () if last else (residuals[-1], total, r2_own),
        )
        summed[l], gain_grads[l] = small_grads[:3], small_grads[3]
        hidden_out = small_grads[-1]
        more = l > 0
        inputs = dict(
            part=(dpart, vmem), res=(residuals[l], vmem), gain=(small, vmem),
            grad_in=(gradient, vmem), lrows=(rows[l], vmem), lgrad=(grad_rows, vmem),
            right=(dcat, vmem),
        )
        outputs = dict(
            grad_out=own_rows,
            gout=((shard_rows, packed_width), F32, vmem),
        )
        if more:
            inputs.update(r2=(r2s[l - 1], vmem), branch=(branches[l - 1], vmem))
            outputs.update(full=whole_rows, inner=((8, tokens), F32, vmem))
        else:
            for i in range(layers):
                gvec, gst, gdt = summed[i]
                inputs["esum%d" % i], inputs["esum_%d" % i] = (gvec, vmem), (gdt, vmem)
                inputs["lsum%d" % i] = (gst, vmem)
            for i in range(layers):
                inputs["gsum%d" % i] = (gain_grads[i], vmem)
            early = sum(v.shape[1] for i in range(layers) for v in summed[i])
            outputs.update(
                sums=((8, early), F32, vmem), gain_sums=((8, width), F32, vmem)
            )
        got = comm_call(
            Step(
                partial=True, gather=more, late=more, inner=more, grads=column_chunks,
                chunks=16 if more else 8, lag=2 if more else 1,
                states=bc_width, sums=not more, gain_row=2 * l,
                lazy=("right", "lrows", "lgrad", "res", "grad_in") + (("branch",) if more else ()),
                middle=functools.partial(backward_middle, inner_all if more else None), **common,
            ),
            "between_backward" if more else "last_backward", 17 + l, inputs, outputs,
        )
        gradient = got["grad_out"]
        scattered[l] = got["gout"]
        if more:
            grad_rows, token_rows = got["full"], got["inner"]
    grads = list(
        assemble(scattered, got["sums"], got["gain_sums"], pick, dp_count, heads, bc_width, inner)
    )
    grads[4] = jnp.transpose(grads[4], (1, 2, 0))
    grads[-1] = jnp.transpose(grads[-1], (0, 2, 1))
    return (hidden_out, gradient, *grads)


def solution(mesh):
    placed = (
        P(("dp", "tensor"), None),
        P(("dp", "tensor"), None),
        P(None, "dp"),
        P(None, "dp", "tensor"),
        P(None, "dp", "tensor"),
        P(None, "dp", None),
        P(None, "dp", "tensor"),
        P(None, None, "tensor"),
        P(None, "tensor"),
        P(None, None, "dp"),
        P(None, "dp"),
        P(None, "tensor"),
        P(None, "tensor"),
        P(None, "tensor"),
        P(None, "tensor"),
        P(None, "tensor", "dp"),
    )
    return jax.shard_map(
        shards,
        mesh=mesh,
        in_specs=placed,
        out_specs=(
            P(("dp", "tensor"), None),
            P(("dp", "tensor"), None),
            P(None, "dp"),
            P(None, "dp", "tensor"),
            P(None, "dp", "tensor"),
            P(None, "dp", None),
            P(None, "dp", "tensor"),
            P(None, None, "tensor"),
            P(None, "tensor"),
            P(None, None, "dp"),
            P(None, "dp"),
            P(None, "tensor"),
            P(None, "tensor"),
            P(None, "tensor"),
            P(None, "tensor"),
            P(None, "tensor", "dp"),
        ),
        check_vma=False,
    )
```

```python
import functools
import types

import jax
import jax.numpy as jnp
from jax import lax
import numpy as np
from jax.sharding import PartitionSpec as P
import jax.experimental.pallas as pl
import jax.experimental.pallas.tpu as pltpu

GROUP = 256
EPSILON = 1e-05
BF = jnp.bfloat16
F32 = jnp.float32
WIDTH = 64
MIB = 1024 * 1024
WCHUNK = 384


def nn(a, b):
    return lax.dot_general(a, b, (((1,), (0,)), ((), ())), preferred_element_type=F32)


def tn(a, b):
    return lax.dot_general(a, b, (((0,), (0,)), ((), ())), preferred_element_type=F32)


def nt(a, b):
    return lax.dot_general(a, b, (((1,), (1,)), ((), ())), preferred_element_type=F32)


def parts3(v):
    one = v.astype(BF)
    rest = v - one.astype(F32)
    two = rest.astype(BF)
    three = (rest - two.astype(F32)).astype(BF)
    return one, two, three


def sum_rows(select, v):
    one, two, three = parts3(v)
    return nn(select, one) + nn(select, two) + nn(select, three)


def sum_lanes(v, select):
    one = v.astype(BF)
    two = (v - one.astype(F32)).astype(BF)
    return nn(one, select) + nn(two, select)


def silu_parts(v):
    sig = 1.0 / (1.0 + jnp.exp(-v))
    return sig, v * sig


def softplus(v):
    return jnp.maximum(v, 0.0) + jnp.log1p(jnp.exp(-jnp.abs(v)))


def pair_spread(column_values, pair, lane_low):
    low = column_values[:, 2 * pair : 2 * pair + 1]
    high = column_values[:, 2 * pair + 1 : 2 * pair + 2]
    return jnp.where(lane_low, low, high)


def spread(column_values, pairs, lane_low):
    return jnp.concatenate([pair_spread(column_values, p, lane_low) for p in range(pairs)], axis=1)


def conv_pre(padded, taps, bias, length):
    count = 4
    total = bias
    for k in range(count):
        total = total + taps[k : k + 1, :] * padded[pl.ds(8 - (count - 1) + k, length), :]
    return total


def blocks_of(w_ref, inner, bc_width):
    sizes = (bc_width, 128, inner, inner, inner)
    starts = [sum(sizes[:i]) for i in range(5)]
    return [w_ref.at[:, pl.ds(s, z)] for s, z in zip(starts, sizes)]


def small_refs(vec_ref, cst_ref, tiny_ref):
    vec, cst, tiny = vec_ref.at[0], cst_ref.at[0], tiny_ref.at[0]
    return (
        vec.at[0:4], vec.at[4:5], vec.at[5:6], vec.at[6:7],
        cst.at[0:4], cst.at[4:5], tiny.at[0:1], tiny.at[1:2],
    )


def fwd_kernel(
    first, last, rows_ref, w_ref, vec_ref, cst_ref, tiny_ref, gain_ref, *rest,
):
    if last:
        gb_ref, *rest = rest
    gate_ref, val_ref, st_ref, dt_ref, y_ref, ent_ref, pre_ref, ssq_ref, part_ref, *rest = rest
    if first:
        normed_ref, *rest = rest
    if last:
        part2_ref, dm_ref, mixed_ref, *rest = rest
    state, vpad, spad = rest[-3:]
    step = pl.program_id(0)
    length = rows_ref.shape[0]
    cv_ref, cvb_ref, skip_ref, gg_ref, cs_ref, csb_ref, sb_ref, rate_ref = small_refs(
        vec_ref, cst_ref, tiny_ref
    )
    inner = gg_ref.shape[1]
    pairs = inner // 128
    wbc_ref, wdt_ref, wz_ref, wx_ref, wot_ref = blocks_of(w_ref, inner, cs_ref.shape[1])

    @pl.when(step == 0)
    def _():
        state[...] = jnp.zeros_like(state)
        vpad[0:8, :] = jnp.zeros((8, inner), F32)
        spad[0:8, :] = jnp.zeros((8, spad.shape[1]), F32)

    @pl.when(step > 0)
    def _():
        vpad[0:8, :] = vpad[length : length + 8, :]
        spad[0:8, :] = spad[length : length + 8, :]

    rows = rows_ref[...]
    if first:
        rows = rows.astype(F32)
        r1 = lax.rsqrt(jnp.mean(rows * rows, axis=1, keepdims=True) + EPSILON)
        rows = (rows * r1 * gain_ref[0:1, :]).astype(BF)
        normed_ref[...] = rows
    gate_ref[...] = nn(rows, wz_ref[...])
    val = nn(rows, wx_ref[...])
    val_ref[...] = val
    vpad[8 : length + 8, :] = val
    st = nn(rows, wbc_ref[...])
    st_ref[...] = st
    spad[8 : length + 8, :] = st
    dt_in = nn(rows, wdt_ref[...])
    dt_ref[...] = dt_in

    pre = conv_pre(vpad, cv_ref, cvb_ref[...], length)
    pre_ref[...] = pre
    _, v = silu_parts(pre)
    _, bc = silu_parts(conv_pre(spad, cs_ref, csb_ref[...], length))
    half = bc.shape[1] // 2
    bb = bc[:, :half].astype(BF)
    cb = bc[:, half:].astype(BF)
    dt = softplus(dt_in + sb_ref[...])
    q_index = lax.broadcasted_iota(jnp.int32, (length, length), 0)
    s_index = lax.broadcasted_iota(jnp.int32, (length, length), 1)
    causal = q_index >= s_index
    tril = jnp.where(causal, 1.0, 0.0).astype(BF)
    a = sum_rows(tril, dt * rate_ref[...])
    a_rows = a.T
    lane_low = lax.broadcasted_iota(jnp.int32, (length, 128), 1) < WIDTH
    dt_x = spread(dt, pairs, lane_low)
    a_x = spread(a, pairs, lane_low)
    x = v * dt_x
    xb = x.astype(BF)
    scores = jnp.where(causal, nt(cb, bb), 0.0)
    inside = []
    zero = jnp.zeros((length, 128), BF)
    for p in range(pairs):
        xp = xb[:, 128 * p : 128 * (p + 1)]
        total = None
        for j in range(2):
            h = 2 * p + j
            decay = jnp.exp(jnp.minimum(a[:, h : h + 1] - a_rows[h : h + 1, :], 0.0))
            m = (scores * decay).astype(BF)
            term = nn(m, jnp.where(lane_low, xp, zero) if j == 0 else jnp.where(lane_low, zero, xp))
            total = term if total is None else total + term
        inside.append(total)
    entering = state[...]
    ent_ref[0] = entering
    outside = jnp.exp(a_x) * nn(cb, entering.astype(BF))
    a_last = a_x[length - 1 : length, :]
    xw = (x * jnp.exp(a_last - a_x)).astype(BF)
    state[...] = jnp.exp(a_last) * entering + nn(bc[:, :half].T.astype(BF), xw)
    y = jnp.concatenate(inside, axis=1) + outside + skip_ref[...] * v
    y_ref[...] = y
    _, sgate = silu_parts(gate_ref[...])
    gated = y * sgate
    square = (gated * gated).astype(BF)
    ssq_ref[...] = nt(jnp.ones((8, inner), BF), square)
    mixed = (gated * gg_ref[...]).astype(BF)
    part = nt(mixed, wot_ref[...]).astype(BF)
    if not last:
        part_ref[...] = part
    else:
        cut = length // 2
        part_ref[0], part2_ref[0] = part[:cut], part[cut:]
        mixed_ref[0] = mixed[cut:]
        dm = nn(gb_ref[0], wot_ref[...])
        dm_ref[0] = dm
        dots = token_dots(dm, mixed[:cut])
        row = lax.broadcasted_iota(jnp.int32, (8, length), 0)
        ssq_ref[...] = jnp.where(row == 0, ssq_ref[...], 0.0)
        ssq_ref[1:2, 0:cut] = dots[0:1]


def token_dots(dm, mixed):
    product = (dm * mixed.astype(F32)).astype(BF)
    return nt(jnp.ones((8, product.shape[1]), BF), product)


def whole(shape):
    return pl.BlockSpec(shape, lambda i: (0,) * len(shape), pipeline_mode=pl.Buffered(1))


def layer_specs(params, l):
    return [
        pl.BlockSpec((1,) + p.shape[1:], lambda i: (l, 0, 0), pipeline_mode=pl.Buffered(1))
        for p in params[:-1]
    ] + [whole(params[-1].shape)]


def forward_mix(rows, packed, params, l, gb=None):
    first, last = l == 0, gb is not None
    tokens, width = rows.shape
    inner = params[0].shape[2]
    bc_width = params[1].shape[2]
    dt_width = 128
    half = bc_width // 2
    q = GROUP
    blocks = tokens // q
    tok = lambda n: pl.BlockSpec((q, n), lambda i: (i, 0))
    outs = [
        ((tokens, inner), F32, tok(inner)),
        ((tokens, inner), F32, tok(inner)),
        ((tokens, bc_width), F32, tok(bc_width)),
        ((tokens, dt_width), F32, tok(dt_width)),
        ((tokens, inner), F32, tok(inner)),
        ((blocks, half, inner), F32, pl.BlockSpec((1, half, inner), lambda i: (i, 0, 0))),
        ((tokens, inner), F32, tok(inner)),
        ((8, tokens), F32, pl.BlockSpec((8, q), lambda i: (0, i))),
    ]
    half_of = lambda n: pl.BlockSpec((1, q // 2, n), lambda i: (i, 0, 0))
    if not last:
        outs.append(((tokens, width), BF, tok(width)))
    if first:
        outs.append(((tokens, width), BF, tok(width)))
    if last:
        for n, kind in ((width, BF), (width, BF), (inner, F32), (inner, BF)):
            outs.append(((blocks, q // 2, n), kind, half_of(n)))
    return pl.pallas_call(
        functools.partial(fwd_kernel, first, last),
        grid=(blocks,),
        in_specs=[tok(width), whole(packed.shape)]
        + layer_specs(params, l)
        + ([half_of(width)] if last else []),
        out_specs=[o[2] for o in outs],
        out_shape=[jax.ShapeDtypeStruct(o[0], o[1]) for o in outs],
        scratch_shapes=[
            pltpu.VMEM((half, inner), F32),
            pltpu.VMEM((q + 8, inner), F32),
            pltpu.VMEM((q + 8, bc_width), F32),
        ],
        compiler_params=pltpu.CompilerParams(
            dimension_semantics=("arbitrary",), vmem_limit_bytes=56 * MIB
        ),
        name="mix_forward",
    )(rows, packed, *params, *([gb] if last else []))


def bwd_kernel(
    ready, layer, gb_ref, e_ref, rows_ref, gate_ref, val_ref, st_ref, stp_ref, dt_ref, y_ref,
    ent_ref, pre_ref, w_ref, vec_ref, cst_ref, tiny_ref, gain_ref, pick_ref, *rest,
):
    if ready:
        dm2_ref, *rest = rest
    dcat_ref, dpart_ref, gvec_ref, gst_ref, gdt_ref, ggain_ref, *rest = rest
    dstate, spad, dvpad, dspad = rest
    step = pl.program_id(0)
    blocks = pl.num_programs(0)
    length = y_ref.shape[0]
    cv_ref, cvb_ref, skip_ref, gg_ref, cs_ref, csb_ref, sb_ref, rate_ref = small_refs(
        vec_ref, cst_ref, tiny_ref
    )
    inner = gg_ref.shape[1]
    bc_width = cs_ref.shape[1]
    wbc_ref, wdt_ref, wz_ref, wx_ref, wot_ref = blocks_of(w_ref, inner, bc_width)
    dst_ref, ddt_ref, dgate_ref, dval_ref, mixed_ref = blocks_of(dcat_ref, inner, bc_width)
    half = bc_width // 2
    pairs = inner // 128

    @pl.when(step == 0)
    def _():
        dstate[...] = jnp.zeros_like(dstate)
        dvpad[length : length + 8, :] = jnp.zeros((8, inner), F32)
        dspad[length : length + 8, :] = jnp.zeros((8, bc_width), F32)
        gvec_ref[...] = jnp.zeros_like(gvec_ref)
        gst_ref[...] = jnp.zeros_like(gst_ref)
        gdt_ref[...] = jnp.zeros_like(gdt_ref)
        ggain_ref[...] = jnp.zeros_like(ggain_ref)

    @pl.when(step > 0)
    def _():
        dvpad[length : length + 8, :] = dvpad[0:8, :]
        dspad[length : length + 8, :] = dspad[0:8, :]

    first = step == blocks - 1
    spad[0:8, :] = jnp.where(first, 0.0, stp_ref[...])
    spad[8 : length + 8, :] = st_ref[...]

    pre_v = pre_ref[...]
    sig_v, v = silu_parts(pre_v)
    pre_s = conv_pre(spad, cs_ref, csb_ref[...], length)
    sig_s, bc = silu_parts(pre_s)
    bb = bc[:, :half].astype(BF)
    cb = bc[:, half:].astype(BF)
    z = dt_ref[...] + sb_ref[...]
    dt = softplus(z)
    rate = rate_ref[...]
    s_index = lax.broadcasted_iota(jnp.int32, (length, length), 0)
    q_index = lax.broadcasted_iota(jnp.int32, (length, length), 1)
    upper = q_index >= s_index
    a = sum_rows(jnp.where(s_index >= q_index, 1.0, 0.0).astype(BF), dt * rate)
    a_rows = a.T
    lane_low = lax.broadcasted_iota(jnp.int32, (length, 128), 1) < WIDTH
    dt_x = spread(dt, pairs, lane_low)
    a_x = spread(a, pairs, lane_low)
    x = v * dt_x
    xb = x.astype(BF)
    skip = skip_ref[...]

    y = y_ref[...]
    gate = gate_ref[...]
    sig_g, sgate = silu_parts(gate)
    gated = y * sgate
    per_token = e_ref[...].T
    e, r2 = per_token[:, 0:1], per_token[:, 1:2]
    if ready:
        dm = jnp.concatenate([gb_ref[0], dm2_ref[0]], axis=0) * r2
    else:
        dm = nn(gb_ref[...], wot_ref[...]) * r2
    dgated = dm * gg_ref[...] - e * gated
    mixed_ref[...] = (gated * r2 * gg_ref[...]).astype(BF)
    dgate = (dgated * y * (sig_g * (1.0 + gate * (1.0 - sig_g)))).astype(BF)
    dgate_ref[...] = dgate
    dy = dgated * sgate
    dyb = dy.astype(BF)
    dyf = dyb.astype(F32)

    scores = jnp.where(upper, nt(bb, cb), 0.0)
    zero = jnp.zeros((length, 128), BF)
    dscores = jnp.zeros((length, length), F32)
    dx_list = []
    for p in range(pairs):
        xp = xb[:, 128 * p : 128 * (p + 1)]
        dp = dyb[:, 128 * p : 128 * (p + 1)]
        total = None
        for j in range(2):
            h = 2 * p + j
            decay = jnp.exp(jnp.minimum(a_rows[h : h + 1, :] - a[:, h : h + 1], 0.0))
            m = (scores * decay).astype(BF)
            dh = jnp.where(lane_low, dp, zero) if j == 0 else jnp.where(lane_low, zero, dp)
            term = nn(m, dh)
            total = term if total is None else total + term
            dscores = dscores + nt(xp, dh) * decay
        dx_list.append(total)
    dx_in = jnp.concatenate(dx_list, axis=1)
    dscores = jnp.where(upper, dscores, 0.0)
    db = nn(dscores.astype(BF), cb)
    dc = nn(dscores.T.astype(BF), bb)

    entering = ent_ref[0]
    dleaving = dstate[...]
    dleaving_b = dleaving.astype(BF)
    ea = jnp.exp(a_x)
    a_last = a_x[length - 1 : length, :]
    ea_last = jnp.exp(a_last)
    w = jnp.exp(a_last - a_x)
    dxw = nn(bb, dleaving_b) * w
    db = db + nt((x * w).astype(BF), dleaving_b)
    eady = (ea * dyf).astype(BF)
    dc = dc + nt(eady, entering.astype(BF))
    dstate[...] = ea_last * dleaving + nn(bc[:, half:].T.astype(BF), eady)
    dx = dx_in + dxw
    u = x * dxw
    last_add = jnp.sum(u, axis=0, keepdims=True) + ea_last * jnp.sum(
        entering * dleaving, axis=0, keepdims=True
    )
    da_x = dyf * (y - skip * v) - xb.astype(F32) * dx_in - u
    row_index = lax.broadcasted_iota(jnp.int32, (length, inner), 0)
    da_x = da_x + jnp.where(row_index == length - 1, last_add, 0.0)
    pick = pick_ref[...]
    da = sum_lanes(da_x, pick)
    dr = sum_rows(jnp.where(upper, 1.0, 0.0).astype(BF), da)
    ddt = sum_lanes(dx * v, pick) + dr * rate
    dz = ddt * (1.0 / (1.0 + jnp.exp(-z)))
    ddtb = dz.astype(BF)
    ddt_ref[...] = ddtb
    gdt_ref[0:1, :] += jnp.sum(dz, axis=0, keepdims=True)
    gdt_ref[1:2, :] += jnp.sum(dr * dt * rate, axis=0, keepdims=True)

    dpre_v = (skip * dy + dt_x * dx) * (sig_v * (1.0 + pre_v * (1.0 - sig_v)))
    dvpad[0:length, :] = dpre_v
    dval = jnp.zeros((length, inner), F32)
    val = val_ref[...]
    for k in range(4):
        later = dvpad[pl.ds(3 - k, length), :]
        dval = dval + cv_ref[k : k + 1, :] * later
        gvec_ref[k : k + 1, :] += jnp.sum(later * val, axis=0, keepdims=True)
    gvec_ref[4:5, :] += jnp.sum(dpre_v, axis=0, keepdims=True)
    gvec_ref[5:6, :] += jnp.sum(gated * dm, axis=0, keepdims=True)
    gvec_ref[6:7, :] += jnp.sum(dy * v, axis=0, keepdims=True)
    dvalb = dval.astype(BF)
    dval_ref[...] = dvalb

    dbc = jnp.concatenate([db, dc], axis=1)
    dpre_s = dbc * (sig_s * (1.0 + pre_s * (1.0 - sig_s)))
    dspad[0:length, :] = dpre_s
    dst = jnp.zeros((length, bc_width), F32)
    st = st_ref[...]
    for k in range(4):
        later = dspad[pl.ds(3 - k, length), :]
        dst = dst + cs_ref[k : k + 1, :] * later
        gst_ref[k : k + 1, :] += jnp.sum(later * st, axis=0, keepdims=True)
    gst_ref[4:5, :] += jnp.sum(dpre_s, axis=0, keepdims=True)
    dstb = dst.astype(BF)
    dst_ref[...] = dstb
    dpart = nt(dgate, wz_ref[...]) + nt(dvalb, wx_ref[...])
    dpart = dpart + nt(dstb, wbc_ref[...]) + nt(ddtb, wdt_ref[...])
    dpart_ref[...] = dpart.astype(BF)
    ggain_ref[0:1, :] += jnp.sum(rows_ref[...].astype(F32) * dpart, axis=0, keepdims=True)

    @pl.when(step == blocks - 1)
    def _():
        ggain_ref[0:1, :] = ggain_ref[0:1, :] / gain_ref[2 * layer : 2 * layer + 1, :]


def backward_mix(gb, ready, e_rows, rows, kept, packed, params, pick, l):
    gate, val, st, dt, y, ent, pre = kept
    tokens, width = y.shape[0], packed.shape[0]
    inner = params[0].shape[2]
    bc_width = params[1].shape[2]
    dt_width = 128
    packed_width = packed.shape[1]
    half = bc_width // 2
    q = GROUP
    blocks = tokens // q
    back = lambda i: blocks - 1 - i
    tok = lambda n: pl.BlockSpec((q, n), lambda i: (back(i), 0))
    halo = lambda n: pl.BlockSpec(
        (8, n), lambda i: (jnp.maximum(back(i) * (q // 8) - 1, 0), 0)
    )
    fixed = lambda r, c: pl.BlockSpec((r, c), lambda i: (0, 0))
    outs = [
        ((tokens, packed_width), BF, tok(packed_width)),
        ((tokens, width), BF, tok(width)),
        ((8, inner), F32, fixed(8, inner)),
        ((8, bc_width), F32, fixed(8, bc_width)),
        ((8, dt_width), F32, fixed(8, dt_width)),
        ((8, width), F32, fixed(8, width)),
    ]
    half_of = pl.BlockSpec((1, q // 2, inner), lambda i: (back(i), 0, 0))
    gb, more = (gb[0], [gb[1]]) if ready else (gb, [])
    return pl.pallas_call(
        functools.partial(bwd_kernel, ready, l),
        grid=(blocks,),
        in_specs=[
            half_of if ready else tok(width),
            pl.BlockSpec((8, q), lambda i: (0, back(i))),
            tok(width),
            tok(inner), tok(inner), tok(bc_width), halo(bc_width), tok(dt_width),
            tok(inner),
            pl.BlockSpec((1, half, inner), lambda i: (back(i), 0, 0)),
            tok(inner),
        ]
        + [whole(packed.shape)] + layer_specs(params, l) + [whole(pick.shape)]
        + [half_of] * len(more),
        out_specs=[o[2] for o in outs],
        out_shape=[jax.ShapeDtypeStruct(o[0], o[1]) for o in outs],
        scratch_shapes=[
            pltpu.VMEM((half, inner), F32),
            pltpu.VMEM((q + 8, bc_width), F32),
            pltpu.VMEM((q + 8, inner), F32),
            pltpu.VMEM((q + 8, bc_width), F32),
        ],
        compiler_params=pltpu.CompilerParams(
            dimension_semantics=("arbitrary",), vmem_limit_bytes=60 * MIB
        ),
        name="mix_backward",
    )(gb, e_rows, rows, gate, val, st, st, dt, y, ent, pre, packed, *params, pick, *more)


class Step:
    def __init__(self, **given):
        self.rows = 0
        self.width = 0
        self.line = 4
        self.chunks = 8
        self.hop = 1
        self.pass_hop = 1
        self.slack = 0
        self.partial = False
        self.gather = False
        self.late = False
        self.scale = False
        self.inner = False
        self.layer = 0
        self.small = 0
        self.gain_row = 0
        self.weights = 0
        self.grads = 0
        self.double = 2
        self.tail = 2
        self.lag = 1
        self.states = 0
        self.sums = False
        self.bits = 0
        self.middle = None
        self.halves = False
        self.lazy = ()
        self.__dict__.update(given)


def remote(src, dst, send, recv, device):
    return pltpu.make_async_remote_copy(
        src_ref=src, dst_ref=dst, send_sem=send, recv_sem=recv,
        device_id=device, device_id_type=pl.DeviceIdType.MESH,
    )


def when(condition):
    return pl.when(condition)


def pack_weights(r, l):
    start = 0
    for part in (r.p_bc.at[l], r.p_dt.at[l], r.p_z.at[l], r.p_x.at[l], r.p_out.at[l]):
        r.wown[:, start : start + part.shape[1]] = part[...]
        start += part.shape[1]


def comm_kernel(o, names, *refs):
    r = types.SimpleNamespace(**dict(zip(names, refs)))
    r.gain_row = slice(o.gain_row, o.gain_row + 1)
    r.gbuf = [v for k, v in zip(names, refs) if k.startswith("gbuf")]
    n, count, rows = o.line, o.chunks, o.rows
    size = rows // count
    t = lax.axis_index("tensor")
    me = lax.axis_index("dp")
    own_bits = [(me // (1 << b)) % 2 for b in range(o.bits)]
    partner = [me + (1 - 2 * own_bits[b]) * (1 << b) for b in range(o.bits)]

    lazy = []
    for i, name in enumerate(o.lazy):
        near = getattr(r, name + "_v")
        lazy.append(pltpu.make_async_copy(getattr(r, name), near, r.lazy_sem.at[i]))
        setattr(r, name, near)
    if o.halves:
        for i, far in enumerate((r.half0, r.half1)):
            lazy.append(pltpu.make_async_copy(far, r.lgrad.at[:, i], r.half_sem.at[i]))
    for copy in lazy:
        copy.start()

    barrier = pltpu.get_barrier_semaphore()
    for k in range(1, n):
        pl.semaphore_signal(
            barrier, inc=1, device_id={"tensor": lax.rem(t + k, n)},
            device_id_type=pl.DeviceIdType.MESH,
        )
    over_dp = o.weights or o.grads
    r.early = [v for k, v in zip(names, refs) if k.startswith("esum")]
    r.lined = [v for k, v in zip(names, refs) if k.startswith("lsum")]
    r.gains = [v for k, v in zip(names, refs) if k.startswith("gsum")]
    if over_dp:
        for b in range(o.bits):
            pl.semaphore_signal(
                barrier, inc=1, device_id={"dp": partner[b]}, device_id_type=pl.DeviceIdType.MESH
            )
    pl.semaphore_wait(barrier, n - 1 + (o.bits if over_dp else 0))

    def at(s, c):
        return pl.ds(pl.multiple_of(s * rows + c * size, size), size)

    def piece(c):
        return pl.ds(pl.multiple_of(c * size, size), size)

    def hop(side, s, c, src):
        buf = r.rbuf if side == 0 else r.lbuf
        return remote(
            src, buf.at[s, piece(c)], r.rs_send.at[side, s], r.rs_recv.at[side, s, c],
            {"tensor": t + 1 if side == 0 else t - 1},
        )

    def reduce_items(side, c):
        buf = r.rbuf if side == 0 else r.lbuf
        edge = t == 0 if side == 0 else t == n - 1
        order = range(n - 1, 0, -1) if side == 0 else range(0, n - 1)
        for s in order:
            further = s > t if side == 0 else s < t

            @when(further & edge)
            def _():
                hop(side, s, c, r.part.at[at(s, c)]).start()

            @when(further & jnp.logical_not(edge))
            def _():
                hop(side, s, c, buf.at[s, piece(c)]).wait_recv()
                total = buf[s, piece(c), :].astype(F32) + r.part[at(s, c), :].astype(F32)
                buf[s, piece(c), :] = total.astype(BF)
                hop(side, s, c, buf.at[s, piece(c)]).start()

    def own_total(c):
        acc = r.acc
        acc[...] = r.part[at(t, c), :].astype(F32)

        @when(t > 0)
        def _():
            hop(0, t, c, r.rbuf.at[t, piece(c)]).wait_recv()
            acc[...] += r.rbuf[t, piece(c), :].astype(F32)

        @when(t < n - 1)
        def _():
            hop(1, t, c, r.lbuf.at[t, piece(c)]).wait_recv()
            acc[...] += r.lbuf[t, piece(c), :].astype(F32)

    def pass_on(side, s, c):
        spot = r.full.at[at(s, c)]
        return remote(
            spot, spot, r.ag_send.at[side, s], r.ag_recv.at[side, s, c],
            {"tensor": t + 1 if side == 0 else t - 1},
        )

    def forward_items(side, tau):
        order = range(n - 2, -1, -1) if side == 0 else range(1, n)
        for s in order:
            away = t - s if side == 0 else s - t
            late = o.hop * max(s, n - 1 - s) + o.slack if o.late else 0
            c = tau - late - o.pass_hop * away

            @when((away > 0) & (c >= 0) & (c < count))
            def _():
                pass_on(side, s, c).wait_recv()

                @when(t < n - 1 if side == 0 else t > 0)
                def _():
                    pass_on(side, s, c).start()

    def spot_of(k, ref):
        return ref.at[:, pl.ds(pl.multiple_of(k * rows, rows), rows)]

    def square_copy(k):
        dest = lax.rem(t + k, n)
        return remote(
            spot_of(dest, r.ssq), r.sqbuf.at[k - 1], r.sq_send.at[k - 1],
            r.sq_recv.at[k - 1], {"tensor": dest},
        )

    def inner_copy(k):
        return remote(
            spot_of(t, r.inner), spot_of(t, r.inner), r.in_send.at[k - 1],
            r.in_recv.at[k - 1], {"tensor": lax.rem(t + k, n)},
        )

    def inner_arrival(k):
        source = lax.rem(t + n - k, n)
        return remote(
            spot_of(source, r.inner), spot_of(source, r.inner), r.in_send.at[k - 1],
            r.in_recv.at[k - 1], {"tensor": source},
        )

    def bit_order(parity):
        high = list(range(o.bits - 1, 0, -1))
        if parity == 1:
            high = high[1:] + high[:1]
        return high + [0]

    def cols(j):
        return pl.ds(pl.multiple_of(j * WCHUNK, WCHUNK), WCHUNK)

    def spots(known):
        return tuple(slice(None) if b in known else own_bits[b] for b in range(o.bits - 1, -1, -1))

    def weight_copy(parity, stage, j):
        order = bit_order(parity)
        depth = r.wown.shape[0] // o.weights
        strip = pl.ds(pl.multiple_of(j * depth, depth), depth)
        spot = r.wfull.at[(*spots(order[:stage]), strip)]
        src = r.wown.at[strip] if stage == 0 else spot
        return remote(
            src, spot, r.wg_send.at[stage, j], r.wg_recv.at[stage, j],
            {"dp": partner[order[stage]]},
        )

    def small_columns():
        lanes_at = pl.ds(o.small // 128 * 128, 128)
        return pltpu.make_async_copy(
            r.wfull.at[(*spots(range(o.bits)), slice(None), lanes_at)], r.columns, r.small_sem
        )

    def small_items(tau):
        done = (o.weights + 1) // 2 + o.bits

        @when(tau == done)
        def _():
            small_columns().start()

        @when(tau == done + 1)
        def _():
            small_columns().wait()
            turned = r.columns[...].reshape(o.width, 128).astype(F32).T
            r.small[...] = turned[o.small % 128 : o.small % 128 + 8, :]

    def own_weights():
        return pltpu.make_async_copy(r.wown, r.wfull.at[spots([])], r.wl_sem)

    def each_parity(pair, fn):
        for parity in range(2):
            j = 2 * pair + parity

            @when((j >= 0) & (j < o.weights))
            def _():
                fn(parity, j)

    def weight_items(tau):
        for stage in range(o.bits + 1):
            def run(parity, j):
                if stage > 0:
                    weight_copy(parity, stage - 1, j).wait_recv()
                if stage < o.bits:
                    weight_copy(parity, stage, j).start()
            each_parity(tau - stage, run)

    def grad_order(parity):
        high = list(range(1, o.bits))
        if parity == 1:
            high = high[1:] + high[:1]
        return [0] + high

    def grad_spot(parity, stage, mine):
        order = grad_order(parity)
        done, bit = order[:stage], order[stage]
        spot = []
        for b in range(o.bits - 1, -1, -1):
            if b in done:
                spot.append(own_bits[b])
            elif b == bit:
                spot.append(own_bits[b] if mine else 1 - own_bits[b])
            else:
                spot.append(slice(None))
        return tuple(spot)

    def grad_copy(parity, stage, j):
        order = grad_order(parity)
        return remote(
            r.grad.at[(j, *grad_spot(parity, stage, False))], r.gbuf[stage].at[j],
            r.gr_send.at[stage, j], r.gr_recv.at[stage, j],
            {"dp": partner[order[stage]]},
        )

    def products(turn, i):
        product(jnp.where(turn >= 0, chunk_of(turn), -1), i)

        @when((turn >= 0) & (turn < o.double))
        def _():
            product(2 * turn + 1, i)

    def product(j, i):
        slab = o.width // 2
        inner_shape = (2,) * (o.bits - 1) + (slab >> (o.bits - 1), WCHUNK)

        def one(left):
            rows_of_slab = left[..., pl.ds(i * slab, slab)].reshape(-1, slab)
            out = tn(rows_of_slab, r.right[:, cols(j)])
            r.grad[j, i] = out.astype(BF).reshape(inner_shape)

        @when((j >= 0) & (j < o.grads - o.tail))
        def _():
            one(r.lrows)

        @when((j >= o.grads - o.tail) & (j < o.grads))
        def _():
            one(r.lgrad)

    def chunk_of(turn):
        return jnp.where(turn < o.double, 2 * turn, turn + o.double)

    def each_chunk(turn, fn):
        j = chunk_of(turn)
        for parity in range(2):
            @when((turn >= 0) & (j < o.grads) & (lax.rem(j, 2) == parity))
            def _():
                fn(parity, j)

        @when((turn >= 0) & (turn < o.double))
        def _():
            fn(1, 2 * turn + 1)

    def grad_items(tau):
        products(tau, 1)

        def first(parity, j):
            grad_copy(parity, 0, j).start()

        each_chunk(tau, first)
        for stage in range(1, o.bits + 1):
            def run(parity, j):
                grad_copy(parity, stage - 1, j).wait_recv()
                spot = grad_spot(parity, stage - 1, True)
                free = [i for i, v in enumerate(spot) if isinstance(v, slice)]
                buf = r.gbuf[stage - 1]
                for combo in range(1 << len(free)):
                    pick = [(combo >> i) % 2 for i in range(len(free))]
                    full = list(spot)
                    for i, v in zip(free, pick):
                        full[i] = v
                    total = r.grad[(j, *full)].astype(F32) + buf[(j, *pick)].astype(F32)
                    if stage < o.bits:
                        r.grad[(j, *full)] = total.astype(BF)
                    else:
                        r.gout[:, cols(j)] = total
                if stage < o.bits:
                    grad_copy(parity, stage, j).start()
            each_chunk(tau - grad_lag(stage), run)

    def grad_lag(stage):
        return o.lag * (2 * stage - 1) if stage else 0

    def share(buf, send, recv, k):
        return remote(buf.at[t], buf.at[t], send.at[k - 1], recv.at[k - 1],
                      {"tensor": lax.rem(t + k, n)})

    def shared(buf, send, recv):
        for k in range(1, n):
            source = lax.rem(t + n - k, n)
            remote(buf.at[source], buf.at[source], send.at[k - 1], recv.at[k - 1],
                   {"tensor": source}).wait_recv()

    def line_total(buf):
        total = buf[0]
        for k in range(1, n):
            total = total + buf[k]
        return total

    def double(acc, buf, send, recv, b):
        return remote(acc.at[b], buf.at[b], send.at[b], recv.at[b], {"dp": partner[b]})

    def doubled(acc, buf, send, recv, b):
        double(acc, buf, send, recv, b).wait_recv()
        acc[b + 1] = acc[b] + buf[b]

    def lanes(index, ref):
        return slice(index * ref.shape[1], (index + 1) * ref.shape[1])

    line_groups, dp_groups = [], []
    if o.sums:
        line_groups = [(r.lbank, r.lb_send, r.lb_recv), (r.gbank, r.gb_send, r.gb_recv)]
        dp_groups = [
            (r.dbank, r.dbuf, r.db_send, r.db_recv), (r.hbank, r.hbuf, r.hb_send, r.hb_recv)
        ]

    def sum_items(tau):
        @when(tau == 2)
        def _():
            for g in line_groups:
                shared(*g)
            off = 0
            for v in r.early:
                r.dbank[0, :, off : off + v.shape[1]] = v[...]
                off += v.shape[1]
            r.dbank[0, :, off:] = line_total(r.lbank)
            r.hbank[0] = line_total(r.gbank)
            for g in dp_groups:
                double(*g, 0).start()

        for b in range(o.bits):
            @when(tau == 4 + b)
            def _():
                for g in dp_groups:
                    doubled(*g, b)
                    if b < o.bits - 1:
                        double(*g, b + 1).start()

    def state_items(tau):
        at_first = grad_lag(o.bits) + 1
        quarter = r.gout.shape[0] // n

        @when(tau == at_first)
        def _():
            for s in range(n):
                r.qsend[s] = r.gout[s * quarter : (s + 1) * quarter, 0 : o.states].astype(BF)
            for k in range(1, n):
                state_out(k).start()

        @when(tau == at_first + 2)
        def _():
            total = r.qsend[t].astype(F32)
            for k in range(1, n):
                state_out(k).wait_recv()
                total = total + r.qbuf[k - 1].astype(F32)
            r.qall[t] = total.astype(BF)
            for k in range(1, n):
                share(r.qall, r.qa_send, r.qa_recv, k).start()

    def state_out(k):
        dest = lax.rem(t + k, n)
        return remote(r.qsend.at[dest], r.qbuf.at[k - 1], r.qs_send.at[k - 1],
                      r.qs_recv.at[k - 1], {"tensor": dest})

    if o.sums:
        off = 0
        for v in r.lined:
            r.lbank[t, :, off : off + v.shape[1]] = v[...]
            off += v.shape[1]
        for i, v in enumerate(r.gains):
            r.gbank[t, :, lanes(i, v)] = v[0:1, :]
        for g in line_groups:
            for k in range(1, n):
                share(*g, k).start()
    if o.scale:
        for k in range(1, n):
            square_copy(k).start()
    if o.weights:
        pack_weights(r, o.layer)
        own_weights().start()
    if o.scale:
        total = spot_of(t, r.ssq)[...]
        for k in range(1, n):
            square_copy(k).wait_recv()
            total = total + r.sqbuf[k - 1]
        scale = lax.rsqrt(total / (o.scale * 1.0) + EPSILON)
        r.r2[...] = jnp.broadcast_to(scale.T[:, 0:1], (rows, 128))
    if o.gather and not o.late:
        r.full[pl.ds(pl.multiple_of(t * rows, rows), rows), :] = o.payload(r)
    if o.middle is not None:
        o.middle(r, None, None)

    ends = [count + o.hop * (n - 1) + o.slack]
    if o.late:
        ends.append(ends[0] + o.pass_hop * (n - 1))
    elif o.gather:
        ends.append(count + o.pass_hop * (n - 1))
    if o.weights:
        ends.append((o.weights + 1) // 2 + o.bits + (2 if o.small else 0))
    if o.grads:
        ends.append(1 + o.grads - o.double + grad_lag(o.bits))
        ends.append(grad_lag(o.bits) + 5)
    if o.sums:
        ends.append(4 + o.bits)

    def iteration(tau, _):
        if lazy:
            @when(tau == 1)
            def _():
                for copy in lazy:
                    copy.wait()
        if o.grads:
            products(tau - 1, 0)
        if o.partial:
            for side in range(2):
                c = tau - o.hop * (t if side == 0 else n - 1 - t)

                @when((c >= 0) & (c < count))
                def _():
                    reduce_items(side, c)

            c_own = tau - o.hop * jnp.maximum(t, n - 1 - t) - o.slack

            @when((c_own >= 0) & (c_own < count))
            def _():
                own_total(c_own)
                out = o.middle(r, piece(c_own), r.acc[...])
                if o.late:
                    r.full[at(t, c_own), :] = out
        if o.gather:
            c_out = tau - o.hop * jnp.maximum(t, n - 1 - t) - o.slack if o.late else tau

            @when((c_out >= 0) & (c_out < count))
            def _():
                @when(t < n - 1)
                def _():
                    pass_on(0, t, c_out).start()

                @when(t > 0)
                def _():
                    pass_on(1, t, c_out).start()

            for side in range(2):
                forward_items(side, tau)
        if o.weights:
            @when(tau == 1)
            def _():
                own_weights().wait()
            weight_items(tau)
            if o.small:
                small_items(tau)
        if o.grads:
            grad_items(tau - 1)
            state_items(tau - 1)
        if o.sums:
            sum_items(tau)
        return 0

    lax.fori_loop(0, max(ends), iteration, 0)

    if o.inner:
        spot_of(t, r.inner)[...] = r.icol[...].T[0:8, :]
        for k in range(1, n):
            inner_copy(k).start()
        for k in range(1, n):
            inner_arrival(k).wait_recv()
        for k in range(1, n):
            inner_copy(k).wait_send()
    if o.sums:
        r.sums[...] = r.dbank[o.bits]
        for i, v in enumerate(r.gains):
            r.gain_sums[i : i + 1, :] = r.hbank[o.bits, :, lanes(i, v)]
        for g in line_groups:
            for k in range(1, n):
                share(*g, k).wait_send()
        for g in dp_groups:
            for b in range(o.bits):
                double(*g, b).wait_send()
    if o.grads:
        shared(r.qall, r.qa_send, r.qa_recv)
        quarter = r.gout.shape[0] // n
        for s in range(n):
            r.gout[s * quarter : (s + 1) * quarter, 0 : o.states] = r.qall[s].astype(F32)
        for k in range(1, n):
            state_out(k).wait_send()
            share(r.qall, r.qa_send, r.qa_recv, k).wait_send()
    if o.scale:
        for k in range(1, n):
            square_copy(k).wait_send()
    for s in range(n):
        for side in range(2):
            inside = t < n - 1 if side == 0 else t > 0
            if o.partial:
                @when((s > t if side == 0 else s < t) & inside)
                def _():
                    buf = (r.rbuf if side == 0 else r.lbuf).at[s]
                    remote(
                        buf, buf, r.rs_send.at[side, s], r.rs_recv.at[side, s, 0],
                        {"tensor": t + 1 if side == 0 else t - 1},
                    ).wait_send()
            if o.gather:
                @when((s <= t if side == 0 else s >= t) & inside)
                def _():
                    spot = r.full.at[pl.ds(s * rows, rows)]
                    remote(
                        spot, spot, r.ag_send.at[side, s], r.ag_recv.at[side, s, 0],
                        {"tensor": t + 1 if side == 0 else t - 1},
                    ).wait_send()
    for j in range(o.weights):
        for stage in range(o.bits):
            weight_copy(j % 2, stage, jnp.int32(j)).wait_send()
    for j in range(o.grads):
        for stage in range(o.bits):
            grad_copy(j % 2, stage, jnp.int32(j)).wait_send()


def comm_call(o, name, collective, inputs, outputs, **scratch):
    n, count, rows, width = o.line, o.chunks, o.rows, o.width
    dma = pltpu.SemaphoreType.DMA
    if o.lazy:
        for key in o.lazy:
            value = inputs[key][0]
            inputs[key] = (value, pl.ANY)
            scratch[key + "_v"] = pltpu.VMEM(value.shape, value.dtype)
        scratch.update(lazy_sem=dma((len(o.lazy),)))
    if o.halves:
        scratch.update(lgrad=pltpu.VMEM((n, 2, rows // 2, width), BF), half_sem=dma((2,)))
    if o.partial:
        scratch.update(
            rbuf=pltpu.VMEM((n, rows, width), BF),
            lbuf=pltpu.VMEM((n, rows, width), BF),
            acc=pltpu.VMEM((rows // count, width), F32),
            rs_send=dma((2, n)),
            rs_recv=dma((2, n, count)),
        )
    if o.gather:
        scratch.update(ag_send=dma((2, n)), ag_recv=dma((2, n, count)))
    if o.scale:
        scratch.update(
            sqbuf=pltpu.VMEM((n - 1, 8, rows), F32), sq_send=dma((n - 1,)), sq_recv=dma((n - 1,))
        )
    if o.inner:
        scratch.update(
            icol=pltpu.VMEM((rows, 128), F32), in_send=dma((n - 1,)), in_recv=dma((n - 1,))
        )
    if o.weights:
        rows_of_pack = inputs["p_bc"][0].shape[1]
        pack_width = sum(v[0].shape[2] for k, v in inputs.items() if k.startswith("p_"))
        scratch.update(
            columns=pltpu.VMEM((*(2,) * o.bits, rows_of_pack, 128), BF),
            small_sem=dma(()),
            wown=pltpu.VMEM((rows_of_pack, pack_width), BF),
            wl_sem=dma(()),
            wg_send=dma((o.bits, o.weights)),
            wg_recv=dma((o.bits, o.weights)),
        )
    if o.grads:
        depth = o.width >> o.bits
        scratch.update(
            grad=pltpu.VMEM((o.grads, *(2,) * o.bits, depth, WCHUNK), BF),
            gr_send=dma((o.bits, o.grads)),
            gr_recv=dma((o.bits, o.grads)),
        )
        for stage in range(o.bits):
            scratch["gbuf%d" % stage] = pltpu.VMEM(
                (o.grads, *(2,) * (o.bits - 1 - stage), depth, WCHUNK), BF
            )
        part = (n, (width >> o.bits) // n, o.states)
        scratch.update(
            qsend=pltpu.VMEM(part, BF), qall=pltpu.VMEM(part, BF),
            qbuf=pltpu.VMEM((n - 1,) + part[1:], BF),
            qs_send=dma((n - 1,)), qs_recv=dma((n - 1,)),
            qa_send=dma((n - 1,)), qa_recv=dma((n - 1,)),
        )
    if o.sums:
        def lanes_of(start):
            return sum(v[0].shape[1] for k, v in inputs.items() if k.startswith(start))

        lined, early, gains = lanes_of("lsum"), lanes_of("esum"), lanes_of("gsum")
        for one, two, tall, line_width, dp_width in (
            ("lb", "db", 8, lined, lined + early), ("gb", "hb", 1, gains, gains)
        ):
            scratch[one + "ank"] = pltpu.VMEM((n, tall, line_width), F32)
            scratch[two + "ank"] = pltpu.VMEM((o.bits + 1, tall, dp_width), F32)
            scratch[two + "uf"] = pltpu.VMEM((o.bits, tall, dp_width), F32)
            for key, size in ((one, n - 1), (two, o.bits)):
                scratch[key + "_send"] = dma((size,))
                scratch[key + "_recv"] = dma((size,))
    names = [*inputs, *outputs, *scratch]
    out = pl.pallas_call(
        functools.partial(comm_kernel, o, names),
        in_specs=[pl.BlockSpec(memory_space=i[1]) for i in inputs.values()],
        out_specs=[pl.BlockSpec(memory_space=i[2]) for i in outputs.values()],
        out_shape=[jax.ShapeDtypeStruct(i[0], i[1]) for i in outputs.values()],
        scratch_shapes=list(scratch.values()),
        compiler_params=pltpu.CompilerParams(
            collective_id=collective, has_side_effects=True, vmem_limit_bytes=62 * MIB
        ),
        name=name,
    )(*[i[0] for i in inputs.values()])
    return dict(zip(outputs, out))


def meet_kernel(
    n, inner_all, own_ref, grad_ref, mixed_ref, w_ref,
    out_ref, scale_ref, dm_ref, stage, near, bank, send, recv, sem,
):
    t = lax.axis_index("tensor")
    inner = near.shape[1]
    weight = pltpu.make_async_copy(w_ref.at[:, pl.ds(w_ref.shape[1] - inner, inner)], near, sem)
    weight.start()
    barrier = pltpu.get_barrier_semaphore()
    for k in range(1, n):
        pl.semaphore_signal(
            barrier, inc=1, device_id={"tensor": lax.rem(t + k, n)},
            device_id_type=pl.DeviceIdType.MESH,
        )
    stage[...] = own_ref[...]
    rows, cut = scale_ref.shape[0], grad_ref.shape[1]
    weight.wait()
    for s in range(n):
        dm = nn(grad_ref[s], near[...])
        dm_ref[s] = dm
        stage[1:2, (s + 1) * rows - cut : (s + 1) * rows] = token_dots(dm, mixed_ref[s])[0:1]
    pl.semaphore_wait(barrier, n - 1)
    copies = [
        remote(stage, bank.at[t], send.at[k - 1], recv.at[k - 1], {"tensor": lax.rem(t + k, n)})
        for k in range(1, n)
    ]
    for copy in copies:
        copy.start()
    bank[t] = stage[...]
    for k in range(1, n):
        source = lax.rem(t + n - k, n)
        remote(
            stage, bank.at[source], send.at[k - 1], recv.at[k - 1], {"tensor": source}
        ).wait_recv()
    total = bank[0]
    for s in range(1, n):
        total = total + bank[s]
    scale = lax.rsqrt(total[0:1, :] / inner_all + EPSILON)
    row = lax.broadcasted_iota(jnp.int32, total.shape, 0)
    e = scale * scale * scale * (total[1:2, :] / inner_all)
    out_ref[...] = jnp.where(row == 0, e, scale)
    mine = out_ref[:, pl.ds(pl.multiple_of(t * rows, rows), rows)].T
    scale_ref[...] = jnp.broadcast_to(mine[:, 1:2], scale_ref.shape)
    for copy in copies:
        copy.wait_send()


def meet(own, grad, mixed, packed, n, inner_all, collective):
    vmem = pl.BlockSpec(memory_space=pltpu.VMEM)
    dma = pltpu.SemaphoreType.DMA
    inner = mixed.shape[2]
    return pl.pallas_call(
        functools.partial(meet_kernel, n, inner_all),
        in_specs=[vmem, vmem, vmem, pl.BlockSpec(memory_space=pl.ANY)],
        out_specs=[vmem, vmem, vmem],
        out_shape=[
            jax.ShapeDtypeStruct(own.shape, F32),
            jax.ShapeDtypeStruct((own.shape[1] // n, 128), F32),
            jax.ShapeDtypeStruct(mixed.shape, F32),
        ],
        scratch_shapes=[
            pltpu.VMEM(own.shape, F32), pltpu.VMEM((packed.shape[0], inner), BF),
            pltpu.VMEM((n,) + own.shape, F32), dma((n - 1,)), dma((n - 1,)), dma(()),
        ],
        compiler_params=pltpu.CompilerParams(
            collective_id=collective, has_side_effects=True, vmem_limit_bytes=62 * MIB
        ),
        name="turn_around",
    )(own, grad, mixed, packed)


def plain_payload(r):
    return r.own[...]


def token_columns(first, second):
    lane = lax.broadcasted_iota(jnp.int32, (first.shape[0], 128), 1)
    return jnp.where(lane == 0, first, second)


def forward_middle(r, at, total):
    if at is None:
        return None
    branch = total * r.r2[at, 0:1]
    residual = r.res[at, :].astype(F32) + branch
    r.branch[at, :] = branch
    r.res_out[at, :] = residual
    r1 = lax.rsqrt(jnp.mean(residual * residual, axis=1, keepdims=True) + EPSILON)
    return (residual * r1 * r.gain[r.gain_row, :]).astype(BF)


def backward_middle(inner_all, r, at, total):
    if at is None:
        return None
    res = r.res[at, :].astype(F32)
    width = res.shape[1]
    r1 = lax.rsqrt(jnp.mean(res * res, axis=1, keepdims=True) + EPSILON)
    hat = res * r1
    dn = total * r.gain[r.gain_row, :]
    cross = jnp.sum(dn * hat, axis=1, keepdims=True) / width
    grad = r.grad_in[at, :].astype(F32) + r1 * (dn - hat * cross)
    r.grad_out[at, :] = grad
    if inner_all is None:
        return None
    r2 = r.r2[at, 0:1]
    dot = jnp.sum(grad.astype(BF).astype(F32) * r.branch[at, :], axis=1, keepdims=True)
    r.icol[at, :] = token_columns(r2 * r2 * dot / inner_all, r2)
    return grad.astype(BF)


def assemble_kernel(layers, dp_count, heads, bc_width, inner, *refs):
    gouts, (sums, gains, pick), refs = refs[:layers], refs[layers : layers + 3], refs[layers + 3 :]
    res, scale, *halves = refs[:4]
    norm, gz, gx, gbc, gdt, cv, cvb, cs, csb, sb, ld, sk, gg, po, hidden = refs[4:]
    me = lax.axis_index("dp")
    cut = halves[0].shape[0]
    for i, half in enumerate(halves):
        at = slice(i * cut, (i + 1) * cut)
        hidden[at, :] = res[at, :] + scale[at, 0:1] * half[...].astype(F32)

    def own(v):
        share = v.shape[1] // dp_count
        return pltpu.roll(v, v.shape[1] - me * share, 1)[:, :share]

    norm[...] = own(gains[...])[0:layers]
    for l in range(layers):
        full = gouts[l]
        first = bc_width + 128
        gbc[l] = full[:, 0:bc_width]
        gdt[:, l, :] = full[:, bc_width:first].T[0:heads, :]
        gz[l] = full[:, first : first + inner]
        gx[l] = full[:, first + inner : first + 2 * inner]
        po[l] = full[:, first + 2 * inner :]
        base = l * (inner + 128)
        vec = sums[:, base : base + inner]
        step = sums[:, base + inner : base + inner + 128]
        start = layers * (inner + 128) + l * bc_width
        state = own(sums[:, start : start + bc_width])
        cv[l] = vec[0:4]
        cvb[l : l + 1] = vec[4:5]
        gg[l : l + 1] = vec[5:6]
        one, two, three = parts3(vec)
        head_sums = nn(one, pick[...]) + nn(two, pick[...]) + nn(three, pick[...])
        sk[l : l + 1] = head_sums[6:7, 0:heads]
        sb[l : l + 1] = step[0:1, 0:heads]
        ld[l : l + 1] = step[1:2, 0:heads]
        cs[l] = state[0:4]
        csb[l : l + 1] = state[4:5]


def assemble(gouts, sums, gains, pick, dp_count, heads, bc_width, inner, hidden):
    layers, (rows, _) = len(gouts), gouts[0].shape
    vmem = pl.BlockSpec(memory_space=pltpu.VMEM)
    share = bc_width // dp_count
    shapes = [
        (layers, gains.shape[1] // dp_count),
        (layers, rows, inner), (layers, rows, inner), (layers, rows, bc_width),
        (heads, layers, rows), (layers, 4, inner), (layers, inner), (layers, 4, share),
        (layers, share), (layers, heads), (layers, heads), (layers, heads), (layers, inner),
        (layers, rows, inner), hidden[0].shape,
    ]
    inputs = [*gouts, sums, gains, pick, *hidden]
    return pl.pallas_call(
        functools.partial(assemble_kernel, layers, dp_count, heads, bc_width, inner),
        in_specs=[vmem] * len(inputs),
        out_specs=[vmem] * len(shapes),
        out_shape=[jax.ShapeDtypeStruct(v, F32) for v in shapes],
        compiler_params=pltpu.CompilerParams(vmem_limit_bytes=62 * MIB),
        name="assemble",
    )(*inputs)


def shards(
    hidden_in,
    out_grad,
    norm_gain,
    proj_z,
    proj_x,
    proj_bc,
    proj_dt,
    conv_value,
    conv_value_bias,
    conv_state,
    conv_state_bias,
    step_bias,
    log_decay,
    skip_gain,
    gate_gain,
    proj_out,
):
    tensor_count = lax.axis_size("tensor")
    dp_count = lax.axis_size("dp")
    bits = dp_count.bit_length() - 1
    layers, shard_rows, inner = proj_z.shape
    rows_own, width = hidden_in.shape
    tokens = rows_own * tensor_count
    heads = step_bias.shape[1]
    bc_width = proj_bc.shape[2]
    inner_all = inner * tensor_count
    packed_width = bc_width + 128 + 3 * inner
    column_chunks, row_chunks = packed_width // WCHUNK, shard_rows // 16
    vmem, far = pltpu.VMEM, pl.ANY

    small = jnp.concatenate([conv_state.reshape(layers, -1), conv_state_bias], axis=1)
    small = jnp.pad(small, ((0, 0), (0, shard_rows - small.shape[1])))
    extra = jnp.stack([norm_gain, small], axis=1).reshape(2 * layers, shard_rows).T
    step_block = jnp.concatenate(
        [
            proj_dt,
            jnp.broadcast_to(extra[None], (layers,) + extra.shape),
            jnp.zeros((layers, shard_rows, 128 - heads - 2 * layers), BF),
        ],
        axis=2,
    )
    out_turned = jnp.transpose(proj_out, (0, 2, 1))
    full_shape = ((2,) * bits) + (shard_rows, packed_width)
    common = dict(rows=rows_own, width=width, line=tensor_count, bits=bits)

    weight_in = dict(
        p_bc=(proj_bc, vmem), p_dt=(step_block, vmem), p_z=(proj_z, vmem), p_x=(proj_x, vmem),
        p_out=(out_turned, vmem),
    )
    weight_out = dict(wfull=(full_shape, BF, far))

    vec = jnp.concatenate(
        [
            conv_value,
            conv_value_bias[:, None],
            jnp.repeat(skip_gain, WIDTH, axis=1)[:, None],
            gate_gain[:, None],
        ],
        axis=1,
    ).astype(F32)
    tiny = jnp.stack([step_bias.astype(F32), -jnp.exp(log_decay.astype(F32))], axis=1)
    tiny = jnp.pad(tiny, ((0, 0), (0, 0), (0, 128 - heads)))
    pick = jnp.asarray(np.arange(inner)[:, None] // WIDTH == np.arange(128)[None, :], BF)

    whole_rows, own_rows = ((tokens, width), BF, vmem), ((rows_own, width), F32, vmem)
    got = comm_call(
        Step(gather=True, payload=plain_payload, weights=row_chunks,
             small=bc_width + heads, **common),
        "gather_first", 1,
        dict(own=(hidden_in, vmem), **weight_in),
        dict(full=whole_rows, small=((8, width), F32, vmem), **weight_out),
    )
    x_rows = got["full"]
    out_grad, x_rows = lax.optimization_barrier((out_grad, x_rows))
    cut = rows_own // 2

    def gather_half(v):
        return lax.all_gather(v, "tensor", axis=0)

    first_half = gather_half(out_grad[:cut])
    packed = [got["wfull"].reshape(width, packed_width)]
    small = got["small"]
    per = bc_width // dp_count
    smalls = small[1 : 2 * layers : 2].reshape(layers, dp_count, shard_rows)[:, :, : 5 * per]
    cst = jnp.transpose(smalls.reshape(layers, dp_count, 5, per), (0, 2, 1, 3))
    cst = cst.reshape(layers, 5, bc_width)
    params = (vec, cst, tiny, small)

    out = forward_mix(x_rows, packed[0], params, 0)
    saved, rows = [out[:7]], [out[9]]
    residuals, branches, r2s = [hidden_in], [], []
    for l in range(layers - 1):
        got = comm_call(
            Step(
                partial=True, gather=True, late=True, scale=inner_all, middle=forward_middle, chunks=16,
                weights=row_chunks, layer=l + 1, gain_row=2 * (l + 1), **common,
            ),
            "between_forward", 2 + l,
            dict(part=(out[8], vmem), ssq=(out[7], vmem), res=(residuals[l], vmem),
                 gain=(small, vmem), **weight_in),
            dict(full=whole_rows, branch=own_rows, res_out=own_rows,
                 r2=((rows_own, 128), F32, vmem), **weight_out),
        )
        if l + 1 == layers - 1:
            last_grad, got["full"] = lax.optimization_barrier((out_grad[cut:], got["full"]))
            second_half = gather_half(last_grad)
        rows.append(got["full"])
        branches.append(got["branch"])
        residuals.append(got["res_out"])
        r2s.append(got["r2"])
        packed.append(got["wfull"].reshape(width, packed_width))
        gb = first_half if l + 1 == layers - 1 else None
        out = forward_mix(rows[-1], packed[-1], params, l + 1, gb)
        saved.append(out[:7])
    def scatter_half(v):
        return lax.psum_scatter(
            v.reshape(-1, width), "tensor", scatter_dimension=0, tiled=True
        )

    branch_halves = [scatter_half(out[8])]
    token_rows, r2_own, second_product = meet(
        out[7], second_half, out[11], packed[-1], tensor_count, inner_all, 16
    )
    grad_rows = None
    gradient = out_grad
    scattered, summed, gain_grads = [None] * layers, [None] * layers, [None] * layers
    for l in reversed(range(layers)):
        last = l == layers - 1
        dcat, dpart, *small_grads = backward_mix(
            (out[10], second_product) if last else grad_rows, last, token_rows, rows[l], saved[l],
            packed[l], params, pick, l,
        )
        summed[l], gain_grads[l] = small_grads[:3], small_grads[3]
        more = l > 0
        inputs = dict(
            part=(dpart, vmem), res=(residuals[l], vmem), gain=(small, vmem),
            grad_in=(gradient, vmem), lrows=(rows[l], vmem), right=(dcat, vmem),
        )
        if last:
            inputs.update(half0=(first_half, far), half1=(second_half, far))
        else:
            inputs.update(lgrad=(grad_rows, vmem))
        outputs = dict(
            grad_out=own_rows,
            gout=((shard_rows, packed_width), F32, vmem),
        )
        if more:
            inputs.update(r2=(r2s[l - 1], vmem), branch=(branches[l - 1], vmem))
            outputs.update(full=whole_rows, inner=((8, tokens), F32, vmem))
        else:
            for i in range(layers):
                gvec, gst, gdt = summed[i]
                inputs["esum%d" % i], inputs["esum_%d" % i] = (gvec, vmem), (gdt, vmem)
                inputs["lsum%d" % i] = (gst, vmem)
            for i in range(layers):
                inputs["gsum%d" % i] = (gain_grads[i], vmem)
            early = sum(v.shape[1] for i in range(layers) for v in summed[i])
            outputs.update(
                sums=((8, early), F32, vmem), gain_sums=((8, width), F32, vmem)
            )
        got = comm_call(
            Step(
                partial=True, gather=more, late=more, inner=more, grads=column_chunks,
                chunks=16 if more else 8, lag=2 if more else 1,
                states=bc_width, sums=not more, gain_row=2 * l,
                halves=last, double=0 if more else 2,
                lazy=("right", "lrows", "res", "grad_in")
                + (() if last else ("lgrad",)) + (("branch",) if more else ()),
                middle=functools.partial(backward_middle, inner_all if more else None), **common,
            ),
            "between_backward" if more else "last_backward", 17 + l, inputs, outputs,
        )
        gradient = got["grad_out"]
        scattered[l] = got["gout"]
        if more:
            grad_rows, token_rows = got["full"], got["inner"]
        if last:
            second_part, gradient = lax.optimization_barrier((out[9], gradient))
            branch_halves.append(scatter_half(second_part))
    grads = list(
        assemble(
            scattered, got["sums"], got["gain_sums"], pick, dp_count, heads, bc_width, inner,
            [residuals[-1], r2_own, *branch_halves],
        )
    )
    hidden_out = grads.pop()
    grads[4] = jnp.transpose(grads[4], (1, 2, 0))
    grads[-1] = jnp.transpose(grads[-1], (0, 2, 1))
    return (hidden_out, gradient, *grads)


def solution(mesh):
    placed = (
        P(("dp", "tensor"), None),
        P(("dp", "tensor"), None),
        P(None, "dp"),
        P(None, "dp", "tensor"),
        P(None, "dp", "tensor"),
        P(None, "dp", None),
        P(None, "dp", "tensor"),
        P(None, None, "tensor"),
        P(None, "tensor"),
        P(None, None, "dp"),
        P(None, "dp"),
        P(None, "tensor"),
        P(None, "tensor"),
        P(None, "tensor"),
        P(None, "tensor"),
        P(None, "tensor", "dp"),
    )
    return jax.shard_map(
        shards,
        mesh=mesh,
        in_specs=placed,
        out_specs=(
            P(("dp", "tensor"), None),
            P(("dp", "tensor"), None),
            P(None, "dp"),
            P(None, "dp", "tensor"),
            P(None, "dp", "tensor"),
            P(None, "dp", None),
            P(None, "dp", "tensor"),
            P(None, None, "tensor"),
            P(None, "tensor"),
            P(None, None, "dp"),
            P(None, "dp"),
            P(None, "tensor"),
            P(None, "tensor"),
            P(None, "tensor"),
            P(None, "tensor"),
            P(None, "tensor", "dp"),
        ),
        check_vma=False,
    )
```

```python
import functools
import types

import jax
import jax.numpy as jnp
from jax import lax
import numpy as np
from jax.sharding import PartitionSpec as P
import jax.experimental.pallas as pl
import jax.experimental.pallas.tpu as pltpu

GROUP = 256
EPSILON = 1e-05
BF = jnp.bfloat16
F32 = jnp.float32
WIDTH = 64
GAIN_ROWS = 6
MIB = 1024 * 1024
WCHUNK = 384


def nn(a, b):
    return lax.dot_general(a, b, (((1,), (0,)), ((), ())), preferred_element_type=F32)


def tn(a, b):
    return lax.dot_general(a, b, (((0,), (0,)), ((), ())), preferred_element_type=F32)


def nt(a, b):
    return lax.dot_general(a, b, (((1,), (1,)), ((), ())), preferred_element_type=F32)


def parts3(v):
    one = v.astype(BF)
    rest = v - one.astype(F32)
    two = rest.astype(BF)
    three = (rest - two.astype(F32)).astype(BF)
    return one, two, three


def sum_rows(select, v):
    one, two, three = parts3(v)
    return nn(select, one) + nn(select, two) + nn(select, three)


def sum_lanes(v, select):
    one = v.astype(BF)
    two = (v - one.astype(F32)).astype(BF)
    return nn(one, select) + nn(two, select)


def silu_parts(v):
    sig = 1.0 / (1.0 + jnp.exp(-v))
    return sig, v * sig


def softplus(v):
    return jnp.maximum(v, 0.0) + jnp.log1p(jnp.exp(-jnp.abs(v)))


def pair_spread(column_values, pair, lane_low):
    low = column_values[:, 2 * pair : 2 * pair + 1]
    high = column_values[:, 2 * pair + 1 : 2 * pair + 2]
    return jnp.where(lane_low, low, high)


def spread(column_values, pairs, lane_low):
    return jnp.concatenate([pair_spread(column_values, p, lane_low) for p in range(pairs)], axis=1)


def conv_pre(padded, taps, bias, length):
    count = 4
    total = bias
    for k in range(count):
        total = total + taps[k : k + 1, :] * padded[pl.ds(8 - (count - 1) + k, length), :]
    return total


def blocks_of(w_ref, inner, bc_width):
    sizes = (bc_width, 128, inner, inner, inner)
    starts = [sum(sizes[:i]) for i in range(5)]
    return [w_ref.at[:, pl.ds(s, z)] for s, z in zip(starts, sizes)]


def small_refs(vec_ref, cst_ref, tiny_ref):
    vec, cst, tiny = vec_ref.at[0], cst_ref.at[0], tiny_ref.at[0]
    return (
        vec.at[0:4], vec.at[4:5], vec.at[5:6], vec.at[6:7],
        cst.at[0:4], cst.at[4:5], tiny.at[0:1], tiny.at[1:2],
    )


def fwd_kernel(
    first, last, rows_ref, w_ref, vec_ref, cst_ref, tiny_ref, gain_ref, *rest,
):
    if last:
        gb_ref, *rest = rest
    gate_ref, val_ref, st_ref, dt_ref, y_ref, ent_ref, pre_ref, ssq_ref, part_ref, *rest = rest
    if first:
        normed_ref, *rest = rest
    if last:
        part2_ref, dm_ref, mixed_ref, *rest = rest
    state, vpad, spad = rest[-3:]
    step = pl.program_id(0)
    length = rows_ref.shape[0]
    cv_ref, cvb_ref, skip_ref, gg_ref, cs_ref, csb_ref, sb_ref, rate_ref = small_refs(
        vec_ref, cst_ref, tiny_ref
    )
    inner = gg_ref.shape[1]
    pairs = inner // 128
    wbc_ref, wdt_ref, wz_ref, wx_ref, wot_ref = blocks_of(w_ref, inner, cs_ref.shape[1])

    @pl.when(step == 0)
    def _():
        state[...] = jnp.zeros_like(state)
        vpad[0:8, :] = jnp.zeros((8, inner), F32)
        spad[0:8, :] = jnp.zeros((8, spad.shape[1]), F32)

    @pl.when(step > 0)
    def _():
        vpad[0:8, :] = vpad[length : length + 8, :]
        spad[0:8, :] = spad[length : length + 8, :]

    rows = rows_ref[...]
    if first:
        rows = rows.astype(F32)
        r1 = lax.rsqrt(jnp.mean(rows * rows, axis=1, keepdims=True) + EPSILON)
        rows = (rows * r1 * gain_ref[0:1, :]).astype(BF)
        normed_ref[...] = rows
    gate_ref[...] = nn(rows, wz_ref[...])
    val = nn(rows, wx_ref[...])
    val_ref[...] = val
    vpad[8 : length + 8, :] = val
    st = nn(rows, wbc_ref[...])
    st_ref[...] = st
    spad[8 : length + 8, :] = st
    dt_in = nn(rows, wdt_ref[...])
    dt_ref[...] = dt_in

    pre = conv_pre(vpad, cv_ref, cvb_ref[...], length)
    pre_ref[...] = pre
    _, v = silu_parts(pre)
    _, bc = silu_parts(conv_pre(spad, cs_ref, csb_ref[...], length))
    half = bc.shape[1] // 2
    bb = bc[:, :half].astype(BF)
    cb = bc[:, half:].astype(BF)
    dt = softplus(dt_in + sb_ref[...])
    q_index = lax.broadcasted_iota(jnp.int32, (length, length), 0)
    s_index = lax.broadcasted_iota(jnp.int32, (length, length), 1)
    causal = q_index >= s_index
    tril = jnp.where(causal, 1.0, 0.0).astype(BF)
    a = sum_rows(tril, dt * rate_ref[...])
    a_rows = a.T
    lane_low = lax.broadcasted_iota(jnp.int32, (length, 128), 1) < WIDTH
    dt_x = spread(dt, pairs, lane_low)
    a_x = spread(a, pairs, lane_low)
    x = v * dt_x
    xb = x.astype(BF)
    scores = jnp.where(causal, nt(cb, bb), 0.0)
    inside = []
    zero = jnp.zeros((length, 128), BF)
    for p in range(pairs):
        xp = xb[:, 128 * p : 128 * (p + 1)]
        total = None
        for j in range(2):
            h = 2 * p + j
            decay = jnp.exp(jnp.minimum(a[:, h : h + 1] - a_rows[h : h + 1, :], 0.0))
            m = (scores * decay).astype(BF)
            term = nn(m, jnp.where(lane_low, xp, zero) if j == 0 else jnp.where(lane_low, zero, xp))
            total = term if total is None else total + term
        inside.append(total)
    entering = state[...]
    ent_ref[0] = entering
    outside = jnp.exp(a_x) * nn(cb, entering.astype(BF))
    a_last = a_x[length - 1 : length, :]
    xw = (x * jnp.exp(a_last - a_x)).astype(BF)
    state[...] = jnp.exp(a_last) * entering + nn(bc[:, :half].T.astype(BF), xw)
    y = jnp.concatenate(inside, axis=1) + outside + skip_ref[...] * v
    y_ref[...] = y
    _, sgate = silu_parts(gate_ref[...])
    gated = y * sgate
    square = (gated * gated).astype(BF)
    ssq_ref[...] = nt(jnp.ones((8, inner), BF), square)
    mixed = (gated * gg_ref[...]).astype(BF)
    part = nt(mixed, wot_ref[...]).astype(BF)
    if not last:
        part_ref[...] = part
    else:
        part_ref[0], part2_ref[0] = part[: length // 2], part[length // 2 :]
        cut = gb_ref.shape[1]
        mixed_ref[0] = mixed[cut:]
        dm = nn(gb_ref[0], wot_ref[...])
        dm_ref[0] = dm
        dots = token_dots(dm, mixed[:cut])
        row = lax.broadcasted_iota(jnp.int32, (8, length), 0)
        ssq_ref[...] = jnp.where(row == 0, ssq_ref[...], 0.0)
        ssq_ref[1:2, 0:cut] = dots[0:1]


def token_dots(dm, mixed):
    product = (dm * mixed.astype(F32)).astype(BF)
    return nt(jnp.ones((8, product.shape[1]), BF), product)


def whole(shape):
    return pl.BlockSpec(shape, lambda i: (0,) * len(shape), pipeline_mode=pl.Buffered(1))


def layer_specs(params, l):
    return [
        pl.BlockSpec((1,) + p.shape[1:], lambda i: (l, 0, 0), pipeline_mode=pl.Buffered(1))
        for p in params[:-1]
    ] + [whole(params[-1].shape)]


def forward_mix(rows, packed, params, l, gb=None):
    first, last = l == 0, gb is not None
    tokens, width = rows.shape
    inner = params[0].shape[2]
    bc_width = params[1].shape[2]
    dt_width = 128
    half = bc_width // 2
    q = GROUP
    blocks = tokens // q
    tok = lambda n: pl.BlockSpec((q, n), lambda i: (i, 0))
    outs = [
        ((tokens, inner), F32, tok(inner)),
        ((tokens, inner), F32, tok(inner)),
        ((tokens, bc_width), F32, tok(bc_width)),
        ((tokens, dt_width), F32, tok(dt_width)),
        ((tokens, inner), F32, tok(inner)),
        ((blocks, half, inner), F32, pl.BlockSpec((1, half, inner), lambda i: (i, 0, 0))),
        ((tokens, inner), F32, tok(inner)),
        ((8, tokens), F32, pl.BlockSpec((8, q), lambda i: (0, i))),
    ]
    half_of = lambda rows, n: pl.BlockSpec((1, rows, n), lambda i: (i, 0, 0))
    if not last:
        outs.append(((tokens, width), BF, tok(width)))
    if first:
        outs.append(((tokens, width), BF, tok(width)))
    if last:
        cut = gb.shape[1]
        for r, n, kind in (
            (q // 2, width, BF), (q // 2, width, BF), (cut, inner, F32), (q - cut, inner, BF)
        ):
            outs.append(((blocks, r, n), kind, half_of(r, n)))
    return pl.pallas_call(
        functools.partial(fwd_kernel, first, last),
        grid=(blocks,),
        in_specs=[tok(width), whole(packed.shape)]
        + layer_specs(params, l)
        + ([half_of(cut, width)] if last else []),
        out_specs=[o[2] for o in outs],
        out_shape=[jax.ShapeDtypeStruct(o[0], o[1]) for o in outs],
        scratch_shapes=[
            pltpu.VMEM((half, inner), F32),
            pltpu.VMEM((q + 8, inner), F32),
            pltpu.VMEM((q + 8, bc_width), F32),
        ],
        compiler_params=pltpu.CompilerParams(
            dimension_semantics=("arbitrary",), vmem_limit_bytes=56 * MIB
        ),
        name="mix_forward",
    )(rows, packed, *params, *([gb] if last else []))


def bwd_kernel(
    ready, layer, gb_ref, e_ref, rows_ref, gate_ref, val_ref, st_ref, stp_ref, dt_ref, y_ref,
    ent_ref, pre_ref, w_ref, vec_ref, cst_ref, tiny_ref, gain_ref, pick_ref, *rest,
):
    if ready:
        dm2_ref, *rest = rest
    dcat_ref, dpart_ref, gvec_ref, gst_ref, gdt_ref, ggain_ref, *rest = rest
    dstate, spad, dvpad, dspad = rest
    step = pl.program_id(0)
    blocks = pl.num_programs(0)
    length = y_ref.shape[0]
    cv_ref, cvb_ref, skip_ref, gg_ref, cs_ref, csb_ref, sb_ref, rate_ref = small_refs(
        vec_ref, cst_ref, tiny_ref
    )
    inner = gg_ref.shape[1]
    bc_width = cs_ref.shape[1]
    wbc_ref, wdt_ref, wz_ref, wx_ref, wot_ref = blocks_of(w_ref, inner, bc_width)
    dst_ref, ddt_ref, dgate_ref, dval_ref, mixed_ref = blocks_of(dcat_ref, inner, bc_width)
    half = bc_width // 2
    pairs = inner // 128

    @pl.when(step == 0)
    def _():
        dstate[...] = jnp.zeros_like(dstate)
        dvpad[length : length + 8, :] = jnp.zeros((8, inner), F32)
        dspad[length : length + 8, :] = jnp.zeros((8, bc_width), F32)
        gvec_ref[...] = jnp.zeros_like(gvec_ref)
        gst_ref[...] = jnp.zeros_like(gst_ref)
        gdt_ref[...] = jnp.zeros_like(gdt_ref)
        ggain_ref[...] = jnp.zeros_like(ggain_ref)

    @pl.when(step > 0)
    def _():
        dvpad[length : length + 8, :] = dvpad[0:8, :]
        dspad[length : length + 8, :] = dspad[0:8, :]

    first = step == blocks - 1
    spad[0:8, :] = jnp.where(first, 0.0, stp_ref[...])
    spad[8 : length + 8, :] = st_ref[...]

    pre_v = pre_ref[...]
    sig_v, v = silu_parts(pre_v)
    pre_s = conv_pre(spad, cs_ref, csb_ref[...], length)
    sig_s, bc = silu_parts(pre_s)
    bb = bc[:, :half].astype(BF)
    cb = bc[:, half:].astype(BF)
    z = dt_ref[...] + sb_ref[...]
    dt = softplus(z)
    rate = rate_ref[...]
    s_index = lax.broadcasted_iota(jnp.int32, (length, length), 0)
    q_index = lax.broadcasted_iota(jnp.int32, (length, length), 1)
    upper = q_index >= s_index
    a = sum_rows(jnp.where(s_index >= q_index, 1.0, 0.0).astype(BF), dt * rate)
    a_rows = a.T
    lane_low = lax.broadcasted_iota(jnp.int32, (length, 128), 1) < WIDTH
    dt_x = spread(dt, pairs, lane_low)
    a_x = spread(a, pairs, lane_low)
    x = v * dt_x
    xb = x.astype(BF)
    skip = skip_ref[...]

    y = y_ref[...]
    gate = gate_ref[...]
    sig_g, sgate = silu_parts(gate)
    gated = y * sgate
    per_token = e_ref[...].T
    e, r2 = per_token[:, 0:1], per_token[:, 1:2]
    if ready:
        dm = jnp.concatenate([gb_ref[0], dm2_ref[0]], axis=0) * r2
    else:
        dm = nn(gb_ref[...], wot_ref[...]) * r2
    dgated = dm * gg_ref[...] - e * gated
    mixed_ref[...] = (gated * r2 * gg_ref[...]).astype(BF)
    dgate = (dgated * y * (sig_g * (1.0 + gate * (1.0 - sig_g)))).astype(BF)
    dgate_ref[...] = dgate
    dy = dgated * sgate
    dyb = dy.astype(BF)
    dyf = dyb.astype(F32)

    scores = jnp.where(upper, nt(bb, cb), 0.0)
    zero = jnp.zeros((length, 128), BF)
    dscores = jnp.zeros((length, length), F32)
    dx_list = []
    for p in range(pairs):
        xp = xb[:, 128 * p : 128 * (p + 1)]
        dp = dyb[:, 128 * p : 128 * (p + 1)]
        total = None
        for j in range(2):
            h = 2 * p + j
            decay = jnp.exp(jnp.minimum(a_rows[h : h + 1, :] - a[:, h : h + 1], 0.0))
            m = (scores * decay).astype(BF)
            dh = jnp.where(lane_low, dp, zero) if j == 0 else jnp.where(lane_low, zero, dp)
            term = nn(m, dh)
            total = term if total is None else total + term
            dscores = dscores + nt(xp, dh) * decay
        dx_list.append(total)
    dx_in = jnp.concatenate(dx_list, axis=1)
    dscores = jnp.where(upper, dscores, 0.0)
    db = nn(dscores.astype(BF), cb)
    dc = nn(dscores.T.astype(BF), bb)

    entering = ent_ref[0]
    dleaving = dstate[...]
    dleaving_b = dleaving.astype(BF)
    ea = jnp.exp(a_x)
    a_last = a_x[length - 1 : length, :]
    ea_last = jnp.exp(a_last)
    w = jnp.exp(a_last - a_x)
    dxw = nn(bb, dleaving_b) * w
    db = db + nt((x * w).astype(BF), dleaving_b)
    eady = (ea * dyf).astype(BF)
    dc = dc + nt(eady, entering.astype(BF))
    dstate[...] = ea_last * dleaving + nn(bc[:, half:].T.astype(BF), eady)
    dx = dx_in + dxw
    u = x * dxw
    last_add = jnp.sum(u, axis=0, keepdims=True) + ea_last * jnp.sum(
        entering * dleaving, axis=0, keepdims=True
    )
    da_x = dyf * (y - skip * v) - xb.astype(F32) * dx_in - u
    row_index = lax.broadcasted_iota(jnp.int32, (length, inner), 0)
    da_x = da_x + jnp.where(row_index == length - 1, last_add, 0.0)
    pick = pick_ref[...]
    da = sum_lanes(da_x, pick)
    dr = sum_rows(jnp.where(upper, 1.0, 0.0).astype(BF), da)
    ddt = sum_lanes(dx * v, pick) + dr * rate
    dz = ddt * (1.0 / (1.0 + jnp.exp(-z)))
    ddtb = dz.astype(BF)
    ddt_ref[...] = ddtb
    gdt_ref[0:1, :] += jnp.sum(dz, axis=0, keepdims=True)
    gdt_ref[1:2, :] += jnp.sum(dr * dt * rate, axis=0, keepdims=True)

    dpre_v = (skip * dy + dt_x * dx) * (sig_v * (1.0 + pre_v * (1.0 - sig_v)))
    dvpad[0:length, :] = dpre_v
    dval = jnp.zeros((length, inner), F32)
    val = val_ref[...]
    for k in range(4):
        later = dvpad[pl.ds(3 - k, length), :]
        dval = dval + cv_ref[k : k + 1, :] * later
        gvec_ref[k : k + 1, :] += jnp.sum(later * val, axis=0, keepdims=True)
    gvec_ref[4:5, :] += jnp.sum(dpre_v, axis=0, keepdims=True)
    gvec_ref[5:6, :] += jnp.sum(gated * dm, axis=0, keepdims=True)
    gvec_ref[6:7, :] += jnp.sum(dy * v, axis=0, keepdims=True)
    dvalb = dval.astype(BF)
    dval_ref[...] = dvalb

    dbc = jnp.concatenate([db, dc], axis=1)
    dpre_s = dbc * (sig_s * (1.0 + pre_s * (1.0 - sig_s)))
    dspad[0:length, :] = dpre_s
    dst = jnp.zeros((length, bc_width), F32)
    st = st_ref[...]
    for k in range(4):
        later = dspad[pl.ds(3 - k, length), :]
        dst = dst + cs_ref[k : k + 1, :] * later
        gst_ref[k : k + 1, :] += jnp.sum(later * st, axis=0, keepdims=True)
    gst_ref[4:5, :] += jnp.sum(dpre_s, axis=0, keepdims=True)
    dstb = dst.astype(BF)
    dst_ref[...] = dstb
    dpart = nt(dgate, wz_ref[...]) + nt(dvalb, wx_ref[...])
    dpart = dpart + nt(dstb, wbc_ref[...]) + nt(ddtb, wdt_ref[...])
    dpart_ref[...] = dpart.astype(BF)
    ggain_ref[0:1, :] += jnp.sum(rows_ref[...].astype(F32) * dpart, axis=0, keepdims=True)

    @pl.when(step == blocks - 1)
    def _():
        ggain_ref[0:1, :] = ggain_ref[0:1, :] / gain_ref[GAIN_ROWS * layer : GAIN_ROWS * layer + 1, :]


def backward_mix(gb, ready, e_rows, rows, kept, packed, params, pick, l):
    gate, val, st, dt, y, ent, pre = kept
    tokens, width = y.shape[0], packed.shape[0]
    inner = params[0].shape[2]
    bc_width = params[1].shape[2]
    dt_width = 128
    packed_width = packed.shape[1]
    half = bc_width // 2
    q = GROUP
    blocks = tokens // q
    back = lambda i: blocks - 1 - i
    tok = lambda n: pl.BlockSpec((q, n), lambda i: (back(i), 0))
    halo = lambda n: pl.BlockSpec(
        (8, n), lambda i: (jnp.maximum(back(i) * (q // 8) - 1, 0), 0)
    )
    fixed = lambda r, c: pl.BlockSpec((r, c), lambda i: (0, 0))
    outs = [
        ((tokens, packed_width), BF, tok(packed_width)),
        ((tokens, width), BF, tok(width)),
        ((8, inner), F32, fixed(8, inner)),
        ((8, bc_width), F32, fixed(8, bc_width)),
        ((8, dt_width), F32, fixed(8, dt_width)),
        ((8, width), F32, fixed(8, width)),
    ]
    half_of = lambda v: pl.BlockSpec((1,) + v.shape[1:], lambda i: (back(i), 0, 0))
    gb, more = (gb[0], [gb[1]]) if ready else (gb, [])
    return pl.pallas_call(
        functools.partial(bwd_kernel, ready, l),
        grid=(blocks,),
        in_specs=[
            half_of(gb) if ready else tok(width),
            pl.BlockSpec((8, q), lambda i: (0, back(i))),
            tok(width),
            tok(inner), tok(inner), tok(bc_width), halo(bc_width), tok(dt_width),
            tok(inner),
            pl.BlockSpec((1, half, inner), lambda i: (back(i), 0, 0)),
            tok(inner),
        ]
        + [whole(packed.shape)] + layer_specs(params, l) + [whole(pick.shape)]
        + [half_of(v) for v in more],
        out_specs=[o[2] for o in outs],
        out_shape=[jax.ShapeDtypeStruct(o[0], o[1]) for o in outs],
        scratch_shapes=[
            pltpu.VMEM((half, inner), F32),
            pltpu.VMEM((q + 8, bc_width), F32),
            pltpu.VMEM((q + 8, inner), F32),
            pltpu.VMEM((q + 8, bc_width), F32),
        ],
        compiler_params=pltpu.CompilerParams(
            dimension_semantics=("arbitrary",), vmem_limit_bytes=60 * MIB
        ),
        name="mix_backward",
    )(gb, e_rows, rows, gate, val, st, st, dt, y, ent, pre, packed, *params, pick, *more)


class Step:
    def __init__(self, **given):
        self.rows = 0
        self.width = 0
        self.line = 4
        self.chunks = 8
        self.hop = 1
        self.pass_hop = 1
        self.slack = 0
        self.partial = False
        self.gather = False
        self.late = False
        self.scale = False
        self.inner = False
        self.layer = 0
        self.small = 0
        self.gain_row = 0
        self.weights = 0
        self.grads = 0
        self.double = 2
        self.tail = 2
        self.lag = 1
        self.states = 0
        self.sums = False
        self.bits = 0
        self.middle = None
        self.early = ()
        self.halves = False
        self.lazy = ()
        self.__dict__.update(given)


def remote(src, dst, send, recv, device):
    return pltpu.make_async_remote_copy(
        src_ref=src, dst_ref=dst, send_sem=send, recv_sem=recv,
        device_id=device, device_id_type=pl.DeviceIdType.MESH,
    )


def when(condition):
    return pl.when(condition)


def pack_weights(r, l):
    start = 0
    for part in (r.p_bc.at[l], r.p_dt.at[l], r.p_z.at[l], r.p_x.at[l], r.p_out.at[l]):
        r.wown[:, start : start + part.shape[1]] = part[...]
        start += part.shape[1]


def comm_kernel(o, names, *refs):
    r = types.SimpleNamespace(**dict(zip(names, refs)))
    r.gain_row = slice(o.gain_row, o.gain_row + 1)
    r.gbuf = [v for k, v in zip(names, refs) if k.startswith("gbuf")]
    n, count, rows = o.line, o.chunks, o.rows
    size = rows // count
    t = lax.axis_index("tensor")
    me = lax.axis_index("dp")
    own_bits = [(me // (1 << b)) % 2 for b in range(o.bits)]
    partner = [me + (1 - 2 * own_bits[b]) * (1 << b) for b in range(o.bits)]

    lazy = []
    for i, name in enumerate(o.lazy):
        near = getattr(r, name + "_v")
        lazy.append(pltpu.make_async_copy(getattr(r, name), near, r.lazy_sem.at[i]))
        setattr(r, name, near)
    leaving = []
    for i, name in enumerate(o.early):
        near = getattr(r, name + "_v")
        leaving.append((near, getattr(r, name), r.early_sem.at[i]))
        setattr(r, name, near)
    if o.halves:
        start = 0
        for i, far in enumerate((r.half0, r.half1)):
            near = r.lgrad.at[:, pl.ds(start, far.shape[1])]
            lazy.append(pltpu.make_async_copy(far, near, r.half_sem.at[i]))
            start += far.shape[1]
    for copy in lazy:
        copy.start()

    barrier = pltpu.get_barrier_semaphore()
    for k in range(1, n):
        pl.semaphore_signal(
            barrier, inc=1, device_id={"tensor": lax.rem(t + k, n)},
            device_id_type=pl.DeviceIdType.MESH,
        )
    over_dp = o.weights or o.grads
    r.early = [v for k, v in zip(names, refs) if k.startswith("esum")]
    r.lined = [v for k, v in zip(names, refs) if k.startswith("lsum")]
    r.gains = [v for k, v in zip(names, refs) if k.startswith("gsum")]
    if over_dp:
        for b in range(o.bits):
            pl.semaphore_signal(
                barrier, inc=1, device_id={"dp": partner[b]}, device_id_type=pl.DeviceIdType.MESH
            )
    pl.semaphore_wait(barrier, n - 1 + (o.bits if over_dp else 0))

    def at(s, c):
        return pl.ds(pl.multiple_of(s * rows + c * size, size), size)

    def piece(c):
        return pl.ds(pl.multiple_of(c * size, size), size)

    def hop(side, s, c, src):
        buf = r.rbuf if side == 0 else r.lbuf
        return remote(
            src, buf.at[s, piece(c)], r.rs_send.at[side, s], r.rs_recv.at[side, s, c],
            {"tensor": t + 1 if side == 0 else t - 1},
        )

    def reduce_items(side, c):
        buf = r.rbuf if side == 0 else r.lbuf
        edge = t == 0 if side == 0 else t == n - 1
        order = range(n - 1, 0, -1) if side == 0 else range(0, n - 1)
        for s in order:
            further = s > t if side == 0 else s < t

            @when(further & edge)
            def _():
                hop(side, s, c, r.part.at[at(s, c)]).start()

            @when(further & jnp.logical_not(edge))
            def _():
                hop(side, s, c, buf.at[s, piece(c)]).wait_recv()
                total = buf[s, piece(c), :].astype(F32) + r.part[at(s, c), :].astype(F32)
                buf[s, piece(c), :] = total.astype(BF)
                hop(side, s, c, buf.at[s, piece(c)]).start()

    def own_total(c):
        acc = r.acc
        acc[...] = r.part[at(t, c), :].astype(F32)

        @when(t > 0)
        def _():
            hop(0, t, c, r.rbuf.at[t, piece(c)]).wait_recv()
            acc[...] += r.rbuf[t, piece(c), :].astype(F32)

        @when(t < n - 1)
        def _():
            hop(1, t, c, r.lbuf.at[t, piece(c)]).wait_recv()
            acc[...] += r.lbuf[t, piece(c), :].astype(F32)

    def pass_on(side, s, c):
        spot = r.full.at[at(s, c)]
        return remote(
            spot, spot, r.ag_send.at[side, s], r.ag_recv.at[side, s, c],
            {"tensor": t + 1 if side == 0 else t - 1},
        )

    def forward_items(side, tau):
        order = range(n - 2, -1, -1) if side == 0 else range(1, n)
        for s in order:
            away = t - s if side == 0 else s - t
            late = o.hop * max(s, n - 1 - s) + o.slack if o.late else 0
            c = tau - late - o.pass_hop * away

            @when((away > 0) & (c >= 0) & (c < count))
            def _():
                pass_on(side, s, c).wait_recv()

                @when(t < n - 1 if side == 0 else t > 0)
                def _():
                    pass_on(side, s, c).start()

    def spot_of(k, ref):
        return ref.at[:, pl.ds(pl.multiple_of(k * rows, rows), rows)]

    def square_copy(k):
        dest = lax.rem(t + k, n)
        return remote(
            spot_of(dest, r.ssq), r.sqbuf.at[k - 1], r.sq_send.at[k - 1],
            r.sq_recv.at[k - 1], {"tensor": dest},
        )

    def inner_copy(k):
        return remote(
            spot_of(t, r.inner), spot_of(t, r.inner), r.in_send.at[k - 1],
            r.in_recv.at[k - 1], {"tensor": lax.rem(t + k, n)},
        )

    def inner_arrival(k):
        source = lax.rem(t + n - k, n)
        return remote(
            spot_of(source, r.inner), spot_of(source, r.inner), r.in_send.at[k - 1],
            r.in_recv.at[k - 1], {"tensor": source},
        )

    def bit_order(parity):
        high = list(range(o.bits - 1, 0, -1))
        if parity == 1:
            high = high[1:] + high[:1]
        return high + [0]

    def cols(j):
        return pl.ds(pl.multiple_of(j * WCHUNK, WCHUNK), WCHUNK)

    def spots(known):
        return tuple(slice(None) if b in known else own_bits[b] for b in range(o.bits - 1, -1, -1))

    def weight_copy(parity, stage, j):
        order = bit_order(parity)
        depth = r.wown.shape[0] // o.weights
        strip = pl.ds(pl.multiple_of(j * depth, depth), depth)
        spot = r.wfull.at[(*spots(order[:stage]), strip)]
        src = r.wown.at[strip] if stage == 0 else spot
        return remote(
            src, spot, r.wg_send.at[stage, j], r.wg_recv.at[stage, j],
            {"dp": partner[order[stage]]},
        )

    def small_columns():
        lanes_at = pl.ds(o.small // 128 * 128, 128)
        return pltpu.make_async_copy(
            r.wfull.at[(*spots(range(o.bits)), slice(None), lanes_at)], r.columns, r.small_sem
        )

    def small_items(tau):
        done = (o.weights + 1) // 2 + o.bits

        @when(tau == done)
        def _():
            small_columns().start()

        @when(tau == done + 1)
        def _():
            small_columns().wait()
            turned = r.columns[...].reshape(o.width, 128).astype(F32).T
            r.small[...] = turned[o.small % 128 : o.small % 128 + 16, :]

    def own_weights():
        return pltpu.make_async_copy(r.wown, r.wfull.at[spots([])], r.wl_sem)

    def each_parity(pair, fn):
        for parity in range(2):
            j = 2 * pair + parity

            @when((j >= 0) & (j < o.weights))
            def _():
                fn(parity, j)

    def weight_items(tau):
        for stage in range(o.bits + 1):
            def run(parity, j):
                if stage > 0:
                    weight_copy(parity, stage - 1, j).wait_recv()
                if stage < o.bits:
                    weight_copy(parity, stage, j).start()
            each_parity(tau - stage, run)

    def grad_order(parity):
        high = list(range(1, o.bits))
        if parity == 1:
            high = high[1:] + high[:1]
        return [0] + high

    def grad_spot(parity, stage, mine):
        order = grad_order(parity)
        done, bit = order[:stage], order[stage]
        spot = []
        for b in range(o.bits - 1, -1, -1):
            if b in done:
                spot.append(own_bits[b])
            elif b == bit:
                spot.append(own_bits[b] if mine else 1 - own_bits[b])
            else:
                spot.append(slice(None))
        return tuple(spot)

    def grad_copy(parity, stage, j):
        order = grad_order(parity)
        return remote(
            r.grad.at[(j, *grad_spot(parity, stage, False))], r.gbuf[stage].at[j],
            r.gr_send.at[stage, j], r.gr_recv.at[stage, j],
            {"dp": partner[order[stage]]},
        )

    def products(turn, i):
        product(jnp.where(turn >= 0, chunk_of(turn), -1), i)

        @when((turn >= 0) & (turn < o.double))
        def _():
            product(2 * turn + 1, i)

    def product(j, i):
        slab = o.width // 2
        inner_shape = (2,) * (o.bits - 1) + (slab >> (o.bits - 1), WCHUNK)

        def one(left):
            rows_of_slab = left[..., pl.ds(i * slab, slab)].reshape(-1, slab)
            out = tn(rows_of_slab, r.right[:, cols(j)])
            r.grad[j, i] = out.astype(BF).reshape(inner_shape)

        @when((j >= 0) & (j < o.grads - o.tail))
        def _():
            one(r.lrows)

        @when((j >= o.grads - o.tail) & (j < o.grads))
        def _():
            one(r.lgrad)

    def chunk_of(turn):
        return jnp.where(turn < o.double, 2 * turn, turn + o.double)

    def each_chunk(turn, fn):
        j = chunk_of(turn)
        for parity in range(2):
            @when((turn >= 0) & (j < o.grads) & (lax.rem(j, 2) == parity))
            def _():
                fn(parity, j)

        @when((turn >= 0) & (turn < o.double))
        def _():
            fn(1, 2 * turn + 1)

    def grad_items(tau):
        products(tau, 1)

        def first(parity, j):
            grad_copy(parity, 0, j).start()

        each_chunk(tau, first)
        for stage in range(1, o.bits + 1):
            def run(parity, j):
                grad_copy(parity, stage - 1, j).wait_recv()
                spot = grad_spot(parity, stage - 1, True)
                free = [i for i, v in enumerate(spot) if isinstance(v, slice)]
                buf = r.gbuf[stage - 1]
                for combo in range(1 << len(free)):
                    pick = [(combo >> i) % 2 for i in range(len(free))]
                    full = list(spot)
                    for i, v in zip(free, pick):
                        full[i] = v
                    total = r.grad[(j, *full)].astype(F32) + buf[(j, *pick)].astype(F32)
                    if stage < o.bits:
                        r.grad[(j, *full)] = total.astype(BF)
                    else:
                        r.gnear[:, cols(j)] = total

                        @when(j > 0)
                        def _():
                            grad_leave(j).start()
                if stage < o.bits:
                    grad_copy(parity, stage, j).start()
            each_chunk(tau - grad_lag(stage), run)

    def grad_leave(j):
        return pltpu.make_async_copy(r.gnear.at[:, cols(j)], r.gout.at[:, cols(j)], r.leave_sem)

    def grad_lag(stage):
        return o.lag * (2 * stage - 1) if stage else 0

    def share(buf, send, recv, k):
        return remote(buf.at[t], buf.at[t], send.at[k - 1], recv.at[k - 1],
                      {"tensor": lax.rem(t + k, n)})

    def shared(buf, send, recv):
        for k in range(1, n):
            source = lax.rem(t + n - k, n)
            remote(buf.at[source], buf.at[source], send.at[k - 1], recv.at[k - 1],
                   {"tensor": source}).wait_recv()

    def line_total(buf):
        total = buf[0]
        for k in range(1, n):
            total = total + buf[k]
        return total

    def double(acc, buf, send, recv, b):
        return remote(acc.at[b], buf.at[b], send.at[b], recv.at[b], {"dp": partner[b]})

    def doubled(acc, buf, send, recv, b):
        double(acc, buf, send, recv, b).wait_recv()
        acc[b + 1] = acc[b] + buf[b]

    def lanes(index, ref):
        return slice(index * ref.shape[1], (index + 1) * ref.shape[1])

    line_groups, dp_groups = [], []
    if o.sums:
        line_groups = [(r.lbank, r.lb_send, r.lb_recv), (r.gbank, r.gb_send, r.gb_recv)]
        dp_groups = [
            (r.dbank, r.dbuf, r.db_send, r.db_recv), (r.hbank, r.hbuf, r.hb_send, r.hb_recv)
        ]

    def sum_items(tau):
        @when(tau == 2)
        def _():
            for g in line_groups:
                shared(*g)
            off = 0
            for v in r.early:
                r.dbank[0, :, off : off + v.shape[1]] = v[...]
                off += v.shape[1]
            r.dbank[0, :, off:] = line_total(r.lbank)
            r.hbank[0] = line_total(r.gbank)
            for g in dp_groups:
                double(*g, 0).start()

        for b in range(o.bits):
            @when(tau == 4 + b)
            def _():
                for g in dp_groups:
                    doubled(*g, b)
                    if b < o.bits - 1:
                        double(*g, b + 1).start()

    def state_items(tau):
        at_first = grad_lag(o.bits) + 1
        quarter = r.gout.shape[0] // n

        @when(tau == at_first)
        def _():
            for s in range(n):
                r.qsend[s] = r.gnear[s * quarter : (s + 1) * quarter, 0 : o.states].astype(BF)
            for k in range(1, n):
                state_out(k).start()

        @when(tau == at_first + 2)
        def _():
            total = r.qsend[t].astype(F32)
            for k in range(1, n):
                state_out(k).wait_recv()
                total = total + r.qbuf[k - 1].astype(F32)
            r.qall[t] = total.astype(BF)
            for k in range(1, n):
                share(r.qall, r.qa_send, r.qa_recv, k).start()

    def state_out(k):
        dest = lax.rem(t + k, n)
        return remote(r.qsend.at[dest], r.qbuf.at[k - 1], r.qs_send.at[k - 1],
                      r.qs_recv.at[k - 1], {"tensor": dest})

    if o.sums:
        off = 0
        for v in r.lined:
            r.lbank[t, :, off : off + v.shape[1]] = v[...]
            off += v.shape[1]
        for i, v in enumerate(r.gains):
            r.gbank[t, :, lanes(i, v)] = v[0:1, :]
        for g in line_groups:
            for k in range(1, n):
                share(*g, k).start()
    if o.scale:
        for k in range(1, n):
            square_copy(k).start()
    if o.weights:
        pack_weights(r, o.layer)
        own_weights().start()
    if o.scale:
        total = spot_of(t, r.ssq)[...]
        for k in range(1, n):
            square_copy(k).wait_recv()
            total = total + r.sqbuf[k - 1]
        scale = lax.rsqrt(total / (o.scale * 1.0) + EPSILON)
        r.r2[...] = jnp.broadcast_to(scale.T[:, 0:1], (rows, 128))
    if o.gather and not o.late:
        r.full[pl.ds(pl.multiple_of(t * rows, rows), rows), :] = o.payload(r)
    if o.middle is not None:
        o.middle(r, None, None)

    ends = [count + o.hop * (n - 1) + o.slack]
    if o.late:
        ends.append(ends[0] + o.pass_hop * (n - 1))
    elif o.gather:
        ends.append(count + o.pass_hop * (n - 1))
    if o.weights:
        ends.append((o.weights + 1) // 2 + o.bits + (2 if o.small else 0))
    if o.grads:
        ends.append(1 + o.grads - o.double + grad_lag(o.bits))
        ends.append(grad_lag(o.bits) + 5)
    if o.sums:
        ends.append(4 + o.bits)

    def iteration(tau, _):
        if lazy:
            @when(tau == 1)
            def _():
                for copy in lazy:
                    copy.wait()
        if o.grads:
            products(tau - 1, 0)
        if o.partial:
            for side in range(2):
                c = tau - o.hop * (t if side == 0 else n - 1 - t)

                @when((c >= 0) & (c < count))
                def _():
                    reduce_items(side, c)

            c_own = tau - o.hop * jnp.maximum(t, n - 1 - t) - o.slack

            @when((c_own >= 0) & (c_own < count))
            def _():
                own_total(c_own)
                out = o.middle(r, piece(c_own), r.acc[...])
                for near, far, sem in leaving:
                    spot = piece(c_own)
                    pltpu.make_async_copy(near.at[spot], far.at[spot], sem).start()
                if o.late:
                    r.full[at(t, c_own), :] = out
        if o.gather:
            c_out = tau - o.hop * jnp.maximum(t, n - 1 - t) - o.slack if o.late else tau

            @when((c_out >= 0) & (c_out < count))
            def _():
                @when(t < n - 1)
                def _():
                    pass_on(0, t, c_out).start()

                @when(t > 0)
                def _():
                    pass_on(1, t, c_out).start()

            for side in range(2):
                forward_items(side, tau)
        if o.weights:
            @when(tau == 1)
            def _():
                own_weights().wait()
            weight_items(tau)
            if o.small:
                small_items(tau)
        if o.grads:
            grad_items(tau - 1)
            state_items(tau - 1)
        if o.sums:
            sum_items(tau)
        return 0

    lax.fori_loop(0, max(ends), iteration, 0)

    if o.inner:
        spot_of(t, r.inner)[...] = r.icol[...].T[0:8, :]
        for k in range(1, n):
            inner_copy(k).start()
        for k in range(1, n):
            inner_arrival(k).wait_recv()
        for k in range(1, n):
            inner_copy(k).wait_send()
    if o.sums:
        r.sums[...] = r.dbank[o.bits]
        for i, v in enumerate(r.gains):
            r.gain_sums[i : i + 1, :] = r.hbank[o.bits, :, lanes(i, v)]
        for g in line_groups:
            for k in range(1, n):
                share(*g, k).wait_send()
        for g in dp_groups:
            for b in range(o.bits):
                double(*g, b).wait_send()
    if o.grads:
        shared(r.qall, r.qa_send, r.qa_recv)
        quarter = r.gout.shape[0] // n
        for s in range(n):
            r.gnear[s * quarter : (s + 1) * quarter, 0 : o.states] = r.qall[s].astype(F32)
        grad_leave(jnp.int32(0)).start()
        for k in range(1, n):
            state_out(k).wait_send()
            share(r.qall, r.qa_send, r.qa_recv, k).wait_send()
    if o.scale:
        for k in range(1, n):
            square_copy(k).wait_send()
    for s in range(n):
        for side in range(2):
            inside = t < n - 1 if side == 0 else t > 0
            if o.partial:
                @when((s > t if side == 0 else s < t) & inside)
                def _():
                    buf = (r.rbuf if side == 0 else r.lbuf).at[s]
                    remote(
                        buf, buf, r.rs_send.at[side, s], r.rs_recv.at[side, s, 0],
                        {"tensor": t + 1 if side == 0 else t - 1},
                    ).wait_send()
            if o.gather:
                @when((s <= t if side == 0 else s >= t) & inside)
                def _():
                    spot = r.full.at[pl.ds(s * rows, rows)]
                    remote(
                        spot, spot, r.ag_send.at[side, s], r.ag_recv.at[side, s, 0],
                        {"tensor": t + 1 if side == 0 else t - 1},
                    ).wait_send()
    for j in range(o.weights):
        for stage in range(o.bits):
            weight_copy(j % 2, stage, jnp.int32(j)).wait_send()
    for j in range(o.grads):
        for stage in range(o.bits):
            grad_copy(j % 2, stage, jnp.int32(j)).wait_send()
    if o.grads:
        pltpu.make_async_copy(r.gnear, r.gout, r.leave_sem).wait()
    for near, far, sem in leaving:
        pltpu.make_async_copy(near, far, sem).wait()


def comm_call(o, name, collective, inputs, outputs, **scratch):
    n, count, rows, width = o.line, o.chunks, o.rows, o.width
    dma = pltpu.SemaphoreType.DMA
    if o.lazy:
        for key in o.lazy:
            value = inputs[key][0]
            inputs[key] = (value, pl.ANY)
            scratch[key + "_v"] = pltpu.VMEM(value.shape, value.dtype)
        scratch.update(lazy_sem=dma((len(o.lazy),)))
    if o.early:
        for key in o.early:
            shape, kind, _ = outputs[key]
            outputs[key] = (shape, kind, pl.ANY)
            scratch[key + "_v"] = pltpu.VMEM(shape, kind)
        scratch.update(early_sem=dma((len(o.early),)))
    if o.halves:
        scratch.update(lgrad=pltpu.VMEM((n, rows, width), BF), half_sem=dma((2,)))
    if o.partial:
        scratch.update(
            rbuf=pltpu.VMEM((n, rows, width), BF),
            lbuf=pltpu.VMEM((n, rows, width), BF),
            acc=pltpu.VMEM((rows // count, width), F32),
            rs_send=dma((2, n)),
            rs_recv=dma((2, n, count)),
        )
    if o.gather:
        scratch.update(ag_send=dma((2, n)), ag_recv=dma((2, n, count)))
    if o.scale:
        scratch.update(
            sqbuf=pltpu.VMEM((n - 1, 8, rows), F32), sq_send=dma((n - 1,)), sq_recv=dma((n - 1,))
        )
    if o.inner:
        scratch.update(
            icol=pltpu.VMEM((rows, 128), F32), in_send=dma((n - 1,)), in_recv=dma((n - 1,))
        )
    if o.weights:
        rows_of_pack = inputs["p_bc"][0].shape[1]
        pack_width = sum(v[0].shape[2] for k, v in inputs.items() if k.startswith("p_"))
        scratch.update(
            columns=pltpu.VMEM((*(2,) * o.bits, rows_of_pack, 128), BF),
            small_sem=dma(()),
            wown=pltpu.VMEM((rows_of_pack, pack_width), BF),
            wl_sem=dma(()),
            wg_send=dma((o.bits, o.weights)),
            wg_recv=dma((o.bits, o.weights)),
        )
    if o.grads:
        depth = o.width >> o.bits
        scratch.update(
            grad=pltpu.VMEM((o.grads, *(2,) * o.bits, depth, WCHUNK), BF),
            gr_send=dma((o.bits, o.grads)),
            gr_recv=dma((o.bits, o.grads)),
        )
        for stage in range(o.bits):
            scratch["gbuf%d" % stage] = pltpu.VMEM(
                (o.grads, *(2,) * (o.bits - 1 - stage), depth, WCHUNK), BF
            )
        scratch.update(
            gnear=pltpu.VMEM(outputs["gout"][0], F32), leave_sem=dma(()),
        )
        part = (n, (width >> o.bits) // n, o.states)
        scratch.update(
            qsend=pltpu.VMEM(part, BF), qall=pltpu.VMEM(part, BF),
            qbuf=pltpu.VMEM((n - 1,) + part[1:], BF),
            qs_send=dma((n - 1,)), qs_recv=dma((n - 1,)),
            qa_send=dma((n - 1,)), qa_recv=dma((n - 1,)),
        )
    if o.sums:
        def lanes_of(start):
            return sum(v[0].shape[1] for k, v in inputs.items() if k.startswith(start))

        lined, early, gains = lanes_of("lsum"), lanes_of("esum"), lanes_of("gsum")
        for one, two, tall, line_width, dp_width in (
            ("lb", "db", 8, lined, lined + early), ("gb", "hb", 1, gains, gains)
        ):
            scratch[one + "ank"] = pltpu.VMEM((n, tall, line_width), F32)
            scratch[two + "ank"] = pltpu.VMEM((o.bits + 1, tall, dp_width), F32)
            scratch[two + "uf"] = pltpu.VMEM((o.bits, tall, dp_width), F32)
            for key, size in ((one, n - 1), (two, o.bits)):
                scratch[key + "_send"] = dma((size,))
                scratch[key + "_recv"] = dma((size,))
    names = [*inputs, *outputs, *scratch]
    out = pl.pallas_call(
        functools.partial(comm_kernel, o, names),
        in_specs=[pl.BlockSpec(memory_space=i[1]) for i in inputs.values()],
        out_specs=[pl.BlockSpec(memory_space=i[2]) for i in outputs.values()],
        out_shape=[jax.ShapeDtypeStruct(i[0], i[1]) for i in outputs.values()],
        scratch_shapes=list(scratch.values()),
        compiler_params=pltpu.CompilerParams(
            collective_id=collective, has_side_effects=True, vmem_limit_bytes=62 * MIB
        ),
        name=name,
    )(*[i[0] for i in inputs.values()])
    return dict(zip(outputs, out))


def meet_kernel(
    n, inner_all, own_ref, grad_ref, mixed_ref, w_ref,
    out_ref, scale_ref, dm_ref, stage, near, bank, send, recv, sem,
):
    t = lax.axis_index("tensor")
    inner = near.shape[1]
    weight = pltpu.make_async_copy(w_ref.at[:, pl.ds(w_ref.shape[1] - inner, inner)], near, sem)
    weight.start()
    barrier = pltpu.get_barrier_semaphore()
    for k in range(1, n):
        pl.semaphore_signal(
            barrier, inc=1, device_id={"tensor": lax.rem(t + k, n)},
            device_id_type=pl.DeviceIdType.MESH,
        )
    stage[...] = own_ref[...]
    rows, cut = scale_ref.shape[0], grad_ref.shape[1]
    weight.wait()
    for s in range(n):
        dm = nn(grad_ref[s], near[...])
        dm_ref[s] = dm
        stage[1:2, (s + 1) * rows - cut : (s + 1) * rows] = token_dots(dm, mixed_ref[s])[0:1]
    pl.semaphore_wait(barrier, n - 1)
    copies = [
        remote(stage, bank.at[t], send.at[k - 1], recv.at[k - 1], {"tensor": lax.rem(t + k, n)})
        for k in range(1, n)
    ]
    for copy in copies:
        copy.start()
    bank[t] = stage[...]
    for k in range(1, n):
        source = lax.rem(t + n - k, n)
        remote(
            stage, bank.at[source], send.at[k - 1], recv.at[k - 1], {"tensor": source}
        ).wait_recv()
    total = bank[0]
    for s in range(1, n):
        total = total + bank[s]
    scale = lax.rsqrt(total[0:1, :] / inner_all + EPSILON)
    row = lax.broadcasted_iota(jnp.int32, total.shape, 0)
    e = scale * scale * scale * (total[1:2, :] / inner_all)
    out_ref[...] = jnp.where(row == 0, e, scale)
    mine = out_ref[:, pl.ds(pl.multiple_of(t * rows, rows), rows)].T
    scale_ref[...] = jnp.broadcast_to(mine[:, 1:2], scale_ref.shape)
    for copy in copies:
        copy.wait_send()


def meet(own, grad, mixed, packed, n, inner_all, collective):
    vmem = pl.BlockSpec(memory_space=pltpu.VMEM)
    dma = pltpu.SemaphoreType.DMA
    inner = mixed.shape[2]
    return pl.pallas_call(
        functools.partial(meet_kernel, n, inner_all),
        in_specs=[vmem, vmem, vmem, pl.BlockSpec(memory_space=pl.ANY)],
        out_specs=[vmem, vmem, vmem],
        out_shape=[
            jax.ShapeDtypeStruct(own.shape, F32),
            jax.ShapeDtypeStruct((own.shape[1] // n, 128), F32),
            jax.ShapeDtypeStruct(mixed.shape, F32),
        ],
        scratch_shapes=[
            pltpu.VMEM(own.shape, F32), pltpu.VMEM((packed.shape[0], inner), BF),
            pltpu.VMEM((n,) + own.shape, F32), dma((n - 1,)), dma((n - 1,)), dma(()),
        ],
        compiler_params=pltpu.CompilerParams(
            collective_id=collective, has_side_effects=True, vmem_limit_bytes=62 * MIB
        ),
        name="turn_around",
    )(own, grad, mixed, packed)


def plain_payload(r):
    return r.own[...]


def token_columns(first, second):
    lane = lax.broadcasted_iota(jnp.int32, (first.shape[0], 128), 1)
    return jnp.where(lane == 0, first, second)


def forward_middle(r, at, total):
    if at is None:
        return None
    branch = total * r.r2[at, 0:1]
    residual = r.res[at, :].astype(F32) + branch
    r.branch[at, :] = branch
    r.res_out[at, :] = residual
    r1 = lax.rsqrt(jnp.mean(residual * residual, axis=1, keepdims=True) + EPSILON)
    return (residual * r1 * r.gain[r.gain_row, :]).astype(BF)


def backward_middle(inner_all, r, at, total):
    if at is None:
        return None
    res = r.res[at, :].astype(F32)
    width = res.shape[1]
    r1 = lax.rsqrt(jnp.mean(res * res, axis=1, keepdims=True) + EPSILON)
    hat = res * r1
    dn = total * r.gain[r.gain_row, :]
    cross = jnp.sum(dn * hat, axis=1, keepdims=True) / width
    grad = r.grad_in[at, :].astype(F32) + r1 * (dn - hat * cross)
    r.grad_out[at, :] = grad
    if inner_all is None:
        return None
    r2 = r.r2[at, 0:1]
    dot = jnp.sum(grad.astype(BF).astype(F32) * r.branch[at, :], axis=1, keepdims=True)
    r.icol[at, :] = token_columns(r2 * r2 * dot / inner_all, r2)
    return grad.astype(BF)


def assemble_kernel(layers, dp_count, heads, bc_width, inner, *refs):
    gouts, (sums, gains, pick), refs = refs[:layers], refs[layers : layers + 3], refs[layers + 3 :]
    res, scale, *halves = refs[:4]
    norm, gz, gx, gbc, gdt, cv, cvb, cs, csb, sb, ld, sk, gg, po, hidden = refs[4:]
    me = lax.axis_index("dp")
    start = 0
    for half in halves:
        at = slice(start, start + half.shape[0])
        start += half.shape[0]
        hidden[at, :] = res[at, :] + scale[at, 0:1] * half[...].astype(F32)

    def own(v):
        share = v.shape[1] // dp_count
        return pltpu.roll(v, v.shape[1] - me * share, 1)[:, :share]

    norm[...] = own(gains[...])[0:layers]
    for l in range(layers):
        full = gouts[l]
        first = bc_width + 128
        gbc[l] = full[:, 0:bc_width]
        gdt[:, l, :] = full[:, bc_width:first].T[0:heads, :]
        gz[l] = full[:, first : first + inner]
        gx[l] = full[:, first + inner : first + 2 * inner]
        po[l] = full[:, first + 2 * inner :]
        base = l * (inner + 128)
        vec = sums[:, base : base + inner]
        step = sums[:, base + inner : base + inner + 128]
        start = layers * (inner + 128) + l * bc_width
        state = own(sums[:, start : start + bc_width])
        cv[l] = vec[0:4]
        cvb[l : l + 1] = vec[4:5]
        gg[l : l + 1] = vec[5:6]
        one, two, three = parts3(vec)
        head_sums = nn(one, pick[...]) + nn(two, pick[...]) + nn(three, pick[...])
        sk[l : l + 1] = head_sums[6:7, 0:heads]
        sb[l : l + 1] = step[0:1, 0:heads]
        ld[l : l + 1] = step[1:2, 0:heads]
        cs[l] = state[0:4]
        csb[l : l + 1] = state[4:5]


def assemble(gouts, sums, gains, pick, dp_count, heads, bc_width, inner, hidden):
    layers, (rows, _) = len(gouts), gouts[0].shape
    vmem = pl.BlockSpec(memory_space=pltpu.VMEM)
    share = bc_width // dp_count
    shapes = [
        (layers, gains.shape[1] // dp_count),
        (layers, rows, inner), (layers, rows, inner), (layers, rows, bc_width),
        (heads, layers, rows), (layers, 4, inner), (layers, inner), (layers, 4, share),
        (layers, share), (layers, heads), (layers, heads), (layers, heads), (layers, inner),
        (layers, rows, inner), hidden[0].shape,
    ]
    inputs = [*gouts, sums, gains, pick, *hidden]
    return pl.pallas_call(
        functools.partial(assemble_kernel, layers, dp_count, heads, bc_width, inner),
        in_specs=[vmem] * len(inputs),
        out_specs=[vmem] * len(shapes),
        out_shape=[jax.ShapeDtypeStruct(v, F32) for v in shapes],
        compiler_params=pltpu.CompilerParams(vmem_limit_bytes=62 * MIB),
        name="assemble",
    )(*inputs)


def shards(
    hidden_in,
    out_grad,
    norm_gain,
    proj_z,
    proj_x,
    proj_bc,
    proj_dt,
    conv_value,
    conv_value_bias,
    conv_state,
    conv_state_bias,
    step_bias,
    log_decay,
    skip_gain,
    gate_gain,
    proj_out,
):
    tensor_count = lax.axis_size("tensor")
    dp_count = lax.axis_size("dp")
    bits = dp_count.bit_length() - 1
    layers, shard_rows, inner = proj_z.shape
    rows_own, width = hidden_in.shape
    tokens = rows_own * tensor_count
    heads = step_bias.shape[1]
    bc_width = proj_bc.shape[2]
    inner_all = inner * tensor_count
    packed_width = bc_width + 128 + 3 * inner
    column_chunks, row_chunks = packed_width // WCHUNK, shard_rows // 16
    vmem, far = pltpu.VMEM, pl.ANY

    taps = jnp.concatenate([conv_state, conv_state_bias[:, None]], axis=1)
    taps = jnp.pad(taps, ((0, 0), (0, 0), (0, shard_rows - taps.shape[2])))
    extra = jnp.concatenate([norm_gain[:, None], taps], axis=1)
    per_layer = extra.shape[1]
    extra = extra.reshape(per_layer * layers, shard_rows).T
    step_block = jnp.concatenate(
        [
            proj_dt,
            jnp.broadcast_to(extra[None], (layers,) + extra.shape),
            jnp.zeros((layers, shard_rows, 128 - heads - extra.shape[1]), BF),
        ],
        axis=2,
    )
    out_turned = jnp.transpose(proj_out, (0, 2, 1))
    full_shape = ((2,) * bits) + (shard_rows, packed_width)
    common = dict(rows=rows_own, width=width, line=tensor_count, bits=bits)

    weight_in = dict(
        p_bc=(proj_bc, vmem), p_dt=(step_block, vmem), p_z=(proj_z, vmem), p_x=(proj_x, vmem),
        p_out=(out_turned, vmem),
    )
    weight_out = dict(wfull=(full_shape, BF, far))

    vec = jnp.concatenate(
        [
            conv_value,
            conv_value_bias[:, None],
            jnp.repeat(skip_gain, WIDTH, axis=1)[:, None],
            gate_gain[:, None],
        ],
        axis=1,
    ).astype(F32)
    tiny = jnp.stack([step_bias.astype(F32), -jnp.exp(log_decay.astype(F32))], axis=1)
    tiny = jnp.pad(tiny, ((0, 0), (0, 0), (0, 128 - heads)))
    pick = jnp.asarray(np.arange(inner)[:, None] // WIDTH == np.arange(128)[None, :], BF)

    whole_rows, own_rows = ((tokens, width), BF, vmem), ((rows_own, width), F32, vmem)
    got = comm_call(
        Step(gather=True, payload=plain_payload, weights=row_chunks,
             small=bc_width + heads, **common),
        "gather_first", 1,
        dict(own=(hidden_in, vmem), **weight_in),
        dict(full=whole_rows, small=((16, width), F32, vmem), **weight_out),
    )
    x_rows = got["full"]
    out_grad, x_rows = lax.optimization_barrier((out_grad, x_rows))
    cut = rows_own * 5 // 8

    def gather_half(v):
        return lax.all_gather(v, "tensor", axis=0)

    first_half = gather_half(out_grad[:cut])
    packed = [got["wfull"].reshape(width, packed_width)]
    small = got["small"]
    per = bc_width // dp_count
    smalls = small[: per_layer * layers].reshape(layers, per_layer, dp_count, shard_rows)
    cst = smalls[:, 1:, :, :per].reshape(layers, per_layer - 1, bc_width)
    params = (vec, cst, tiny, small)

    out = forward_mix(x_rows, packed[0], params, 0)
    saved, rows = [out[:7]], [out[9]]
    residuals, branches, r2s = [hidden_in], [], []
    for l in range(layers - 1):
        got = comm_call(
            Step(
                partial=True, gather=True, late=True, scale=inner_all, middle=forward_middle, chunks=16,
                early=("branch", "res_out"),
                weights=row_chunks, layer=l + 1, gain_row=per_layer * (l + 1), **common,
            ),
            "between_forward", 2 + l,
            dict(part=(out[8], vmem), ssq=(out[7], vmem), res=(residuals[l], vmem),
                 gain=(small, vmem), **weight_in),
            dict(full=whole_rows, branch=own_rows, res_out=own_rows,
                 r2=((rows_own, 128), F32, vmem), **weight_out),
        )
        if l + 1 == layers - 1:
            last_grad, got["full"] = lax.optimization_barrier((out_grad[cut:], got["full"]))
            second_half = gather_half(last_grad)
        rows.append(got["full"])
        branches.append(got["branch"])
        residuals.append(got["res_out"])
        r2s.append(got["r2"])
        packed.append(got["wfull"].reshape(width, packed_width))
        gb = first_half if l + 1 == layers - 1 else None
        out = forward_mix(rows[-1], packed[-1], params, l + 1, gb)
        saved.append(out[:7])
    def scatter_half(v):
        return lax.psum_scatter(
            v.reshape(-1, width), "tensor", scatter_dimension=0, tiled=True
        )

    branch_halves = [scatter_half(out[8])]
    token_rows, r2_own, second_product = meet(
        out[7], second_half, out[11], packed[-1], tensor_count, inner_all, 16
    )
    grad_rows = None
    gradient = out_grad
    scattered, summed, gain_grads = [None] * layers, [None] * layers, [None] * layers
    for l in reversed(range(layers)):
        last = l == layers - 1
        dcat, dpart, *small_grads = backward_mix(
            (out[10], second_product) if last else grad_rows, last, token_rows, rows[l], saved[l],
            packed[l], params, pick, l,
        )
        summed[l], gain_grads[l] = small_grads[:3], small_grads[3]
        more = l > 0
        inputs = dict(
            part=(dpart, vmem), res=(residuals[l], vmem), gain=(small, vmem),
            grad_in=(gradient, vmem), lrows=(rows[l], vmem), right=(dcat, vmem),
        )
        if last:
            inputs.update(half0=(first_half, far), half1=(second_half, far))
        else:
            inputs.update(lgrad=(grad_rows, vmem))
        outputs = dict(
            grad_out=own_rows,
            gout=((shard_rows, packed_width), F32, far),
        )
        if more:
            inputs.update(r2=(r2s[l - 1], vmem), branch=(branches[l - 1], vmem))
            outputs.update(full=whole_rows, inner=((8, tokens), F32, vmem))
        else:
            for i in range(layers):
                gvec, gst, gdt = summed[i]
                inputs["esum%d" % i], inputs["esum_%d" % i] = (gvec, vmem), (gdt, vmem)
                inputs["lsum%d" % i] = (gst, vmem)
            for i in range(layers):
                inputs["gsum%d" % i] = (gain_grads[i], vmem)
            early = sum(v.shape[1] for i in range(layers) for v in summed[i])
            outputs.update(
                sums=((8, early), F32, vmem), gain_sums=((8, width), F32, vmem)
            )
        got = comm_call(
            Step(
                partial=True, gather=more, late=more, inner=more, grads=column_chunks,
                chunks=16 if more else 8, lag=2 if more else 1,
                states=bc_width, sums=not more, gain_row=per_layer * l,
                early=("grad_out",), halves=last, double=0 if more else 2,
                lazy=("right", "lrows", "res", "grad_in")
                + (() if last else ("lgrad",)) + (("branch",) if more else ()),
                middle=functools.partial(backward_middle, inner_all if more else None), **common,
            ),
            "between_backward" if more else "last_backward", 17 + l, inputs, outputs,
        )
        gradient = got["grad_out"]
        scattered[l] = got["gout"]
        if more:
            grad_rows, token_rows = got["full"], got["inner"]
        if last:
            second_part, gradient = lax.optimization_barrier((out[9], gradient))
            branch_halves.append(scatter_half(second_part))
    grads = list(
        assemble(
            scattered, got["sums"], got["gain_sums"], pick, dp_count, heads, bc_width, inner,
            [residuals[-1], r2_own, *branch_halves],
        )
    )
    hidden_out = grads.pop()
    grads[4] = jnp.transpose(grads[4], (1, 2, 0))
    grads[-1] = jnp.transpose(grads[-1], (0, 2, 1))
    return (hidden_out, gradient, *grads)


def solution(mesh):
    placed = (
        P(("dp", "tensor"), None),
        P(("dp", "tensor"), None),
        P(None, "dp"),
        P(None, "dp", "tensor"),
        P(None, "dp", "tensor"),
        P(None, "dp", None),
        P(None, "dp", "tensor"),
        P(None, None, "tensor"),
        P(None, "tensor"),
        P(None, None, "dp"),
        P(None, "dp"),
        P(None, "tensor"),
        P(None, "tensor"),
        P(None, "tensor"),
        P(None, "tensor"),
        P(None, "tensor", "dp"),
    )
    return jax.shard_map(
        shards,
        mesh=mesh,
        in_specs=placed,
        out_specs=(
            P(("dp", "tensor"), None),
            P(("dp", "tensor"), None),
            P(None, "dp"),
            P(None, "dp", "tensor"),
            P(None, "dp", "tensor"),
            P(None, "dp", None),
            P(None, "dp", "tensor"),
            P(None, None, "tensor"),
            P(None, "tensor"),
            P(None, None, "dp"),
            P(None, "dp"),
            P(None, "tensor"),
            P(None, "tensor"),
            P(None, "tensor"),
            P(None, "tensor"),
            P(None, "tensor", "dp"),
        ),
        check_vma=False,
    )
```

```python
import functools
import types

import jax
import jax.numpy as jnp
from jax import lax
import numpy as np
from jax.sharding import PartitionSpec as P
import jax.experimental.pallas as pl
import jax.experimental.pallas.tpu as pltpu

GROUP = 256
EPSILON = 1e-05
BF = jnp.bfloat16
F32 = jnp.float32
WIDTH = 64
GAIN_ROWS = 6
MIB = 1024 * 1024
WCHUNK = 384


def nn(a, b):
    return lax.dot_general(a, b, (((1,), (0,)), ((), ())), preferred_element_type=F32)


def tn(a, b):
    return lax.dot_general(a, b, (((0,), (0,)), ((), ())), preferred_element_type=F32)


def nt(a, b):
    return lax.dot_general(a, b, (((1,), (1,)), ((), ())), preferred_element_type=F32)


def parts3(v):
    one = v.astype(BF)
    rest = v - one.astype(F32)
    two = rest.astype(BF)
    three = (rest - two.astype(F32)).astype(BF)
    return one, two, three


def sum_rows(select, v):
    one, two, three = parts3(v)
    return nn(select, one) + nn(select, two) + nn(select, three)


def sum_lanes(v, select):
    one = v.astype(BF)
    two = (v - one.astype(F32)).astype(BF)
    return nn(one, select) + nn(two, select)


def silu_parts(v):
    sig = 1.0 / (1.0 + jnp.exp(-v))
    return sig, v * sig


def softplus(v):
    return jnp.maximum(v, 0.0) + jnp.log1p(jnp.exp(-jnp.abs(v)))


def pair_spread(column_values, pair, lane_low):
    low = column_values[:, 2 * pair : 2 * pair + 1]
    high = column_values[:, 2 * pair + 1 : 2 * pair + 2]
    return jnp.where(lane_low, low, high)


def spread(column_values, pairs, lane_low):
    return jnp.concatenate([pair_spread(column_values, p, lane_low) for p in range(pairs)], axis=1)


def conv_pre(padded, taps, bias, length):
    count = 4
    total = bias
    for k in range(count):
        total = total + taps[k : k + 1, :] * padded[pl.ds(8 - (count - 1) + k, length), :]
    return total


def blocks_of(w_ref, inner, bc_width):
    sizes = (bc_width, 128, inner, inner, inner)
    starts = [sum(sizes[:i]) for i in range(5)]
    return [w_ref.at[:, pl.ds(s, z)] for s, z in zip(starts, sizes)]


def small_refs(vec_ref, cst_ref, tiny_ref):
    vec, cst, tiny = vec_ref.at[0], cst_ref.at[0], tiny_ref.at[0]
    return (
        vec.at[0:4], vec.at[4:5], vec.at[5:6], vec.at[6:7],
        cst.at[0:4], cst.at[4:5], tiny.at[0:1], tiny.at[1:2],
    )


def fwd_kernel(
    first, last, rows_ref, w_ref, vec_ref, cst_ref, tiny_ref, gain_ref, *rest,
):
    if last:
        gb_ref, *rest = rest
    gate_ref, val_ref, st_ref, dt_ref, y_ref, ent_ref, pre_ref, ssq_ref, part_ref, *rest = rest
    if first:
        normed_ref, *rest = rest
    if last:
        part2_ref, dm_ref, mixed_ref, *rest = rest
    state, vpad, spad = rest[-3:]
    step = pl.program_id(0)
    length = rows_ref.shape[0]
    cv_ref, cvb_ref, skip_ref, gg_ref, cs_ref, csb_ref, sb_ref, rate_ref = small_refs(
        vec_ref, cst_ref, tiny_ref
    )
    inner = gg_ref.shape[1]
    pairs = inner // 128
    wbc_ref, wdt_ref, wz_ref, wx_ref, wot_ref = blocks_of(w_ref, inner, cs_ref.shape[1])

    @pl.when(step == 0)
    def _():
        state[...] = jnp.zeros_like(state)
        vpad[0:8, :] = jnp.zeros((8, inner), F32)
        spad[0:8, :] = jnp.zeros((8, spad.shape[1]), F32)

    @pl.when(step > 0)
    def _():
        vpad[0:8, :] = vpad[length : length + 8, :]
        spad[0:8, :] = spad[length : length + 8, :]

    rows = rows_ref[...]
    if first:
        rows = rows.astype(F32)
        r1 = lax.rsqrt(jnp.mean(rows * rows, axis=1, keepdims=True) + EPSILON)
        rows = (rows * r1 * gain_ref[0:1, :]).astype(BF)
        normed_ref[...] = rows
    gate_ref[...] = nn(rows, wz_ref[...])
    val = nn(rows, wx_ref[...])
    val_ref[...] = val
    vpad[8 : length + 8, :] = val
    st = nn(rows, wbc_ref[...])
    st_ref[...] = st
    spad[8 : length + 8, :] = st
    dt_in = nn(rows, wdt_ref[...])
    dt_ref[...] = dt_in

    pre = conv_pre(vpad, cv_ref, cvb_ref[...], length)
    pre_ref[...] = pre
    _, v = silu_parts(pre)
    _, bc = silu_parts(conv_pre(spad, cs_ref, csb_ref[...], length))
    half = bc.shape[1] // 2
    bb = bc[:, :half].astype(BF)
    cb = bc[:, half:].astype(BF)
    dt = softplus(dt_in + sb_ref[...])
    q_index = lax.broadcasted_iota(jnp.int32, (length, length), 0)
    s_index = lax.broadcasted_iota(jnp.int32, (length, length), 1)
    causal = q_index >= s_index
    tril = jnp.where(causal, 1.0, 0.0).astype(BF)
    a = sum_rows(tril, dt * rate_ref[...])
    a_rows = a.T
    lane_low = lax.broadcasted_iota(jnp.int32, (length, 128), 1) < WIDTH
    dt_x = spread(dt, pairs, lane_low)
    a_x = spread(a, pairs, lane_low)
    x = v * dt_x
    xb = x.astype(BF)
    scores = jnp.where(causal, nt(cb, bb), 0.0)
    inside = []
    zero = jnp.zeros((length, 128), BF)
    for p in range(pairs):
        xp = xb[:, 128 * p : 128 * (p + 1)]
        total = None
        for j in range(2):
            h = 2 * p + j
            decay = jnp.exp(jnp.minimum(a[:, h : h + 1] - a_rows[h : h + 1, :], 0.0))
            m = (scores * decay).astype(BF)
            term = nn(m, jnp.where(lane_low, xp, zero) if j == 0 else jnp.where(lane_low, zero, xp))
            total = term if total is None else total + term
        inside.append(total)
    entering = state[...]
    ent_ref[0] = entering
    outside = jnp.exp(a_x) * nn(cb, entering.astype(BF))
    a_last = a_x[length - 1 : length, :]
    xw = (x * jnp.exp(a_last - a_x)).astype(BF)
    state[...] = jnp.exp(a_last) * entering + nn(bc[:, :half].T.astype(BF), xw)
    y = jnp.concatenate(inside, axis=1) + outside + skip_ref[...] * v
    y_ref[...] = y
    _, sgate = silu_parts(gate_ref[...])
    gated = y * sgate
    square = (gated * gated).astype(BF)
    ssq_ref[...] = nt(jnp.ones((8, inner), BF), square)
    mixed = (gated * gg_ref[...]).astype(BF)
    part = nt(mixed, wot_ref[...]).astype(BF)
    if not last:
        part_ref[...] = part
    else:
        part_ref[0], part2_ref[0] = part[: length // 2], part[length // 2 :]
        cut = gb_ref.shape[1]
        mixed_ref[0] = mixed[cut:]
        dm = nn(gb_ref[0], wot_ref[...])
        dm_ref[0] = dm
        dots = token_dots(dm, mixed[:cut])
        row = lax.broadcasted_iota(jnp.int32, (8, length), 0)
        ssq_ref[...] = jnp.where(row == 0, ssq_ref[...], 0.0)
        ssq_ref[1:2, 0:cut] = dots[0:1]


def token_dots(dm, mixed):
    product = (dm * mixed.astype(F32)).astype(BF)
    return nt(jnp.ones((8, product.shape[1]), BF), product)


def whole(shape):
    return pl.BlockSpec(shape, lambda i: (0,) * len(shape), pipeline_mode=pl.Buffered(1))


def layer_specs(params, l):
    return [
        pl.BlockSpec((1,) + p.shape[1:], lambda i: (l, 0, 0), pipeline_mode=pl.Buffered(1))
        for p in params[:-1]
    ] + [whole(params[-1].shape)]


def forward_mix(rows, packed, params, l, gb=None):
    first, last = l == 0, gb is not None
    tokens, width = rows.shape
    inner = params[0].shape[2]
    bc_width = params[1].shape[2]
    dt_width = 128
    half = bc_width // 2
    q = GROUP
    blocks = tokens // q
    tok = lambda n: pl.BlockSpec((q, n), lambda i: (i, 0))
    outs = [
        ((tokens, inner), F32, tok(inner)),
        ((tokens, inner), F32, tok(inner)),
        ((tokens, bc_width), F32, tok(bc_width)),
        ((tokens, dt_width), F32, tok(dt_width)),
        ((tokens, inner), F32, tok(inner)),
        ((blocks, half, inner), F32, pl.BlockSpec((1, half, inner), lambda i: (i, 0, 0))),
        ((tokens, inner), F32, tok(inner)),
        ((8, tokens), F32, pl.BlockSpec((8, q), lambda i: (0, i))),
    ]
    half_of = lambda rows, n: pl.BlockSpec((1, rows, n), lambda i: (i, 0, 0))
    if not last:
        outs.append(((tokens, width), BF, tok(width)))
    if first:
        outs.append(((tokens, width), BF, tok(width)))
    if last:
        cut = gb.shape[1]
        for r, n, kind in (
            (q // 2, width, BF), (q // 2, width, BF), (cut, inner, F32), (q - cut, inner, BF)
        ):
            outs.append(((blocks, r, n), kind, half_of(r, n)))
    return pl.pallas_call(
        functools.partial(fwd_kernel, first, last),
        grid=(blocks,),
        in_specs=[tok(width), whole(packed.shape)]
        + layer_specs(params, l)
        + ([half_of(cut, width)] if last else []),
        out_specs=[o[2] for o in outs],
        out_shape=[jax.ShapeDtypeStruct(o[0], o[1]) for o in outs],
        scratch_shapes=[
            pltpu.VMEM((half, inner), F32),
            pltpu.VMEM((q + 8, inner), F32),
            pltpu.VMEM((q + 8, bc_width), F32),
        ],
        compiler_params=pltpu.CompilerParams(
            dimension_semantics=("arbitrary",), vmem_limit_bytes=56 * MIB
        ),
        name="mix_forward",
    )(rows, packed, *params, *([gb] if last else []))


def bwd_kernel(
    ready, layer, gb_ref, e_ref, rows_ref, gate_ref, val_ref, st_ref, stp_ref, dt_ref, y_ref,
    ent_ref, pre_ref, w_ref, vec_ref, cst_ref, tiny_ref, gain_ref, pick_ref, *rest,
):
    if ready:
        dm2_ref, *rest = rest
    dcat_ref, dpart_ref, gvec_ref, gst_ref, gdt_ref, ggain_ref, *rest = rest
    dstate, spad, dvpad, dspad = rest
    step = pl.program_id(0)
    blocks = pl.num_programs(0)
    length = y_ref.shape[0]
    cv_ref, cvb_ref, skip_ref, gg_ref, cs_ref, csb_ref, sb_ref, rate_ref = small_refs(
        vec_ref, cst_ref, tiny_ref
    )
    inner = gg_ref.shape[1]
    bc_width = cs_ref.shape[1]
    wbc_ref, wdt_ref, wz_ref, wx_ref, wot_ref = blocks_of(w_ref, inner, bc_width)
    dst_ref, ddt_ref, dgate_ref, dval_ref, mixed_ref = blocks_of(dcat_ref, inner, bc_width)
    half = bc_width // 2
    pairs = inner // 128

    @pl.when(step == 0)
    def _():
        dstate[...] = jnp.zeros_like(dstate)
        dvpad[length : length + 8, :] = jnp.zeros((8, inner), F32)
        dspad[length : length + 8, :] = jnp.zeros((8, bc_width), F32)
        gvec_ref[...] = jnp.zeros_like(gvec_ref)
        gst_ref[...] = jnp.zeros_like(gst_ref)
        gdt_ref[...] = jnp.zeros_like(gdt_ref)
        ggain_ref[...] = jnp.zeros_like(ggain_ref)

    @pl.when(step > 0)
    def _():
        dvpad[length : length + 8, :] = dvpad[0:8, :]
        dspad[length : length + 8, :] = dspad[0:8, :]

    first = step == blocks - 1
    spad[0:8, :] = jnp.where(first, 0.0, stp_ref[...])
    spad[8 : length + 8, :] = st_ref[...]

    pre_v = pre_ref[...]
    sig_v, v = silu_parts(pre_v)
    pre_s = conv_pre(spad, cs_ref, csb_ref[...], length)
    sig_s, bc = silu_parts(pre_s)
    bb = bc[:, :half].astype(BF)
    cb = bc[:, half:].astype(BF)
    z = dt_ref[...] + sb_ref[...]
    dt = softplus(z)
    rate = rate_ref[...]
    s_index = lax.broadcasted_iota(jnp.int32, (length, length), 0)
    q_index = lax.broadcasted_iota(jnp.int32, (length, length), 1)
    upper = q_index >= s_index
    a = sum_rows(jnp.where(s_index >= q_index, 1.0, 0.0).astype(BF), dt * rate)
    a_rows = a.T
    lane_low = lax.broadcasted_iota(jnp.int32, (length, 128), 1) < WIDTH
    dt_x = spread(dt, pairs, lane_low)
    a_x = spread(a, pairs, lane_low)
    x = v * dt_x
    xb = x.astype(BF)
    skip = skip_ref[...]

    y = y_ref[...]
    gate = gate_ref[...]
    sig_g, sgate = silu_parts(gate)
    gated = y * sgate
    per_token = e_ref[...].T
    e, r2 = per_token[:, 0:1], per_token[:, 1:2]
    if ready:
        dm = jnp.concatenate([gb_ref[0], dm2_ref[0]], axis=0) * r2
    else:
        dm = nn(gb_ref[...], wot_ref[...]) * r2
    dgated = dm * gg_ref[...] - e * gated
    mixed_ref[...] = (gated * r2 * gg_ref[...]).astype(BF)
    dgate = (dgated * y * (sig_g * (1.0 + gate * (1.0 - sig_g)))).astype(BF)
    dgate_ref[...] = dgate
    dy = dgated * sgate
    dyb = dy.astype(BF)
    dyf = dyb.astype(F32)

    scores = jnp.where(upper, nt(bb, cb), 0.0)
    zero = jnp.zeros((length, 128), BF)
    dscores = jnp.zeros((length, length), F32)
    dx_list = []
    for p in range(pairs):
        xp = xb[:, 128 * p : 128 * (p + 1)]
        dp = dyb[:, 128 * p : 128 * (p + 1)]
        total = None
        for j in range(2):
            h = 2 * p + j
            decay = jnp.exp(jnp.minimum(a_rows[h : h + 1, :] - a[:, h : h + 1], 0.0))
            m = (scores * decay).astype(BF)
            dh = jnp.where(lane_low, dp, zero) if j == 0 else jnp.where(lane_low, zero, dp)
            term = nn(m, dh)
            total = term if total is None else total + term
            dscores = dscores + nt(xp, dh) * decay
        dx_list.append(total)
    dx_in = jnp.concatenate(dx_list, axis=1)
    dscores = jnp.where(upper, dscores, 0.0)
    db = nn(dscores.astype(BF), cb)
    dc = nn(dscores.T.astype(BF), bb)

    entering = ent_ref[0]
    dleaving = dstate[...]
    dleaving_b = dleaving.astype(BF)
    ea = jnp.exp(a_x)
    a_last = a_x[length - 1 : length, :]
    ea_last = jnp.exp(a_last)
    w = jnp.exp(a_last - a_x)
    dxw = nn(bb, dleaving_b) * w
    db = db + nt((x * w).astype(BF), dleaving_b)
    eady = (ea * dyf).astype(BF)
    dc = dc + nt(eady, entering.astype(BF))
    dstate[...] = ea_last * dleaving + nn(bc[:, half:].T.astype(BF), eady)
    dx = dx_in + dxw
    u = x * dxw
    last_add = jnp.sum(u, axis=0, keepdims=True) + ea_last * jnp.sum(
        entering * dleaving, axis=0, keepdims=True
    )
    da_x = dyf * (y - skip * v) - xb.astype(F32) * dx_in - u
    row_index = lax.broadcasted_iota(jnp.int32, (length, inner), 0)
    da_x = da_x + jnp.where(row_index == length - 1, last_add, 0.0)
    pick = pick_ref[...]
    da = sum_lanes(da_x, pick)
    dr = sum_rows(jnp.where(upper, 1.0, 0.0).astype(BF), da)
    ddt = sum_lanes(dx * v, pick) + dr * rate
    dz = ddt * (1.0 / (1.0 + jnp.exp(-z)))
    ddtb = dz.astype(BF)
    ddt_ref[...] = ddtb
    gdt_ref[0:1, :] += jnp.sum(dz, axis=0, keepdims=True)
    gdt_ref[1:2, :] += jnp.sum(dr * dt * rate, axis=0, keepdims=True)

    dpre_v = (skip * dy + dt_x * dx) * (sig_v * (1.0 + pre_v * (1.0 - sig_v)))
    dvpad[0:length, :] = dpre_v
    dval = jnp.zeros((length, inner), F32)
    val = val_ref[...]
    for k in range(4):
        later = dvpad[pl.ds(3 - k, length), :]
        dval = dval + cv_ref[k : k + 1, :] * later
        gvec_ref[k : k + 1, :] += jnp.sum(later * val, axis=0, keepdims=True)
    gvec_ref[4:5, :] += jnp.sum(dpre_v, axis=0, keepdims=True)
    gvec_ref[5:6, :] += jnp.sum(gated * dm, axis=0, keepdims=True)
    gvec_ref[6:7, :] += jnp.sum(dy * v, axis=0, keepdims=True)
    dvalb = dval.astype(BF)
    dval_ref[...] = dvalb

    dbc = jnp.concatenate([db, dc], axis=1)
    dpre_s = dbc * (sig_s * (1.0 + pre_s * (1.0 - sig_s)))
    dspad[0:length, :] = dpre_s
    dst = jnp.zeros((length, bc_width), F32)
    st = st_ref[...]
    for k in range(4):
        later = dspad[pl.ds(3 - k, length), :]
        dst = dst + cs_ref[k : k + 1, :] * later
        gst_ref[k : k + 1, :] += jnp.sum(later * st, axis=0, keepdims=True)
    gst_ref[4:5, :] += jnp.sum(dpre_s, axis=0, keepdims=True)
    dstb = dst.astype(BF)
    dst_ref[...] = dstb
    dpart = nt(dgate, wz_ref[...]) + nt(dvalb, wx_ref[...])
    dpart = dpart + nt(dstb, wbc_ref[...]) + nt(ddtb, wdt_ref[...])
    dpart_ref[...] = dpart.astype(BF)
    ggain_ref[0:1, :] += jnp.sum(rows_ref[...].astype(F32) * dpart, axis=0, keepdims=True)

    @pl.when(step == blocks - 1)
    def _():
        ggain_ref[0:1, :] = ggain_ref[0:1, :] / gain_ref[GAIN_ROWS * layer : GAIN_ROWS * layer + 1, :]


def backward_mix(gb, ready, e_rows, rows, kept, packed, params, pick, l):
    gate, val, st, dt, y, ent, pre = kept
    tokens, width = y.shape[0], packed.shape[0]
    inner = params[0].shape[2]
    bc_width = params[1].shape[2]
    dt_width = 128
    packed_width = packed.shape[1]
    half = bc_width // 2
    q = GROUP
    blocks = tokens // q
    back = lambda i: blocks - 1 - i
    tok = lambda n: pl.BlockSpec((q, n), lambda i: (back(i), 0))
    halo = lambda n: pl.BlockSpec(
        (8, n), lambda i: (jnp.maximum(back(i) * (q // 8) - 1, 0), 0)
    )
    fixed = lambda r, c: pl.BlockSpec((r, c), lambda i: (0, 0))
    outs = [
        ((tokens, packed_width), BF, tok(packed_width)),
        ((tokens, width), BF, tok(width)),
        ((8, inner), F32, fixed(8, inner)),
        ((8, bc_width), F32, fixed(8, bc_width)),
        ((8, dt_width), F32, fixed(8, dt_width)),
        ((8, width), F32, fixed(8, width)),
    ]
    half_of = lambda v: pl.BlockSpec((1,) + v.shape[1:], lambda i: (back(i), 0, 0))
    gb, more = (gb[0], [gb[1]]) if ready else (gb, [])
    return pl.pallas_call(
        functools.partial(bwd_kernel, ready, l),
        grid=(blocks,),
        in_specs=[
            half_of(gb) if ready else tok(width),
            pl.BlockSpec((8, q), lambda i: (0, back(i))),
            tok(width),
            tok(inner), tok(inner), tok(bc_width), halo(bc_width), tok(dt_width),
            tok(inner),
            pl.BlockSpec((1, half, inner), lambda i: (back(i), 0, 0)),
            tok(inner),
        ]
        + [whole(packed.shape)] + layer_specs(params, l) + [whole(pick.shape)]
        + [half_of(v) for v in more],
        out_specs=[o[2] for o in outs],
        out_shape=[jax.ShapeDtypeStruct(o[0], o[1]) for o in outs],
        scratch_shapes=[
            pltpu.VMEM((half, inner), F32),
            pltpu.VMEM((q + 8, bc_width), F32),
            pltpu.VMEM((q + 8, inner), F32),
            pltpu.VMEM((q + 8, bc_width), F32),
        ],
        compiler_params=pltpu.CompilerParams(
            dimension_semantics=("arbitrary",), vmem_limit_bytes=60 * MIB
        ),
        name="mix_backward",
    )(gb, e_rows, rows, gate, val, st, st, dt, y, ent, pre, packed, *params, pick, *more)


class Step:
    def __init__(self, **given):
        self.rows = 0
        self.width = 0
        self.line = 4
        self.chunks = 8
        self.hop = 1
        self.pass_hop = 1
        self.slack = 0
        self.partial = False
        self.gather = False
        self.late = False
        self.scale = False
        self.inner = False
        self.layer = 0
        self.small = 0
        self.gain_row = 0
        self.weights = 0
        self.grads = 0
        self.double = 2
        self.tail = 2
        self.lag = 1
        self.states = 0
        self.sums = False
        self.bits = 0
        self.middle = None
        self.early = ()
        self.halves = False
        self.lazy = ()
        self.__dict__.update(given)


def remote(src, dst, send, recv, device):
    return pltpu.make_async_remote_copy(
        src_ref=src, dst_ref=dst, send_sem=send, recv_sem=recv,
        device_id=device, device_id_type=pl.DeviceIdType.MESH,
    )


def when(condition):
    return pl.when(condition)


def pack_weights(r, l):
    start = 0
    for part in (r.p_bc.at[l], r.p_dt.at[l], r.p_z.at[l], r.p_x.at[l], r.p_out.at[l]):
        r.wown[:, start : start + part.shape[1]] = part[...]
        start += part.shape[1]


def comm_kernel(o, names, *refs):
    r = types.SimpleNamespace(**dict(zip(names, refs)))
    r.gain_row = slice(o.gain_row, o.gain_row + 1)
    r.gbuf = [v for k, v in zip(names, refs) if k.startswith("gbuf")]
    n, count, rows = o.line, o.chunks, o.rows
    size = rows // count
    t = lax.axis_index("tensor")
    me = lax.axis_index("dp")
    own_bits = [(me // (1 << b)) % 2 for b in range(o.bits)]
    partner = [me + (1 - 2 * own_bits[b]) * (1 << b) for b in range(o.bits)]

    lazy = []
    for i, name in enumerate(o.lazy):
        near = getattr(r, name + "_v")
        lazy.append(pltpu.make_async_copy(getattr(r, name), near, r.lazy_sem.at[i]))
        setattr(r, name, near)
    leaving = []
    for i, name in enumerate(o.early):
        near = getattr(r, name + "_v")
        leaving.append((near, getattr(r, name), r.early_sem.at[i]))
        setattr(r, name, near)
    if o.halves:
        start = 0
        for i, far in enumerate((r.half0, r.half1)):
            near = r.lgrad.at[:, pl.ds(start, far.shape[1])]
            lazy.append(pltpu.make_async_copy(far, near, r.half_sem.at[i]))
            start += far.shape[1]
    for copy in lazy:
        copy.start()

    barrier = pltpu.get_barrier_semaphore()
    for k in range(1, n):
        pl.semaphore_signal(
            barrier, inc=1, device_id={"tensor": lax.rem(t + k, n)},
            device_id_type=pl.DeviceIdType.MESH,
        )
    over_dp = o.weights or o.grads
    r.early = [v for k, v in zip(names, refs) if k.startswith("esum")]
    r.lined = [v for k, v in zip(names, refs) if k.startswith("lsum")]
    r.gains = [v for k, v in zip(names, refs) if k.startswith("gsum")]
    if over_dp:
        for b in range(o.bits):
            pl.semaphore_signal(
                barrier, inc=1, device_id={"dp": partner[b]}, device_id_type=pl.DeviceIdType.MESH
            )
    pl.semaphore_wait(barrier, n - 1 + (o.bits if over_dp else 0))

    def at(s, c):
        return pl.ds(pl.multiple_of(s * rows + c * size, size), size)

    def piece(c):
        return pl.ds(pl.multiple_of(c * size, size), size)

    def hop(side, s, c, src):
        buf = r.rbuf if side == 0 else r.lbuf
        return remote(
            src, buf.at[s, piece(c)], r.rs_send.at[side, s], r.rs_recv.at[side, s, c],
            {"tensor": t + 1 if side == 0 else t - 1},
        )

    def reduce_items(side, c):
        buf = r.rbuf if side == 0 else r.lbuf
        edge = t == 0 if side == 0 else t == n - 1
        order = range(n - 1, 0, -1) if side == 0 else range(0, n - 1)
        for s in order:
            further = s > t if side == 0 else s < t

            @when(further & edge)
            def _():
                hop(side, s, c, r.part.at[at(s, c)]).start()

            @when(further & jnp.logical_not(edge))
            def _():
                hop(side, s, c, buf.at[s, piece(c)]).wait_recv()
                total = buf[s, piece(c), :].astype(F32) + r.part[at(s, c), :].astype(F32)
                buf[s, piece(c), :] = total.astype(BF)
                hop(side, s, c, buf.at[s, piece(c)]).start()

    def own_total(c):
        acc = r.acc
        acc[...] = r.part[at(t, c), :].astype(F32)

        @when(t > 0)
        def _():
            hop(0, t, c, r.rbuf.at[t, piece(c)]).wait_recv()
            acc[...] += r.rbuf[t, piece(c), :].astype(F32)

        @when(t < n - 1)
        def _():
            hop(1, t, c, r.lbuf.at[t, piece(c)]).wait_recv()
            acc[...] += r.lbuf[t, piece(c), :].astype(F32)

    def pass_on(side, s, c):
        spot = r.full.at[at(s, c)]
        return remote(
            spot, spot, r.ag_send.at[side, s], r.ag_recv.at[side, s, c],
            {"tensor": t + 1 if side == 0 else t - 1},
        )

    def forward_items(side, tau):
        order = range(n - 2, -1, -1) if side == 0 else range(1, n)
        for s in order:
            away = t - s if side == 0 else s - t
            late = o.hop * max(s, n - 1 - s) + o.slack if o.late else 0
            c = tau - late - o.pass_hop * away

            @when((away > 0) & (c >= 0) & (c < count))
            def _():
                pass_on(side, s, c).wait_recv()

                @when(t < n - 1 if side == 0 else t > 0)
                def _():
                    pass_on(side, s, c).start()

    def spot_of(k, ref):
        return ref.at[:, pl.ds(pl.multiple_of(k * rows, rows), rows)]

    def square_copy(k):
        dest = lax.rem(t + k, n)
        return remote(
            spot_of(dest, r.ssq), r.sqbuf.at[k - 1], r.sq_send.at[k - 1],
            r.sq_recv.at[k - 1], {"tensor": dest},
        )

    def inner_copy(k):
        return remote(
            spot_of(t, r.inner), spot_of(t, r.inner), r.in_send.at[k - 1],
            r.in_recv.at[k - 1], {"tensor": lax.rem(t + k, n)},
        )

    def inner_arrival(k):
        source = lax.rem(t + n - k, n)
        return remote(
            spot_of(source, r.inner), spot_of(source, r.inner), r.in_send.at[k - 1],
            r.in_recv.at[k - 1], {"tensor": source},
        )

    def bit_order(parity):
        high = list(range(o.bits - 1, 0, -1))
        if parity == 1:
            high = high[1:] + high[:1]
        return high + [0]

    def cols(j):
        return pl.ds(pl.multiple_of(j * WCHUNK, WCHUNK), WCHUNK)

    def spots(known):
        return tuple(slice(None) if b in known else own_bits[b] for b in range(o.bits - 1, -1, -1))

    def weight_copy(parity, stage, j):
        order = bit_order(parity)
        depth = r.wown.shape[0] // o.weights
        strip = pl.ds(pl.multiple_of(j * depth, depth), depth)
        spot = r.wfull.at[(*spots(order[:stage]), strip)]
        src = r.wown.at[strip] if stage == 0 else spot
        return remote(
            src, spot, r.wg_send.at[stage, j], r.wg_recv.at[stage, j],
            {"dp": partner[order[stage]]},
        )

    def small_columns():
        lanes_at = pl.ds(o.small // 128 * 128, 128)
        return pltpu.make_async_copy(
            r.wfull.at[(*spots(range(o.bits)), slice(None), lanes_at)], r.columns, r.small_sem
        )

    def small_items(tau):
        done = (o.weights + 1) // 2 + o.bits

        @when(tau == done)
        def _():
            small_columns().start()

        @when(tau == done + 1)
        def _():
            small_columns().wait()
            turned = r.columns[...].reshape(o.width, 128).astype(F32).T
            r.small[...] = turned[o.small % 128 : o.small % 128 + 16, :]

    def own_weights():
        return pltpu.make_async_copy(r.wown, r.wfull.at[spots([])], r.wl_sem)

    def each_parity(pair, fn):
        for parity in range(2):
            j = 2 * pair + parity

            @when((j >= 0) & (j < o.weights))
            def _():
                fn(parity, j)

    def weight_items(tau):
        for stage in range(o.bits + 1):
            def run(parity, j):
                if stage > 0:
                    weight_copy(parity, stage - 1, j).wait_recv()
                if stage < o.bits:
                    weight_copy(parity, stage, j).start()
            each_parity(tau - stage, run)

    def grad_order(parity):
        high = list(range(1, o.bits))
        if parity == 1:
            high = high[1:] + high[:1]
        return [0] + high

    def grad_spot(parity, stage, mine):
        order = grad_order(parity)
        done, bit = order[:stage], order[stage]
        spot = []
        for b in range(o.bits - 1, -1, -1):
            if b in done:
                spot.append(own_bits[b])
            elif b == bit:
                spot.append(own_bits[b] if mine else 1 - own_bits[b])
            else:
                spot.append(slice(None))
        return tuple(spot)

    def grad_copy(parity, stage, j):
        order = grad_order(parity)
        return remote(
            r.grad.at[(j, *grad_spot(parity, stage, False))], r.gbuf[stage].at[j],
            r.gr_send.at[stage, j], r.gr_recv.at[stage, j],
            {"dp": partner[order[stage]]},
        )

    def products(turn, i):
        product(jnp.where(turn >= 0, chunk_of(turn), -1), i)

        @when((turn >= 0) & (turn < o.double))
        def _():
            product(2 * turn + 1, i)

    def product(j, i):
        slab = o.width // 2
        inner_shape = (2,) * (o.bits - 1) + (slab >> (o.bits - 1), WCHUNK)

        def one(left):
            rows_of_slab = left[..., pl.ds(i * slab, slab)].reshape(-1, slab)
            out = tn(rows_of_slab, r.right[:, cols(j)])
            r.grad[j, i] = out.astype(BF).reshape(inner_shape)

        @when((j >= 0) & (j < o.grads - o.tail))
        def _():
            one(r.lrows)

        @when((j >= o.grads - o.tail) & (j < o.grads))
        def _():
            one(r.lgrad)

    def chunk_of(turn):
        return jnp.where(turn < o.double, 2 * turn, turn + o.double)

    def each_chunk(turn, fn):
        j = chunk_of(turn)
        for parity in range(2):
            @when((turn >= 0) & (j < o.grads) & (lax.rem(j, 2) == parity))
            def _():
                fn(parity, j)

        @when((turn >= 0) & (turn < o.double))
        def _():
            fn(1, 2 * turn + 1)

    def grad_items(tau):
        products(tau, 1)

        def first(parity, j):
            grad_copy(parity, 0, j).start()

        each_chunk(tau, first)
        for stage in range(1, o.bits + 1):
            def run(parity, j):
                grad_copy(parity, stage - 1, j).wait_recv()
                spot = grad_spot(parity, stage - 1, True)
                free = [i for i, v in enumerate(spot) if isinstance(v, slice)]
                buf = r.gbuf[stage - 1]
                for combo in range(1 << len(free)):
                    pick = [(combo >> i) % 2 for i in range(len(free))]
                    full = list(spot)
                    for i, v in zip(free, pick):
                        full[i] = v
                    total = r.grad[(j, *full)].astype(F32) + buf[(j, *pick)].astype(F32)
                    if stage < o.bits:
                        r.grad[(j, *full)] = total.astype(BF)
                    else:
                        r.gnear[:, cols(j)] = total

                        @when(j > 0)
                        def _():
                            grad_leave(j).start()
                if stage < o.bits:
                    grad_copy(parity, stage, j).start()
            each_chunk(tau - grad_lag(stage), run)

    def grad_leave(j):
        return pltpu.make_async_copy(r.gnear.at[:, cols(j)], r.gout.at[:, cols(j)], r.leave_sem)

    def grad_lag(stage):
        return o.lag * (2 * stage - 1) if stage else 0

    def share(buf, send, recv, k):
        return remote(buf.at[t], buf.at[t], send.at[k - 1], recv.at[k - 1],
                      {"tensor": lax.rem(t + k, n)})

    def shared(buf, send, recv):
        for k in range(1, n):
            source = lax.rem(t + n - k, n)
            remote(buf.at[source], buf.at[source], send.at[k - 1], recv.at[k - 1],
                   {"tensor": source}).wait_recv()

    def line_total(buf):
        total = buf[0]
        for k in range(1, n):
            total = total + buf[k]
        return total

    def double(acc, buf, send, recv, b):
        return remote(acc.at[b], buf.at[b], send.at[b], recv.at[b], {"dp": partner[b]})

    def doubled(acc, buf, send, recv, b):
        double(acc, buf, send, recv, b).wait_recv()
        acc[b + 1] = acc[b] + buf[b]

    def lanes(index, ref):
        return slice(index * ref.shape[1], (index + 1) * ref.shape[1])

    line_groups, dp_groups = [], []
    if o.sums:
        line_groups = [(r.lbank, r.lb_send, r.lb_recv), (r.gbank, r.gb_send, r.gb_recv)]
        dp_groups = [
            (r.dbank, r.dbuf, r.db_send, r.db_recv), (r.hbank, r.hbuf, r.hb_send, r.hb_recv)
        ]

    def sum_items(tau):
        @when(tau == 2)
        def _():
            for g in line_groups:
                shared(*g)
            off = 0
            for v in r.early:
                r.dbank[0, :, off : off + v.shape[1]] = v[...]
                off += v.shape[1]
            r.dbank[0, :, off:] = line_total(r.lbank)
            r.hbank[0] = line_total(r.gbank)
            for g in dp_groups:
                double(*g, 0).start()

        for b in range(o.bits):
            @when(tau == 4 + b)
            def _():
                for g in dp_groups:
                    doubled(*g, b)
                    if b < o.bits - 1:
                        double(*g, b + 1).start()

    def state_items(tau):
        at_first = grad_lag(o.bits) + 1
        quarter = r.gout.shape[0] // n

        @when(tau == at_first)
        def _():
            for s in range(n):
                r.qsend[s] = r.gnear[s * quarter : (s + 1) * quarter, 0 : o.states].astype(BF)
            for k in range(1, n):
                state_out(k).start()

        @when(tau == at_first + 2)
        def _():
            total = r.qsend[t].astype(F32)
            for k in range(1, n):
                state_out(k).wait_recv()
                total = total + r.qbuf[k - 1].astype(F32)
            r.qall[t] = total.astype(BF)
            for k in range(1, n):
                share(r.qall, r.qa_send, r.qa_recv, k).start()

    def state_out(k):
        dest = lax.rem(t + k, n)
        return remote(r.qsend.at[dest], r.qbuf.at[k - 1], r.qs_send.at[k - 1],
                      r.qs_recv.at[k - 1], {"tensor": dest})

    if o.sums:
        off = 0
        for v in r.lined:
            r.lbank[t, :, off : off + v.shape[1]] = v[...]
            off += v.shape[1]
        for i, v in enumerate(r.gains):
            r.gbank[t, :, lanes(i, v)] = v[0:1, :]
        for g in line_groups:
            for k in range(1, n):
                share(*g, k).start()
    if o.scale:
        for k in range(1, n):
            square_copy(k).start()
    if o.weights:
        pack_weights(r, o.layer)
        own_weights().start()
    if o.scale:
        total = spot_of(t, r.ssq)[...]
        for k in range(1, n):
            square_copy(k).wait_recv()
            total = total + r.sqbuf[k - 1]
        scale = lax.rsqrt(total / (o.scale * 1.0) + EPSILON)
        r.r2[...] = jnp.broadcast_to(scale.T[:, 0:1], (rows, 128))
    if o.gather and not o.late:
        r.full[pl.ds(pl.multiple_of(t * rows, rows), rows), :] = o.payload(r)
    if o.middle is not None:
        o.middle(r, None, None)

    ends = [count + o.hop * (n - 1) + o.slack]
    if o.late:
        ends.append(ends[0] + o.pass_hop * (n - 1))
    elif o.gather:
        ends.append(count + o.pass_hop * (n - 1))
    if o.weights:
        ends.append((o.weights + 1) // 2 + o.bits + (2 if o.small else 0))
    if o.grads:
        ends.append(1 + o.grads - o.double + grad_lag(o.bits))
        ends.append(grad_lag(o.bits) + 5)
    if o.sums:
        ends.append(4 + o.bits)

    def iteration(tau, _):
        if lazy:
            @when(tau == 1)
            def _():
                for copy in lazy:
                    copy.wait()
        if o.grads:
            products(tau - 1, 0)
        if o.partial:
            for side in range(2):
                c = tau - o.hop * (t if side == 0 else n - 1 - t)

                @when((c >= 0) & (c < count))
                def _():
                    reduce_items(side, c)

            c_own = tau - o.hop * jnp.maximum(t, n - 1 - t) - o.slack

            @when((c_own >= 0) & (c_own < count))
            def _():
                own_total(c_own)
                out = o.middle(r, piece(c_own), r.acc[...])
                for near, far, sem in leaving:
                    spot = piece(c_own)
                    pltpu.make_async_copy(near.at[spot], far.at[spot], sem).start()
                if o.late:
                    r.full[at(t, c_own), :] = out
        if o.gather:
            c_out = tau - o.hop * jnp.maximum(t, n - 1 - t) - o.slack if o.late else tau

            @when((c_out >= 0) & (c_out < count))
            def _():
                @when(t < n - 1)
                def _():
                    pass_on(0, t, c_out).start()

                @when(t > 0)
                def _():
                    pass_on(1, t, c_out).start()

            for side in range(2):
                forward_items(side, tau)
        if o.weights:
            @when(tau == 1)
            def _():
                own_weights().wait()
            weight_items(tau)
            if o.small:
                small_items(tau)
        if o.grads:
            grad_items(tau - 1)
            state_items(tau - 1)
        if o.sums:
            sum_items(tau)
        return 0

    lax.fori_loop(0, max(ends), iteration, 0)

    if o.inner:
        spot_of(t, r.inner)[...] = r.icol[...].T[0:8, :]
        for k in range(1, n):
            inner_copy(k).start()
        for k in range(1, n):
            inner_arrival(k).wait_recv()
        for k in range(1, n):
            inner_copy(k).wait_send()
    if o.sums:
        r.sums[...] = r.dbank[o.bits]
        for i, v in enumerate(r.gains):
            r.gain_sums[i : i + 1, :] = r.hbank[o.bits, :, lanes(i, v)]
        for g in line_groups:
            for k in range(1, n):
                share(*g, k).wait_send()
        for g in dp_groups:
            for b in range(o.bits):
                double(*g, b).wait_send()
    if o.grads:
        shared(r.qall, r.qa_send, r.qa_recv)
        quarter = r.gout.shape[0] // n
        for s in range(n):
            r.gnear[s * quarter : (s + 1) * quarter, 0 : o.states] = r.qall[s].astype(F32)
        grad_leave(jnp.int32(0)).start()
        for k in range(1, n):
            state_out(k).wait_send()
            share(r.qall, r.qa_send, r.qa_recv, k).wait_send()
    if o.scale:
        for k in range(1, n):
            square_copy(k).wait_send()
    for s in range(n):
        for side in range(2):
            inside = t < n - 1 if side == 0 else t > 0
            if o.partial:
                @when((s > t if side == 0 else s < t) & inside)
                def _():
                    buf = (r.rbuf if side == 0 else r.lbuf).at[s]
                    remote(
                        buf, buf, r.rs_send.at[side, s], r.rs_recv.at[side, s, 0],
                        {"tensor": t + 1 if side == 0 else t - 1},
                    ).wait_send()
            if o.gather:
                @when((s <= t if side == 0 else s >= t) & inside)
                def _():
                    spot = r.full.at[pl.ds(s * rows, rows)]
                    remote(
                        spot, spot, r.ag_send.at[side, s], r.ag_recv.at[side, s, 0],
                        {"tensor": t + 1 if side == 0 else t - 1},
                    ).wait_send()
    for j in range(o.weights):
        for stage in range(o.bits):
            weight_copy(j % 2, stage, jnp.int32(j)).wait_send()
    for j in range(o.grads):
        for stage in range(o.bits):
            grad_copy(j % 2, stage, jnp.int32(j)).wait_send()
    if o.grads:
        pltpu.make_async_copy(r.gnear, r.gout, r.leave_sem).wait()
    for near, far, sem in leaving:
        pltpu.make_async_copy(near, far, sem).wait()


def comm_call(o, name, collective, inputs, outputs, **scratch):
    n, count, rows, width = o.line, o.chunks, o.rows, o.width
    dma = pltpu.SemaphoreType.DMA
    if o.lazy:
        for key in o.lazy:
            value = inputs[key][0]
            inputs[key] = (value, pl.ANY)
            scratch[key + "_v"] = pltpu.VMEM(value.shape, value.dtype)
        scratch.update(lazy_sem=dma((len(o.lazy),)))
    if o.early:
        for key in o.early:
            shape, kind, _ = outputs[key]
            outputs[key] = (shape, kind, pl.ANY)
            scratch[key + "_v"] = pltpu.VMEM(shape, kind)
        scratch.update(early_sem=dma((len(o.early),)))
    if o.halves:
        scratch.update(lgrad=pltpu.VMEM((n, rows, width), BF), half_sem=dma((2,)))
    if o.partial:
        scratch.update(
            rbuf=pltpu.VMEM((n, rows, width), BF),
            lbuf=pltpu.VMEM((n, rows, width), BF),
            acc=pltpu.VMEM((rows // count, width), F32),
            rs_send=dma((2, n)),
            rs_recv=dma((2, n, count)),
        )
    if o.gather:
        scratch.update(ag_send=dma((2, n)), ag_recv=dma((2, n, count)))
    if o.scale:
        scratch.update(
            sqbuf=pltpu.VMEM((n - 1, 8, rows), F32), sq_send=dma((n - 1,)), sq_recv=dma((n - 1,))
        )
    if o.inner:
        scratch.update(
            icol=pltpu.VMEM((rows, 128), F32), in_send=dma((n - 1,)), in_recv=dma((n - 1,))
        )
    if o.weights:
        rows_of_pack = inputs["p_bc"][0].shape[1]
        pack_width = sum(v[0].shape[2] for k, v in inputs.items() if k.startswith("p_"))
        scratch.update(
            columns=pltpu.VMEM((*(2,) * o.bits, rows_of_pack, 128), BF),
            small_sem=dma(()),
            wown=pltpu.VMEM((rows_of_pack, pack_width), BF),
            wl_sem=dma(()),
            wg_send=dma((o.bits, o.weights)),
            wg_recv=dma((o.bits, o.weights)),
        )
    if o.grads:
        depth = o.width >> o.bits
        scratch.update(
            grad=pltpu.VMEM((o.grads, *(2,) * o.bits, depth, WCHUNK), BF),
            gr_send=dma((o.bits, o.grads)),
            gr_recv=dma((o.bits, o.grads)),
        )
        for stage in range(o.bits):
            scratch["gbuf%d" % stage] = pltpu.VMEM(
                (o.grads, *(2,) * (o.bits - 1 - stage), depth, WCHUNK), BF
            )
        scratch.update(
            gnear=pltpu.VMEM(outputs["gout"][0], F32), leave_sem=dma(()),
        )
        part = (n, (width >> o.bits) // n, o.states)
        scratch.update(
            qsend=pltpu.VMEM(part, BF), qall=pltpu.VMEM(part, BF),
            qbuf=pltpu.VMEM((n - 1,) + part[1:], BF),
            qs_send=dma((n - 1,)), qs_recv=dma((n - 1,)),
            qa_send=dma((n - 1,)), qa_recv=dma((n - 1,)),
        )
    if o.sums:
        def lanes_of(start):
            return sum(v[0].shape[1] for k, v in inputs.items() if k.startswith(start))

        lined, early, gains = lanes_of("lsum"), lanes_of("esum"), lanes_of("gsum")
        for one, two, tall, line_width, dp_width in (
            ("lb", "db", 8, lined, lined + early), ("gb", "hb", 1, gains, gains)
        ):
            scratch[one + "ank"] = pltpu.VMEM((n, tall, line_width), F32)
            scratch[two + "ank"] = pltpu.VMEM((o.bits + 1, tall, dp_width), F32)
            scratch[two + "uf"] = pltpu.VMEM((o.bits, tall, dp_width), F32)
            for key, size in ((one, n - 1), (two, o.bits)):
                scratch[key + "_send"] = dma((size,))
                scratch[key + "_recv"] = dma((size,))
    names = [*inputs, *outputs, *scratch]
    out = pl.pallas_call(
        functools.partial(comm_kernel, o, names),
        in_specs=[pl.BlockSpec(memory_space=i[1]) for i in inputs.values()],
        out_specs=[pl.BlockSpec(memory_space=i[2]) for i in outputs.values()],
        out_shape=[jax.ShapeDtypeStruct(i[0], i[1]) for i in outputs.values()],
        scratch_shapes=list(scratch.values()),
        compiler_params=pltpu.CompilerParams(
            collective_id=collective, has_side_effects=True, vmem_limit_bytes=62 * MIB
        ),
        name=name,
    )(*[i[0] for i in inputs.values()])
    return dict(zip(outputs, out))


def meet_kernel(
    n, inner_all, own_ref, grad_ref, mixed_ref, w_ref,
    out_ref, scale_ref, dm_ref, stage, near, bank, send, recv, sem,
):
    t = lax.axis_index("tensor")
    inner = near.shape[1]
    weight = pltpu.make_async_copy(w_ref.at[:, pl.ds(w_ref.shape[1] - inner, inner)], near, sem)
    weight.start()
    barrier = pltpu.get_barrier_semaphore()
    for k in range(1, n):
        pl.semaphore_signal(
            barrier, inc=1, device_id={"tensor": lax.rem(t + k, n)},
            device_id_type=pl.DeviceIdType.MESH,
        )
    stage[...] = own_ref[...]
    rows, cut = scale_ref.shape[0], grad_ref.shape[1]
    weight.wait()
    for s in range(n):
        dm = nn(grad_ref[s], near[...])
        dm_ref[s] = dm
        stage[1:2, (s + 1) * rows - cut : (s + 1) * rows] = token_dots(dm, mixed_ref[s])[0:1]
    pl.semaphore_wait(barrier, n - 1)
    copies = [
        remote(stage, bank.at[t], send.at[k - 1], recv.at[k - 1], {"tensor": lax.rem(t + k, n)})
        for k in range(1, n)
    ]
    for copy in copies:
        copy.start()
    bank[t] = stage[...]
    for k in range(1, n):
        source = lax.rem(t + n - k, n)
        remote(
            stage, bank.at[source], send.at[k - 1], recv.at[k - 1], {"tensor": source}
        ).wait_recv()
    total = bank[0]
    for s in range(1, n):
        total = total + bank[s]
    scale = lax.rsqrt(total[0:1, :] / inner_all + EPSILON)
    row = lax.broadcasted_iota(jnp.int32, total.shape, 0)
    e = scale * scale * scale * (total[1:2, :] / inner_all)
    out_ref[...] = jnp.where(row == 0, e, scale)
    mine = out_ref[:, pl.ds(pl.multiple_of(t * rows, rows), rows)].T
    scale_ref[...] = jnp.broadcast_to(mine[:, 1:2], scale_ref.shape)
    for copy in copies:
        copy.wait_send()


def meet(own, grad, mixed, packed, n, inner_all, collective):
    vmem = pl.BlockSpec(memory_space=pltpu.VMEM)
    dma = pltpu.SemaphoreType.DMA
    inner = mixed.shape[2]
    return pl.pallas_call(
        functools.partial(meet_kernel, n, inner_all),
        in_specs=[vmem, vmem, vmem, pl.BlockSpec(memory_space=pl.ANY)],
        out_specs=[vmem, vmem, vmem],
        out_shape=[
            jax.ShapeDtypeStruct(own.shape, F32),
            jax.ShapeDtypeStruct((own.shape[1] // n, 128), F32),
            jax.ShapeDtypeStruct(mixed.shape, F32),
        ],
        scratch_shapes=[
            pltpu.VMEM(own.shape, F32), pltpu.VMEM((packed.shape[0], inner), BF),
            pltpu.VMEM((n,) + own.shape, F32), dma((n - 1,)), dma((n - 1,)), dma(()),
        ],
        compiler_params=pltpu.CompilerParams(
            collective_id=collective, has_side_effects=True, vmem_limit_bytes=62 * MIB
        ),
        name="turn_around",
    )(own, grad, mixed, packed)


def plain_payload(r):
    return r.own[...]


def token_columns(first, second):
    lane = lax.broadcasted_iota(jnp.int32, (first.shape[0], 128), 1)
    return jnp.where(lane == 0, first, second)


def forward_middle(r, at, total):
    if at is None:
        return None
    branch = total * r.r2[at, 0:1]
    residual = r.res[at, :].astype(F32) + branch
    r.branch[at, :] = branch
    r.res_out[at, :] = residual
    r1 = lax.rsqrt(jnp.mean(residual * residual, axis=1, keepdims=True) + EPSILON)
    return (residual * r1 * r.gain[r.gain_row, :]).astype(BF)


def backward_middle(inner_all, r, at, total):
    if at is None:
        return None
    res = r.res[at, :].astype(F32)
    width = res.shape[1]
    r1 = lax.rsqrt(jnp.mean(res * res, axis=1, keepdims=True) + EPSILON)
    hat = res * r1
    dn = total * r.gain[r.gain_row, :]
    cross = jnp.sum(dn * hat, axis=1, keepdims=True) / width
    grad = r.grad_in[at, :].astype(F32) + r1 * (dn - hat * cross)
    r.grad_out[at, :] = grad
    if inner_all is None:
        return None
    r2 = r.r2[at, 0:1]
    dot = jnp.sum(grad.astype(BF).astype(F32) * r.branch[at, :], axis=1, keepdims=True)
    r.icol[at, :] = token_columns(r2 * r2 * dot / inner_all, r2)
    return grad.astype(BF)


def assemble_kernel(layers, dp_count, heads, bc_width, inner, *refs):
    gouts, (sums, gains, pick), refs = refs[:layers], refs[layers : layers + 3], refs[layers + 3 :]
    res, scale, *halves = refs[:4]
    norm, gz, gx, gbc, gdt, cv, cvb, cs, csb, sb, ld, sk, gg, po, hidden = refs[4:]
    me = lax.axis_index("dp")
    start = 0
    for half in halves:
        at = slice(start, start + half.shape[0])
        start += half.shape[0]
        hidden[at, :] = res[at, :] + scale[at, 0:1] * half[...].astype(F32)

    def own(v):
        share = v.shape[1] // dp_count
        return pltpu.roll(v, v.shape[1] - me * share, 1)[:, :share]

    norm[...] = own(gains[...])[0:layers]
    for l in range(layers):
        full = gouts[l]
        first = bc_width + 128
        gbc[l] = full[:, 0:bc_width]
        gdt[:, l, :] = full[:, bc_width:first].T[0:heads, :]
        gz[l] = full[:, first : first + inner]
        gx[l] = full[:, first + inner : first + 2 * inner]
        po[l] = full[:, first + 2 * inner :]
        base = l * (inner + 128)
        vec = sums[:, base : base + inner]
        step = sums[:, base + inner : base + inner + 128]
        start = layers * (inner + 128) + l * bc_width
        state = own(sums[:, start : start + bc_width])
        cv[l] = vec[0:4]
        cvb[l : l + 1] = vec[4:5]
        gg[l : l + 1] = vec[5:6]
        one, two, three = parts3(vec)
        head_sums = nn(one, pick[...]) + nn(two, pick[...]) + nn(three, pick[...])
        sk[l : l + 1] = head_sums[6:7, 0:heads]
        sb[l : l + 1] = step[0:1, 0:heads]
        ld[l : l + 1] = step[1:2, 0:heads]
        cs[l] = state[0:4]
        csb[l : l + 1] = state[4:5]


def assemble(gouts, sums, gains, pick, dp_count, heads, bc_width, inner, hidden):
    layers, (rows, _) = len(gouts), gouts[0].shape
    vmem = pl.BlockSpec(memory_space=pltpu.VMEM)
    share = bc_width // dp_count
    shapes = [
        (layers, gains.shape[1] // dp_count),
        (layers, rows, inner), (layers, rows, inner), (layers, rows, bc_width),
        (heads, layers, rows), (layers, 4, inner), (layers, inner), (layers, 4, share),
        (layers, share), (layers, heads), (layers, heads), (layers, heads), (layers, inner),
        (layers, rows, inner), hidden[0].shape,
    ]
    inputs = [*gouts, sums, gains, pick, *hidden]
    return pl.pallas_call(
        functools.partial(assemble_kernel, layers, dp_count, heads, bc_width, inner),
        in_specs=[vmem] * len(inputs),
        out_specs=[vmem] * len(shapes),
        out_shape=[jax.ShapeDtypeStruct(v, F32) for v in shapes],
        compiler_params=pltpu.CompilerParams(vmem_limit_bytes=62 * MIB),
        name="assemble",
    )(*inputs)


def shards(
    hidden_in,
    out_grad,
    norm_gain,
    proj_z,
    proj_x,
    proj_bc,
    proj_dt,
    conv_value,
    conv_value_bias,
    conv_state,
    conv_state_bias,
    step_bias,
    log_decay,
    skip_gain,
    gate_gain,
    proj_out,
):
    tensor_count = lax.axis_size("tensor")
    dp_count = lax.axis_size("dp")
    bits = dp_count.bit_length() - 1
    layers, shard_rows, inner = proj_z.shape
    rows_own, width = hidden_in.shape
    tokens = rows_own * tensor_count
    heads = step_bias.shape[1]
    bc_width = proj_bc.shape[2]
    inner_all = inner * tensor_count
    packed_width = bc_width + 128 + 3 * inner
    column_chunks, row_chunks = packed_width // WCHUNK, shard_rows // 16
    vmem, far = pltpu.VMEM, pl.ANY

    taps = jnp.concatenate([conv_state, conv_state_bias[:, None]], axis=1)
    taps = jnp.pad(taps, ((0, 0), (0, 0), (0, shard_rows - taps.shape[2])))
    extra = jnp.concatenate([norm_gain[:, None], taps], axis=1)
    per_layer = extra.shape[1]
    extra = extra.reshape(per_layer * layers, shard_rows).T
    step_block = jnp.concatenate(
        [
            proj_dt,
            jnp.broadcast_to(extra[None], (layers,) + extra.shape),
            jnp.zeros((layers, shard_rows, 128 - heads - extra.shape[1]), BF),
        ],
        axis=2,
    )
    out_turned = jnp.transpose(proj_out, (0, 2, 1))
    full_shape = ((2,) * bits) + (shard_rows, packed_width)
    common = dict(rows=rows_own, width=width, line=tensor_count, bits=bits)

    weight_in = dict(
        p_bc=(proj_bc, vmem), p_dt=(step_block, vmem), p_z=(proj_z, vmem), p_x=(proj_x, vmem),
        p_out=(out_turned, vmem),
    )
    weight_out = dict(wfull=(full_shape, BF, far))

    vec = jnp.concatenate(
        [
            conv_value,
            conv_value_bias[:, None],
            jnp.repeat(skip_gain, WIDTH, axis=1)[:, None],
            gate_gain[:, None],
        ],
        axis=1,
    ).astype(F32)
    tiny = jnp.stack([step_bias.astype(F32), -jnp.exp(log_decay.astype(F32))], axis=1)
    tiny = jnp.pad(tiny, ((0, 0), (0, 0), (0, 128 - heads)))
    pick = jnp.asarray(np.arange(inner)[:, None] // WIDTH == np.arange(128)[None, :], BF)

    whole_rows, own_rows = ((tokens, width), BF, vmem), ((rows_own, width), F32, vmem)
    got = comm_call(
        Step(gather=True, payload=plain_payload, weights=row_chunks,
             small=bc_width + heads, **common),
        "gather_first", 1,
        dict(own=(hidden_in, vmem), **weight_in),
        dict(full=whole_rows, small=((16, width), F32, vmem), **weight_out),
    )
    x_rows = got["full"]
    out_grad, x_rows = lax.optimization_barrier((out_grad, x_rows))
    cut = rows_own * 5 // 8

    def gather_half(v):
        return lax.all_gather(v, "tensor", axis=0)

    first_half = gather_half(out_grad[:cut])
    packed = [got["wfull"].reshape(width, packed_width)]
    small = got["small"]
    per = bc_width // dp_count
    smalls = small[: per_layer * layers].reshape(layers, per_layer, dp_count, shard_rows)
    cst = smalls[:, 1:, :, :per].reshape(layers, per_layer - 1, bc_width)
    params = (vec, cst, tiny, small)

    out = forward_mix(x_rows, packed[0], params, 0)
    saved, rows = [out[:7]], [out[9]]
    residuals, branches, r2s = [hidden_in], [], []
    for l in range(layers - 1):
        got = comm_call(
            Step(
                partial=True, gather=True, late=True, scale=inner_all, middle=forward_middle, chunks=16,
                early=("branch", "res_out"),
                weights=row_chunks, layer=l + 1, gain_row=per_layer * (l + 1), **common,
            ),
            "between_forward", 2 + l,
            dict(part=(out[8], vmem), ssq=(out[7], vmem), res=(residuals[l], vmem),
                 gain=(small, vmem), **weight_in),
            dict(full=whole_rows, branch=own_rows, res_out=own_rows,
                 r2=((rows_own, 128), F32, vmem), **weight_out),
        )
        if l + 1 == layers - 1:
            last_grad, got["full"] = lax.optimization_barrier((out_grad[cut:], got["full"]))
            second_half = gather_half(last_grad)
        rows.append(got["full"])
        branches.append(got["branch"])
        residuals.append(got["res_out"])
        r2s.append(got["r2"])
        packed.append(got["wfull"].reshape(width, packed_width))
        gb = first_half if l + 1 == layers - 1 else None
        out = forward_mix(rows[-1], packed[-1], params, l + 1, gb)
        saved.append(out[:7])
    def scatter_half(v):
        return lax.psum_scatter(
            v.reshape(-1, width), "tensor", scatter_dimension=0, tiled=True
        )

    branch_halves = [scatter_half(out[8])]
    token_rows, r2_own, second_product = meet(
        out[7], second_half, out[11], packed[-1], tensor_count, inner_all, 16
    )
    grad_rows = None
    gradient = out_grad
    scattered, summed, gain_grads = [None] * layers, [None] * layers, [None] * layers
    for l in reversed(range(layers)):
        last = l == layers - 1
        dcat, dpart, *small_grads = backward_mix(
            (out[10], second_product) if last else grad_rows, last, token_rows, rows[l], saved[l],
            packed[l], params, pick, l,
        )
        summed[l], gain_grads[l] = small_grads[:3], small_grads[3]
        more = l > 0
        inputs = dict(
            part=(dpart, vmem), res=(residuals[l], vmem), gain=(small, vmem),
            grad_in=(gradient, vmem), lrows=(rows[l], vmem), right=(dcat, vmem),
        )
        if last:
            inputs.update(half0=(first_half, far), half1=(second_half, far))
        else:
            inputs.update(lgrad=(grad_rows, vmem))
        outputs = dict(
            grad_out=own_rows,
            gout=((shard_rows, packed_width), F32, far),
        )
        if more:
            inputs.update(r2=(r2s[l - 1], vmem), branch=(branches[l - 1], vmem))
            outputs.update(full=whole_rows, inner=((8, tokens), F32, vmem))
        else:
            for i in range(layers):
                gvec, gst, gdt = summed[i]
                inputs["esum%d" % i], inputs["esum_%d" % i] = (gvec, vmem), (gdt, vmem)
                inputs["lsum%d" % i] = (gst, vmem)
            for i in range(layers):
                inputs["gsum%d" % i] = (gain_grads[i], vmem)
            early = sum(v.shape[1] for i in range(layers) for v in summed[i])
            outputs.update(
                sums=((8, early), F32, vmem), gain_sums=((8, width), F32, vmem)
            )
        got = comm_call(
            Step(
                partial=True, gather=more, late=more, inner=more, grads=column_chunks,
                chunks=16 if more else 8, lag=3 if more else 1,
                states=bc_width, sums=not more, gain_row=per_layer * l,
                early=("grad_out",), halves=last, double=0 if more else 2,
                lazy=("right", "lrows", "res", "grad_in")
                + (() if last else ("lgrad",)) + (("branch",) if more else ()),
                middle=functools.partial(backward_middle, inner_all if more else None), **common,
            ),
            "between_backward" if more else "last_backward", 17 + l, inputs, outputs,
        )
        gradient = got["grad_out"]
        scattered[l] = got["gout"]
        if more:
            grad_rows, token_rows = got["full"], got["inner"]
        if last:
            second_part, gradient = lax.optimization_barrier((out[9], gradient))
            branch_halves.append(scatter_half(second_part))
    grads = list(
        assemble(
            scattered, got["sums"], got["gain_sums"], pick, dp_count, heads, bc_width, inner,
            [residuals[-1], r2_own, *branch_halves],
        )
    )
    hidden_out = grads.pop()
    grads[4] = jnp.transpose(grads[4], (1, 2, 0))
    grads[-1] = jnp.transpose(grads[-1], (0, 2, 1))
    return (hidden_out, gradient, *grads)


def solution(mesh):
    placed = (
        P(("dp", "tensor"), None),
        P(("dp", "tensor"), None),
        P(None, "dp"),
        P(None, "dp", "tensor"),
        P(None, "dp", "tensor"),
        P(None, "dp", None),
        P(None, "dp", "tensor"),
        P(None, None, "tensor"),
        P(None, "tensor"),
        P(None, None, "dp"),
        P(None, "dp"),
        P(None, "tensor"),
        P(None, "tensor"),
        P(None, "tensor"),
        P(None, "tensor"),
        P(None, "tensor", "dp"),
    )
    return jax.shard_map(
        shards,
        mesh=mesh,
        in_specs=placed,
        out_specs=(
            P(("dp", "tensor"), None),
            P(("dp", "tensor"), None),
            P(None, "dp"),
            P(None, "dp", "tensor"),
            P(None, "dp", "tensor"),
            P(None, "dp", None),
            P(None, "dp", "tensor"),
            P(None, None, "tensor"),
            P(None, "tensor"),
            P(None, None, "dp"),
            P(None, "dp"),
            P(None, "tensor"),
            P(None, "tensor"),
            P(None, "tensor"),
            P(None, "tensor"),
            P(None, "tensor", "dp"),
        ),
        check_vma=False,
    )
```
